32 devices in a mesh: band: 4 (over y, x), loc: 8 (over z, core).
Axes of the slice: x: 2, y: 2, z: 4, core: 2. Of those that a mesh axis runs over, the one named last changes fastest.
Arguments:
- tokens: bfloat16 [2048, 16, 768], P('loc', 'band'), may hold values from -6 to 6
- band_index: int32 [16], replicated, may hold values from 0 to 15, each once
- band_table: float32 [16, 768], replicated, may hold values from -3 to 3
- window_ids: int32 [2048], replicated, may hold values from 0 to 1, as said below
- spatial_qkv: bfloat16 [768, 2304], replicated
- spatial_out: bfloat16 [768, 768], replicated, may hold values from -0.21875 to 0.21875
- channel_qkv: bfloat16 [768, 2304], replicated
- channel_out: bfloat16 [768, 768], replicated, may hold values from -0.21875 to 0.21875
- up_weight: bfloat16 [768, 3072], replicated, may hold values from -0.21875 to 0.21875
- down_weight: bfloat16 [3072, 768], replicated, may hold values from -0.109375 to 0.109375
Outputs:
- joined: bfloat16 [2048, 16, 768], P('loc', 'band')
The draws below stay inside these ranges and needn't reach their ends.
Inputs may be any that keep to these rules, and one draw needn't show every extreme that they name: `window_ids`: each of the 2 windows holds exactly 1024 locations, and each aligned block of 256 locations holds exactly 128 locations of each window. `band_index`: each of the 16 band numbers once.
All inputs are finite; a program needn't handle non-finite values.
Results may differ from the reference program's by a relative error of at most 0.014.
Values may be sent and summed in bfloat16 or wider, within the bound.
No kernel may reach another device: no remote copies, remote signals or barrier semaphores. Data moves between devices by JAX's collectives and lax.ppermute only.
A program may use at most 128 MiB of HBM per device.

```python
import jax
import jax.numpy as jnp
from jax import lax

D = 768
HEADS = 12
HEAD_DIM = 64
FF = 3072
BANDS = 16
LOC_DEV = 256
WINDOWS = 2
LOCS = 2048


def draw_window_ids(key, part):
    blocks = LOCS // LOC_DEV
    keys = jax.random.split(jax.random.fold_in(key, 7), blocks)
    order = jax.vmap(lambda one: jax.random.permutation(one, LOC_DEV))(keys)
    return (order % WINDOWS).reshape(LOCS).astype(jnp.int32)


def projection_draw(key, salt):
    first, second, third = jax.random.split(jax.random.fold_in(key, salt), 3)
    factor = D ** (-0.5)
    w_query = jax.random.normal(first, (D, D), jnp.float32) * factor
    w_value = jax.random.normal(third, (D, D), jnp.float32) * factor
    w_key = jax.random.normal(second, (D, D), jnp.float32) * factor
    return jnp.concatenate([w_query, w_key, w_value], axis=1)


def draw_spatial_qkv(key, part):
    return projection_draw(key, 11).astype(jnp.bfloat16)


def draw_channel_qkv(key, part):
    return projection_draw(key, 23).astype(jnp.bfloat16)


def level_of(stream_key, shape, shards, smallest, top_value):
    factor_of = 1.0
    for position, blocks in shards:
        draws = jax.random.uniform(jax.random.fold_in(jax.random.fold_in(stream_key, 6), position), (blocks,), jnp.float32, smallest / len(shards), top_value / len(shards))
        factor_of = factor_of * jnp.repeat(jnp.exp(draws), shape[position] // blocks).reshape((-1,) + (1,) * (len(shape) - 1 - position))
    return factor_of


def noise(rng, extent, width, bound, pieces=(), kind=jnp.bfloat16):
    array = jax.random.normal(rng, extent, jnp.float32) * width
    if len(pieces) > 0:
        array = level_of(rng, extent, pieces, -0.22, 0.18) * array
    return jnp.clip(array, min=-bound, max=bound).astype(kind)


def setup_inputs(seed: int = 0) -> dict:
    splits = jax.random.split(jax.random.key(seed), 11)
    return {
        "tokens": noise(splits[0], (LOCS, BANDS, D), 1.0, 6.0, ((0, 8), (1, 4))),
        "band_index": jax.random.permutation(splits[1], BANDS).astype(jnp.int32),
        "band_table": noise(splits[2], (BANDS, D), 0.5, 3.0, (), jnp.float32),
        "window_ids": draw_window_ids(jax.random.fold_in(splits[10], 71), 0),
        "spatial_qkv": draw_spatial_qkv(jax.random.fold_in(splits[10], 71), 0),
        "spatial_out": noise(splits[5], (D, D), D ** -0.5, 0.21875),
        "channel_qkv": draw_channel_qkv(jax.random.fold_in(splits[10], 71), 0),
        "channel_out": noise(splits[7], (D, D), D ** -0.5, 0.21875),
        "up_weight": noise(splits[8], (D, FF), D ** -0.5, 0.21875),
        "down_weight": noise(splits[9], (FF, D), FF ** -0.5, 0.109375),
    }


def norm_rows(values):
    centre = values - lax.optimization_barrier(jnp.mean(values, axis=-1, keepdims=True))
    spread = lax.optimization_barrier(jnp.mean(centre * centre, axis=-1, keepdims=True))
    return centre * lax.rsqrt(spread + 1e-05)

def reference(tokens, band_index, band_table, window_ids, spatial_qkv, spatial_out, channel_qkv, channel_out, up_weight, down_weight):
    scale = HEAD_DIM ** (-0.5)
    onehot = (band_index[:, None] == jnp.arange(BANDS, dtype=jnp.int32)[None, :]).astype(jnp.float32)
    embed = jnp.dot(onehot, band_table, precision=lax.Precision.HIGHEST)
    start = tokens.astype(jnp.float32) + embed[None]
    normed = norm_rows(start).astype(jnp.bfloat16).reshape(-1, D)
    sqkv = jnp.dot(normed, spatial_qkv, preferred_element_type=jnp.float32).astype(jnp.bfloat16)
    sqkv = sqkv.reshape(LOCS, BANDS, 3, HEADS, HEAD_DIM)
    same = window_ids[:, None] == window_ids[None, :]

    def one_head(index):
        band = index // HEADS
        head = index % HEADS
        query = sqkv[:, band, 0, head]
        keys = sqkv[:, band, 1, head]
        values = sqkv[:, band, 2, head]
        scores = jnp.dot(query, keys.T, preferred_element_type=jnp.float32) * scale
        masked = jnp.where(same, scores, -1e+30)
        peak = lax.optimization_barrier(jnp.max(masked, axis=-1, keepdims=True))
        expo = jnp.where(same, jnp.exp(masked - peak), 0.0)
        total = lax.optimization_barrier(jnp.sum(expo, axis=-1, keepdims=True))
        summed = jnp.dot(expo.astype(jnp.bfloat16), values, preferred_element_type=jnp.float32)
        return (summed / total).astype(jnp.bfloat16)
    heads_out = lax.map(one_head, jnp.arange(BANDS * HEADS, dtype=jnp.int32))
    sattn = heads_out.reshape(BANDS, HEADS, LOCS, HEAD_DIM).transpose(2, 0, 1, 3).reshape(-1, D)
    mid = (start.reshape(-1, D) + jnp.dot(sattn, spatial_out, preferred_element_type=jnp.float32)).astype(jnp.bfloat16)
    normed2 = norm_rows(mid.astype(jnp.float32)).astype(jnp.bfloat16)
    cqkv = jnp.dot(normed2, channel_qkv, preferred_element_type=jnp.float32).astype(jnp.bfloat16)
    cqkv = cqkv.reshape(LOCS, BANDS, 3, HEADS, HEAD_DIM).astype(jnp.float32)
    cscores = jnp.einsum('lbhe,lche->lhbc', cqkv[:, :, 0], cqkv[:, :, 1]) * scale
    cpeak = lax.optimization_barrier(jnp.max(cscores, axis=-1, keepdims=True))
    cex = jnp.exp(cscores - cpeak)
    ctotal = lax.optimization_barrier(jnp.sum(cex, axis=-1))
    csum = jnp.einsum('lhbc,lche->lbhe', cex.astype(jnp.bfloat16).astype(jnp.float32), cqkv[:, :, 2])
    cattn = (csum / jnp.transpose(ctotal, (0, 2, 1))[..., None]).astype(jnp.bfloat16).reshape(-1, D)
    after = mid.astype(jnp.float32) + jnp.dot(cattn, channel_out, preferred_element_type=jnp.float32)
    normed3 = norm_rows(after).astype(jnp.bfloat16)
    hidden = jax.nn.gelu(jnp.dot(normed3, up_weight, preferred_element_type=jnp.float32), approximate=True).astype(jnp.bfloat16)
    joined = after + jnp.dot(hidden, down_weight, preferred_element_type=jnp.float32)
    return joined.astype(jnp.bfloat16).reshape(LOCS, BANDS, D)
```

```python
import functools

import jax
import jax.numpy as jnp
from jax import lax
from jax.experimental import pallas as pl
from jax.experimental.pallas import tpu as pltpu
from jax.sharding import PartitionSpec as P

HEADS = 12
HEAD_DIM = 64
WINDOWS = 2
CHUNKS = 2
LATE_SLOTS = 2
TILE_LOCS = 16
LANES = 128
QUERY_SCALE = HEAD_DIM ** (-0.5) * 1.4426950408889634
VMEM_LIMIT = 56 * 1024 * 1024

F32 = jnp.float32
BF16 = jnp.bfloat16


def dot(left, right):
    return jnp.dot(left, right, preferred_element_type=F32)


def dot_t(left, right):
    return lax.dot_general(left, right, (((1,), (1,)), ((), ())), preferred_element_type=F32)


def norm_rows(values):
    centre = values - jnp.mean(values, axis=-1, keepdims=True)
    spread = jnp.mean(centre * centre, axis=-1, keepdims=True)
    return centre * lax.rsqrt(spread + 1e-05)


def call(kernel, out_shape, flops, nbytes, **kwargs):
    return pl.pallas_call(
        kernel,
        out_shape=out_shape,
        compiler_params=pltpu.CompilerParams(vmem_limit_bytes=VMEM_LIMIT),
        cost_estimate=pl.CostEstimate(flops=flops, bytes_accessed=nbytes, transcendentals=0),
        **kwargs,
    )


def exchange(value, axis, step):
    if step == 0:
        return value
    return lax.ppermute(value, axis, [(i, i ^ step) for i in range(lax.axis_size(axis))])


class Plan:
    def __init__(self, tokens):
        self.loc_dev, self.band_dev, self.width = tokens.shape
        self.locs = lax.axis_size("loc")
        self.groups = lax.axis_size("band")
        self.share = self.locs // (self.band_dev * WINDOWS)
        assert self.share * self.band_dev * WINDOWS == self.locs
        self.block = self.loc_dev // WINDOWS
        self.rows = self.block // self.share
        self.chunks = CHUNKS
        self.chunk_rows = self.rows // self.chunks
        self.part_rows = self.chunk_rows // self.groups
        assert self.part_rows * self.groups * self.chunks * self.share == self.block


def location_keys(plan, ids):
    size = plan.loc_dev
    row = jnp.broadcast_to(ids.astype(F32), (size, size))
    first = lax.broadcasted_iota(jnp.int32, (size, size), 0)
    second = lax.broadcasted_iota(jnp.int32, (size, size), 1)
    column = jnp.sum(jnp.where(first == second, row, 0.0), axis=1, keepdims=True)
    before = jnp.where((column == row) & (first < second), 1.0, 0.0)
    rank = jnp.sum(before, axis=0, keepdims=True)
    return ids.astype(F32) * plan.block + rank


def arrange(plan, tokens, ids):
    def kernel(ids_ref, x_ref, *rest):
        outs, bands = rest[: plan.locs], rest[plan.locs]
        me = lax.axis_index("loc")
        group = lax.axis_index("band")
        keys = location_keys(plan, ids_ref[pl.ds(me, 1), :])
        for band in range(plan.band_dev):
            bands[band] = x_ref[:, band, :]
        place = lax.broadcasted_iota(jnp.int32, (plan.rows, plan.loc_dev), 0)
        chunk = place // plan.chunk_rows
        owner = (place // plan.part_rows) % plan.groups
        rank = chunk * plan.chunk_rows + (owner ^ group) * plan.part_rows + place % plan.part_rows
        for slot in range(plan.locs):
            peer = me ^ slot
            window = peer % WINDOWS
            part = (peer // WINDOWS) % plan.share
            band = peer // (WINDOWS * plan.share)
            wanted = rank + (window * plan.block + part * plan.rows)
            pick = jnp.where(wanted.astype(F32) == keys, 1.0, 0.0).astype(BF16)
            outs[slot][...] = dot(pick, bands[band]).astype(BF16)

    shape = jax.ShapeDtypeStruct((plan.rows, plan.width), BF16)
    return call(
        kernel,
        [shape] * plan.locs,
        2 * plan.loc_dev * tokens.size,
        4 * tokens.size,
        scratch_shapes=[pltpu.VMEM((plan.band_dev, plan.loc_dev, plan.width), BF16)],
    )(ids, tokens)


def embed_row(plan, index_ref, table_ref):
    band = lax.axis_index("loc") // (WINDOWS * plan.share)
    number = index_ref[lax.axis_index("band") * plan.band_dev + band]
    return table_ref[pl.ds(number, 1), :]


SMEM = pl.BlockSpec(memory_space=pltpu.SMEM)
VMEM = pl.BlockSpec(memory_space=pltpu.VMEM)


def project(plan, slots, index, table, weights):
    count = len(slots)
    width = plan.width

    def kernel(index_ref, table_ref, w_ref, *rest):
        ins, (q_ref, k_ref, v_ref) = rest[:count], rest[count:]
        embed = embed_row(plan, index_ref, table_ref)
        for first in range(0, count, 2):
            some = ins[first : first + 2]
            rows = jnp.concatenate([ref[...].astype(F32) for ref in some], axis=0) + embed
            normed = norm_rows(rows).astype(BF16)
            here = pl.ds(first * plan.rows, len(some) * plan.rows)
            q_ref[here, :] = (dot(normed, w_ref[:, :width]) * QUERY_SCALE).astype(BF16)
            k_ref[here, :] = dot(normed, w_ref[:, width : 2 * width]).astype(BF16)
            v_ref[here, :] = dot(normed, w_ref[:, 2 * width :]).astype(BF16)

    rows = count * plan.rows
    shape = jax.ShapeDtypeStruct((rows, width), BF16)
    return call(
        kernel,
        [shape] * 3,
        2 * rows * width * 3 * width,
        2 * (4 * rows * width + 3 * width * width),
        in_specs=[SMEM, VMEM, VMEM] + [VMEM] * count,
    )(index, table, weights, *slots)


def head_sums(scores, values, ones):
    peak = functools.reduce(
        jnp.maximum, [jnp.max(piece, axis=-1, keepdims=True) for piece in scores]
    )
    total = None
    for piece, value in zip(scores, values):
        part = dot(
            jnp.exp2(piece - peak).astype(BF16), jnp.concatenate([value, ones(value)], axis=1)
        )
        total = part if total is None else total + part
    return total[:, :LANES] / total[:, LANES:]


def ones_like_block(value):
    return jnp.ones(value.shape, BF16)


def pair_attention(query, keys, values, mask=None):
    lane = lax.broadcasted_iota(jnp.int32, query.shape, 1)
    result = None
    for head in range(LANES // HEAD_DIM):
        inside = (lane // HEAD_DIM) == head
        only = jnp.where(inside, query, jnp.zeros_like(query))
        scores = [dot_t(only, piece) for piece in keys]
        if mask is not None:
            scores = [jnp.where(mask, piece, -1e30) for piece in scores]
        mine = head_sums(scores, values, ones_like_block)
        result = mine if result is None else jnp.where(inside, mine, result)
    return result.astype(BF16)


def attend(plan, chunk, query, keys, values, slots, index, table, spatial_out):
    width, rows = plan.width, plan.chunk_rows
    pieces, sources = len(keys), len(query)
    counts = [piece.shape[0] // plan.rows for piece in query]
    total = plan.locs * rows
    pairs = width // LANES

    def kernel(index_ref, table_ref, w_ref, *rest):
        q_refs, rest = rest[:sources], rest[sources:]
        k_refs, rest = rest[:pieces], rest[pieces:]
        v_refs, rest = rest[:pieces], rest[pieces:]
        slot_refs, rest = rest[: plan.locs], rest[plan.locs :]
        outs, result = rest[: plan.locs], rest[plan.locs]
        pair = pl.program_id(0)
        query_rows = jnp.concatenate(
            [ref[...].reshape(count * rows, LANES) for ref, count in zip(q_refs, counts)], axis=0
        )
        result[pair] = pair_attention(
            query_rows, [ref[...] for ref in k_refs], [ref[...] for ref in v_refs]
        )

        @pl.when(pair == pairs - 1)
        def _():
            embed = embed_row(plan, index_ref, table_ref)
            attended = jnp.concatenate([result[i] for i in range(pairs)], axis=1)
            added = dot(attended, w_ref[...])
            for slot in range(plan.locs):
                start = slot_refs[slot][...].astype(F32) + embed
                outs[slot][...] = (start + added[slot * rows : (slot + 1) * rows]).astype(BF16)

    q_specs = [pl.BlockSpec((count, rows, LANES), lambda p: (0, chunk, p)) for count in counts]
    kv_specs = [pl.BlockSpec((piece.shape[0], LANES), lambda p: (0, p)) for piece in keys]
    slot_specs = [pl.BlockSpec((rows, width), lambda p: (chunk, 0))] * plan.locs
    out_specs = [pl.BlockSpec((rows, width), lambda p: (0, 0))] * plan.locs
    key_rows = sum(piece.shape[0] for piece in keys)
    return call(
        kernel,
        [jax.ShapeDtypeStruct((rows, width), BF16)] * plan.locs,
        16 * total * key_rows * width,
        2 * width * (2 * key_rows + 3 * total + width),
        grid=(pairs,),
        in_specs=[SMEM, VMEM, VMEM] + q_specs + kv_specs + kv_specs + slot_specs,
        out_specs=out_specs,
        scratch_shapes=[pltpu.VMEM((pairs, total, LANES), BF16)],
    )(
        index,
        table,
        spatial_out,
        *[piece.reshape(count, plan.rows, width) for piece, count in zip(query, counts)],
        *keys,
        *values,
        *slots,
    )


def regroup(plan, slots):
    rows = plan.part_rows
    if rows % 16:
        stacked = jnp.stack(slots).reshape(plan.locs, plan.groups, rows, plan.width)
        return [stacked[:, owner] for owner in range(plan.groups)]

    def kernel(*refs):
        ins, outs, sems = refs[: plan.locs], refs[plan.locs : -1], refs[-1]
        copies = [
            pltpu.make_async_copy(
                ins[slot].at[pl.ds(owner * rows, rows), :],
                outs[owner].at[slot],
                sems.at[slot * plan.groups + owner],
            )
            for slot in range(plan.locs)
            for owner in range(plan.groups)
        ]
        for copy in copies:
            copy.start()
        for copy in copies:
            copy.wait()

    shape = jax.ShapeDtypeStruct((plan.locs, rows, plan.width), BF16)
    anywhere = pl.BlockSpec(memory_space=pl.ANY)
    return call(
        kernel,
        [shape] * plan.groups,
        0,
        4 * plan.locs * plan.chunk_rows * plan.width,
        in_specs=[anywhere] * plan.locs,
        out_specs=[anywhere] * plan.groups,
        scratch_shapes=[pltpu.SemaphoreType.DMA((plan.locs * plan.groups,))],
    )(*slots)


def channel(plan, parts, channel_qkv, channel_out, up_weight, down_weight):
    groups, width = plan.groups, plan.width
    bands, locations, _ = parts[0].shape
    tile = TILE_LOCS
    assert locations % tile == 0
    rows = groups * bands * tile

    def kernel(qkv_ref, out_ref, up_ref, down_ref, *refs):
        ins, outs = refs[:groups], refs[groups:]
        mid = jnp.concatenate(
            [ref[...].reshape(bands * tile, width) for ref in ins], axis=0
        ).astype(F32)
        normed = norm_rows(mid).astype(BF16)
        query = (dot(normed, qkv_ref[:, :width]) * QUERY_SCALE).astype(BF16)
        keys = dot(normed, qkv_ref[:, width : 2 * width]).astype(BF16)
        values = dot(normed, qkv_ref[:, 2 * width :]).astype(BF16)
        first = lax.broadcasted_iota(jnp.int32, (rows, rows), 0)
        second = lax.broadcasted_iota(jnp.int32, (rows, rows), 1)
        mask = (first % tile) == (second % tile)
        attended = []
        for pair in range(width // LANES):
            here = slice(pair * LANES, (pair + 1) * LANES)
            attended.append(
                pair_attention(query[:, here], [keys[:, here]], [values[:, here]], mask)
            )
        after = mid + dot(jnp.concatenate(attended, axis=1), out_ref[...])
        normed = norm_rows(after).astype(BF16)
        hidden = jax.nn.gelu(dot(normed, up_ref[...]), approximate=True).astype(BF16)
        joined = (after + dot(hidden, down_ref[...])).astype(BF16)
        for owner in range(groups):
            outs[owner][...] = joined[owner * bands * tile : (owner + 1) * bands * tile].reshape(
                bands, tile, width
            )

    block = pl.BlockSpec((bands, tile, width), lambda i: (0, i, 0))
    weights = channel_qkv.size + channel_out.size + up_weight.size + down_weight.size
    count = groups * bands * locations
    return call(
        kernel,
        [jax.ShapeDtypeStruct((bands, locations, width), BF16)] * groups,
        2 * count * weights,
        2 * (2 * count * width + weights),
        grid=(locations // tile,),
        in_specs=[VMEM] * 4 + [block] * groups,
        out_specs=[block] * groups,
    )(channel_qkv, channel_out, up_weight, down_weight, *parts)


def restore(plan, ids, returned):
    locations = plan.loc_dev // (plan.chunks * plan.groups)

    def kernel(ids_ref, *refs):
        ins, out_ref = refs[:-1], refs[-1]
        me = lax.axis_index("loc")
        group = lax.axis_index("band")
        keys = location_keys(plan, ids_ref[pl.ds(me, 1), :])
        place = lax.broadcasted_iota(jnp.int32, (plan.loc_dev, plan.loc_dev), 0)
        inner = place % plan.part_rows
        window = (place // plan.part_rows) % WINDOWS ^ (me % WINDOWS)
        part = (place // (plan.part_rows * WINDOWS)) % plan.share ^ (me // WINDOWS) % plan.share
        owner = (place // locations) % plan.groups ^ group
        chunk = place // (locations * plan.groups)
        wanted = (
            window * plan.block
            + part * plan.rows
            + chunk * plan.chunk_rows
            + owner * plan.part_rows
            + inner
        )
        pick = jnp.where(wanted.astype(F32) == keys, 1.0, 0.0).astype(BF16)
        mine = me // (WINDOWS * plan.share)
        for band in range(plan.band_dev):
            rows = jnp.concatenate([ref[band ^ mine] for ref in ins], axis=0)
            out_ref[:, band, :] = lax.dot_general(
                pick, rows, (((0,), (0,)), ((), ())), preferred_element_type=F32
            ).astype(BF16)

    arrays = [array for chunk in returned for array in chunk]
    size = plan.loc_dev * plan.band_dev * plan.width
    return call(
        kernel,
        jax.ShapeDtypeStruct((plan.loc_dev, plan.band_dev, plan.width), BF16),
        2 * plan.loc_dev * size,
        4 * size,
    )(ids, *arrays)


def body(
    tokens,
    band_index,
    band_table,
    window_ids,
    spatial_qkv,
    spatial_out,
    channel_qkv,
    channel_out,
    up_weight,
    down_weight,
):
    plan = Plan(tokens)
    ids = window_ids.reshape(plan.locs, plan.loc_dev)
    sent = arrange(plan, tokens, ids)
    slots = [exchange(value, "loc", step) for step, value in enumerate(sent)]
    split = plan.locs - LATE_SLOTS
    early = project(plan, slots[:split], band_index, band_table, spatial_qkv)
    late = project(plan, slots[split:], band_index, band_table, spatial_qkv)
    query, keys, values = zip(early, late)
    if plan.share > 1:
        same = [
            [(band * plan.share + part) * WINDOWS + window for part in range(plan.share)]
            for band in range(plan.band_dev)
            for window in range(WINDOWS)
        ]
        gather = functools.partial(
            lax.all_gather, axis_name="loc", axis_index_groups=same, axis=0, tiled=True
        )
        keys = [gather(jnp.concatenate(keys, axis=0))]
        values = [gather(jnp.concatenate(values, axis=0))]
    returned = []
    for chunk in range(plan.chunks):
        mid = attend(
            plan, chunk, query, keys, values, slots, band_index, band_table, spatial_out
        )
        back = [exchange(value, "loc", step) for step, value in enumerate(mid)]
        parts = regroup(plan, back)
        parts = [exchange(value, "band", step) for step, value in enumerate(parts)]
        parts = [part.reshape(plan.band_dev, -1, plan.width) for part in parts]
        done = channel(plan, parts, channel_qkv, channel_out, up_weight, down_weight)
        returned.append([exchange(value, "band", step) for step, value in enumerate(done)])
    return restore(plan, ids, returned)


def solution(mesh):
    placed = (P("loc", "band", None), P(), P(), P(), P(), P(), P(), P(), P(), P())
    return jax.shard_map(
        body, mesh=mesh, in_specs=placed, out_specs=P("loc", "band", None), check_vma=False
    )
```

```python
import functools

import jax
import jax.numpy as jnp
from jax import lax
from jax.experimental import pallas as pl
from jax.experimental.pallas import tpu as pltpu
from jax.sharding import PartitionSpec as P

HEADS = 12
HEAD_DIM = 64
WINDOWS = 2
CHUNKS = 2
LATE_SLOTS = 2
TILE_LOCS = 16
STEP_PAIRS = 2
ROW_TILE = 256
LANES = 128
QUERY_SCALE = HEAD_DIM ** (-0.5) * 1.4426950408889634
VMEM_LIMIT = 56 * 1024 * 1024

F32 = jnp.float32
BF16 = jnp.bfloat16


def dot(left, right):
    return jnp.dot(left, right, preferred_element_type=F32)


def dot_t(left, right):
    return lax.dot_general(left, right, (((1,), (1,)), ((), ())), preferred_element_type=F32)


def norm_rows(values):
    centre = values - jnp.mean(values, axis=-1, keepdims=True)
    spread = jnp.mean(centre * centre, axis=-1, keepdims=True)
    return centre * lax.rsqrt(spread + 1e-05)


def gelu(values):
    inner = values * (0.7978845608028654 + 0.035677408136300125 * (values * values))
    return (0.5 * values) * (1.0 + jnp.tanh(inner))


def call(kernel, out_shape, flops, nbytes, **kwargs):
    return pl.pallas_call(
        kernel,
        out_shape=out_shape,
        compiler_params=pltpu.CompilerParams(vmem_limit_bytes=VMEM_LIMIT),
        cost_estimate=pl.CostEstimate(flops=flops, bytes_accessed=nbytes, transcendentals=0),
        **kwargs,
    )


def exchange(value, axis, step):
    if step == 0:
        return value
    return lax.ppermute(value, axis, [(i, i ^ step) for i in range(lax.axis_size(axis))])


class Plan:
    def __init__(self, tokens):
        self.loc_dev, self.band_dev, self.width = tokens.shape
        self.locs = lax.axis_size("loc")
        self.groups = lax.axis_size("band")
        self.share = self.locs // (self.band_dev * WINDOWS)
        assert self.share * self.band_dev * WINDOWS == self.locs
        self.block = self.loc_dev // WINDOWS
        self.rows = self.block // self.share
        self.chunks = CHUNKS
        self.chunk_rows = self.rows // self.chunks
        self.part_rows = self.chunk_rows // self.groups
        assert self.part_rows * self.groups * self.chunks * self.share == self.block


def location_keys(plan, ids):
    size = plan.loc_dev
    row = jnp.broadcast_to(ids.astype(F32), (size, size))
    first = lax.broadcasted_iota(jnp.int32, (size, size), 0)
    second = lax.broadcasted_iota(jnp.int32, (size, size), 1)
    column = jnp.sum(jnp.where(first == second, row, 0.0), axis=1, keepdims=True)
    before = jnp.where((column == row) & (first < second), 1.0, 0.0)
    rank = jnp.sum(before, axis=0, keepdims=True)
    return ids.astype(F32) * plan.block + rank


def arrange(plan, tokens, ids):
    def kernel(ids_ref, x_ref, *rest):
        outs, bands = rest[: plan.locs], rest[plan.locs]
        me = lax.axis_index("loc")
        group = lax.axis_index("band")
        keys = location_keys(plan, ids_ref[pl.ds(me, 1), :])
        for band in range(plan.band_dev):
            bands[band] = x_ref[:, band, :]
        place = lax.broadcasted_iota(jnp.int32, (plan.rows, plan.loc_dev), 0)
        chunk = place // plan.chunk_rows
        owner = (place // plan.part_rows) % plan.groups
        rank = chunk * plan.chunk_rows + (owner ^ group) * plan.part_rows + place % plan.part_rows
        for slot in range(plan.locs):
            peer = me ^ slot
            window = peer % WINDOWS
            part = (peer // WINDOWS) % plan.share
            band = peer // (WINDOWS * plan.share)
            wanted = rank + (window * plan.block + part * plan.rows)
            pick = jnp.where(wanted.astype(F32) == keys, 1.0, 0.0).astype(BF16)
            outs[slot][...] = dot(pick, bands[band]).astype(BF16)

    shape = jax.ShapeDtypeStruct((plan.rows, plan.width), BF16)
    return call(
        kernel,
        [shape] * plan.locs,
        2 * plan.loc_dev * tokens.size,
        4 * tokens.size,
        scratch_shapes=[pltpu.VMEM((plan.band_dev, plan.loc_dev, plan.width), BF16)],
    )(ids, tokens)


def embed_row(plan, index_ref, table_ref):
    band = lax.axis_index("loc") // (WINDOWS * plan.share)
    number = index_ref[lax.axis_index("band") * plan.band_dev + band]
    return table_ref[pl.ds(number, 1), :]


SMEM = pl.BlockSpec(memory_space=pltpu.SMEM)
VMEM = pl.BlockSpec(memory_space=pltpu.VMEM)
ANY = pl.BlockSpec(memory_space=pl.ANY)


def project(plan, slots, index, table, weights):
    count = len(slots)
    width = plan.width

    def kernel(index_ref, table_ref, w_ref, *rest):
        ins, (q_ref, k_ref, v_ref) = rest[:count], rest[count:]
        embed = embed_row(plan, index_ref, table_ref)
        for first in range(0, count, 2):
            some = ins[first : first + 2]
            rows = jnp.concatenate([ref[...].astype(F32) for ref in some], axis=0) + embed
            normed = norm_rows(rows).astype(BF16)
            here = pl.ds(first * plan.rows, len(some) * plan.rows)
            q_ref[here, :] = (dot(normed, w_ref[:, :width]) * QUERY_SCALE).astype(BF16)
            k_ref[here, :] = dot(normed, w_ref[:, width : 2 * width]).astype(BF16)
            v_ref[here, :] = dot(normed, w_ref[:, 2 * width :]).astype(BF16)

    rows = count * plan.rows
    shape = jax.ShapeDtypeStruct((rows, width), BF16)
    return call(
        kernel,
        [shape] * 3,
        2 * rows * width * 3 * width,
        2 * (4 * rows * width + 3 * width * width),
        in_specs=[SMEM, VMEM, VMEM] + [VMEM] * count,
    )(index, table, weights, *slots)


def run_units(units, mask=None):
    def scores_of(unit):
        query, keys, _ = unit
        scores = [dot_t(query, piece) for piece in keys]
        if mask is not None:
            scores = [jnp.where(mask, piece, -1e30) for piece in scores]
        return scores

    results = []
    ahead = scores_of(units[0])
    for number, (_, _, values) in enumerate(units):
        scores = ahead
        if number + 1 < len(units):
            ahead = scores_of(units[number + 1])
        peak = functools.reduce(
            jnp.maximum, [jnp.max(piece, axis=-1, keepdims=True) for piece in scores]
        )
        total = None
        for piece, value in zip(scores, values):
            part = dot(jnp.exp2(piece - peak).astype(BF16), value)
            total = part if total is None else total + part
        results.append(total[:, :LANES] / total[:, LANES:])
    return results


def with_ones(value):
    return jnp.concatenate([value, jnp.ones(value.shape, BF16)], axis=1)


def head_masks(rows):
    lane = lax.broadcasted_iota(jnp.int32, (rows, LANES), 1)
    return [(lane // HEAD_DIM) == head for head in range(LANES // HEAD_DIM)]


def head_units(query, keys, values):
    return [
        (jnp.where(inside, query, jnp.zeros_like(query)), keys, values)
        for inside in head_masks(query.shape[0])
    ]


def join_heads(results):
    joined = results[0]
    for inside, result in zip(head_masks(joined.shape[0])[1:], results[1:]):
        joined = jnp.where(inside, result, joined)
    return joined.astype(BF16)


def attend(plan, chunk, query, keys, values, slots, index, table, spatial_out):
    width, rows = plan.width, plan.chunk_rows
    pieces, sources = len(keys), len(query)
    counts = [piece.shape[0] // plan.rows for piece in query]
    total = plan.locs * rows
    pairs = width // LANES
    step_pairs = STEP_PAIRS
    lanes = step_pairs * LANES
    steps = pairs // step_pairs
    row_tile = min(total, ROW_TILE)
    heads = LANES // HEAD_DIM

    def kernel(index_ref, table_ref, w_ref, *rest):
        q_refs, rest = rest[:sources], rest[sources:]
        k_refs, rest = rest[:pieces], rest[pieces:]
        v_refs, rest = rest[:pieces], rest[pieces:]
        slot_refs, rest = rest[: plan.locs], rest[plan.locs :]
        outs, result = rest[: plan.locs], rest[plan.locs]
        step = pl.program_id(0)
        query_rows = jnp.concatenate(
            [ref[...].reshape(count * rows, lanes) for ref, count in zip(q_refs, counts)], axis=0
        )
        units = []
        for pair in range(step_pairs):
            here = slice(pair * LANES, (pair + 1) * LANES)
            pair_keys = [ref[:, here] for ref in k_refs]
            pair_values = [with_ones(ref[:, here]) for ref in v_refs]
            for first in range(0, total, row_tile):
                units += head_units(
                    query_rows[first : first + row_tile, here], pair_keys, pair_values
                )
        results = run_units(units)
        for pair in range(step_pairs):
            for number, first in enumerate(range(0, total, row_tile)):
                at = (pair * (total // row_tile) + number) * heads
                result[step * step_pairs + pair, pl.ds(first, row_tile), :] = join_heads(
                    results[at : at + heads]
                )

        @pl.when(step == steps - 1)
        def _():
            embed = embed_row(plan, index_ref, table_ref)
            attended = jnp.concatenate([result[i] for i in range(pairs)], axis=1)
            added = dot(attended, w_ref[...])
            for slot in range(plan.locs):
                start = slot_refs[slot][...].astype(F32) + embed
                outs[slot][...] = (start + added[slot * rows : (slot + 1) * rows]).astype(BF16)

    q_specs = [pl.BlockSpec((count, rows, lanes), lambda p: (0, chunk, p)) for count in counts]
    kv_specs = [pl.BlockSpec((piece.shape[0], lanes), lambda p: (0, p)) for piece in keys]
    slot_specs = [pl.BlockSpec((rows, width), lambda p: (chunk, 0))] * plan.locs
    out_specs = [pl.BlockSpec((rows, width), lambda p: (0, 0))] * plan.locs
    key_rows = sum(piece.shape[0] for piece in keys)
    return call(
        kernel,
        [jax.ShapeDtypeStruct((rows, width), BF16)] * plan.locs,
        16 * total * key_rows * width,
        2 * width * (2 * key_rows + 3 * total + width),
        grid=(steps,),
        in_specs=[SMEM, VMEM, VMEM] + q_specs + kv_specs + kv_specs + slot_specs,
        out_specs=out_specs,
        scratch_shapes=[pltpu.VMEM((pairs, total, LANES), BF16)],
    )(
        index,
        table,
        spatial_out,
        *[piece.reshape(count, plan.rows, width) for piece, count in zip(query, counts)],
        *keys,
        *values,
        *slots,
    )


def regroup(plan, slots):
    rows = plan.part_rows
    if rows % 16:
        stacked = jnp.stack(slots).reshape(plan.locs, plan.groups, rows, plan.width)
        return [stacked[:, owner] for owner in range(plan.groups)]

    def kernel(*refs):
        ins, outs = refs[: plan.locs], refs[plan.locs :]
        for slot in range(plan.locs):
            for owner in range(plan.groups):
                outs[owner][slot] = ins[slot][owner * rows : (owner + 1) * rows, :]

    shape = jax.ShapeDtypeStruct((plan.locs, rows, plan.width), BF16)
    return call(
        kernel,
        [shape] * plan.groups,
        0,
        4 * plan.locs * plan.chunk_rows * plan.width,
        in_specs=[VMEM] * plan.locs,
        out_specs=[VMEM] * plan.groups,
    )(*slots)


def channel(plan, parts, channel_qkv, channel_out, up_weight, down_weight):
    groups, width = plan.groups, plan.width
    bands, locations, _ = parts[0].shape
    tile = TILE_LOCS
    assert locations % tile == 0
    tiles = locations // tile
    rows = groups * bands * tile
    blocks = up_weight.shape[1] // width

    def kernel(qkv_hbm, out_hbm, up_hbm, down_hbm, *refs):
        ins, refs = refs[:groups], refs[groups:]
        outs, (qkv_ref, out_ref, up_ref, down_ref, sems) = refs[:groups], refs[groups:]
        copies = [pltpu.make_async_copy(qkv_hbm, qkv_ref, sems.at[0])]
        copies.append(pltpu.make_async_copy(out_hbm, out_ref, sems.at[1]))
        for block in range(blocks):
            here = pl.ds(block * width, width)
            copies.append(
                pltpu.make_async_copy(
                    up_hbm.at[:, here], up_ref.at[:, here], sems.at[2 + 2 * block]
                )
            )
            copies.append(
                pltpu.make_async_copy(
                    down_hbm.at[here, :], down_ref.at[here, :], sems.at[3 + 2 * block]
                )
            )
        for copy in copies:
            copy.start()
        mid = jnp.concatenate(
            [
                ref[:, index * tile : (index + 1) * tile, :].reshape(bands * tile, width)
                for index in range(tiles)
                for ref in ins
            ],
            axis=0,
        ).astype(F32)
        normed = norm_rows(mid).astype(BF16)
        copies[0].wait()
        query = (dot(normed, qkv_ref[:, :width]) * QUERY_SCALE).astype(BF16)
        keys = dot(normed, qkv_ref[:, width : 2 * width]).astype(BF16)
        values = dot(normed, qkv_ref[:, 2 * width :]).astype(BF16)
        first = lax.broadcasted_iota(jnp.int32, (rows, rows), 0)
        second = lax.broadcasted_iota(jnp.int32, (rows, rows), 1)
        mask = (first % tile) == (second % tile)
        heads = LANES // HEAD_DIM
        pairs = width // LANES
        units = []
        for index in range(tiles):
            mine = slice(index * rows, (index + 1) * rows)
            for pair in range(pairs):
                here = slice(pair * LANES, (pair + 1) * LANES)
                units += head_units(
                    query[mine, here], [keys[mine, here]], [with_ones(values[mine, here])]
                )
        results = run_units(units, mask)
        joined = [join_heads(results[at : at + heads]) for at in range(0, len(results), heads)]
        attended = jnp.concatenate(
            [
                jnp.concatenate(joined[index * pairs : (index + 1) * pairs], axis=1)
                for index in range(tiles)
            ],
            axis=0,
        )
        copies[1].wait()
        after = mid + dot(attended, out_ref[...])
        normed = norm_rows(after).astype(BF16)

        def raised(block):
            copies[2 + 2 * block].wait()
            return dot(normed, up_ref[:, block * width : (block + 1) * width])

        ahead = raised(0)
        for block in range(blocks):
            hidden = ahead
            if block + 1 < blocks:
                ahead = raised(block + 1)
            hidden = gelu(hidden).astype(BF16)
            copies[3 + 2 * block].wait()
            after = after + dot(hidden, down_ref[block * width : (block + 1) * width, :])
        after = after.astype(BF16)
        for index in range(tiles):
            for owner in range(groups):
                at = index * rows + owner * bands * tile
                outs[owner][:, index * tile : (index + 1) * tile, :] = after[
                    at : at + bands * tile
                ].reshape(bands, tile, width)

    weights = [channel_qkv, channel_out, up_weight, down_weight]
    size = sum(weight.size for weight in weights)
    count = groups * bands * locations
    return call(
        kernel,
        [jax.ShapeDtypeStruct((bands, locations, width), BF16)] * groups,
        2 * count * size,
        2 * (2 * count * width + size),
        in_specs=[ANY] * 4 + [VMEM] * groups,
        out_specs=[VMEM] * groups,
        scratch_shapes=[pltpu.VMEM(weight.shape, BF16) for weight in weights]
        + [pltpu.SemaphoreType.DMA((2 + 2 * blocks,))],
    )(*weights, *parts)


def restore(plan, ids, returned):
    locations = plan.loc_dev // (plan.chunks * plan.groups)

    def kernel(ids_ref, *refs):
        ins, out_ref = refs[:-1], refs[-1]
        me = lax.axis_index("loc")
        group = lax.axis_index("band")
        keys = location_keys(plan, ids_ref[pl.ds(me, 1), :])
        place = lax.broadcasted_iota(jnp.int32, (plan.loc_dev, plan.loc_dev), 0)
        inner = place % plan.part_rows
        window = (place // plan.part_rows) % WINDOWS ^ (me % WINDOWS)
        part = (place // (plan.part_rows * WINDOWS)) % plan.share ^ (me // WINDOWS) % plan.share
        owner = (place // locations) % plan.groups ^ group
        chunk = place // (locations * plan.groups)
        wanted = (
            window * plan.block
            + part * plan.rows
            + chunk * plan.chunk_rows
            + owner * plan.part_rows
            + inner
        )
        pick = jnp.where(wanted.astype(F32) == keys, 1.0, 0.0).astype(BF16)
        mine = me // (WINDOWS * plan.share)
        for band in range(plan.band_dev):
            rows = jnp.concatenate([ref[band ^ mine] for ref in ins], axis=0)
            out_ref[:, band, :] = lax.dot_general(
                pick, rows, (((0,), (0,)), ((), ())), preferred_element_type=F32
            ).astype(BF16)

    arrays = [array for chunk in returned for array in chunk]
    size = plan.loc_dev * plan.band_dev * plan.width
    return call(
        kernel,
        jax.ShapeDtypeStruct((plan.loc_dev, plan.band_dev, plan.width), BF16),
        2 * plan.loc_dev * size,
        4 * size,
    )(ids, *arrays)


def body(
    tokens,
    band_index,
    band_table,
    window_ids,
    spatial_qkv,
    spatial_out,
    channel_qkv,
    channel_out,
    up_weight,
    down_weight,
):
    plan = Plan(tokens)
    ids = window_ids.reshape(plan.locs, plan.loc_dev)
    sent = arrange(plan, tokens, ids)
    slots = [exchange(value, "loc", step) for step, value in enumerate(sent)]
    split = plan.locs - LATE_SLOTS
    early = project(plan, slots[:split], band_index, band_table, spatial_qkv)
    late = project(plan, slots[split:], band_index, band_table, spatial_qkv)
    query, keys, values = zip(early, late)
    if plan.share > 1:
        same = [
            [(band * plan.share + part) * WINDOWS + window for part in range(plan.share)]
            for band in range(plan.band_dev)
            for window in range(WINDOWS)
        ]
        gather = functools.partial(
            lax.all_gather, axis_name="loc", axis_index_groups=same, axis=0, tiled=True
        )
        keys = [gather(jnp.concatenate(keys, axis=0))]
        values = [gather(jnp.concatenate(values, axis=0))]
    returned = []
    for chunk in range(plan.chunks):
        mid = attend(
            plan, chunk, query, keys, values, slots, band_index, band_table, spatial_out
        )
        back = [exchange(value, "loc", step) for step, value in enumerate(mid)]
        parts = regroup(plan, back)
        parts = [exchange(value, "band", step) for step, value in enumerate(parts)]
        parts = [part.reshape(plan.band_dev, -1, plan.width) for part in parts]
        done = channel(plan, parts, channel_qkv, channel_out, up_weight, down_weight)
        returned.append([exchange(value, "band", step) for step, value in enumerate(done)])
    return restore(plan, ids, returned)


def solution(mesh):
    placed = (P("loc", "band", None), P(), P(), P(), P(), P(), P(), P(), P(), P())
    return jax.shard_map(
        body, mesh=mesh, in_specs=placed, out_specs=P("loc", "band", None), check_vma=False
    )
```

```python
import functools

import jax
import jax.numpy as jnp
from jax import lax
from jax.experimental import pallas as pl
from jax.experimental.pallas import tpu as pltpu
from jax.sharding import PartitionSpec as P

HEADS = 12
HEAD_DIM = 64
WINDOWS = 2
CHUNKS = 2
LATE_SLOTS = 2
TILE_LOCS = 16
STEP_PAIRS = 2
ROW_TILE = 256
LANES = 128
QUERY_SCALE = HEAD_DIM ** (-0.5) * 1.4426950408889634
VMEM_LIMIT = 56 * 1024 * 1024

F32 = jnp.float32
BF16 = jnp.bfloat16


def dot(left, right):
    return jnp.dot(left, right, preferred_element_type=F32)


def dot_t(left, right):
    return lax.dot_general(left, right, (((1,), (1,)), ((), ())), preferred_element_type=F32)


def norm_rows(values):
    centre = values - jnp.mean(values, axis=-1, keepdims=True)
    spread = jnp.mean(centre * centre, axis=-1, keepdims=True)
    return centre * lax.rsqrt(spread + 1e-05)


def gelu(values):
    inner = values * (0.7978845608028654 + 0.035677408136300125 * (values * values))
    return (0.5 * values) * (1.0 + jnp.tanh(inner))


def call(kernel, out_shape, flops, nbytes, **kwargs):
    return pl.pallas_call(
        kernel,
        out_shape=out_shape,
        compiler_params=pltpu.CompilerParams(vmem_limit_bytes=VMEM_LIMIT),
        cost_estimate=pl.CostEstimate(flops=flops, bytes_accessed=nbytes, transcendentals=0),
        **kwargs,
    )


def exchange(value, axis, step):
    if step == 0:
        return value
    return lax.ppermute(value, axis, [(i, i ^ step) for i in range(lax.axis_size(axis))])


def swap(value, axis):
    return lax.all_to_all(value, axis, split_axis=0, concat_axis=0, tiled=True)


class Plan:
    def __init__(self, tokens):
        self.loc_dev, self.band_dev, self.width = tokens.shape
        self.locs = lax.axis_size("loc")
        self.groups = lax.axis_size("band")
        self.share = self.locs // (self.band_dev * WINDOWS)
        assert self.share * self.band_dev * WINDOWS == self.locs
        self.block = self.loc_dev // WINDOWS
        self.rows = self.block // self.share
        self.chunks = CHUNKS
        self.chunk_rows = self.rows // self.chunks
        self.part_rows = self.chunk_rows // self.groups
        assert self.part_rows * self.groups * self.chunks * self.share == self.block


def location_keys(plan, ids):
    size = plan.loc_dev
    row = jnp.broadcast_to(ids.astype(F32), (size, size))
    first = lax.broadcasted_iota(jnp.int32, (size, size), 0)
    second = lax.broadcasted_iota(jnp.int32, (size, size), 1)
    column = jnp.sum(jnp.where(first == second, row, 0.0), axis=1, keepdims=True)
    before = jnp.where((column == row) & (first < second), 1.0, 0.0)
    rank = jnp.sum(before, axis=0, keepdims=True)
    return ids.astype(F32) * plan.block + rank


def arrange(plan, tokens, ids):
    def kernel(ids_ref, x_ref, *rest):
        outs, bands = rest[: plan.locs], rest[plan.locs]
        me = lax.axis_index("loc")
        keys = location_keys(plan, ids_ref[pl.ds(me, 1), :])
        for band in range(plan.band_dev):
            bands[band] = x_ref[:, band, :]
        place = lax.broadcasted_iota(jnp.int32, (plan.rows, plan.loc_dev), 0)
        chunk = place // plan.chunk_rows
        owner = (place // plan.part_rows) % plan.groups
        rank = chunk * plan.chunk_rows + owner * plan.part_rows + place % plan.part_rows
        for slot in range(plan.locs):
            peer = me ^ slot
            window = peer % WINDOWS
            part = (peer // WINDOWS) % plan.share
            band = peer // (WINDOWS * plan.share)
            wanted = rank + (window * plan.block + part * plan.rows)
            pick = jnp.where(wanted.astype(F32) == keys, 1.0, 0.0).astype(BF16)
            outs[slot][...] = dot(pick, bands[band]).astype(BF16)

    shape = jax.ShapeDtypeStruct((plan.rows, plan.width), BF16)
    return call(
        kernel,
        [shape] * plan.locs,
        2 * plan.loc_dev * tokens.size,
        4 * tokens.size,
        scratch_shapes=[pltpu.VMEM((plan.band_dev, plan.loc_dev, plan.width), BF16)],
    )(ids, tokens)


def embed_row(plan, index_ref, table_ref):
    band = lax.axis_index("loc") // (WINDOWS * plan.share)
    number = index_ref[lax.axis_index("band") * plan.band_dev + band]
    return table_ref[pl.ds(number, 1), :]


SMEM = pl.BlockSpec(memory_space=pltpu.SMEM)
VMEM = pl.BlockSpec(memory_space=pltpu.VMEM)
ANY = pl.BlockSpec(memory_space=pl.ANY)


def project(plan, slots, index, table, weights):
    count = len(slots)
    width = plan.width

    def kernel(index_ref, table_ref, w_ref, *rest):
        ins, (q_ref, k_ref, v_ref) = rest[:count], rest[count:]
        embed = embed_row(plan, index_ref, table_ref)
        for first in range(0, count, 2):
            some = ins[first : first + 2]
            rows = jnp.concatenate([ref[...].astype(F32) for ref in some], axis=0) + embed
            normed = norm_rows(rows).astype(BF16)
            here = pl.ds(first * plan.rows, len(some) * plan.rows)
            q_ref[here, :] = (dot(normed, w_ref[:, :width]) * QUERY_SCALE).astype(BF16)
            k_ref[here, :] = dot(normed, w_ref[:, width : 2 * width]).astype(BF16)
            v_ref[here, :] = dot(normed, w_ref[:, 2 * width :]).astype(BF16)

    rows = count * plan.rows
    shape = jax.ShapeDtypeStruct((rows, width), BF16)
    return call(
        kernel,
        [shape] * 3,
        2 * rows * width * 3 * width,
        2 * (4 * rows * width + 3 * width * width),
        in_specs=[SMEM, VMEM, VMEM] + [VMEM] * count,
    )(index, table, weights, *slots)


def run_units(units, mask=None):
    def scores_of(unit):
        query, keys, _ = unit
        scores = [dot_t(query, piece) for piece in keys]
        if mask is not None:
            scores = [jnp.where(mask, piece, -1e30) for piece in scores]
        return scores

    results = []
    ahead = scores_of(units[0])
    for number, (_, _, values) in enumerate(units):
        scores = ahead
        if number + 1 < len(units):
            ahead = scores_of(units[number + 1])
        peak = functools.reduce(
            jnp.maximum, [jnp.max(piece, axis=-1, keepdims=True) for piece in scores]
        )
        total = None
        for piece, value in zip(scores, values):
            part = dot(jnp.exp2(piece - peak).astype(BF16), value)
            total = part if total is None else total + part
        results.append(total[:, :LANES] / total[:, LANES:])
    return results


def with_ones(value):
    return jnp.concatenate([value, jnp.ones(value.shape, BF16)], axis=1)


def head_masks(rows):
    lane = lax.broadcasted_iota(jnp.int32, (rows, LANES), 1)
    return [(lane // HEAD_DIM) == head for head in range(LANES // HEAD_DIM)]


def head_units(query, keys, values):
    return [
        (jnp.where(inside, query, jnp.zeros_like(query)), keys, values)
        for inside in head_masks(query.shape[0])
    ]


def join_heads(results):
    joined = results[0]
    for inside, result in zip(head_masks(joined.shape[0])[1:], results[1:]):
        joined = jnp.where(inside, result, joined)
    return joined.astype(BF16)


def attend(plan, chunk, query, keys, values, slots, index, table, spatial_out):
    width, rows = plan.width, plan.chunk_rows
    pieces, sources = len(keys), len(query)
    counts = [piece.shape[0] // plan.rows for piece in query]
    total = plan.locs * rows
    pairs = width // LANES
    step_pairs = STEP_PAIRS
    lanes = step_pairs * LANES
    steps = pairs // step_pairs
    row_tile = min(total, ROW_TILE)
    heads = LANES // HEAD_DIM

    def kernel(index_ref, table_ref, w_ref, *rest):
        q_refs, rest = rest[:sources], rest[sources:]
        k_refs, rest = rest[:pieces], rest[pieces:]
        v_refs, rest = rest[:pieces], rest[pieces:]
        slot_refs, rest = rest[: plan.locs], rest[plan.locs :]
        out_ref, result = rest
        me = lax.axis_index("loc")
        step = pl.program_id(0)
        query_rows = jnp.concatenate(
            [ref[...].reshape(count * rows, lanes) for ref, count in zip(q_refs, counts)], axis=0
        )
        units = []
        for pair in range(step_pairs):
            here = slice(pair * LANES, (pair + 1) * LANES)
            pair_keys = [ref[:, here] for ref in k_refs]
            pair_values = [with_ones(ref[:, here]) for ref in v_refs]
            for first in range(0, total, row_tile):
                units += head_units(
                    query_rows[first : first + row_tile, here], pair_keys, pair_values
                )
        results = run_units(units)
        for pair in range(step_pairs):
            for number, first in enumerate(range(0, total, row_tile)):
                at = (pair * (total // row_tile) + number) * heads
                result[step * step_pairs + pair, pl.ds(first, row_tile), :] = join_heads(
                    results[at : at + heads]
                )

        @pl.when(step == steps - 1)
        def _():
            embed = embed_row(plan, index_ref, table_ref)
            attended = jnp.concatenate([result[i] for i in range(pairs)], axis=1)
            added = dot(attended, w_ref[...])
            for slot in range(plan.locs):
                start = slot_refs[slot][...].astype(F32) + embed
                out_ref[me ^ slot] = (start + added[slot * rows : (slot + 1) * rows]).astype(BF16)

    q_specs = [pl.BlockSpec((count, rows, lanes), lambda p: (0, chunk, p)) for count in counts]
    kv_specs = [pl.BlockSpec((piece.shape[0], lanes), lambda p: (0, p)) for piece in keys]
    slot_specs = [pl.BlockSpec((rows, width), lambda p: (chunk, 0))] * plan.locs
    out_specs = pl.BlockSpec((plan.locs, rows, width), lambda p: (0, 0, 0))
    key_rows = sum(piece.shape[0] for piece in keys)
    return call(
        kernel,
        jax.ShapeDtypeStruct((plan.locs, rows, width), BF16),
        16 * total * key_rows * width,
        2 * width * (2 * key_rows + 3 * total + width),
        grid=(steps,),
        in_specs=[SMEM, VMEM, VMEM] + q_specs + kv_specs + kv_specs + slot_specs,
        out_specs=out_specs,
        scratch_shapes=[pltpu.VMEM((pairs, total, LANES), BF16)],
    )(
        index,
        table,
        spatial_out,
        *[piece.reshape(count, plan.rows, width) for piece, count in zip(query, counts)],
        *keys,
        *values,
        *slots,
    )


def regroup(plan, slots):
    rows = plan.part_rows
    if rows % 16:
        split = slots.reshape(plan.locs, plan.groups, rows, plan.width)
        return split.transpose(1, 0, 2, 3)

    def kernel(in_ref, out_ref):
        for slot in range(plan.locs):
            for owner in range(plan.groups):
                out_ref[owner, slot] = in_ref[slot, owner * rows : (owner + 1) * rows, :]

    return call(
        kernel,
        jax.ShapeDtypeStruct((plan.groups, plan.locs, rows, plan.width), BF16),
        0,
        4 * plan.locs * plan.chunk_rows * plan.width,
        in_specs=[VMEM],
        out_specs=VMEM,
    )(slots)


def channel(plan, parts, channel_qkv, channel_out, up_weight, down_weight):
    groups, width = plan.groups, plan.width
    _, bands, locations, _ = parts.shape
    tile = TILE_LOCS
    assert locations % tile == 0
    tiles = locations // tile
    rows = groups * bands * tile
    blocks = up_weight.shape[1] // width

    def kernel(qkv_hbm, out_hbm, up_hbm, down_hbm, *refs):
        in_ref, done_ref, qkv_ref, out_ref, up_ref, down_ref, sems = refs
        copies = [pltpu.make_async_copy(qkv_hbm, qkv_ref, sems.at[0])]
        copies.append(pltpu.make_async_copy(out_hbm, out_ref, sems.at[1]))
        for block in range(blocks):
            here = pl.ds(block * width, width)
            copies.append(
                pltpu.make_async_copy(
                    up_hbm.at[:, here], up_ref.at[:, here], sems.at[2 + 2 * block]
                )
            )
            copies.append(
                pltpu.make_async_copy(
                    down_hbm.at[here, :], down_ref.at[here, :], sems.at[3 + 2 * block]
                )
            )
        for copy in copies:
            copy.start()
        mid = jnp.concatenate(
            [
                in_ref[owner, :, index * tile : (index + 1) * tile, :].reshape(bands * tile, width)
                for index in range(tiles)
                for owner in range(groups)
            ],
            axis=0,
        ).astype(F32)
        normed = norm_rows(mid).astype(BF16)
        copies[0].wait()
        query = (dot(normed, qkv_ref[:, :width]) * QUERY_SCALE).astype(BF16)
        keys = dot(normed, qkv_ref[:, width : 2 * width]).astype(BF16)
        values = dot(normed, qkv_ref[:, 2 * width :]).astype(BF16)
        first = lax.broadcasted_iota(jnp.int32, (rows, rows), 0)
        second = lax.broadcasted_iota(jnp.int32, (rows, rows), 1)
        mask = (first % tile) == (second % tile)
        heads = LANES // HEAD_DIM
        pairs = width // LANES
        units = []
        for index in range(tiles):
            mine = slice(index * rows, (index + 1) * rows)
            for pair in range(pairs):
                here = slice(pair * LANES, (pair + 1) * LANES)
                units += head_units(
                    query[mine, here], [keys[mine, here]], [with_ones(values[mine, here])]
                )
        results = run_units(units, mask)
        joined = [join_heads(results[at : at + heads]) for at in range(0, len(results), heads)]
        attended = jnp.concatenate(
            [
                jnp.concatenate(joined[index * pairs : (index + 1) * pairs], axis=1)
                for index in range(tiles)
            ],
            axis=0,
        )
        copies[1].wait()
        after = mid + dot(attended, out_ref[...])
        normed = norm_rows(after).astype(BF16)

        def raised(block):
            copies[2 + 2 * block].wait()
            return dot(normed, up_ref[:, block * width : (block + 1) * width])

        ahead = raised(0)
        for block in range(blocks):
            hidden = ahead
            if block + 1 < blocks:
                ahead = raised(block + 1)
            hidden = gelu(hidden).astype(BF16)
            copies[3 + 2 * block].wait()
            after = after + dot(hidden, down_ref[block * width : (block + 1) * width, :])
        after = after.astype(BF16)
        for index in range(tiles):
            for owner in range(groups):
                at = index * rows + owner * bands * tile
                done_ref[owner, :, index * tile : (index + 1) * tile, :] = after[
                    at : at + bands * tile
                ].reshape(bands, tile, width)

    weights = [channel_qkv, channel_out, up_weight, down_weight]
    size = sum(weight.size for weight in weights)
    count = groups * bands * locations
    return call(
        kernel,
        jax.ShapeDtypeStruct(parts.shape, BF16),
        2 * count * size,
        2 * (2 * count * width + size),
        in_specs=[ANY] * 4 + [VMEM],
        out_specs=VMEM,
        scratch_shapes=[pltpu.VMEM(weight.shape, BF16) for weight in weights]
        + [pltpu.SemaphoreType.DMA((2 + 2 * blocks,))],
    )(*weights, parts)


def restore(plan, ids, returned):
    locations = plan.loc_dev // (plan.chunks * plan.groups)

    def kernel(ids_ref, *refs):
        ins, out_ref = refs[:-1], refs[-1]
        me = lax.axis_index("loc")
        keys = location_keys(plan, ids_ref[pl.ds(me, 1), :])
        place = lax.broadcasted_iota(jnp.int32, (plan.loc_dev, plan.loc_dev), 0)
        inner = place % plan.part_rows
        window = (place // plan.part_rows) % WINDOWS
        part = (place // (plan.part_rows * WINDOWS)) % plan.share
        part_owner = (place // locations) % plan.groups
        chunk = place // (locations * plan.groups)
        wanted = (
            window * plan.block
            + part * plan.rows
            + chunk * plan.chunk_rows
            + part_owner * plan.part_rows
            + inner
        )
        pick = jnp.where(wanted.astype(F32) == keys, 1.0, 0.0).astype(BF16)
        for band in range(plan.band_dev):
            rows = jnp.concatenate(
                [ref[owner, band] for ref in ins for owner in range(plan.groups)], axis=0
            )
            out_ref[:, band, :] = lax.dot_general(
                pick, rows, (((0,), (0,)), ((), ())), preferred_element_type=F32
            ).astype(BF16)

    size = plan.loc_dev * plan.band_dev * plan.width
    return call(
        kernel,
        jax.ShapeDtypeStruct((plan.loc_dev, plan.band_dev, plan.width), BF16),
        2 * plan.loc_dev * size,
        4 * size,
    )(ids, *returned)


def body(
    tokens,
    band_index,
    band_table,
    window_ids,
    spatial_qkv,
    spatial_out,
    channel_qkv,
    channel_out,
    up_weight,
    down_weight,
):
    plan = Plan(tokens)
    ids = window_ids.reshape(plan.locs, plan.loc_dev)
    sent = arrange(plan, tokens, ids)
    slots = [exchange(value, "loc", step) for step, value in enumerate(sent)]
    split = plan.locs - LATE_SLOTS
    early = project(plan, slots[:split], band_index, band_table, spatial_qkv)
    late = project(plan, slots[split:], band_index, band_table, spatial_qkv)
    query, keys, values = zip(early, late)
    if plan.share > 1:
        same = [
            [(band * plan.share + part) * WINDOWS + window for part in range(plan.share)]
            for band in range(plan.band_dev)
            for window in range(WINDOWS)
        ]
        gather = functools.partial(
            lax.all_gather, axis_name="loc", axis_index_groups=same, axis=0, tiled=True
        )
        keys = [gather(jnp.concatenate(keys, axis=0))]
        values = [gather(jnp.concatenate(values, axis=0))]
    returned = []
    for chunk in range(plan.chunks):
        mid = attend(
            plan, chunk, query, keys, values, slots, band_index, band_table, spatial_out
        )
        back = swap(mid, "loc")
        parts = swap(regroup(plan, back), "band")
        parts = parts.reshape(plan.groups, plan.band_dev, -1, plan.width)
        done = channel(plan, parts, channel_qkv, channel_out, up_weight, down_weight)
        returned.append(swap(done, "band"))
    return restore(plan, ids, returned)


def solution(mesh):
    placed = (P("loc", "band", None), P(), P(), P(), P(), P(), P(), P(), P(), P())
    return jax.shard_map(
        body, mesh=mesh, in_specs=placed, out_specs=P("loc", "band", None), check_vma=False
    )
```

```python
import functools

import jax
import jax.numpy as jnp
from jax import lax
from jax.experimental import pallas as pl
from jax.experimental.pallas import tpu as pltpu
from jax.sharding import PartitionSpec as P

HEADS = 12
HEAD_DIM = 64
WINDOWS = 2
CHUNKS = 2
LATE_SLOTS = 2
TILE_LOCS = 16
NORM_ROWS = 128
COLUMNS = 256
UNIT_ROWS = 128
UNITS_STEP = 2
CHANNEL_PAIRS = 2
MLP_BLOCKS = 2
LANES = 128
QUERY_SCALE = HEAD_DIM ** (-0.5) * 1.4426950408889634
VMEM_LIMIT = 40 * 1024 * 1024

F32 = jnp.float32
BF16 = jnp.bfloat16


def dot(left, right):
    return jnp.dot(left, right, preferred_element_type=F32)


def dot_t(left, right):
    return lax.dot_general(left, right, (((1,), (1,)), ((), ())), preferred_element_type=F32)


def norm_rows(values):
    centre = values - jnp.mean(values, axis=-1, keepdims=True)
    spread = jnp.mean(centre * centre, axis=-1, keepdims=True)
    return centre * lax.rsqrt(spread + 1e-05)


def gelu(values):
    inner = values * (0.7978845608028654 + 0.035677408136300125 * (values * values))
    return (0.5 * values) * (1.0 + jnp.tanh(inner))


def call(kernel, out_shape, flops, nbytes, **kwargs):
    return pl.pallas_call(
        kernel,
        out_shape=out_shape,
        compiler_params=pltpu.CompilerParams(vmem_limit_bytes=VMEM_LIMIT),
        cost_estimate=pl.CostEstimate(flops=flops, bytes_accessed=nbytes, transcendentals=0),
        **kwargs,
    )


def exchange(value, axis, step):
    if step == 0:
        return value
    return lax.ppermute(value, axis, [(i, i ^ step) for i in range(lax.axis_size(axis))])


class Plan:
    def __init__(self, tokens):
        self.loc_dev, self.band_dev, self.width = tokens.shape
        self.locs = lax.axis_size("loc")
        self.groups = lax.axis_size("band")
        self.share = self.locs // (self.band_dev * WINDOWS)
        assert self.share * self.band_dev * WINDOWS == self.locs
        self.block = self.loc_dev // WINDOWS
        self.rows = self.block // self.share
        self.chunks = CHUNKS
        self.chunk_rows = self.rows // self.chunks
        self.part_rows = self.chunk_rows // self.groups
        assert self.part_rows * self.groups * self.chunks * self.share == self.block


def location_keys(plan, ids):
    size = plan.loc_dev
    row = jnp.broadcast_to(ids.astype(F32), (size, size))
    first = lax.broadcasted_iota(jnp.int32, (size, size), 0)
    second = lax.broadcasted_iota(jnp.int32, (size, size), 1)
    column = jnp.sum(jnp.where(first == second, row, 0.0), axis=1, keepdims=True)
    before = jnp.where((column == row) & (first < second), 1.0, 0.0)
    rank = jnp.sum(before, axis=0, keepdims=True)
    return ids.astype(F32) * plan.block + rank


def arrange(plan, tokens, ids):
    def kernel(ids_ref, x_ref, *rest):
        outs, bands = rest[: plan.locs], rest[plan.locs]
        me = lax.axis_index("loc")
        group = lax.axis_index("band")
        keys = location_keys(plan, ids_ref[pl.ds(me, 1), :])
        for band in range(plan.band_dev):
            bands[band] = x_ref[:, band, :]
        place = lax.broadcasted_iota(jnp.int32, (plan.rows, plan.loc_dev), 0)
        chunk = place // plan.chunk_rows
        owner = (place // plan.part_rows) % plan.groups
        rank = chunk * plan.chunk_rows + (owner ^ group) * plan.part_rows + place % plan.part_rows
        for slot in range(plan.locs):
            peer = me ^ slot
            window = peer % WINDOWS
            part = (peer // WINDOWS) % plan.share
            band = peer // (WINDOWS * plan.share)
            wanted = rank + (window * plan.block + part * plan.rows)
            pick = jnp.where(wanted.astype(F32) == keys, 1.0, 0.0).astype(BF16)
            outs[slot][...] = dot(pick, bands[band]).astype(BF16)

    shape = jax.ShapeDtypeStruct((plan.rows, plan.width), BF16)
    return call(
        kernel,
        [shape] * plan.locs,
        2 * plan.loc_dev * tokens.size,
        4 * tokens.size,
        scratch_shapes=[pltpu.VMEM((plan.band_dev, plan.loc_dev, plan.width), BF16)],
    )(ids, tokens)


def embed_row(plan, index_ref, table_ref):
    band = lax.axis_index("loc") // (WINDOWS * plan.share)
    number = index_ref[lax.axis_index("band") * plan.band_dev + band]
    return table_ref[pl.ds(number, 1), :]


SMEM = pl.BlockSpec(memory_space=pltpu.SMEM)
VMEM = pl.BlockSpec(memory_space=pltpu.VMEM)
ANY = pl.BlockSpec(memory_space=pl.ANY)


def loop(count, step):
    lax.fori_loop(0, count, lambda i, _: (step(i), 0)[1], 0)


def aligned(index, size):
    return pl.ds(pl.multiple_of(index * size, size), size)


def norm_into(target, rows_of, rows):
    tile = min(rows, NORM_ROWS)

    def step(index):
        here = aligned(index, tile)
        target[here, :] = norm_rows(rows_of(here)).astype(BF16)

    loop(rows // tile, step)


def project(plan, slots, index, table, weights, after=()):
    count = len(slots)
    width = plan.width
    rows = count * plan.rows
    blocks = width // COLUMNS

    def kernel(index_ref, table_ref, w_ref, *rest):
        ins, (q_ref, k_ref, v_ref, joined, normed) = rest[:count], rest[count + len(after) :]
        embed = embed_row(plan, index_ref, table_ref)
        for slot in range(count):
            joined[pl.ds(slot * plan.rows, plan.rows), :] = ins[slot][...]
        norm_into(normed, lambda here: joined[here, :].astype(F32) + embed, rows)
        for number, (ref, factor) in enumerate(((q_ref, QUERY_SCALE), (k_ref, 1.0), (v_ref, 1.0))):

            def step(block):
                here = aligned(block, COLUMNS)
                there = pl.ds(
                    pl.multiple_of(number * width + block * COLUMNS, COLUMNS), COLUMNS
                )
                ref[:, here] = (dot(normed[...], w_ref[:, there]) * factor).astype(BF16)

            loop(blocks, step)

    shape = jax.ShapeDtypeStruct((rows, width), BF16)
    return call(
        kernel,
        [shape] * 3,
        2 * rows * width * 3 * width,
        2 * (4 * rows * width + 3 * width * width),
        in_specs=[SMEM, VMEM, VMEM] + [VMEM] * count + [ANY] * len(after),
        out_specs=[VMEM] * 3,
        scratch_shapes=[pltpu.VMEM((rows, width), BF16)] * 2,
    )(index, table, weights, *slots, *after)


def head_masks(rows):
    lane = lax.broadcasted_iota(jnp.int32, (rows, LANES), 1)
    return [(lane // HEAD_DIM) == head for head in range(LANES // HEAD_DIM)]


def stack_heads(query):
    return jnp.concatenate(
        [jnp.where(inside, query, jnp.zeros_like(query)) for inside in head_masks(query.shape[0])],
        axis=0,
    )


def join_heads(stacked):
    heads = LANES // HEAD_DIM
    rows = stacked.shape[0] // heads
    joined = stacked[:rows]
    for head, inside in list(enumerate(head_masks(rows)))[1:]:
        joined = jnp.where(inside, stacked[head * rows : (head + 1) * rows], joined)
    return joined.astype(BF16)


def with_ones(value):
    return jnp.concatenate([value, jnp.ones(value.shape, BF16)], axis=1)


def run_units(units, mask=None):
    def scores_of(unit):
        query, keys, _ = unit
        scores = [dot_t(query, piece) for piece in keys]
        if mask is not None:
            scores = [jnp.where(mask, piece, -1e30) for piece in scores]
        return scores

    results = []
    ahead = scores_of(units[0])
    for number, (_, _, values) in enumerate(units):
        scores = ahead
        if number + 1 < len(units):
            ahead = scores_of(units[number + 1])
        peak = functools.reduce(
            jnp.maximum, [jnp.max(piece, axis=-1, keepdims=True) for piece in scores]
        )
        total = None
        for piece, value in zip(scores, values):
            part = dot(jnp.exp2(piece - peak).astype(BF16), value)
            total = part if total is None else total + part
        results.append(join_heads(total[:, :LANES] / total[:, LANES:]))
    return results


def attend(plan, chunk, query, keys, values, slots, index, table, spatial_out):
    width, rows = plan.width, plan.chunk_rows
    pieces, sources = len(keys), len(query)
    total = plan.locs * rows
    pairs = width // LANES
    unit = min(total, UNIT_ROWS)
    per_step = min(UNITS_STEP, total // unit)
    key_counts = [piece.shape[0] for piece in keys]

    def kernel(index_ref, table_ref, w_ref, *rest):
        q_refs, rest = rest[:sources], rest[sources:]
        k_refs, rest = rest[:pieces], rest[pieces:]
        v_refs, rest = rest[:pieces], rest[pieces:]
        slot_refs, rest = rest[: plan.locs], rest[plan.locs :]
        outs, (asked, result, added, *ones_refs) = rest[: plan.locs], rest[plan.locs :]
        at = 0
        for ref in q_refs:
            for slot in range(ref.shape[0] // plan.rows):
                asked[pl.ds(at, rows), :] = ref[pl.ds(slot * plan.rows + chunk * rows, rows), :]
                at += rows
        for ref in ones_refs:
            ref[:, LANES:] = jnp.ones((ref.shape[0], LANES), BF16)

        def pair_step(pair):
            here = aligned(pair, LANES)
            for ref, v_ref in zip(ones_refs, v_refs):
                ref[:, :LANES] = v_ref[:, here]
            pair_keys = [ref[:, here] for ref in k_refs]
            pair_values = [ref[...] for ref in ones_refs]

            def row_step(step):
                places = [
                    pl.ds(pl.multiple_of((step * per_step + i) * unit, unit), unit)
                    for i in range(per_step)
                ]
                units = [
                    (stack_heads(asked[place, here]), pair_keys, pair_values) for place in places
                ]
                for place, done in zip(places, run_units(units)):
                    result[place, here] = done

            loop(total // (unit * per_step), row_step)

        loop(pairs, pair_step)

        def out_step(block):
            here = aligned(block, COLUMNS)
            added[:, here] = dot(result[...], w_ref[:, here])

        loop(width // COLUMNS, out_step)
        embed = embed_row(plan, index_ref, table_ref)
        for slot in range(plan.locs):
            start = slot_refs[slot][pl.ds(chunk * rows, rows), :].astype(F32) + embed
            outs[slot][...] = (start + added[pl.ds(slot * rows, rows), :]).astype(BF16)

    key_rows = sum(key_counts)
    return call(
        kernel,
        [jax.ShapeDtypeStruct((rows, width), BF16)] * plan.locs,
        16 * total * key_rows * width,
        2 * width * (2 * key_rows + 3 * total + width),
        in_specs=[SMEM] + [VMEM] * (2 + sources + 2 * pieces + plan.locs),
        out_specs=[VMEM] * plan.locs,
        scratch_shapes=[
            pltpu.VMEM((total, width), BF16),
            pltpu.VMEM((total, width), BF16),
            pltpu.VMEM((total, width), F32),
        ]
        + [pltpu.VMEM((count, 2 * LANES), BF16) for count in key_counts],
    )(index, table, spatial_out, *query, *keys, *values, *slots)


def regroup(plan, slots, after=()):
    rows = plan.part_rows
    if rows % 16:
        stacked = jnp.stack(slots).reshape(plan.locs, plan.groups, rows, plan.width)
        return [stacked[:, owner] for owner in range(plan.groups)]

    def kernel(*refs):
        ins, outs = refs[: plan.locs], refs[plan.locs + len(after) :]
        for slot in range(plan.locs):
            for owner in range(plan.groups):
                outs[owner][slot] = ins[slot][owner * rows : (owner + 1) * rows, :]

    shape = jax.ShapeDtypeStruct((plan.locs, rows, plan.width), BF16)
    return call(
        kernel,
        [shape] * plan.groups,
        0,
        4 * plan.locs * plan.chunk_rows * plan.width,
        in_specs=[VMEM] * plan.locs + [ANY] * len(after),
        out_specs=[VMEM] * plan.groups,
    )(*slots, *after)


def channel(plan, parts, channel_qkv, channel_out, up_weight, down_weight):
    groups, width = plan.groups, plan.width
    bands, locations, _ = parts[0].shape
    tile = TILE_LOCS
    assert locations % tile == 0
    tiles = locations // tile
    rows = groups * bands * tile

    def kernel(qkv_hbm, out_hbm, up_hbm, down_hbm, *refs):
        ins, refs = refs[:groups], refs[groups:]
        outs, refs = refs[:groups], refs[groups:]
        qkv_ref, out_ref, up_ref, down_ref, mid, normed, packed, attended, sems = refs
        copies = [
            pltpu.make_async_copy(source, target, sems.at[number])
            for number, (source, target) in enumerate(
                (
                    (qkv_hbm, qkv_ref),
                    (out_hbm, out_ref),
                    (up_hbm, up_ref),
                    (down_hbm, down_ref),
                )
            )
        ]
        for copy in copies:
            copy.start()
        for index in range(tiles):
            for owner in range(groups):
                at = index * rows + owner * bands * tile
                mid[pl.ds(at, bands * tile), :] = (
                    ins[owner][:, index * tile : (index + 1) * tile, :]
                    .reshape(bands * tile, width)
                    .astype(F32)
                )
        norm_into(normed, lambda here: mid[here, :], tiles * rows)
        copies[0].wait()

        def packed_step(block):
            here = aligned(block, COLUMNS)
            factor = jnp.where(block < width // COLUMNS, QUERY_SCALE, 1.0)
            packed[:, here] = (dot(normed[...], qkv_ref[:, here]) * factor).astype(BF16)

        loop(3 * width // COLUMNS, packed_step)
        pairs = width // LANES
        stacked = rows * (LANES // HEAD_DIM)
        first = lax.broadcasted_iota(jnp.int32, (stacked, rows), 0)
        second = lax.broadcasted_iota(jnp.int32, (stacked, rows), 1)
        mask = (first % tile) == (second % tile)

        def attention_step(number):
            index = number // (pairs // CHANNEL_PAIRS)
            mine = aligned(index, rows)
            units = []
            places = []
            for i in range(CHANNEL_PAIRS):
                pair = number % (pairs // CHANNEL_PAIRS) * CHANNEL_PAIRS + i
                query = packed[mine, aligned(pair, LANES)]
                keys = packed[mine, aligned(pair + pairs, LANES)]
                values = packed[mine, aligned(pair + 2 * pairs, LANES)]
                units.append((stack_heads(query), [keys], [with_ones(values)]))
                places.append(aligned(pair, LANES))
            for place, done in zip(places, run_units(units, mask)):
                attended[mine, place] = done

        loop(tiles * pairs // CHANNEL_PAIRS, attention_step)
        copies[1].wait()

        def out_step(block):
            here = aligned(block, COLUMNS)
            mid[:, here] += dot(attended[...], out_ref[:, here])

        loop(width // COLUMNS, out_step)
        norm_into(normed, lambda here: mid[here, :], tiles * rows)
        copies[2].wait()
        copies[3].wait()

        def mlp_step(block):
            places = [aligned(block * MLP_BLOCKS + i, COLUMNS) for i in range(MLP_BLOCKS)]
            raised = [dot(normed[...], up_ref[:, place]) for place in places]
            for place, value in zip(places, raised):
                mid[...] += dot(gelu(value).astype(BF16), down_ref[place, :])

        loop(up_weight.shape[1] // (COLUMNS * MLP_BLOCKS), mlp_step)
        for index in range(tiles):
            for owner in range(groups):
                at = index * rows + owner * bands * tile
                outs[owner][:, index * tile : (index + 1) * tile, :] = (
                    mid[pl.ds(at, bands * tile), :].astype(BF16).reshape(bands, tile, width)
                )

    weights = [channel_qkv, channel_out, up_weight, down_weight]
    size = sum(weight.size for weight in weights)
    count = groups * bands * locations
    return call(
        kernel,
        [jax.ShapeDtypeStruct((bands, locations, width), BF16)] * groups,
        2 * count * size,
        2 * (2 * count * width + size),
        in_specs=[ANY] * 4 + [VMEM] * groups,
        out_specs=[VMEM] * groups,
        scratch_shapes=[pltpu.VMEM(weight.shape, BF16) for weight in weights]
        + [
            pltpu.VMEM((tiles * rows, width), F32),
            pltpu.VMEM((tiles * rows, width), BF16),
            pltpu.VMEM((tiles * rows, 3 * width), BF16),
            pltpu.VMEM((tiles * rows, width), BF16),
            pltpu.SemaphoreType.DMA((len(weights),)),
        ],
    )(*weights, *parts)


def restore(plan, ids, returned):
    locations = plan.loc_dev // (plan.chunks * plan.groups)

    def kernel(ids_ref, *refs):
        ins, out_ref = refs[:-1], refs[-1]
        me = lax.axis_index("loc")
        group = lax.axis_index("band")
        keys = location_keys(plan, ids_ref[pl.ds(me, 1), :])
        place = lax.broadcasted_iota(jnp.int32, (plan.loc_dev, plan.loc_dev), 0)
        inner = place % plan.part_rows
        window = (place // plan.part_rows) % WINDOWS ^ (me % WINDOWS)
        part = (place // (plan.part_rows * WINDOWS)) % plan.share ^ (me // WINDOWS) % plan.share
        owner = (place // locations) % plan.groups ^ group
        chunk = place // (locations * plan.groups)
        wanted = (
            window * plan.block
            + part * plan.rows
            + chunk * plan.chunk_rows
            + owner * plan.part_rows
            + inner
        )
        pick = jnp.where(wanted.astype(F32) == keys, 1.0, 0.0).astype(BF16)
        mine = me // (WINDOWS * plan.share)
        for band in range(plan.band_dev):
            rows = jnp.concatenate([ref[band ^ mine] for ref in ins], axis=0)
            out_ref[:, band, :] = lax.dot_general(
                pick, rows, (((0,), (0,)), ((), ())), preferred_element_type=F32
            ).astype(BF16)

    arrays = [array for chunk in returned for array in chunk]
    size = plan.loc_dev * plan.band_dev * plan.width
    return call(
        kernel,
        jax.ShapeDtypeStruct((plan.loc_dev, plan.band_dev, plan.width), BF16),
        2 * plan.loc_dev * size,
        4 * size,
    )(ids, *arrays)


def body(
    tokens,
    band_index,
    band_table,
    window_ids,
    spatial_qkv,
    spatial_out,
    channel_qkv,
    channel_out,
    up_weight,
    down_weight,
):
    plan = Plan(tokens)
    ids = window_ids.reshape(plan.locs, plan.loc_dev)
    sent = arrange(plan, tokens, ids)
    slots = [exchange(value, "loc", step) for step, value in enumerate(sent)]
    split = plan.locs - LATE_SLOTS
    early = project(plan, slots[:split], band_index, band_table, spatial_qkv)
    late = project(plan, slots[split:], band_index, band_table, spatial_qkv, early[:1])
    query, keys, values = zip(early, late)
    if plan.share > 1:
        same = [
            [(band * plan.share + part) * WINDOWS + window for part in range(plan.share)]
            for band in range(plan.band_dev)
            for window in range(WINDOWS)
        ]
        gather = functools.partial(
            lax.all_gather, axis_name="loc", axis_index_groups=same, axis=0, tiled=True
        )
        keys = [gather(jnp.concatenate(keys, axis=0))]
        values = [gather(jnp.concatenate(values, axis=0))]
    returned = []
    done = []
    for chunk in range(plan.chunks):
        mid = attend(
            plan, chunk, query, keys, values, slots, band_index, band_table, spatial_out
        )
        back = [exchange(value, "loc", step) for step, value in enumerate(mid)]
        parts = regroup(plan, back, done[:1])
        parts = [exchange(value, "band", step) for step, value in enumerate(parts)]
        parts = [part.reshape(plan.band_dev, -1, plan.width) for part in parts]
        done = channel(plan, parts, channel_qkv, channel_out, up_weight, down_weight)
        returned.append([exchange(value, "band", step) for step, value in enumerate(done)])
    return restore(plan, ids, returned)


def solution(mesh):
    placed = (P("loc", "band", None), P(), P(), P(), P(), P(), P(), P(), P(), P())
    return jax.shard_map(
        body, mesh=mesh, in_specs=placed, out_specs=P("loc", "band", None), check_vma=False
    )
```

```python
import functools

import jax
import jax.numpy as jnp
from jax import lax
from jax.experimental import pallas as pl
from jax.experimental.pallas import tpu as pltpu
from jax.sharding import PartitionSpec as P

HEADS = 12
HEAD_DIM = 64
WINDOWS = 2
CHUNKS = 2
LATE_SLOTS = 4
TILE_LOCS = 16
GROUP_LOCS = 8
NORM_ROWS = 128
UNIT_ROWS = 128
STEP_PAIRS = 2
ROW_TILE = 256
LANES = 128
QUERY_SCALE = HEAD_DIM ** (-0.5)
VMEM_LIMIT = 28 * 1024 * 1024

F32 = jnp.float32
BF16 = jnp.bfloat16


def dot(left, right):
    return jnp.dot(left, right, preferred_element_type=F32)


def dot_t(left, right):
    return lax.dot_general(left, right, (((1,), (1,)), ((), ())), preferred_element_type=F32)


def norm_rows(values):
    centre = values - jnp.mean(values, axis=-1, keepdims=True)
    spread = jnp.mean(centre * centre, axis=-1, keepdims=True)
    return centre * lax.rsqrt(spread + 1e-05)


def gelu(values):
    inner = values * (0.7978845608028654 + 0.035677408136300125 * (values * values))
    return (0.5 * values) * (1.0 + jnp.tanh(inner))


def call(kernel, out_shape, flops, nbytes, **kwargs):
    return pl.pallas_call(
        kernel,
        out_shape=out_shape,
        compiler_params=pltpu.CompilerParams(vmem_limit_bytes=VMEM_LIMIT),
        cost_estimate=pl.CostEstimate(flops=flops, bytes_accessed=nbytes, transcendentals=0),
        **kwargs,
    )


def exchange(value, axis, step):
    if step == 0:
        return value
    return lax.ppermute(value, axis, [(i, i ^ step) for i in range(lax.axis_size(axis))])


def exchange_all(values):
    got = list(values)
    for step in reversed(range(len(values))):
        got[step] = exchange(values[step], "loc", step)
    return got


class Plan:
    def __init__(self, tokens):
        self.loc_dev, self.band_dev, self.width = tokens.shape
        self.locs = lax.axis_size("loc")
        self.groups = lax.axis_size("band")
        self.share = self.locs // (self.band_dev * WINDOWS)
        assert self.share * self.band_dev * WINDOWS == self.locs
        self.block = self.loc_dev // WINDOWS
        self.rows = self.block // self.share
        self.chunks = CHUNKS
        self.chunk_rows = self.rows // self.chunks
        self.part_rows = self.chunk_rows // self.groups
        assert self.part_rows * self.groups * self.chunks * self.share == self.block


def location_keys(plan, ids):
    size = plan.loc_dev
    row = jnp.broadcast_to(ids.astype(F32), (size, size))
    first = lax.broadcasted_iota(jnp.int32, (size, size), 0)
    second = lax.broadcasted_iota(jnp.int32, (size, size), 1)
    column = jnp.sum(jnp.where(first == second, row, 0.0), axis=1, keepdims=True)
    before = jnp.where((column == row) & (first < second), 1.0, 0.0)
    rank = jnp.sum(before, axis=0, keepdims=True)
    return ids.astype(F32) * plan.block + rank


def arrange(plan, tokens, ids):
    def kernel(ids_ref, x_ref, *rest):
        outs, bands = rest[: plan.locs], rest[plan.locs]
        me = lax.axis_index("loc")
        group = lax.axis_index("band")
        keys = location_keys(plan, ids_ref[pl.ds(me, 1), :])
        for band in range(plan.band_dev):
            bands[band] = x_ref[:, band, :]
        place = lax.broadcasted_iota(jnp.int32, (plan.rows, plan.loc_dev), 0)
        chunk = place // plan.chunk_rows
        owner = (place // plan.part_rows) % plan.groups
        rank = chunk * plan.chunk_rows + (owner ^ group) * plan.part_rows + place % plan.part_rows
        for slot in range(plan.locs):
            peer = me ^ slot
            window = peer % WINDOWS
            part = (peer // WINDOWS) % plan.share
            band = peer // (WINDOWS * plan.share)
            wanted = rank + (window * plan.block + part * plan.rows)
            pick = jnp.where(wanted.astype(F32) == keys, 1.0, 0.0).astype(BF16)
            outs[slot][...] = dot(pick, bands[band]).astype(BF16)

    shape = jax.ShapeDtypeStruct((plan.rows, plan.width), BF16)
    return call(
        kernel,
        [shape] * plan.locs,
        2 * plan.loc_dev * tokens.size,
        4 * tokens.size,
        scratch_shapes=[pltpu.VMEM((plan.band_dev, plan.loc_dev, plan.width), BF16)],
    )(ids, tokens)


def embed_row(plan, index_ref, table_ref):
    band = lax.axis_index("loc") // (WINDOWS * plan.share)
    number = index_ref[lax.axis_index("band") * plan.band_dev + band]
    return table_ref[pl.ds(number, 1), :]


SMEM = pl.BlockSpec(memory_space=pltpu.SMEM)
VMEM = pl.BlockSpec(memory_space=pltpu.VMEM)
ANY = pl.BlockSpec(memory_space=pl.ANY)


def loop(count, step):
    lax.fori_loop(0, count, lambda i, _: (step(i), 0)[1], 0)


def aligned(index, size):
    return pl.ds(pl.multiple_of(index * size, size), size)


def norm_into(target, rows_of, rows):
    tile = min(rows, NORM_ROWS)

    def step(index):
        here = aligned(index, tile)
        target[here, :] = norm_rows(rows_of(here)).astype(BF16)

    loop(rows // tile, step)


def project(plan, slots, index, table, weights, after=()):
    count = len(slots)
    width = plan.width

    def kernel(index_ref, table_ref, w_ref, *rest):
        ins, (q_ref, k_ref, v_ref) = rest[:count], rest[count + len(after) :]
        embed = embed_row(plan, index_ref, table_ref)
        for first in range(0, count, 2):
            some = ins[first : first + 2]
            rows = jnp.concatenate([ref[...].astype(F32) for ref in some], axis=0) + embed
            normed = norm_rows(rows).astype(BF16)
            here = pl.ds(first * plan.rows, len(some) * plan.rows)
            q_ref[here, :] = (dot(normed, w_ref[:, :width]) * QUERY_SCALE).astype(BF16)
            k_ref[here, :] = dot(normed, w_ref[:, width : 2 * width]).astype(BF16)
            v_ref[here, :] = dot(normed, w_ref[:, 2 * width :]).astype(BF16)

    rows = count * plan.rows
    shape = jax.ShapeDtypeStruct((rows, width), BF16)
    return call(
        kernel,
        [shape] * 3,
        2 * rows * width * 3 * width,
        2 * (4 * rows * width + 3 * width * width),
        in_specs=[SMEM, VMEM, VMEM] + [VMEM] * count + [ANY] * len(after),
        out_specs=[VMEM] * 3,
    )(index, table, weights, *slots, *after)


def head_masks(rows):
    lane = lax.broadcasted_iota(jnp.int32, (rows, LANES), 1)
    return [(lane // HEAD_DIM) == head for head in range(LANES // HEAD_DIM)]


def stack_heads(query):
    return jnp.concatenate(
        [jnp.where(inside, query, jnp.zeros_like(query)) for inside in head_masks(query.shape[0])],
        axis=0,
    )


def join_heads(stacked):
    heads = LANES // HEAD_DIM
    rows = stacked.shape[0] // heads
    joined = stacked[:rows]
    for head, inside in list(enumerate(head_masks(rows)))[1:]:
        joined = jnp.where(inside, stacked[head * rows : (head + 1) * rows], joined)
    return joined


def with_ones(value):
    return jnp.concatenate([value, jnp.ones(value.shape, BF16)], axis=1)


def run_units(units, mask=None):
    def scores_of(unit):
        query, keys, _ = unit
        scores = [dot_t(query, piece) for piece in keys]
        if mask is not None:
            scores = [jnp.where(mask, piece, -1e30) for piece in scores]
        return scores

    results = []
    ahead = scores_of(units[0])
    for number, (_, _, values) in enumerate(units):
        scores = ahead
        if number + 1 < len(units):
            ahead = scores_of(units[number + 1])
        peak = functools.reduce(
            jnp.maximum, [jnp.max(piece, axis=-1, keepdims=True) for piece in scores]
        )
        total = None
        for piece, value in zip(scores, values):
            part = dot(jnp.exp(piece - peak).astype(BF16), value)
            total = part if total is None else total + part
        results.append(
            (join_heads(total[:, :LANES]) / join_heads(total[:, LANES:])).astype(BF16)
        )
    return results


def attend(plan, chunk, query, keys, values, slots, index, table, spatial_out):
    width, rows = plan.width, plan.chunk_rows
    pieces, sources = len(keys), len(query)
    total = plan.locs * rows
    pairs = width // LANES
    unit = min(total, UNIT_ROWS)

    def kernel(index_ref, table_ref, w_ref, *rest):
        q_refs, rest = rest[:sources], rest[sources:]
        k_refs, rest = rest[:pieces], rest[pieces:]
        v_refs, rest = rest[:pieces], rest[pieces:]
        slot_refs, rest = rest[: plan.locs], rest[plan.locs :]
        outs, (asked, result, added) = rest[: plan.locs], rest[plan.locs :]
        at = 0
        for ref in q_refs:
            for slot in range(ref.shape[0] // plan.rows):
                asked[pl.ds(at, rows), :] = ref[pl.ds(slot * plan.rows + chunk * rows, rows), :]
                at += rows
        def step(number):
            units, places = [], []
            for i in range(STEP_PAIRS):
                here = aligned(number * STEP_PAIRS + i, LANES)
                pair_keys = [ref[:, here] for ref in k_refs]
                pair_values = [with_ones(ref[:, here]) for ref in v_refs]
                for first in range(0, total, unit):
                    place = (pl.ds(first, unit), here)
                    units.append((stack_heads(asked[place]), pair_keys, pair_values))
                    places.append(place)
            for place, done in zip(places, run_units(units)):
                result[place] = done

        loop(pairs // STEP_PAIRS, step)
        added[...] = dot(result[...], w_ref[...])
        embed = embed_row(plan, index_ref, table_ref)
        for slot in range(plan.locs):
            start = slot_refs[slot][pl.ds(chunk * rows, rows), :].astype(F32) + embed
            outs[slot][...] = (start + added[pl.ds(slot * rows, rows), :]).astype(BF16)

    key_rows = sum(piece.shape[0] for piece in keys)
    return call(
        kernel,
        [jax.ShapeDtypeStruct((rows, width), BF16)] * plan.locs,
        16 * total * key_rows * width,
        2 * width * (2 * key_rows + 3 * total + width),
        in_specs=[SMEM] + [VMEM] * (2 + sources + 2 * pieces + plan.locs),
        out_specs=[VMEM] * plan.locs,
        scratch_shapes=[
            pltpu.VMEM((total, width), BF16),
            pltpu.VMEM((total, width), BF16),
            pltpu.VMEM((total, width), F32),
        ],
    )(index, table, spatial_out, *query, *keys, *values, *slots)


def regroup(plan, slots, after=()):
    rows = plan.part_rows
    if rows % 16:
        stacked = jnp.stack(slots).reshape(plan.locs, plan.groups, rows, plan.width)
        return [stacked[:, owner] for owner in range(plan.groups)]

    def kernel(*refs):
        ins, outs = refs[: plan.locs], refs[plan.locs + len(after) :]
        for slot in range(plan.locs):
            for owner in range(plan.groups):
                outs[owner][slot] = ins[slot][owner * rows : (owner + 1) * rows, :]

    shape = jax.ShapeDtypeStruct((plan.locs, rows, plan.width), BF16)
    return call(
        kernel,
        [shape] * plan.groups,
        0,
        4 * plan.locs * plan.chunk_rows * plan.width,
        in_specs=[VMEM] * plan.locs + [ANY] * len(after),
        out_specs=[VMEM] * plan.groups,
    )(*slots, *after)


def channel(plan, parts, channel_qkv, channel_out, up_weight, down_weight):
    groups, width = plan.groups, plan.width
    bands, locations, _ = parts[0].shape
    tile, small = TILE_LOCS, GROUP_LOCS
    assert locations % tile == 0
    group_rows = groups * bands * small
    rows = groups * bands * locations
    row_tile = min(rows, ROW_TILE)

    def kernel(qkv_ref, out_ref, up_ref, down_ref, *refs):
        ins, refs = refs[:groups], refs[groups:]
        outs, (mid, normed, packed, attended) = refs[:groups], refs[groups:]
        pieces = [
            (owner, band, first)
            for owner in range(groups)
            for band in range(bands)
            for first in range(0, locations, tile)
        ]

        def places(owner, band, first):
            return [
                pl.ds((at // small) * group_rows + (owner * bands + band) * small, small)
                for at in range(first, first + tile, small)
            ]

        for owner, band, first in pieces:
            piece = ins[owner][band, first : first + tile, :].astype(F32)
            for number, place in enumerate(places(owner, band, first)):
                mid[place, :] = piece[number * small : (number + 1) * small]
        norm_into(normed, lambda here: mid[here, :], rows)

        def packed_step(block):
            here = aligned(block, width)
            factor = jnp.where(block == 0, QUERY_SCALE, 1.0)
            packed[:, here] = (dot(normed[...], qkv_ref[:, here]) * factor).astype(BF16)

        loop(3, packed_step)
        pairs = width // LANES
        stacked = group_rows * (LANES // HEAD_DIM)
        one = lax.broadcasted_iota(jnp.int32, (stacked, group_rows), 0)
        other = lax.broadcasted_iota(jnp.int32, (stacked, group_rows), 1)
        mask = (one % small) == (other % small)

        def attention_step(pair):
            units, spots = [], []
            for first in range(0, rows, group_rows):
                mine = pl.ds(first, group_rows)
                query = packed[mine, aligned(pair, LANES)]
                keys = packed[mine, aligned(pair + pairs, LANES)]
                values = packed[mine, aligned(pair + 2 * pairs, LANES)]
                units.append((stack_heads(query), [keys], [with_ones(values)]))
                spots.append((mine, aligned(pair, LANES)))
            for spot, done in zip(spots, run_units(units, mask)):
                attended[spot] = done

        loop(pairs, attention_step)
        mid[...] += dot(attended[...], out_ref[...])
        norm_into(normed, lambda here: mid[here, :], rows)

        def mlp_step(block):
            here = aligned(block, width)
            tiles = [pl.ds(first, row_tile) for first in range(0, rows, row_tile)]
            raised = [dot(normed[mine, :], up_ref[:, here]) for mine in tiles]
            for mine, value in zip(tiles, raised):
                mid[mine, :] += dot(gelu(value).astype(BF16), down_ref[here, :])

        loop(up_weight.shape[1] // width, mlp_step)
        for owner, band, first in pieces:
            piece = jnp.concatenate(
                [mid[place, :] for place in places(owner, band, first)], axis=0
            )
            outs[owner][band, first : first + tile, :] = piece.astype(BF16)

    weights = [channel_qkv, channel_out, up_weight, down_weight]
    size = sum(weight.size for weight in weights)
    return call(
        kernel,
        [jax.ShapeDtypeStruct((bands, locations, width), BF16)] * groups,
        2 * rows * size,
        2 * (2 * rows * width + size),
        in_specs=[VMEM] * (4 + groups),
        out_specs=[VMEM] * groups,
        scratch_shapes=[
            pltpu.VMEM((rows, width), F32),
            pltpu.VMEM((rows, width), BF16),
            pltpu.VMEM((rows, 3 * width), BF16),
            pltpu.VMEM((rows, width), BF16),
        ],
    )(*weights, *parts)


def restore(plan, ids, returned):
    locations = plan.loc_dev // (plan.chunks * plan.groups)

    def kernel(ids_ref, *refs):
        ins, out_ref = refs[:-1], refs[-1]
        me = lax.axis_index("loc")
        group = lax.axis_index("band")
        keys = location_keys(plan, ids_ref[pl.ds(me, 1), :])
        place = lax.broadcasted_iota(jnp.int32, (plan.loc_dev, plan.loc_dev), 0)
        inner = place % plan.part_rows
        window = (place // plan.part_rows) % WINDOWS ^ (me % WINDOWS)
        part = (place // (plan.part_rows * WINDOWS)) % plan.share ^ (me // WINDOWS) % plan.share
        owner = (place // locations) % plan.groups ^ group
        chunk = place // (locations * plan.groups)
        wanted = (
            window * plan.block
            + part * plan.rows
            + chunk * plan.chunk_rows
            + owner * plan.part_rows
            + inner
        )
        pick = jnp.where(wanted.astype(F32) == keys, 1.0, 0.0).astype(BF16)
        mine = me // (WINDOWS * plan.share)
        for band in range(plan.band_dev):
            rows = jnp.concatenate([ref[band ^ mine] for ref in ins], axis=0)
            out_ref[:, band, :] = lax.dot_general(
                pick, rows, (((0,), (0,)), ((), ())), preferred_element_type=F32
            ).astype(BF16)

    arrays = [array for chunk in returned for array in chunk]
    size = plan.loc_dev * plan.band_dev * plan.width
    return call(
        kernel,
        jax.ShapeDtypeStruct((plan.loc_dev, plan.band_dev, plan.width), BF16),
        2 * plan.loc_dev * size,
        4 * size,
    )(ids, *arrays)


def body(
    tokens,
    band_index,
    band_table,
    window_ids,
    spatial_qkv,
    spatial_out,
    channel_qkv,
    channel_out,
    up_weight,
    down_weight,
):
    plan = Plan(tokens)
    ids = window_ids.reshape(plan.locs, plan.loc_dev)
    sent = arrange(plan, tokens, ids)
    slots = exchange_all(sent)
    split = plan.locs - LATE_SLOTS
    early = project(plan, slots[:split], band_index, band_table, spatial_qkv)
    late = project(plan, slots[split:], band_index, band_table, spatial_qkv, early[:1])
    query, keys, values = zip(early, late)
    if plan.share > 1:
        same = [
            [(band * plan.share + part) * WINDOWS + window for part in range(plan.share)]
            for band in range(plan.band_dev)
            for window in range(WINDOWS)
        ]
        gather = functools.partial(
            lax.all_gather, axis_name="loc", axis_index_groups=same, axis=0, tiled=True
        )
        keys = [gather(jnp.concatenate(keys, axis=0))]
        values = [gather(jnp.concatenate(values, axis=0))]
    mids = [
        attend(plan, chunk, query, keys, values, slots, band_index, band_table, spatial_out)
        for chunk in range(plan.chunks)
    ]
    backs = [exchange_all(mid) for mid in mids]
    returned = []
    done = []
    for chunk in range(plan.chunks):
        ahead = [mid[0] for mid in mids[chunk + 1 : chunk + 2]] + list(done[:1])
        parts = regroup(plan, backs[chunk], ahead)
        parts = [exchange(value, "band", step) for step, value in enumerate(parts)]
        parts = [part.reshape(plan.band_dev, -1, plan.width) for part in parts]
        done = channel(plan, parts, channel_qkv, channel_out, up_weight, down_weight)
        returned.append([exchange(value, "band", step) for step, value in enumerate(done)])
    return restore(plan, ids, returned)


def solution(mesh):
    placed = (P("loc", "band", None), P(), P(), P(), P(), P(), P(), P(), P(), P())
    return jax.shard_map(
        body, mesh=mesh, in_specs=placed, out_specs=P("loc", "band", None), check_vma=False
    )
```

```python
import functools

import jax
import jax.numpy as jnp
from jax import lax
from jax.experimental import pallas as pl
from jax.experimental.pallas import tpu as pltpu
from jax.sharding import PartitionSpec as P

HEADS = 12
HEAD_DIM = 64
WINDOWS = 2
CHUNKS = 2
LATE_SLOTS = 4
TILE_LOCS = 16
GROUP_LOCS = 8
NORM_ROWS = 128
UNIT_ROWS = 128
STEP_PAIRS = 2
ROW_TILE = 256
LANES = 128
QUERY_SCALE = HEAD_DIM ** (-0.5)
VMEM_LIMIT = 28 * 1024 * 1024

F32 = jnp.float32
BF16 = jnp.bfloat16


def dot(left, right):
    return jnp.dot(left, right, preferred_element_type=F32)


def dot_t(left, right):
    return lax.dot_general(left, right, (((1,), (1,)), ((), ())), preferred_element_type=F32)


def norm_rows(values):
    centre = values - jnp.mean(values, axis=-1, keepdims=True)
    spread = jnp.mean(centre * centre, axis=-1, keepdims=True)
    return centre * lax.rsqrt(spread + 1e-05)


def gelu(values):
    inner = values * (0.7978845608028654 + 0.035677408136300125 * (values * values))
    return (0.5 * values) * (1.0 + jnp.tanh(inner))


def call(kernel, out_shape, flops, nbytes, **kwargs):
    return pl.pallas_call(
        kernel,
        out_shape=out_shape,
        compiler_params=pltpu.CompilerParams(vmem_limit_bytes=VMEM_LIMIT),
        cost_estimate=pl.CostEstimate(flops=flops, bytes_accessed=nbytes, transcendentals=0),
        **kwargs,
    )


def exchange(value, axis, step):
    if step == 0:
        return value
    return lax.ppermute(value, axis, [(i, i ^ step) for i in range(lax.axis_size(axis))])


def exchange_all(values):
    got = list(values)
    for step in reversed(range(len(values))):
        got[step] = exchange(values[step], "loc", step)
    return got


class Plan:
    def __init__(self, tokens):
        self.loc_dev, self.band_dev, self.width = tokens.shape
        self.locs = lax.axis_size("loc")
        self.groups = lax.axis_size("band")
        self.share = self.locs // (self.band_dev * WINDOWS)
        assert self.share * self.band_dev * WINDOWS == self.locs
        self.block = self.loc_dev // WINDOWS
        self.rows = self.block // self.share
        self.chunks = CHUNKS
        self.chunk_rows = self.rows // self.chunks
        self.part_rows = self.chunk_rows // self.groups
        assert self.part_rows * self.groups * self.chunks * self.share == self.block


def location_keys(plan, ids):
    size = plan.loc_dev
    row = jnp.broadcast_to(ids.astype(F32), (size, size))
    first = lax.broadcasted_iota(jnp.int32, (size, size), 0)
    second = lax.broadcasted_iota(jnp.int32, (size, size), 1)
    column = jnp.sum(jnp.where(first == second, row, 0.0), axis=1, keepdims=True)
    before = jnp.where((column == row) & (first < second), 1.0, 0.0)
    rank = jnp.sum(before, axis=0, keepdims=True)
    return ids.astype(F32) * plan.block + rank


def arrange(plan, tokens, ids):
    def kernel(ids_ref, x_ref, *rest):
        outs, bands = rest[: plan.locs], rest[plan.locs]
        me = lax.axis_index("loc")
        keys = location_keys(plan, ids_ref[pl.ds(me, 1), :])
        for band in range(plan.band_dev):
            bands[band] = x_ref[:, band, :]
        place = lax.broadcasted_iota(jnp.int32, (plan.rows, plan.loc_dev), 0)
        chunk = place // plan.chunk_rows
        owner = (place // plan.part_rows) % plan.groups
        rank = chunk * plan.chunk_rows + owner * plan.part_rows + place % plan.part_rows
        for slot in range(plan.locs):
            peer = me ^ slot
            window = peer % WINDOWS
            part = (peer // WINDOWS) % plan.share
            band = peer // (WINDOWS * plan.share)
            wanted = rank + (window * plan.block + part * plan.rows)
            pick = jnp.where(wanted.astype(F32) == keys, 1.0, 0.0).astype(BF16)
            outs[slot][...] = dot(pick, bands[band]).astype(BF16)

    shape = jax.ShapeDtypeStruct((plan.rows, plan.width), BF16)
    return call(
        kernel,
        [shape] * plan.locs,
        2 * plan.loc_dev * tokens.size,
        4 * tokens.size,
        scratch_shapes=[pltpu.VMEM((plan.band_dev, plan.loc_dev, plan.width), BF16)],
    )(ids, tokens)


def embed_row(plan, index_ref, table_ref):
    band = lax.axis_index("loc") // (WINDOWS * plan.share)
    number = index_ref[lax.axis_index("band") * plan.band_dev + band]
    return table_ref[pl.ds(number, 1), :]


SMEM = pl.BlockSpec(memory_space=pltpu.SMEM)
VMEM = pl.BlockSpec(memory_space=pltpu.VMEM)
ANY = pl.BlockSpec(memory_space=pl.ANY)


def loop(count, step):
    lax.fori_loop(0, count, lambda i, _: (step(i), 0)[1], 0)


def aligned(index, size):
    return pl.ds(pl.multiple_of(index * size, size), size)


def norm_into(target, rows_of, rows):
    tile = min(rows, NORM_ROWS)

    def step(index):
        here = aligned(index, tile)
        target[here, :] = norm_rows(rows_of(here)).astype(BF16)

    loop(rows // tile, step)


def project(plan, slots, index, table, weights, after=()):
    count = len(slots)
    width = plan.width

    def kernel(index_ref, table_ref, w_ref, *rest):
        ins, (q_ref, k_ref, v_ref) = rest[:count], rest[count + len(after) :]
        embed = embed_row(plan, index_ref, table_ref)
        for first in range(0, count, 2):
            some = ins[first : first + 2]
            rows = jnp.concatenate([ref[...].astype(F32) for ref in some], axis=0) + embed
            normed = norm_rows(rows).astype(BF16)
            here = pl.ds(first * plan.rows, len(some) * plan.rows)
            q_ref[here, :] = (dot(normed, w_ref[:, :width]) * QUERY_SCALE).astype(BF16)
            k_ref[here, :] = dot(normed, w_ref[:, width : 2 * width]).astype(BF16)
            v_ref[here, :] = dot(normed, w_ref[:, 2 * width :]).astype(BF16)

    rows = count * plan.rows
    shape = jax.ShapeDtypeStruct((rows, width), BF16)
    return call(
        kernel,
        [shape] * 3,
        2 * rows * width * 3 * width,
        2 * (4 * rows * width + 3 * width * width),
        in_specs=[SMEM, VMEM, VMEM] + [VMEM] * count + [ANY] * len(after),
        out_specs=[VMEM] * 3,
    )(index, table, weights, *slots, *after)


def head_masks(rows):
    lane = lax.broadcasted_iota(jnp.int32, (rows, LANES), 1)
    return [(lane // HEAD_DIM) == head for head in range(LANES // HEAD_DIM)]


def stack_heads(query):
    return jnp.concatenate(
        [jnp.where(inside, query, jnp.zeros_like(query)) for inside in head_masks(query.shape[0])],
        axis=0,
    )


def join_heads(stacked):
    heads = LANES // HEAD_DIM
    rows = stacked.shape[0] // heads
    joined = stacked[:rows]
    for head, inside in list(enumerate(head_masks(rows)))[1:]:
        joined = jnp.where(inside, stacked[head * rows : (head + 1) * rows], joined)
    return joined


def with_ones(value):
    return jnp.concatenate([value, jnp.ones(value.shape, BF16)], axis=1)


def run_units(units, mask=None):
    def scores_of(unit):
        query, keys, _ = unit
        scores = [dot_t(query, piece) for piece in keys]
        if mask is not None:
            scores = [jnp.where(mask, piece, -1e30) for piece in scores]
        return scores

    results = []
    ahead = scores_of(units[0])
    for number, (_, _, values) in enumerate(units):
        scores = ahead
        if number + 1 < len(units):
            ahead = scores_of(units[number + 1])
        peak = functools.reduce(
            jnp.maximum, [jnp.max(piece, axis=-1, keepdims=True) for piece in scores]
        )
        total = None
        for piece, value in zip(scores, values):
            part = dot(jnp.exp(piece - peak).astype(BF16), value)
            total = part if total is None else total + part
        results.append(
            (join_heads(total[:, :LANES]) / join_heads(total[:, LANES:])).astype(BF16)
        )
    return results


def attend(plan, chunk, query, keys, values, slots, index, table, spatial_out):
    width, rows = plan.width, plan.chunk_rows
    pieces, sources = len(keys), len(query)
    total = plan.locs * rows
    pairs = width // LANES
    unit = min(total, UNIT_ROWS)

    def kernel(index_ref, table_ref, w_ref, *rest):
        q_refs, rest = rest[:sources], rest[sources:]
        k_refs, rest = rest[:pieces], rest[pieces:]
        v_refs, rest = rest[:pieces], rest[pieces:]
        slot_refs, rest = rest[: plan.locs], rest[plan.locs :]
        out_ref, asked, result, added = rest
        me = lax.axis_index("loc")
        at = 0
        for ref in q_refs:
            for slot in range(ref.shape[0] // plan.rows):
                asked[pl.ds(at, rows), :] = ref[pl.ds(slot * plan.rows + chunk * rows, rows), :]
                at += rows
        def step(number):
            units, places = [], []
            for i in range(STEP_PAIRS):
                here = aligned(number * STEP_PAIRS + i, LANES)
                pair_keys = [ref[:, here] for ref in k_refs]
                pair_values = [with_ones(ref[:, here]) for ref in v_refs]
                for first in range(0, total, unit):
                    place = (pl.ds(first, unit), here)
                    units.append((stack_heads(asked[place]), pair_keys, pair_values))
                    places.append(place)
            for place, done in zip(places, run_units(units)):
                result[place] = done

        loop(pairs // STEP_PAIRS, step)
        added[...] = dot(result[...], w_ref[...])
        embed = embed_row(plan, index_ref, table_ref)
        for slot in range(plan.locs):
            start = slot_refs[slot][pl.ds(chunk * rows, rows), :].astype(F32) + embed
            mid = (start + added[pl.ds(slot * rows, rows), :]).astype(BF16)
            for owner in range(plan.groups):
                part = mid[owner * plan.part_rows : (owner + 1) * plan.part_rows]
                out_ref[owner, me ^ slot] = part

    key_rows = sum(piece.shape[0] for piece in keys)
    return call(
        kernel,
        jax.ShapeDtypeStruct((plan.groups, plan.locs, plan.part_rows, width), BF16),
        16 * total * key_rows * width,
        2 * width * (2 * key_rows + 3 * total + width),
        in_specs=[SMEM] + [VMEM] * (2 + sources + 2 * pieces + plan.locs),
        out_specs=VMEM,
        scratch_shapes=[
            pltpu.VMEM((total, width), BF16),
            pltpu.VMEM((total, width), BF16),
            pltpu.VMEM((total, width), F32),
        ],
    )(index, table, spatial_out, *query, *keys, *values, *slots)


def channel(plan, parts, channel_qkv, channel_out, up_weight, down_weight):
    groups, width = plan.groups, plan.width
    _, bands, locations, _ = parts.shape
    tile, small = TILE_LOCS, GROUP_LOCS
    assert locations % tile == 0
    group_rows = groups * bands * small
    rows = groups * bands * locations
    row_tile = min(rows, ROW_TILE)

    def kernel(qkv_ref, out_ref, up_ref, down_ref, *refs):
        in_ref, *refs = refs
        outs, (mid, normed, packed, attended) = refs[:groups], refs[groups:]
        me = lax.axis_index("band")
        pieces = [
            (owner, band, first)
            for owner in range(groups)
            for band in range(bands)
            for first in range(0, locations, tile)
        ]

        def places(owner, band, first):
            return [
                pl.ds((at // small) * group_rows + (owner * bands + band) * small, small)
                for at in range(first, first + tile, small)
            ]

        for owner, band, first in pieces:
            piece = in_ref[me ^ owner, band, first : first + tile, :].astype(F32)
            for number, place in enumerate(places(owner, band, first)):
                mid[place, :] = piece[number * small : (number + 1) * small]
        norm_into(normed, lambda here: mid[here, :], rows)

        def packed_step(block):
            here = aligned(block, width)
            factor = jnp.where(block == 0, QUERY_SCALE, 1.0)
            packed[:, here] = (dot(normed[...], qkv_ref[:, here]) * factor).astype(BF16)

        loop(3, packed_step)
        pairs = width // LANES
        stacked = group_rows * (LANES // HEAD_DIM)
        one = lax.broadcasted_iota(jnp.int32, (stacked, group_rows), 0)
        other = lax.broadcasted_iota(jnp.int32, (stacked, group_rows), 1)
        mask = (one % small) == (other % small)

        def attention_step(pair):
            units, spots = [], []
            for first in range(0, rows, group_rows):
                mine = pl.ds(first, group_rows)
                query = packed[mine, aligned(pair, LANES)]
                keys = packed[mine, aligned(pair + pairs, LANES)]
                values = packed[mine, aligned(pair + 2 * pairs, LANES)]
                units.append((stack_heads(query), [keys], [with_ones(values)]))
                spots.append((mine, aligned(pair, LANES)))
            for spot, done in zip(spots, run_units(units, mask)):
                attended[spot] = done

        loop(pairs, attention_step)
        mid[...] += dot(attended[...], out_ref[...])
        norm_into(normed, lambda here: mid[here, :], rows)

        def mlp_step(block):
            here = aligned(block, width)
            tiles = [pl.ds(first, row_tile) for first in range(0, rows, row_tile)]
            raised = [dot(normed[mine, :], up_ref[:, here]) for mine in tiles]
            for mine, value in zip(tiles, raised):
                mid[mine, :] += dot(gelu(value).astype(BF16), down_ref[here, :])

        loop(up_weight.shape[1] // width, mlp_step)
        for owner, band, first in pieces:
            piece = jnp.concatenate(
                [mid[place, :] for place in places(owner, band, first)], axis=0
            )
            outs[owner][band, first : first + tile, :] = piece.astype(BF16)

    weights = [channel_qkv, channel_out, up_weight, down_weight]
    size = sum(weight.size for weight in weights)
    return call(
        kernel,
        [jax.ShapeDtypeStruct((bands, locations, width), BF16)] * groups,
        2 * rows * size,
        2 * (2 * rows * width + size),
        in_specs=[VMEM] * 5,
        out_specs=[VMEM] * groups,
        scratch_shapes=[
            pltpu.VMEM((rows, width), F32),
            pltpu.VMEM((rows, width), BF16),
            pltpu.VMEM((rows, 3 * width), BF16),
            pltpu.VMEM((rows, width), BF16),
        ],
    )(*weights, parts)


def restore(plan, ids, returned):
    locations = plan.loc_dev // (plan.chunks * plan.groups)

    def kernel(ids_ref, *refs):
        ins, out_ref = refs[:-1], refs[-1]
        me = lax.axis_index("loc")
        group = lax.axis_index("band")
        keys = location_keys(plan, ids_ref[pl.ds(me, 1), :])
        place = lax.broadcasted_iota(jnp.int32, (plan.loc_dev, plan.loc_dev), 0)
        inner = place % plan.part_rows
        window = (place // plan.part_rows) % WINDOWS
        part = (place // (plan.part_rows * WINDOWS)) % plan.share
        owner = (place // locations) % plan.groups ^ group
        chunk = place // (locations * plan.groups)
        wanted = (
            window * plan.block
            + part * plan.rows
            + chunk * plan.chunk_rows
            + owner * plan.part_rows
            + inner
        )
        pick = jnp.where(wanted.astype(F32) == keys, 1.0, 0.0).astype(BF16)
        for band in range(plan.band_dev):
            rows = jnp.concatenate([ref[band] for ref in ins], axis=0)
            out_ref[:, band, :] = lax.dot_general(
                pick, rows, (((0,), (0,)), ((), ())), preferred_element_type=F32
            ).astype(BF16)

    arrays = [array for chunk in returned for array in chunk]
    size = plan.loc_dev * plan.band_dev * plan.width
    return call(
        kernel,
        jax.ShapeDtypeStruct((plan.loc_dev, plan.band_dev, plan.width), BF16),
        2 * plan.loc_dev * size,
        4 * size,
    )(ids, *arrays)


def body(
    tokens,
    band_index,
    band_table,
    window_ids,
    spatial_qkv,
    spatial_out,
    channel_qkv,
    channel_out,
    up_weight,
    down_weight,
):
    plan = Plan(tokens)
    ids = window_ids.reshape(plan.locs, plan.loc_dev)
    sent = arrange(plan, tokens, ids)
    slots = exchange_all(sent)
    split = plan.locs - LATE_SLOTS
    early = project(plan, slots[:split], band_index, band_table, spatial_qkv)
    late = project(plan, slots[split:], band_index, band_table, spatial_qkv, early[:1])
    query, keys, values = zip(early, late)
    if plan.share > 1:
        same = [
            [(band * plan.share + part) * WINDOWS + window for part in range(plan.share)]
            for band in range(plan.band_dev)
            for window in range(WINDOWS)
        ]
        gather = functools.partial(
            lax.all_gather, axis_name="loc", axis_index_groups=same, axis=0, tiled=True
        )
        keys = [gather(jnp.concatenate(keys, axis=0))]
        values = [gather(jnp.concatenate(values, axis=0))]
    mids = [
        attend(plan, chunk, query, keys, values, slots, band_index, band_table, spatial_out)
        for chunk in range(plan.chunks)
    ]
    returned = []
    for mid in mids:
        parts = lax.all_to_all(
            mid.reshape(-1, plan.part_rows, plan.width), ("band", "loc"), 0, 0, tiled=True
        )
        parts = parts.reshape(plan.groups, plan.band_dev, -1, plan.width)
        done = channel(plan, parts, channel_qkv, channel_out, up_weight, down_weight)
        returned.append([exchange(value, "band", step) for step, value in enumerate(done)])
    return restore(plan, ids, returned)


def solution(mesh):
    placed = (P("loc", "band", None), P(), P(), P(), P(), P(), P(), P(), P(), P())
    return jax.shard_map(
        body, mesh=mesh, in_specs=placed, out_specs=P("loc", "band", None), check_vma=False
    )
```

```python
import functools

import jax
import jax.numpy as jnp
from jax import lax
from jax.experimental import pallas as pl
from jax.experimental.pallas import tpu as pltpu
from jax.sharding import PartitionSpec as P

HEADS = 12
HEAD_DIM = 64
WINDOWS = 2
CORES = 2
TILE_LOCS = 16
GROUP_LOCS = 8
NORM_ROWS = 128
UNIT_ROWS = 128
STEP_PAIRS = 2
ROW_TILE = 256
LANES = 128
QUERY_SCALE = HEAD_DIM ** (-0.5)
VMEM_LIMIT = 28 * 1024 * 1024
WIDE_LIMIT = 52 * 1024 * 1024

F32 = jnp.float32
BF16 = jnp.bfloat16


def dot(left, right):
    return jnp.dot(left, right, preferred_element_type=F32)


def dot_t(left, right):
    return lax.dot_general(left, right, (((1,), (1,)), ((), ())), preferred_element_type=F32)


def norm_rows(values):
    centre = values - jnp.mean(values, axis=-1, keepdims=True)
    spread = jnp.mean(centre * centre, axis=-1, keepdims=True)
    return centre * lax.rsqrt(spread + 1e-05)


def gelu(values):
    inner = values * (0.7978845608028654 + 0.035677408136300125 * (values * values))
    return (0.5 * values) * (1.0 + jnp.tanh(inner))


def call(kernel, out_shape, flops, nbytes, limit=VMEM_LIMIT, **kwargs):
    return pl.pallas_call(
        kernel,
        out_shape=out_shape,
        compiler_params=pltpu.CompilerParams(vmem_limit_bytes=limit),
        cost_estimate=pl.CostEstimate(flops=flops, bytes_accessed=nbytes, transcendentals=0),
        **kwargs,
    )


def exchange(value, axis, step):
    if step == 0:
        return value
    return lax.ppermute(value, axis, [(i, i ^ step) for i in range(lax.axis_size(axis))])


class Plan:
    def __init__(self, tokens):
        self.loc_dev, self.band_dev, self.width = tokens.shape
        self.locs = lax.axis_size("loc")
        self.groups = lax.axis_size("band")
        self.rows_count = self.locs // CORES
        self.share = self.rows_count // self.band_dev
        assert self.share * self.band_dev * CORES == self.locs
        self.block = self.loc_dev // WINDOWS
        self.rows = self.block // self.share
        self.part_rows = self.rows // self.groups
        assert self.part_rows * self.groups * self.share * WINDOWS == self.loc_dev


def location_keys(plan, ids_ref):
    size = plan.loc_dev
    lines = size // LANES
    first = lax.axis_index("loc") * lines
    ids = jnp.concatenate([ids_ref[pl.ds(first + i, 1), :] for i in range(lines)], axis=1)
    ids = ids.astype(F32)
    row = jnp.broadcast_to(ids, (size, size))
    first = lax.broadcasted_iota(jnp.int32, (size, size), 0)
    second = lax.broadcasted_iota(jnp.int32, (size, size), 1)
    column = jnp.sum(jnp.where(first == second, row, 0.0), axis=1, keepdims=True)
    before = jnp.where((column == row) & (first < second), 1.0, 0.0)
    rank = jnp.sum(before, axis=0, keepdims=True)
    return ids * plan.block + rank


SMEM = pl.BlockSpec(memory_space=pltpu.SMEM)
VMEM = pl.BlockSpec(memory_space=pltpu.VMEM)
ANY = pl.BlockSpec(memory_space=pl.ANY)


def pick_rows(plan, window, keys, bands, outs):
    row = lax.axis_index("loc") // CORES
    place = lax.broadcasted_iota(jnp.int32, (plan.rows, plan.loc_dev), 0)
    for slot in range(plan.rows_count):
        peer = row ^ slot
        wanted = place + (window * plan.block + (peer % plan.share) * plan.rows)
        pick = jnp.where(wanted.astype(F32) == keys, 1.0, 0.0).astype(BF16)
        outs[slot][...] = dot(pick, bands[peer // plan.share]).astype(BF16)


def arrange_first(plan, tokens, ids):
    count = plan.rows_count

    def kernel(ids_ref, x_ref, *rest):
        outs, (bands, keys_ref) = rest[:count], rest[count:]
        keys = location_keys(plan, ids_ref)
        keys_ref[...] = keys
        for band in range(plan.band_dev):
            bands[band] = x_ref[:, band, :]
        pick_rows(plan, 0, keys, bands, outs)

    return call(
        kernel,
        [jax.ShapeDtypeStruct((plan.rows, plan.width), BF16)] * count
        + [
            jax.ShapeDtypeStruct((plan.band_dev, plan.loc_dev, plan.width), BF16),
            jax.ShapeDtypeStruct((1, plan.loc_dev), F32),
        ],
        2 * plan.loc_dev * tokens.size,
        4 * tokens.size,
        in_specs=[VMEM] * 2,
        out_specs=[VMEM] * (count + 2),
    )(ids, tokens)


def arrange_next(plan, window, bands, keys, after):
    count = plan.rows_count

    def kernel(bands_ref, keys_ref, *rest):
        pick_rows(plan, window, keys_ref[...], bands_ref, rest[len(after) :])

    return call(
        kernel,
        [jax.ShapeDtypeStruct((plan.rows, plan.width), BF16)] * count,
        2 * plan.loc_dev * bands.size,
        4 * bands.size,
        in_specs=[VMEM] * 2 + [ANY] * len(after),
        out_specs=[VMEM] * count,
    )(bands, keys, *after)


def join_slots(plan, slots, after):
    def kernel(*refs):
        for slot in range(len(slots)):
            refs[-1][pl.ds(slot * plan.rows, plan.rows), :] = refs[slot][...]

    return call(
        kernel,
        jax.ShapeDtypeStruct((len(slots) * plan.rows, plan.width), BF16),
        0,
        4 * len(slots) * plan.rows * plan.width,
        in_specs=[VMEM] * len(slots) + [ANY] * len(after),
        out_specs=VMEM,
    )(*slots, *after)


def embed_row(plan, index_ref, table_ref):
    band = lax.axis_index("loc") // (CORES * plan.share)
    number = index_ref[lax.axis_index("band") * plan.band_dev + band]
    return table_ref[pl.ds(number, 1), :]


def loop(count, step):
    lax.fori_loop(0, count, lambda i, _: (step(i), 0)[1], 0)


def aligned(index, size):
    return pl.ds(pl.multiple_of(index * size, size), size)


def norm_into(target, rows_of, rows):
    tile = min(rows, NORM_ROWS)

    def step(index):
        here = aligned(index, tile)
        target[here, :] = norm_rows(rows_of(here)).astype(BF16)

    loop(rows // tile, step)


def project(plan, tokens, index, table, weights, queries, after=()):
    rows, width = tokens.shape
    tile = min(rows, ROW_TILE)
    names = range(3) if queries else range(1, 3)

    def kernel(index_ref, table_ref, w_ref, x_ref, *rest):
        outs = rest[len(after) :]
        embed = embed_row(plan, index_ref, table_ref)
        for first in range(0, rows, tile):
            here = pl.ds(first, tile)
            normed = norm_rows(x_ref[here, :].astype(F32) + embed).astype(BF16)
            for ref, name in zip(outs, names):
                value = dot(normed, w_ref[:, name * width : (name + 1) * width])
                ref[here, :] = (value * QUERY_SCALE if name == 0 else value).astype(BF16)

    return call(
        kernel,
        [jax.ShapeDtypeStruct((rows, width), BF16)] * len(names),
        2 * rows * width * len(names) * width,
        2 * ((1 + len(names)) * rows * width + 3 * width * width),
        in_specs=[SMEM, VMEM, VMEM, VMEM] + [ANY] * len(after),
        out_specs=[VMEM] * len(names),
    )(index, table, weights, tokens, *after)


def head_masks(rows):
    lane = lax.broadcasted_iota(jnp.int32, (rows, LANES), 1)
    return [(lane // HEAD_DIM) == head for head in range(LANES // HEAD_DIM)]


def stack_heads(query):
    return jnp.concatenate(
        [jnp.where(inside, query, jnp.zeros_like(query)) for inside in head_masks(query.shape[0])],
        axis=0,
    )


def join_heads(stacked):
    heads = LANES // HEAD_DIM
    rows = stacked.shape[0] // heads
    joined = stacked[:rows]
    for head, inside in list(enumerate(head_masks(rows)))[1:]:
        joined = jnp.where(inside, stacked[head * rows : (head + 1) * rows], joined)
    return joined


def with_ones(value):
    return jnp.concatenate([value, jnp.ones(value.shape, BF16)], axis=1)


def run_units(units, mask=None):
    def scores_of(unit):
        query, keys, _ = unit
        scores = [dot_t(query, piece) for piece in keys]
        if mask is not None:
            scores = [jnp.where(mask, piece, -1e30) for piece in scores]
        return scores

    results = []
    ahead = scores_of(units[0])
    for number, (_, _, values) in enumerate(units):
        scores = ahead
        if number + 1 < len(units):
            ahead = scores_of(units[number + 1])
        peak = functools.reduce(
            jnp.maximum, [jnp.max(piece, axis=-1, keepdims=True) for piece in scores]
        )
        total = None
        for piece, value in zip(scores, values):
            part = dot(jnp.exp(piece - peak).astype(BF16), value)
            total = part if total is None else total + part
        results.append(
            (join_heads(total[:, :LANES]) / join_heads(total[:, LANES:])).astype(BF16)
        )
    return results


def attend(plan, query, keys, values, tokens, index, table, spatial_out):
    total, width = query.shape
    rows = plan.rows
    pieces = len(keys)
    pairs = width // LANES
    unit = min(total, UNIT_ROWS)

    def kernel(index_ref, table_ref, w_ref, x_ref, q_ref, *rest):
        k_refs, rest = rest[:pieces], rest[pieces:]
        v_refs, (out_ref, result, added) = rest[:pieces], rest[pieces:]

        def step(number):
            units, places = [], []
            for i in range(STEP_PAIRS):
                here = aligned(number * STEP_PAIRS + i, LANES)
                pair_keys = [ref[:, here] for ref in k_refs]
                pair_values = [with_ones(ref[:, here]) for ref in v_refs]
                for first in range(0, total, unit):
                    place = (pl.ds(first, unit), here)
                    units.append((stack_heads(q_ref[place]), pair_keys, pair_values))
                    places.append(place)
            for place, done in zip(places, run_units(units)):
                result[place] = done

        loop(pairs // STEP_PAIRS, step)
        added[...] = dot(result[...], w_ref[...])
        embed = embed_row(plan, index_ref, table_ref)
        row = lax.axis_index("loc") // CORES
        for slot in range(plan.rows_count):
            here = pl.ds(slot * rows, rows)
            mid = (x_ref[here, :].astype(F32) + embed + added[here, :]).astype(BF16)
            for owner in range(plan.groups):
                part = mid[owner * plan.part_rows : (owner + 1) * plan.part_rows]
                out_ref[owner, row ^ slot] = part

    key_rows = sum(piece.shape[0] for piece in keys)
    return call(
        kernel,
        jax.ShapeDtypeStruct((plan.groups, plan.rows_count, plan.part_rows, width), BF16),
        16 * total * key_rows * width,
        2 * width * (2 * key_rows + 3 * total + width),
        in_specs=[SMEM] + [VMEM] * (4 + 2 * pieces),
        out_specs=VMEM,
        scratch_shapes=[pltpu.VMEM((total, width), BF16), pltpu.VMEM((total, width), F32)],
    )(index, table, spatial_out, tokens, query, *keys, *values)


def channel(plan, parts, channel_qkv, channel_out, up_weight, down_weight):
    groups, width = plan.groups, plan.width
    _, bands, locations, _ = parts.shape
    tile, small = TILE_LOCS, GROUP_LOCS
    assert locations % tile == 0
    group_rows = groups * bands * small
    rows = groups * bands * locations
    row_tile = min(rows, ROW_TILE)

    def kernel(qkv_hbm, out_hbm, up_hbm, down_hbm, *refs):
        in_ref, *refs = refs
        outs, refs = refs[:groups], refs[groups:]
        mid, normed, packed, attended, qkv_ref, out_ref, up_ref, down_ref, sems = refs
        me = lax.axis_index("band")
        columns = [pl.ds(first, width) for first in range(0, 3 * width, width)]
        copies = []
        for source, target, spots in (
            (qkv_hbm, qkv_ref, [(slice(None), spot) for spot in columns]),
            (out_hbm, out_ref, [(slice(None), slice(None))]),
            (up_hbm, up_ref, [(slice(None), slice(None))]),
            (down_hbm, down_ref, [(slice(None), slice(None))]),
        ):
            for spot in spots:
                copies.append(
                    pltpu.make_async_copy(
                        source.at[spot], target.at[spot], sems.at[len(copies)]
                    )
                )
        for copy in copies:
            copy.start()
        pieces = [
            (owner, band, first)
            for owner in range(groups)
            for band in range(bands)
            for first in range(0, locations, tile)
        ]

        def places(owner, band, first):
            return [
                pl.ds((at // small) * group_rows + (owner * bands + band) * small, small)
                for at in range(first, first + tile, small)
            ]

        for owner, band, first in pieces:
            piece = in_ref[me ^ owner, band, first : first + tile, :].astype(F32)
            for number, place in enumerate(places(owner, band, first)):
                mid[place, :] = piece[number * small : (number + 1) * small]
        norm_into(normed, lambda here: mid[here, :], rows)

        for number, here in enumerate(columns):
            copies[number].wait()
            factor = QUERY_SCALE if number == 0 else 1.0
            packed[:, here] = (dot(normed[...], qkv_ref[:, here]) * factor).astype(BF16)
        pairs = width // LANES
        stacked = group_rows * (LANES // HEAD_DIM)
        one = lax.broadcasted_iota(jnp.int32, (stacked, group_rows), 0)
        other = lax.broadcasted_iota(jnp.int32, (stacked, group_rows), 1)
        mask = (one % small) == (other % small)

        def attention_step(pair):
            units, spots = [], []
            for first in range(0, rows, group_rows):
                mine = pl.ds(first, group_rows)
                query = packed[mine, aligned(pair, LANES)]
                keys = packed[mine, aligned(pair + pairs, LANES)]
                values = packed[mine, aligned(pair + 2 * pairs, LANES)]
                units.append((stack_heads(query), [keys], [with_ones(values)]))
                spots.append((mine, aligned(pair, LANES)))
            for spot, done in zip(spots, run_units(units, mask)):
                attended[spot] = done

        loop(pairs, attention_step)
        copies[3].wait()
        mid[...] += dot(attended[...], out_ref[...])
        norm_into(normed, lambda here: mid[here, :], rows)

        copies[4].wait()
        copies[5].wait()

        def mlp_step(block):
            here = aligned(block, width)
            tiles = [pl.ds(first, row_tile) for first in range(0, rows, row_tile)]
            raised = [dot(normed[mine, :], up_ref[:, here]) for mine in tiles]
            for mine, value in zip(tiles, raised):
                mid[mine, :] += dot(gelu(value).astype(BF16), down_ref[here, :])

        loop(up_weight.shape[1] // width, mlp_step)
        for owner, band, first in pieces:
            piece = jnp.concatenate(
                [mid[place, :] for place in places(owner, band, first)], axis=0
            )
            outs[owner][band, first : first + tile, :] = piece.astype(BF16)

    weights = [channel_qkv, channel_out, up_weight, down_weight]
    size = sum(weight.size for weight in weights)
    return call(
        kernel,
        [jax.ShapeDtypeStruct((bands, locations, width), BF16)] * groups,
        2 * rows * size,
        2 * (2 * rows * width + size),
        limit=WIDE_LIMIT,
        in_specs=[ANY] * 4 + [VMEM],
        out_specs=[VMEM] * groups,
        scratch_shapes=[
            pltpu.VMEM((rows, width), F32),
            pltpu.VMEM((rows, width), BF16),
            pltpu.VMEM((rows, 3 * width), BF16),
            pltpu.VMEM((rows, width), BF16),
        ]
        + [pltpu.VMEM(weight.shape, BF16) for weight in weights]
        + [pltpu.SemaphoreType.DMA((6,))],
    )(*weights, parts)


def restore(plan, keys, returned):
    def kernel(keys_ref, *refs):
        ins, out_ref = refs[:-1], refs[-1]
        group = lax.axis_index("band")
        place = lax.broadcasted_iota(jnp.int32, (plan.loc_dev, plan.loc_dev), 0)
        inner = place % plan.part_rows
        part = (place // plan.part_rows) % plan.share
        owner = (place // (plan.part_rows * plan.share)) % plan.groups ^ group
        window = place // plan.block
        wanted = window * plan.block + part * plan.rows + owner * plan.part_rows + inner
        pick = jnp.where(wanted.astype(F32) == keys_ref[...], 1.0, 0.0).astype(BF16)
        for band in range(plan.band_dev):
            rows = jnp.concatenate([ref[band] for ref in ins], axis=0)
            out_ref[:, band, :] = lax.dot_general(
                pick, rows, (((0,), (0,)), ((), ())), preferred_element_type=F32
            ).astype(BF16)

    arrays = [array for chunk in returned for array in chunk]
    size = plan.loc_dev * plan.band_dev * plan.width
    return call(
        kernel,
        jax.ShapeDtypeStruct((plan.loc_dev, plan.band_dev, plan.width), BF16),
        2 * plan.loc_dev * size,
        4 * size,
    )(keys, *arrays)


def body(
    tokens,
    band_index,
    band_table,
    window_ids,
    spatial_qkv,
    spatial_out,
    channel_qkv,
    channel_out,
    up_weight,
    down_weight,
):
    plan = Plan(tokens)
    ids = window_ids.reshape(-1, LANES)
    *sent, bands, place_keys = arrange_first(plan, tokens, ids)
    mids, behind, began = [], (), ()
    for window in range(WINDOWS):
        if window > 0:
            sent = arrange_next(plan, window, bands, place_keys, began)
        slots = [exchange(value, "loc", CORES * step) for step, value in enumerate(sent)]
        began = slots[1:2]
        own = join_slots(plan, slots, behind)
        if plan.share == 1:
            other = exchange(own, "loc", 1)
            query, *mine = project(plan, own, band_index, band_table, spatial_qkv, True)
            theirs = project(plan, other, band_index, band_table, spatial_qkv, False, mine[:1])
            keys, values = zip(mine, theirs)
        else:
            step = CORES * plan.share
            same = [list(range(at, at + step)) for at in range(0, plan.locs, step)]
            every = lax.all_gather(own, "loc", axis_index_groups=same, tiled=True)
            query, _, _ = project(plan, own, band_index, band_table, spatial_qkv, True)
            keys, values = zip(
                project(plan, every, band_index, band_table, spatial_qkv, False)
            )
        mid = attend(plan, query, keys, values, own, band_index, band_table, spatial_out)
        behind = (mid,)
        mids.append(mid)
    same = [
        [(g * plan.rows_count + r) * CORES + core for g in range(plan.groups) for r in range(plan.rows_count)]
        for core in range(CORES)
    ]
    returned = []
    for mid in mids:
        parts = lax.all_to_all(
            mid.reshape(-1, plan.part_rows, plan.width),
            ("band", "loc"),
            0,
            0,
            axis_index_groups=same,
            tiled=True,
        )
        parts = parts.reshape(plan.groups, plan.band_dev, -1, plan.width)
        done = channel(plan, parts, channel_qkv, channel_out, up_weight, down_weight)
        returned.append([exchange(value, "band", step) for step, value in enumerate(done)])
    return restore(plan, place_keys, returned)


def solution(mesh):
    placed = (P("loc", "band", None), P(), P(), P(), P(), P(), P(), P(), P(), P())
    return jax.shard_map(
        body, mesh=mesh, in_specs=placed, out_specs=P("loc", "band", None), check_vma=False
    )
```

```python
import functools

import jax
import jax.numpy as jnp
from jax import lax
from jax.experimental import pallas as pl
from jax.experimental.pallas import tpu as pltpu
from jax.sharding import PartitionSpec as P

HEADS = 12
HEAD_DIM = 64
WINDOWS = 2
CORES = 2
TILE_LOCS = 16
GROUP_LOCS = 8
UNIT_ROWS = 256
STEP_PAIRS = 2
ROW_TILE = 256
LANES = 128
QUERY_SCALE = HEAD_DIM ** (-0.5)
VMEM_LIMIT = 28 * 1024 * 1024
WIDE_LIMIT = 52 * 1024 * 1024

F32 = jnp.float32
BF16 = jnp.bfloat16


def dot(left, right):
    return jnp.dot(left, right, preferred_element_type=F32)


def dot_t(left, right):
    return lax.dot_general(left, right, (((1,), (1,)), ((), ())), preferred_element_type=F32)


def norm_rows(values):
    centre = values - jnp.mean(values, axis=-1, keepdims=True)
    spread = jnp.mean(centre * centre, axis=-1, keepdims=True)
    return centre * lax.rsqrt(spread + 1e-05)


def gelu(values):
    inner = values * (0.7978845608028654 + 0.035677408136300125 * (values * values))
    return (0.5 * values) * (1.0 + jnp.tanh(inner))


def call(kernel, out_shape, flops, nbytes, limit=VMEM_LIMIT, **kwargs):
    return pl.pallas_call(
        kernel,
        out_shape=out_shape,
        compiler_params=pltpu.CompilerParams(vmem_limit_bytes=limit),
        cost_estimate=pl.CostEstimate(flops=flops, bytes_accessed=nbytes, transcendentals=0),
        **kwargs,
    )


def exchange(value, axis, step):
    if step == 0:
        return value
    return lax.ppermute(value, axis, [(i, i ^ step) for i in range(lax.axis_size(axis))])


class Plan:
    def __init__(self, tokens):
        self.loc_dev, self.band_dev, self.width = tokens.shape
        self.locs = lax.axis_size("loc")
        self.groups = lax.axis_size("band")
        self.rows_count = self.locs // CORES
        self.share = self.rows_count // self.band_dev
        assert self.share * self.band_dev * CORES == self.locs
        self.block = self.loc_dev // WINDOWS
        self.rows = self.block // self.share
        self.part_rows = self.rows // self.groups
        assert self.part_rows * self.groups * self.share * WINDOWS == self.loc_dev


def location_keys(plan, ids_ref):
    size = plan.loc_dev
    lines = size // LANES
    first = lax.axis_index("loc") * lines
    ids = jnp.concatenate([ids_ref[pl.ds(first + i, 1), :] for i in range(lines)], axis=1)
    ids = ids.astype(F32)
    row = jnp.broadcast_to(ids, (size, size))
    first = lax.broadcasted_iota(jnp.int32, (size, size), 0)
    second = lax.broadcasted_iota(jnp.int32, (size, size), 1)
    column = jnp.sum(jnp.where(first == second, row, 0.0), axis=1, keepdims=True)
    before = jnp.where((column == row) & (first < second), 1.0, 0.0)
    rank = jnp.sum(before, axis=0, keepdims=True)
    return ids * plan.block + rank


SMEM = pl.BlockSpec(memory_space=pltpu.SMEM)
VMEM = pl.BlockSpec(memory_space=pltpu.VMEM)
ANY = pl.BlockSpec(memory_space=pl.ANY)


def pick_rows(plan, window, place_keys, rows, outs):
    row = lax.axis_index("loc") // CORES
    place = lax.broadcasted_iota(jnp.int32, (plan.rows, rows.shape[0]), 0)
    for slot in range(plan.rows_count):
        peer = row ^ slot
        band, part = peer // plan.share, peer % plan.share
        wanted = place + (band * plan.loc_dev + window * plan.block + part * plan.rows)
        pick = jnp.where(wanted.astype(F32) == place_keys, 1.0, 0.0).astype(BF16)
        outs[slot][...] = dot(pick, rows[...]).astype(BF16)


def arrange_first(plan, tokens, ids):
    count = plan.rows_count
    total = plan.loc_dev * plan.band_dev
    assert plan.loc_dev <= 256

    def kernel(ids_ref, x_ref, *rest):
        outs, (rows_ref, keys_ref, place_ref) = rest[:count], rest[count:]
        keys = location_keys(plan, ids_ref)
        keys_ref[...] = keys
        place = lax.broadcasted_iota(jnp.int32, (plan.loc_dev, total), 1)
        location = lax.broadcasted_iota(jnp.int32, (plan.loc_dev, total), 0)
        spread = jnp.where(place // plan.band_dev == location, 1.0, 0.0).astype(BF16)
        wide = dot(jnp.broadcast_to(keys, (16, plan.loc_dev)).astype(BF16), spread)
        band = lax.broadcasted_iota(jnp.int32, (1, total), 1) % plan.band_dev
        place_ref[...] = wide[:1] + (band * plan.loc_dev).astype(F32)
        rows_ref[...] = x_ref[...].reshape(total, plan.width)
        pick_rows(plan, 0, place_ref[...], rows_ref, outs)

    return call(
        kernel,
        [jax.ShapeDtypeStruct((plan.rows, plan.width), BF16)] * count
        + [
            jax.ShapeDtypeStruct((total, plan.width), BF16),
            jax.ShapeDtypeStruct((1, plan.loc_dev), F32),
            jax.ShapeDtypeStruct((1, total), F32),
        ],
        2 * plan.loc_dev * tokens.size,
        4 * tokens.size,
        in_specs=[VMEM] * 2,
        out_specs=[VMEM] * (count + 3),
    )(ids, tokens)


def arrange_next(plan, window, rows, place_keys, after):
    count = plan.rows_count

    def kernel(rows_ref, place_ref, *rest):
        pick_rows(plan, window, place_ref[...], rows_ref, rest[len(after) :])

    return call(
        kernel,
        [jax.ShapeDtypeStruct((plan.rows, plan.width), BF16)] * count,
        2 * plan.loc_dev * rows.size,
        4 * rows.size,
        in_specs=[VMEM] * 2 + [ANY] * len(after),
        out_specs=[VMEM] * count,
    )(rows, place_keys, *after)


def join_slots(plan, slots, after):
    def kernel(*refs):
        for slot in range(len(slots)):
            refs[-1][pl.ds(slot * plan.rows, plan.rows), :] = refs[slot][...]

    return call(
        kernel,
        jax.ShapeDtypeStruct((len(slots) * plan.rows, plan.width), BF16),
        0,
        4 * len(slots) * plan.rows * plan.width,
        in_specs=[VMEM] * len(slots) + [ANY] * len(after),
        out_specs=VMEM,
    )(*slots, *after)


def embed_row(plan, index_ref, table_ref):
    band = lax.axis_index("loc") // (CORES * plan.share)
    number = index_ref[lax.axis_index("band") * plan.band_dev + band]
    return table_ref[pl.ds(number, 1), :]


def loop(count, step, unroll=1):
    lax.fori_loop(0, count, lambda i, _: (step(i), 0)[1], 0, unroll=unroll)


def aligned(index, size):
    return pl.ds(pl.multiple_of(index * size, size), size)


def norm_into(target, source):
    rows = source.shape[0]
    tile = min(rows, ROW_TILE)
    for first in range(0, rows, tile):
        here = pl.ds(first, tile)
        target[here, :] = norm_rows(source[here, :]).astype(BF16)


def project(plan, tokens, index, table, weights, queries, after=()):
    rows, width = tokens.shape
    tile = min(rows, ROW_TILE)
    names = range(3) if queries else range(1, 3)

    def kernel(index_ref, table_ref, w_ref, x_ref, *rest):
        outs = rest[len(after) :]
        embed = embed_row(plan, index_ref, table_ref)
        for first in range(0, rows, tile):
            here = pl.ds(first, tile)
            normed = norm_rows(x_ref[here, :].astype(F32) + embed).astype(BF16)
            for ref, name in zip(outs, names):
                value = dot(normed, w_ref[:, name * width : (name + 1) * width])
                ref[here, :] = (value * QUERY_SCALE if name == 0 else value).astype(BF16)

    return call(
        kernel,
        [jax.ShapeDtypeStruct((rows, width), BF16)] * len(names),
        2 * rows * width * len(names) * width,
        2 * ((1 + len(names)) * rows * width + 3 * width * width),
        in_specs=[SMEM, VMEM, VMEM, VMEM] + [ANY] * len(after),
        out_specs=[VMEM] * len(names),
    )(index, table, weights, tokens, *after)


def head_masks(rows):
    lane = lax.broadcasted_iota(jnp.int32, (rows, LANES), 1)
    return [(lane // HEAD_DIM) == head for head in range(LANES // HEAD_DIM)]


def stack_heads(query):
    return jnp.concatenate(
        [jnp.where(inside, query, jnp.zeros_like(query)) for inside in head_masks(query.shape[0])],
        axis=0,
    )


def join_heads(stacked):
    heads = LANES // HEAD_DIM
    rows = stacked.shape[0] // heads
    joined = stacked[:rows]
    for head, inside in list(enumerate(head_masks(rows)))[1:]:
        joined = jnp.where(inside, stacked[head * rows : (head + 1) * rows], joined)
    return joined


def with_ones(value):
    return jnp.concatenate([value, jnp.ones(value.shape, BF16)], axis=1)


def run_units(units, mask=None):
    def scores_of(unit):
        query, keys, _ = unit
        scores = [dot_t(query, piece) for piece in keys]
        if mask is not None:
            scores = [jnp.where(mask, piece, -1e30) for piece in scores]
        return scores

    results = []
    ahead = scores_of(units[0])
    for number, (_, _, values) in enumerate(units):
        scores = ahead
        if number + 1 < len(units):
            ahead = scores_of(units[number + 1])
        peak = functools.reduce(
            jnp.maximum, [jnp.max(piece, axis=-1, keepdims=True) for piece in scores]
        )
        total = None
        for piece, value in zip(scores, values):
            part = dot(jnp.exp(piece - peak).astype(BF16), value)
            total = part if total is None else total + part
        results.append(
            (join_heads(total[:, :LANES]) / join_heads(total[:, LANES:])).astype(BF16)
        )
    return results


def attend(plan, query, keys, values, tokens, index, table, spatial_out):
    total, width = query.shape
    rows = plan.rows
    pieces = len(keys)
    pairs = width // LANES
    unit = min(total, UNIT_ROWS)

    def kernel(index_ref, table_ref, w_ref, x_ref, q_ref, *rest):
        k_refs, rest = rest[:pieces], rest[pieces:]
        v_refs, (out_ref, result, added) = rest[:pieces], rest[pieces:]

        def step(number):
            units, places = [], []
            for i in range(STEP_PAIRS):
                here = aligned(number * STEP_PAIRS + i, LANES)
                pair_keys = [ref[:, here] for ref in k_refs]
                pair_values = [with_ones(ref[:, here]) for ref in v_refs]
                for first in range(0, total, unit):
                    place = (pl.ds(first, unit), here)
                    units.append((stack_heads(q_ref[place]), pair_keys, pair_values))
                    places.append(place)
            for place, done in zip(places, run_units(units)):
                result[place] = done

        loop(pairs // STEP_PAIRS, step)
        added[...] = dot(result[...], w_ref[...])
        embed = embed_row(plan, index_ref, table_ref)
        row = lax.axis_index("loc") // CORES
        for slot in range(plan.rows_count):
            here = pl.ds(slot * rows, rows)
            mid = (x_ref[here, :].astype(F32) + embed + added[here, :]).astype(BF16)
            for owner in range(plan.groups):
                part = mid[owner * plan.part_rows : (owner + 1) * plan.part_rows]
                out_ref[owner, row ^ slot] = part

    key_rows = sum(piece.shape[0] for piece in keys)
    return call(
        kernel,
        jax.ShapeDtypeStruct((plan.groups, plan.rows_count, plan.part_rows, width), BF16),
        16 * total * key_rows * width,
        2 * width * (2 * key_rows + 3 * total + width),
        in_specs=[SMEM] + [VMEM] * (4 + 2 * pieces),
        out_specs=VMEM,
        scratch_shapes=[pltpu.VMEM((total, width), BF16), pltpu.VMEM((total, width), F32)],
    )(index, table, spatial_out, tokens, query, *keys, *values)


def channel(plan, parts, channel_qkv, channel_out, up_weight, down_weight):
    groups, width = plan.groups, plan.width
    _, bands, locations, _ = parts.shape
    tile, small = TILE_LOCS, GROUP_LOCS
    assert locations % tile == 0
    group_rows = groups * bands * small
    rows = groups * bands * locations
    row_tile = min(rows, ROW_TILE)

    def kernel(qkv_hbm, out_hbm, up_hbm, down_hbm, *refs):
        in_ref, *refs = refs
        outs, refs = refs[:groups], refs[groups:]
        mid, normed, packed, attended, qkv_ref, out_ref, up_ref, down_ref, sems = refs
        me = lax.axis_index("band")
        columns = [pl.ds(first, width) for first in range(0, 3 * width, width)]
        copies = []
        for source, target, spots in (
            (qkv_hbm, qkv_ref, [(slice(None), spot) for spot in columns]),
            (out_hbm, out_ref, [(slice(None), slice(None))]),
            (up_hbm, up_ref, [(slice(None), slice(None))]),
            (down_hbm, down_ref, [(slice(None), slice(None))]),
        ):
            for spot in spots:
                copies.append(
                    pltpu.make_async_copy(
                        source.at[spot], target.at[spot], sems.at[len(copies)]
                    )
                )
        for copy in copies:
            copy.start()
        pieces = [
            (owner, band, first)
            for owner in range(groups)
            for band in range(bands)
            for first in range(0, locations, tile)
        ]

        def places(owner, band, first):
            return [
                pl.ds((at // small) * group_rows + (owner * bands + band) * small, small)
                for at in range(first, first + tile, small)
            ]

        for owner, band, first in pieces:
            piece = in_ref[me ^ owner, band, first : first + tile, :].astype(F32)
            for number, place in enumerate(places(owner, band, first)):
                mid[place, :] = piece[number * small : (number + 1) * small]
        norm_into(normed, mid)

        for number, here in enumerate(columns):
            copies[number].wait()
            factor = QUERY_SCALE if number == 0 else 1.0
            packed[:, here] = (dot(normed[...], qkv_ref[:, here]) * factor).astype(BF16)
        pairs = width // LANES
        stacked = group_rows * (LANES // HEAD_DIM)
        one = lax.broadcasted_iota(jnp.int32, (stacked, group_rows), 0)
        other = lax.broadcasted_iota(jnp.int32, (stacked, group_rows), 1)
        mask = (one % small) == (other % small)

        def attention_step(pair):
            units, spots = [], []
            for first in range(0, rows, group_rows):
                mine = pl.ds(first, group_rows)
                query = packed[mine, aligned(pair, LANES)]
                keys = packed[mine, aligned(pair + pairs, LANES)]
                values = packed[mine, aligned(pair + 2 * pairs, LANES)]
                units.append((stack_heads(query), [keys], [with_ones(values)]))
                spots.append((mine, aligned(pair, LANES)))
            for spot, done in zip(spots, run_units(units, mask)):
                attended[spot] = done

        loop(pairs, attention_step, unroll=2)
        copies[3].wait()
        mid[...] += dot(attended[...], out_ref[...])
        norm_into(normed, mid)

        copies[4].wait()
        copies[5].wait()

        def mlp_step(block):
            here = aligned(block, width)
            tiles = [pl.ds(first, row_tile) for first in range(0, rows, row_tile)]
            raised = [dot(normed[mine, :], up_ref[:, here]) for mine in tiles]
            for mine, value in zip(tiles, raised):
                mid[mine, :] += dot(gelu(value).astype(BF16), down_ref[here, :])

        loop(up_weight.shape[1] // width, mlp_step)
        for owner, band, first in pieces:
            piece = jnp.concatenate(
                [mid[place, :] for place in places(owner, band, first)], axis=0
            )
            outs[owner][band, first : first + tile, :] = piece.astype(BF16)

    weights = [channel_qkv, channel_out, up_weight, down_weight]
    size = sum(weight.size for weight in weights)
    return call(
        kernel,
        [jax.ShapeDtypeStruct((bands, locations, width), BF16)] * groups,
        2 * rows * size,
        2 * (2 * rows * width + size),
        limit=WIDE_LIMIT,
        in_specs=[ANY] * 4 + [VMEM],
        out_specs=[VMEM] * groups,
        scratch_shapes=[
            pltpu.VMEM((rows, width), F32),
            pltpu.VMEM((rows, width), BF16),
            pltpu.VMEM((rows, 3 * width), BF16),
            pltpu.VMEM((rows, width), BF16),
        ]
        + [pltpu.VMEM(weight.shape, BF16) for weight in weights]
        + [pltpu.SemaphoreType.DMA((6,))],
    )(*weights, parts)


def restore(plan, keys, returned):
    def kernel(keys_ref, *refs):
        ins, out_ref = refs[:-1], refs[-1]
        group = lax.axis_index("band")
        place = lax.broadcasted_iota(jnp.int32, (plan.loc_dev, plan.loc_dev), 0)
        inner = place % plan.part_rows
        part = (place // plan.part_rows) % plan.share
        owner = (place // (plan.part_rows * plan.share)) % plan.groups ^ group
        window = place // plan.block
        wanted = window * plan.block + part * plan.rows + owner * plan.part_rows + inner
        pick = jnp.where(wanted.astype(F32) == keys_ref[...], 1.0, 0.0).astype(BF16)
        for band in range(plan.band_dev):
            rows = jnp.concatenate([ref[band] for ref in ins], axis=0)
            out_ref[:, band, :] = lax.dot_general(
                pick, rows, (((0,), (0,)), ((), ())), preferred_element_type=F32
            ).astype(BF16)

    arrays = [array for chunk in returned for array in chunk]
    size = plan.loc_dev * plan.band_dev * plan.width
    return call(
        kernel,
        jax.ShapeDtypeStruct((plan.loc_dev, plan.band_dev, plan.width), BF16),
        2 * plan.loc_dev * size,
        4 * size,
    )(keys, *arrays)


def body(
    tokens,
    band_index,
    band_table,
    window_ids,
    spatial_qkv,
    spatial_out,
    channel_qkv,
    channel_out,
    up_weight,
    down_weight,
):
    plan = Plan(tokens)
    ids = window_ids.reshape(-1, LANES)
    *sent, rows, keys, place_keys = arrange_first(plan, tokens, ids)
    arrived = [[exchange(value, "loc", CORES * step) for step, value in enumerate(sent)]]
    following = []
    for window in range(1, WINDOWS):
        following = arrange_next(plan, window, rows, place_keys, arrived[-1][1:2])
        arrived.append(
            [exchange(value, "loc", CORES * step) for step, value in enumerate(following)]
        )
    mids, behind = [], following[:1]
    for slots in arrived:
        own = join_slots(plan, slots, behind)
        if plan.share == 1:
            other = exchange(own, "loc", 1)
            query, *mine = project(plan, own, band_index, band_table, spatial_qkv, True)
            theirs = project(plan, other, band_index, band_table, spatial_qkv, False, mine[:1])
            all_keys, all_values = zip(mine, theirs)
        else:
            step = CORES * plan.share
            same = [list(range(at, at + step)) for at in range(0, plan.locs, step)]
            every = lax.all_gather(own, "loc", axis_index_groups=same, tiled=True)
            query, _, _ = project(plan, own, band_index, band_table, spatial_qkv, True)
            all_keys, all_values = zip(
                project(plan, every, band_index, band_table, spatial_qkv, False)
            )
        mid = attend(plan, query, all_keys, all_values, own, band_index, band_table, spatial_out)
        behind = [mid]
        mids.append(mid)
    same = [
        [(g * plan.rows_count + r) * CORES + core for g in range(plan.groups) for r in range(plan.rows_count)]
        for core in range(CORES)
    ]
    returned = []
    for mid in mids:
        parts = lax.all_to_all(
            mid.reshape(-1, plan.part_rows, plan.width),
            ("band", "loc"),
            0,
            0,
            axis_index_groups=same,
            tiled=True,
        )
        parts = parts.reshape(plan.groups, plan.band_dev, -1, plan.width)
        done = channel(plan, parts, channel_qkv, channel_out, up_weight, down_weight)
        returned.append([exchange(value, "band", step) for step, value in enumerate(done)])
    return restore(plan, keys, returned)


def solution(mesh):
    placed = (P("loc", "band", None), P(), P(), P(), P(), P(), P(), P(), P(), P())
    return jax.shard_map(
        body, mesh=mesh, in_specs=placed, out_specs=P("loc", "band", None), check_vma=False
    )
```

```python
import functools

import jax
import jax.numpy as jnp
from jax import lax
from jax.experimental import pallas as pl
from jax.experimental.pallas import tpu as pltpu
from jax.sharding import PartitionSpec as P

HEADS = 12
HEAD_DIM = 64
WINDOWS = 2
CORES = 2
TILE_LOCS = 16
GROUP_LOCS = 8
UNIT_ROWS = 256
STEP_PAIRS = 3
ROW_TILE = 256
LANES = 128
QUERY_SCALE = HEAD_DIM ** (-0.5)
VMEM_LIMIT = 28 * 1024 * 1024
WIDE_LIMIT = 52 * 1024 * 1024

F32 = jnp.float32
BF16 = jnp.bfloat16


def dot(left, right):
    return jnp.dot(left, right, preferred_element_type=F32)


def dot_t(left, right):
    return lax.dot_general(left, right, (((1,), (1,)), ((), ())), preferred_element_type=F32)


def norm_rows(values):
    centre = values - jnp.mean(values, axis=-1, keepdims=True)
    spread = jnp.mean(centre * centre, axis=-1, keepdims=True)
    return centre * lax.rsqrt(spread + 1e-05)


def gelu(values):
    inner = values * (0.7978845608028654 + 0.035677408136300125 * (values * values))
    return (0.5 * values) * (1.0 + jnp.tanh(inner))


def call(kernel, out_shape, flops, nbytes, limit=VMEM_LIMIT, **kwargs):
    return pl.pallas_call(
        kernel,
        out_shape=out_shape,
        compiler_params=pltpu.CompilerParams(vmem_limit_bytes=limit),
        cost_estimate=pl.CostEstimate(flops=0, bytes_accessed=0, transcendentals=0),
        **kwargs,
    )


def exchange(value, axis, step):
    if step == 0:
        return value
    return lax.ppermute(value, axis, [(i, i ^ step) for i in range(lax.axis_size(axis))])


class Plan:
    def __init__(self, tokens):
        self.loc_dev, self.band_dev, self.width = tokens.shape
        self.locs = lax.axis_size("loc")
        self.groups = lax.axis_size("band")
        self.rows_count = self.locs // CORES
        self.share = self.rows_count // self.band_dev
        assert self.share * self.band_dev * CORES == self.locs
        self.block = self.loc_dev // WINDOWS
        self.rows = self.block // self.share
        self.part_rows = self.rows // self.groups
        assert self.part_rows * self.groups * self.share * WINDOWS == self.loc_dev


def location_keys(plan, ids_ref):
    size = plan.loc_dev
    lines = size // LANES
    first = lax.axis_index("loc") * lines
    ids = jnp.concatenate([ids_ref[pl.ds(first + i, 1), :] for i in range(lines)], axis=1)
    ids = ids.astype(F32)
    row = jnp.broadcast_to(ids, (size, size))
    first = lax.broadcasted_iota(jnp.int32, (size, size), 0)
    second = lax.broadcasted_iota(jnp.int32, (size, size), 1)
    column = jnp.sum(jnp.where(first == second, row, 0.0), axis=1, keepdims=True)
    before = jnp.where((column == row) & (first < second), 1.0, 0.0)
    rank = jnp.sum(before, axis=0, keepdims=True)
    return ids * plan.block + rank


SMEM = pl.BlockSpec(memory_space=pltpu.SMEM)
VMEM = pl.BlockSpec(memory_space=pltpu.VMEM)
ANY = pl.BlockSpec(memory_space=pl.ANY)


def pick_rows(plan, window, place_keys, rows, outs):
    row = lax.axis_index("loc") // CORES
    place = lax.broadcasted_iota(jnp.int32, (plan.rows, rows.shape[0]), 0)
    for slot in range(plan.rows_count):
        peer = row ^ slot
        band, part = peer // plan.share, peer % plan.share
        wanted = place + (band * plan.loc_dev + window * plan.block + part * plan.rows)
        pick = jnp.where(wanted.astype(F32) == place_keys, 1.0, 0.0).astype(BF16)
        outs[slot][...] = dot(pick, rows[...]).astype(BF16)


def arrange_first(plan, tokens, ids):
    count = plan.rows_count
    total = plan.loc_dev * plan.band_dev
    assert plan.loc_dev <= 256

    def kernel(ids_ref, x_ref, *rest):
        outs, (rows_ref, keys_ref, place_ref) = rest[:count], rest[count:]
        keys = location_keys(plan, ids_ref)
        keys_ref[...] = keys
        place = lax.broadcasted_iota(jnp.int32, (plan.loc_dev, total), 1)
        location = lax.broadcasted_iota(jnp.int32, (plan.loc_dev, total), 0)
        spread = jnp.where(place // plan.band_dev == location, 1.0, 0.0).astype(BF16)
        wide = dot(jnp.broadcast_to(keys, (16, plan.loc_dev)).astype(BF16), spread)
        band = lax.broadcasted_iota(jnp.int32, (1, total), 1) % plan.band_dev
        place_ref[...] = wide[:1] + (band * plan.loc_dev).astype(F32)
        rows_ref[...] = x_ref[...].reshape(total, plan.width)
        pick_rows(plan, 0, place_ref[...], rows_ref, outs)

    return call(
        kernel,
        [jax.ShapeDtypeStruct((plan.rows, plan.width), BF16)] * count
        + [
            jax.ShapeDtypeStruct((total, plan.width), BF16),
            jax.ShapeDtypeStruct((1, plan.loc_dev), F32),
            jax.ShapeDtypeStruct((1, total), F32),
        ],
        2 * plan.loc_dev * tokens.size,
        4 * tokens.size,
        in_specs=[VMEM] * 2,
        out_specs=[VMEM] * (count + 3),
    )(ids, tokens)


def arrange_next(plan, window, rows, place_keys, after):
    count = plan.rows_count

    def kernel(rows_ref, place_ref, *rest):
        pick_rows(plan, window, place_ref[...], rows_ref, rest[len(after) :])

    return call(
        kernel,
        [jax.ShapeDtypeStruct((plan.rows, plan.width), BF16)] * count,
        2 * plan.loc_dev * rows.size,
        4 * rows.size,
        in_specs=[VMEM] * 2 + [ANY] * len(after),
        out_specs=[VMEM] * count,
    )(rows, place_keys, *after)


def join_slots(plan, slots, after):
    def kernel(*refs):
        for slot in range(len(slots)):
            refs[-1][pl.ds(slot * plan.rows, plan.rows), :] = refs[slot][...]

    return call(
        kernel,
        jax.ShapeDtypeStruct((len(slots) * plan.rows, plan.width), BF16),
        0,
        4 * len(slots) * plan.rows * plan.width,
        in_specs=[VMEM] * len(slots) + [ANY] * len(after),
        out_specs=VMEM,
    )(*slots, *after)


def embed_row(plan, index_ref, table_ref):
    band = lax.axis_index("loc") // (CORES * plan.share)
    number = index_ref[lax.axis_index("band") * plan.band_dev + band]
    return table_ref[pl.ds(number, 1), :]


def loop(count, step, unroll=1):
    lax.fori_loop(0, count, lambda i, _: (step(i), 0)[1], 0, unroll=unroll)


def aligned(index, size):
    return pl.ds(pl.multiple_of(index * size, size), size)


def norm_into(target, source):
    rows = source.shape[0]
    tile = min(rows, ROW_TILE)
    for first in range(0, rows, tile):
        here = pl.ds(first, tile)
        target[here, :] = norm_rows(source[here, :]).astype(BF16)


def project(plan, tokens, index, table, weights, queries, after=()):
    rows, width = tokens.shape
    tile = min(rows, ROW_TILE)
    names = range(3) if queries else range(1, 3)

    def kernel(index_ref, table_ref, w_ref, x_ref, *rest):
        outs = rest[len(after) :]
        embed = embed_row(plan, index_ref, table_ref)
        for first in range(0, rows, tile):
            here = pl.ds(first, tile)
            normed = norm_rows(x_ref[here, :].astype(F32) + embed).astype(BF16)
            for ref, name in zip(outs, names):
                value = dot(normed, w_ref[:, name * width : (name + 1) * width])
                ref[here, :] = (value * QUERY_SCALE if name == 0 else value).astype(BF16)

    return call(
        kernel,
        [jax.ShapeDtypeStruct((rows, width), BF16)] * len(names),
        2 * rows * width * len(names) * width,
        2 * ((1 + len(names)) * rows * width + 3 * width * width),
        in_specs=[SMEM, VMEM, VMEM, VMEM] + [ANY] * len(after),
        out_specs=[VMEM] * len(names),
    )(index, table, weights, tokens, *after)


def head_masks(rows):
    lane = lax.broadcasted_iota(jnp.int32, (rows, LANES), 1)
    return [(lane // HEAD_DIM) == head for head in range(LANES // HEAD_DIM)]


def stack_heads(query):
    return jnp.concatenate(
        [jnp.where(inside, query, jnp.zeros_like(query)) for inside in head_masks(query.shape[0])],
        axis=0,
    )


def join_heads(stacked):
    heads = LANES // HEAD_DIM
    rows = stacked.shape[0] // heads
    joined = stacked[:rows]
    for head, inside in list(enumerate(head_masks(rows)))[1:]:
        joined = jnp.where(inside, stacked[head * rows : (head + 1) * rows], joined)
    return joined


def with_ones(value):
    return jnp.concatenate([value, jnp.ones(value.shape, BF16)], axis=1)


def run_units(units, mask=None):
    def scores_of(unit):
        query, keys, _ = unit
        scores = [dot_t(query, piece) for piece in keys]
        if mask is not None:
            scores = [jnp.where(mask, piece, -1e30) for piece in scores]
        return scores

    results = []
    ahead = scores_of(units[0])
    for number, (_, _, values) in enumerate(units):
        scores = ahead
        if number + 1 < len(units):
            ahead = scores_of(units[number + 1])
        peak = functools.reduce(
            jnp.maximum, [jnp.max(piece, axis=-1, keepdims=True) for piece in scores]
        )
        total = None
        for piece, value in zip(scores, values):
            part = dot(jnp.exp(piece - peak).astype(BF16), value)
            total = part if total is None else total + part
        results.append(
            (join_heads(total[:, :LANES]) / join_heads(total[:, LANES:])).astype(BF16)
        )
    return results


def attend(plan, query, keys, values, tokens, index, table, spatial_out):
    total, width = query.shape
    rows = plan.rows
    pieces = len(keys)
    pairs = width // LANES
    unit = min(total, UNIT_ROWS)

    def kernel(index_ref, table_ref, w_ref, x_ref, q_ref, *rest):
        k_refs, rest = rest[:pieces], rest[pieces:]
        v_refs, (out_ref, result, added) = rest[:pieces], rest[pieces:]

        def step(number):
            units, places = [], []
            for i in range(STEP_PAIRS):
                here = aligned(number * STEP_PAIRS + i, LANES)
                pair_keys = [ref[:, here] for ref in k_refs]
                pair_values = [with_ones(ref[:, here]) for ref in v_refs]
                for first in range(0, total, unit):
                    place = (pl.ds(first, unit), here)
                    units.append((stack_heads(q_ref[place]), pair_keys, pair_values))
                    places.append(place)
            for place, done in zip(places, run_units(units)):
                result[place] = done

        loop(pairs // STEP_PAIRS, step)
        added[...] = dot(result[...], w_ref[...])
        embed = embed_row(plan, index_ref, table_ref)
        row = lax.axis_index("loc") // CORES
        for slot in range(plan.rows_count):
            here = pl.ds(slot * rows, rows)
            mid = (x_ref[here, :].astype(F32) + embed + added[here, :]).astype(BF16)
            for owner in range(plan.groups):
                part = mid[owner * plan.part_rows : (owner + 1) * plan.part_rows]
                out_ref[owner, row ^ slot] = part

    key_rows = sum(piece.shape[0] for piece in keys)
    return call(
        kernel,
        jax.ShapeDtypeStruct((plan.groups, plan.rows_count, plan.part_rows, width), BF16),
        16 * total * key_rows * width,
        2 * width * (2 * key_rows + 3 * total + width),
        in_specs=[SMEM] + [VMEM] * (4 + 2 * pieces),
        out_specs=VMEM,
        scratch_shapes=[pltpu.VMEM((total, width), BF16), pltpu.VMEM((total, width), F32)],
    )(index, table, spatial_out, tokens, query, *keys, *values)


def channel(plan, parts, channel_qkv, channel_out, up_weight, down_weight):
    groups, width = plan.groups, plan.width
    _, bands, locations, _ = parts.shape
    tile, small = TILE_LOCS, GROUP_LOCS
    assert locations % tile == 0
    group_rows = groups * bands * small
    rows = groups * bands * locations
    row_tile = min(rows, ROW_TILE)

    def kernel(qkv_hbm, out_hbm, up_hbm, down_hbm, *refs):
        in_ref, *refs = refs
        outs, refs = refs[:groups], refs[groups:]
        mid, normed, packed, attended, qkv_ref, out_ref, up_ref, down_ref, sems = refs
        me = lax.axis_index("band")
        columns = [pl.ds(first, width) for first in range(0, 3 * width, width)]
        copies = []
        for source, target, spots in (
            (qkv_hbm, qkv_ref, [(slice(None), spot) for spot in columns]),
            (out_hbm, out_ref, [(slice(None), slice(None))]),
            (up_hbm, up_ref, [(slice(None), slice(None))]),
            (down_hbm, down_ref, [(slice(None), slice(None))]),
        ):
            for spot in spots:
                copies.append(
                    pltpu.make_async_copy(
                        source.at[spot], target.at[spot], sems.at[len(copies)]
                    )
                )
        for copy in copies:
            copy.start()
        pieces = [
            (owner, band, first)
            for owner in range(groups)
            for band in range(bands)
            for first in range(0, locations, tile)
        ]

        def places(owner, band, first):
            return [
                pl.ds((at // small) * group_rows + (owner * bands + band) * small, small)
                for at in range(first, first + tile, small)
            ]

        for owner, band, first in pieces:
            piece = in_ref[me ^ owner, band, first : first + tile, :].astype(F32)
            for number, place in enumerate(places(owner, band, first)):
                mid[place, :] = piece[number * small : (number + 1) * small]
        norm_into(normed, mid)

        for number, here in enumerate(columns):
            copies[number].wait()
            factor = QUERY_SCALE if number == 0 else 1.0
            packed[:, here] = (dot(normed[...], qkv_ref[:, here]) * factor).astype(BF16)
        pairs = width // LANES
        stacked = group_rows * (LANES // HEAD_DIM)
        one = lax.broadcasted_iota(jnp.int32, (stacked, group_rows), 0)
        other = lax.broadcasted_iota(jnp.int32, (stacked, group_rows), 1)
        mask = (one % small) == (other % small)

        def attention_step(pair):
            units, spots = [], []
            for first in range(0, rows, group_rows):
                mine = pl.ds(first, group_rows)
                query = packed[mine, aligned(pair, LANES)]
                keys = packed[mine, aligned(pair + pairs, LANES)]
                values = packed[mine, aligned(pair + 2 * pairs, LANES)]
                units.append((stack_heads(query), [keys], [with_ones(values)]))
                spots.append((mine, aligned(pair, LANES)))
            for spot, done in zip(spots, run_units(units, mask)):
                attended[spot] = done

        loop(pairs, attention_step, unroll=3)
        copies[3].wait()
        mid[...] += dot(attended[...], out_ref[...])
        norm_into(normed, mid)

        copies[4].wait()
        copies[5].wait()

        def mlp_step(block):
            here = aligned(block, width)
            tiles = [pl.ds(first, row_tile) for first in range(0, rows, row_tile)]
            raised = [dot(normed[mine, :], up_ref[:, here]) for mine in tiles]
            for mine, value in zip(tiles, raised):
                mid[mine, :] += dot(gelu(value).astype(BF16), down_ref[here, :])

        loop(up_weight.shape[1] // width, mlp_step)
        for owner, band, first in pieces:
            piece = jnp.concatenate(
                [mid[place, :] for place in places(owner, band, first)], axis=0
            )
            outs[owner][band, first : first + tile, :] = piece.astype(BF16)

    weights = [channel_qkv, channel_out, up_weight, down_weight]
    size = sum(weight.size for weight in weights)
    return call(
        kernel,
        [jax.ShapeDtypeStruct((bands, locations, width), BF16)] * groups,
        2 * rows * size,
        2 * (2 * rows * width + size),
        limit=WIDE_LIMIT,
        in_specs=[ANY] * 4 + [VMEM],
        out_specs=[VMEM] * groups,
        scratch_shapes=[
            pltpu.VMEM((rows, width), F32),
            pltpu.VMEM((rows, width), BF16),
            pltpu.VMEM((rows, 3 * width), BF16),
            pltpu.VMEM((rows, width), BF16),
        ]
        + [pltpu.VMEM(weight.shape, BF16) for weight in weights]
        + [pltpu.SemaphoreType.DMA((6,))],
    )(*weights, parts)


def restore(plan, keys, returned):
    def kernel(keys_ref, *refs):
        ins, out_ref = refs[:-1], refs[-1]
        group = lax.axis_index("band")
        place = lax.broadcasted_iota(jnp.int32, (plan.loc_dev, plan.loc_dev), 0)
        inner = place % plan.part_rows
        part = (place // plan.part_rows) % plan.share
        owner = (place // (plan.part_rows * plan.share)) % plan.groups ^ group
        window = place // plan.block
        wanted = window * plan.block + part * plan.rows + owner * plan.part_rows + inner
        pick = jnp.where(wanted.astype(F32) == keys_ref[...], 1.0, 0.0).astype(BF16)
        for band in range(plan.band_dev):
            rows = jnp.concatenate([ref[band] for ref in ins], axis=0)
            out_ref[:, band, :] = lax.dot_general(
                pick, rows, (((0,), (0,)), ((), ())), preferred_element_type=F32
            ).astype(BF16)

    arrays = [array for chunk in returned for array in chunk]
    size = plan.loc_dev * plan.band_dev * plan.width
    return call(
        kernel,
        jax.ShapeDtypeStruct((plan.loc_dev, plan.band_dev, plan.width), BF16),
        2 * plan.loc_dev * size,
        4 * size,
    )(keys, *arrays)


def body(
    tokens,
    band_index,
    band_table,
    window_ids,
    spatial_qkv,
    spatial_out,
    channel_qkv,
    channel_out,
    up_weight,
    down_weight,
):
    plan = Plan(tokens)
    ids = window_ids.reshape(-1, LANES)
    *sent, rows, keys, place_keys = arrange_first(plan, tokens, ids)
    arrived = [[exchange(value, "loc", CORES * step) for step, value in enumerate(sent)]]
    following = []
    for window in range(1, WINDOWS):
        following = arrange_next(plan, window, rows, place_keys, arrived[-1][1:2])
        arrived.append(
            [exchange(value, "loc", CORES * step) for step, value in enumerate(following)]
        )
    mids, behind = [], following[:1]
    for slots in arrived:
        own = join_slots(plan, slots, behind)
        if plan.share == 1:
            other = exchange(own, "loc", 1)
            query, *mine = project(plan, own, band_index, band_table, spatial_qkv, True)
            theirs = project(plan, other, band_index, band_table, spatial_qkv, False, mine[:1])
            all_keys, all_values = zip(mine, theirs)
        else:
            step = CORES * plan.share
            same = [list(range(at, at + step)) for at in range(0, plan.locs, step)]
            every = lax.all_gather(own, "loc", axis_index_groups=same, tiled=True)
            query, _, _ = project(plan, own, band_index, band_table, spatial_qkv, True)
            all_keys, all_values = zip(
                project(plan, every, band_index, band_table, spatial_qkv, False)
            )
        mid = attend(plan, query, all_keys, all_values, own, band_index, band_table, spatial_out)
        behind = [mid]
        mids.append(mid)
    same = [
        [(g * plan.rows_count + r) * CORES + core for g in range(plan.groups) for r in range(plan.rows_count)]
        for core in range(CORES)
    ]
    returned = []
    for mid in mids:
        parts = lax.all_to_all(
            mid.reshape(-1, plan.part_rows, plan.width),
            ("band", "loc"),
            0,
            0,
            axis_index_groups=same,
            tiled=True,
        )
        parts = parts.reshape(plan.groups, plan.band_dev, -1, plan.width)
        done = channel(plan, parts, channel_qkv, channel_out, up_weight, down_weight)
        returned.append([exchange(value, "band", step) for step, value in enumerate(done)])
    return restore(plan, keys, returned)


def solution(mesh):
    placed = (P("loc", "band", None), P(), P(), P(), P(), P(), P(), P(), P(), P())
    return jax.shard_map(
        body, mesh=mesh, in_specs=placed, out_specs=P("loc", "band", None), check_vma=False
    )
```

```python
import functools

import jax
import jax.numpy as jnp
from jax import lax
from jax.experimental import pallas as pl
from jax.experimental.pallas import tpu as pltpu
from jax.sharding import PartitionSpec as P

HEADS = 12
HEAD_DIM = 64
WINDOWS = 2
CORES = 2
TILE_LOCS = 16
GROUP_LOCS = 8
UNIT_ROWS = 256
STEP_PAIRS = 3
ROW_TILE = 256
LANES = 128
QUERY_SCALE = HEAD_DIM ** (-0.5)
VMEM_LIMIT = 28 * 1024 * 1024
WIDE_LIMIT = 52 * 1024 * 1024
WHOLE_LIMIT = 61 * 1024 * 1024
LONG = 2**36

F32 = jnp.float32
BF16 = jnp.bfloat16


def dot(left, right):
    return jnp.dot(left, right, preferred_element_type=F32)


def dot_t(left, right):
    return lax.dot_general(left, right, (((1,), (1,)), ((), ())), preferred_element_type=F32)


def norm_rows(values):
    centre = values - jnp.mean(values, axis=-1, keepdims=True)
    spread = jnp.mean(centre * centre, axis=-1, keepdims=True)
    return centre * lax.rsqrt(spread + 1e-05)


def gelu(values):
    inner = values * (0.7978845608028654 + 0.035677408136300125 * (values * values))
    return (0.5 * values) * (1.0 + jnp.tanh(inner))


def call(kernel, out_shape, flops, nbytes, limit=VMEM_LIMIT, **kwargs):
    return pl.pallas_call(
        kernel,
        out_shape=out_shape,
        compiler_params=pltpu.CompilerParams(vmem_limit_bytes=limit),
        cost_estimate=pl.CostEstimate(flops=flops, bytes_accessed=nbytes, transcendentals=0),
        **kwargs,
    )


def exchange(value, axis, step):
    if step == 0:
        return value
    return lax.ppermute(value, axis, [(i, i ^ step) for i in range(lax.axis_size(axis))])


class Plan:
    def __init__(self, tokens):
        self.loc_dev, self.band_dev, self.width = tokens.shape
        self.locs = lax.axis_size("loc")
        self.groups = lax.axis_size("band")
        self.rows_count = self.locs // CORES
        self.share = self.rows_count // self.band_dev
        assert self.share * self.band_dev * CORES == self.locs
        self.block = self.loc_dev // WINDOWS
        self.rows = self.block // self.share
        self.part_rows = self.rows // self.groups
        assert self.part_rows * self.groups * self.share * WINDOWS == self.loc_dev


def location_keys(plan, ids_ref):
    size = plan.loc_dev
    lines = size // LANES
    first = lax.axis_index("loc") * lines
    ids = jnp.concatenate([ids_ref[pl.ds(first + i, 1), :] for i in range(lines)], axis=1)
    ids = ids.astype(F32)
    row = jnp.broadcast_to(ids, (size, size))
    first = lax.broadcasted_iota(jnp.int32, (size, size), 0)
    second = lax.broadcasted_iota(jnp.int32, (size, size), 1)
    column = jnp.sum(jnp.where(first == second, row, 0.0), axis=1, keepdims=True)
    before = jnp.where((column == row) & (first < second), 1.0, 0.0)
    rank = jnp.sum(before, axis=0, keepdims=True)
    return ids * plan.block + rank


SMEM = pl.BlockSpec(memory_space=pltpu.SMEM)
VMEM = pl.BlockSpec(memory_space=pltpu.VMEM)
ANY = pl.BlockSpec(memory_space=pl.ANY)


def pick_rows(plan, window, place_keys, rows, outs):
    row = lax.axis_index("loc") // CORES
    place = lax.broadcasted_iota(jnp.int32, (plan.rows, rows.shape[0]), 0)
    for slot in range(plan.rows_count):
        peer = row ^ slot
        band, part = peer // plan.share, peer % plan.share
        wanted = place + (band * plan.loc_dev + window * plan.block + part * plan.rows)
        pick = jnp.where(wanted.astype(F32) == place_keys, 1.0, 0.0).astype(BF16)
        outs[slot][...] = dot(pick, rows[...]).astype(BF16)


def arrange_first(plan, tokens, ids):
    count = plan.rows_count
    total = plan.loc_dev * plan.band_dev
    assert plan.loc_dev <= 256

    def kernel(ids_hbm, x_hbm, *rest):
        outs, rest = rest[:count], rest[count:]
        rows_ref, keys_ref, place_ref, ids_ref, x_ref, sems = rest
        copies = [
            pltpu.make_async_copy(ids_hbm, ids_ref, sems.at[0]),
            pltpu.make_async_copy(x_hbm, x_ref, sems.at[1]),
        ]
        for copy in copies:
            copy.start()
        copies[0].wait()
        keys = location_keys(plan, ids_ref)
        keys_ref[...] = keys
        place = lax.broadcasted_iota(jnp.int32, (plan.loc_dev, total), 1)
        location = lax.broadcasted_iota(jnp.int32, (plan.loc_dev, total), 0)
        spread = jnp.where(place // plan.band_dev == location, 1.0, 0.0).astype(BF16)
        wide = dot(jnp.broadcast_to(keys, (16, plan.loc_dev)).astype(BF16), spread)
        band = lax.broadcasted_iota(jnp.int32, (1, total), 1) % plan.band_dev
        place_ref[...] = wide[:1] + (band * plan.loc_dev).astype(F32)
        copies[1].wait()
        rows_ref[...] = x_ref[...].reshape(total, plan.width)
        pick_rows(plan, 0, place_ref[...], rows_ref, outs)

    return call(
        kernel,
        [jax.ShapeDtypeStruct((plan.rows, plan.width), BF16)] * count
        + [
            jax.ShapeDtypeStruct((total, plan.width), BF16),
            jax.ShapeDtypeStruct((1, plan.loc_dev), F32),
            jax.ShapeDtypeStruct((1, total), F32),
        ],
        2 * plan.loc_dev * tokens.size,
        4 * tokens.size,
        limit=WHOLE_LIMIT,
        in_specs=[ANY] * 2,
        out_specs=[VMEM] * (count + 3),
        scratch_shapes=[
            pltpu.VMEM(ids.shape, jnp.int32),
            pltpu.VMEM(tokens.shape, BF16),
            pltpu.SemaphoreType.DMA((2,)),
        ],
    )(ids, tokens)


def arrange_next(plan, window, rows, place_keys, after):
    count = plan.rows_count

    def kernel(rows_ref, place_ref, *rest):
        pick_rows(plan, window, place_ref[...], rows_ref, rest[len(after) :])

    return call(
        kernel,
        [jax.ShapeDtypeStruct((plan.rows, plan.width), BF16)] * count,
        2 * plan.loc_dev * rows.size,
        4 * rows.size,
        in_specs=[VMEM] * 2 + [ANY] * len(after),
        out_specs=[VMEM] * count,
    )(rows, place_keys, *after)


def join_slots(plan, slots, after, flops):
    def kernel(*refs):
        for slot in range(len(slots)):
            refs[-1][pl.ds(slot * plan.rows, plan.rows), :] = refs[slot][...]

    return call(
        kernel,
        jax.ShapeDtypeStruct((len(slots) * plan.rows, plan.width), BF16),
        flops,
        4 * len(slots) * plan.rows * plan.width,
        in_specs=[VMEM] * len(slots) + [ANY] * len(after),
        out_specs=VMEM,
    )(*slots, *after)


def embed_row(plan, index_ref, table_ref):
    band = lax.axis_index("loc") // (CORES * plan.share)
    number = index_ref[lax.axis_index("band") * plan.band_dev + band]
    return table_ref[pl.ds(number, 1), :]


def loop(count, step, unroll=1):
    lax.fori_loop(0, count, lambda i, _: (step(i), 0)[1], 0, unroll=unroll)


def aligned(index, size):
    return pl.ds(pl.multiple_of(index * size, size), size)


def norm_into(target, source):
    rows = source.shape[0]
    tile = min(rows, ROW_TILE)
    for first in range(0, rows, tile):
        here = pl.ds(first, tile)
        target[here, :] = norm_rows(source[here, :]).astype(BF16)


def project(plan, tokens, index, table, weights, queries, hide, after=()):
    rows, width = tokens.shape
    tile = min(rows, ROW_TILE)
    names = range(3) if queries else range(1, 3)

    def kernel(index_ref, table_ref, w_ref, x_ref, *rest):
        outs = rest[len(after) :]
        embed = embed_row(plan, index_ref, table_ref)
        for first in range(0, rows, tile):
            here = pl.ds(first, tile)
            normed = norm_rows(x_ref[here, :].astype(F32) + embed).astype(BF16)
            for ref, name in zip(outs, names):
                value = dot(normed, w_ref[:, name * width : (name + 1) * width])
                ref[here, :] = (value * QUERY_SCALE if name == 0 else value).astype(BF16)

    return call(
        kernel,
        [jax.ShapeDtypeStruct((rows, width), BF16)] * len(names),
        hide * 2 * rows * width * len(names) * width,
        hide * 2 * ((1 + len(names)) * rows * width + 3 * width * width),
        in_specs=[SMEM, VMEM, VMEM, VMEM] + [ANY] * len(after),
        out_specs=[VMEM] * len(names),
    )(index, table, weights, tokens, *after)


def head_masks(rows):
    lane = lax.broadcasted_iota(jnp.int32, (rows, LANES), 1)
    return [(lane // HEAD_DIM) == head for head in range(LANES // HEAD_DIM)]


def stack_heads(query):
    return jnp.concatenate(
        [jnp.where(inside, query, jnp.zeros_like(query)) for inside in head_masks(query.shape[0])],
        axis=0,
    )


def join_heads(stacked):
    heads = LANES // HEAD_DIM
    rows = stacked.shape[0] // heads
    joined = stacked[:rows]
    for head, inside in list(enumerate(head_masks(rows)))[1:]:
        joined = jnp.where(inside, stacked[head * rows : (head + 1) * rows], joined)
    return joined


def with_ones(value):
    return jnp.concatenate([value, jnp.ones(value.shape, BF16)], axis=1)


def run_units(units, mask=None):
    def scores_of(unit):
        query, keys, _ = unit
        scores = [dot_t(query, piece) for piece in keys]
        if mask is not None:
            scores = [jnp.where(mask, piece, -1e30) for piece in scores]
        return scores

    results = []
    ahead = scores_of(units[0])
    for number, (_, _, values) in enumerate(units):
        scores = ahead
        if number + 1 < len(units):
            ahead = scores_of(units[number + 1])
        peak = functools.reduce(
            jnp.maximum, [jnp.max(piece, axis=-1, keepdims=True) for piece in scores]
        )
        total = None
        for piece, value in zip(scores, values):
            part = dot(jnp.exp(piece - peak).astype(BF16), value)
            total = part if total is None else total + part
        results.append(
            (join_heads(total[:, :LANES]) / join_heads(total[:, LANES:])).astype(BF16)
        )
    return results


def attend(plan, query, keys, values, tokens, index, table, spatial_out, hide):
    total, width = query.shape
    rows = plan.rows
    pieces = len(keys)
    pairs = width // LANES
    unit = min(total, UNIT_ROWS)

    def kernel(index_ref, table_ref, w_ref, x_ref, q_ref, *rest):
        k_refs, rest = rest[:pieces], rest[pieces:]
        v_refs, (out_ref, result, added) = rest[:pieces], rest[pieces:]

        def step(number):
            units, places = [], []
            for i in range(STEP_PAIRS):
                here = aligned(number * STEP_PAIRS + i, LANES)
                pair_keys = [ref[:, here] for ref in k_refs]
                pair_values = [with_ones(ref[:, here]) for ref in v_refs]
                for first in range(0, total, unit):
                    place = (pl.ds(first, unit), here)
                    units.append((stack_heads(q_ref[place]), pair_keys, pair_values))
                    places.append(place)
            for place, done in zip(places, run_units(units)):
                result[place] = done

        loop(pairs // STEP_PAIRS, step)
        added[...] = dot(result[...], w_ref[...])
        embed = embed_row(plan, index_ref, table_ref)
        row = lax.axis_index("loc") // CORES
        for slot in range(plan.rows_count):
            here = pl.ds(slot * rows, rows)
            mid = (x_ref[here, :].astype(F32) + embed + added[here, :]).astype(BF16)
            for owner in range(plan.groups):
                part = mid[owner * plan.part_rows : (owner + 1) * plan.part_rows]
                out_ref[owner, row ^ slot] = part

    key_rows = sum(piece.shape[0] for piece in keys)
    return call(
        kernel,
        jax.ShapeDtypeStruct((plan.groups, plan.rows_count, plan.part_rows, width), BF16),
        hide * 16 * total * key_rows * width,
        hide * 2 * width * (2 * key_rows + 3 * total + width),
        in_specs=[SMEM] + [VMEM] * (4 + 2 * pieces),
        out_specs=VMEM,
        scratch_shapes=[pltpu.VMEM((total, width), BF16), pltpu.VMEM((total, width), F32)],
    )(index, table, spatial_out, tokens, query, *keys, *values)


def channel(plan, parts, channel_qkv, channel_out, up_weight, down_weight):
    groups, width = plan.groups, plan.width
    _, bands, locations, _ = parts.shape
    tile, small = TILE_LOCS, GROUP_LOCS
    assert locations % tile == 0
    group_rows = groups * bands * small
    rows = groups * bands * locations
    row_tile = min(rows, ROW_TILE)

    def kernel(qkv_hbm, out_hbm, up_hbm, down_hbm, *refs):
        in_ref, *refs = refs
        outs, refs = refs[:groups], refs[groups:]
        mid, normed, packed, attended, qkv_ref, out_ref, up_ref, down_ref, sems = refs
        me = lax.axis_index("band")
        columns = [pl.ds(first, width) for first in range(0, 3 * width, width)]
        copies = []
        for source, target, spots in (
            (qkv_hbm, qkv_ref, [(slice(None), spot) for spot in columns]),
            (out_hbm, out_ref, [(slice(None), slice(None))]),
            (up_hbm, up_ref, [(slice(None), slice(None))]),
            (down_hbm, down_ref, [(slice(None), slice(None))]),
        ):
            for spot in spots:
                copies.append(
                    pltpu.make_async_copy(
                        source.at[spot], target.at[spot], sems.at[len(copies)]
                    )
                )
        for copy in copies:
            copy.start()
        pieces = [
            (owner, band, first)
            for owner in range(groups)
            for band in range(bands)
            for first in range(0, locations, tile)
        ]

        def places(owner, band, first):
            return [
                pl.ds((at // small) * group_rows + (owner * bands + band) * small, small)
                for at in range(first, first + tile, small)
            ]

        for owner, band, first in pieces:
            piece = in_ref[me ^ owner, band, first : first + tile, :].astype(F32)
            for number, place in enumerate(places(owner, band, first)):
                mid[place, :] = piece[number * small : (number + 1) * small]
        norm_into(normed, mid)

        for number, here in enumerate(columns):
            copies[number].wait()
            factor = QUERY_SCALE if number == 0 else 1.0
            packed[:, here] = (dot(normed[...], qkv_ref[:, here]) * factor).astype(BF16)
        pairs = width // LANES
        stacked = group_rows * (LANES // HEAD_DIM)
        one = lax.broadcasted_iota(jnp.int32, (stacked, group_rows), 0)
        other = lax.broadcasted_iota(jnp.int32, (stacked, group_rows), 1)
        mask = (one % small) == (other % small)

        def attention_step(pair):
            units, spots = [], []
            for first in range(0, rows, group_rows):
                mine = pl.ds(first, group_rows)
                query = packed[mine, aligned(pair, LANES)]
                keys = packed[mine, aligned(pair + pairs, LANES)]
                values = packed[mine, aligned(pair + 2 * pairs, LANES)]
                units.append((stack_heads(query), [keys], [with_ones(values)]))
                spots.append((mine, aligned(pair, LANES)))
            for spot, done in zip(spots, run_units(units, mask)):
                attended[spot] = done

        loop(pairs, attention_step, unroll=3)
        copies[3].wait()
        mid[...] += dot(attended[...], out_ref[...])
        norm_into(normed, mid)

        copies[4].wait()
        copies[5].wait()

        def mlp_step(block):
            here = aligned(block, width)
            tiles = [pl.ds(first, row_tile) for first in range(0, rows, row_tile)]
            raised = [dot(normed[mine, :], up_ref[:, here]) for mine in tiles]
            for mine, value in zip(tiles, raised):
                mid[mine, :] += dot(gelu(value).astype(BF16), down_ref[here, :])

        loop(up_weight.shape[1] // width, mlp_step)
        for owner, band, first in pieces:
            piece = jnp.concatenate(
                [mid[place, :] for place in places(owner, band, first)], axis=0
            )
            outs[owner][band, first : first + tile, :] = piece.astype(BF16)

    weights = [channel_qkv, channel_out, up_weight, down_weight]
    size = sum(weight.size for weight in weights)
    return call(
        kernel,
        [jax.ShapeDtypeStruct((bands, locations, width), BF16)] * groups,
        2 * rows * size,
        2 * (2 * rows * width + size),
        limit=WIDE_LIMIT,
        in_specs=[ANY] * 4 + [VMEM],
        out_specs=[VMEM] * groups,
        scratch_shapes=[
            pltpu.VMEM((rows, width), F32),
            pltpu.VMEM((rows, width), BF16),
            pltpu.VMEM((rows, 3 * width), BF16),
            pltpu.VMEM((rows, width), BF16),
        ]
        + [pltpu.VMEM(weight.shape, BF16) for weight in weights]
        + [pltpu.SemaphoreType.DMA((6,))],
    )(*weights, parts)


def restore(plan, keys, returned):
    def kernel(keys_ref, *refs):
        ins, out_ref = refs[:-1], refs[-1]
        group = lax.axis_index("band")
        place = lax.broadcasted_iota(jnp.int32, (plan.loc_dev, plan.loc_dev), 0)
        inner = place % plan.part_rows
        part = (place // plan.part_rows) % plan.share
        owner = (place // (plan.part_rows * plan.share)) % plan.groups ^ group
        window = place // plan.block
        wanted = window * plan.block + part * plan.rows + owner * plan.part_rows + inner
        pick = jnp.where(wanted.astype(F32) == keys_ref[...], 1.0, 0.0).astype(BF16)
        for band in range(plan.band_dev):
            rows = jnp.concatenate([ref[band] for ref in ins], axis=0)
            out_ref[:, band, :] = lax.dot_general(
                pick, rows, (((0,), (0,)), ((), ())), preferred_element_type=F32
            ).astype(BF16)

    arrays = [array for chunk in returned for array in chunk]
    size = plan.loc_dev * plan.band_dev * plan.width
    return call(
        kernel,
        jax.ShapeDtypeStruct((plan.loc_dev, plan.band_dev, plan.width), BF16),
        2 * plan.loc_dev * size,
        4 * size,
    )(keys, *arrays)


def body(
    tokens,
    band_index,
    band_table,
    window_ids,
    spatial_qkv,
    spatial_out,
    channel_qkv,
    channel_out,
    up_weight,
    down_weight,
):
    plan = Plan(tokens)
    ids = window_ids.reshape(-1, LANES)
    *sent, rows, keys, place_keys = arrange_first(plan, tokens, ids)
    arrived = [[exchange(value, "loc", CORES * step) for step, value in enumerate(sent)]]
    following = []
    for window in range(1, WINDOWS):
        following = arrange_next(plan, window, rows, place_keys, arrived[-1][1:2])
        arrived.append(
            [exchange(value, "loc", CORES * step) for step, value in enumerate(following)]
        )
    mids, behind = [], following[:1]
    for window, slots in enumerate(arrived):
        hide = int(window == 0)
        own = join_slots(plan, slots, behind, 0 if hide else LONG)
        if plan.share == 1:
            other = exchange(own, "loc", 1)
            query, *mine = project(plan, own, band_index, band_table, spatial_qkv, True, hide)
            theirs = project(
                plan, other, band_index, band_table, spatial_qkv, False, hide, mine[:1]
            )
            all_keys, all_values = zip(mine, theirs)
        else:
            step = CORES * plan.share
            same = [list(range(at, at + step)) for at in range(0, plan.locs, step)]
            every = lax.all_gather(own, "loc", axis_index_groups=same, tiled=True)
            query, _, _ = project(plan, own, band_index, band_table, spatial_qkv, True, hide)
            all_keys, all_values = zip(
                project(plan, every, band_index, band_table, spatial_qkv, False, hide)
            )
        mid = attend(
            plan, query, all_keys, all_values, own, band_index, band_table, spatial_out, hide
        )
        behind = [mid]
        mids.append(mid)
    same = [
        [(g * plan.rows_count + r) * CORES + core for g in range(plan.groups) for r in range(plan.rows_count)]
        for core in range(CORES)
    ]
    returned = []
    for mid in mids:
        parts = lax.all_to_all(
            mid.reshape(-1, plan.part_rows, plan.width),
            ("band", "loc"),
            0,
            0,
            axis_index_groups=same,
            tiled=True,
        )
        parts = parts.reshape(plan.groups, plan.band_dev, -1, plan.width)
        done = channel(plan, parts, channel_qkv, channel_out, up_weight, down_weight)
        returned.append([exchange(value, "band", step) for step, value in enumerate(done)])
    return restore(plan, keys, returned)


def solution(mesh):
    placed = (P("loc", "band", None), P(), P(), P(), P(), P(), P(), P(), P(), P())
    return jax.shard_map(
        body, mesh=mesh, in_specs=placed, out_specs=P("loc", "band", None), check_vma=False
    )
```

```python
import functools

import jax
import jax.numpy as jnp
from jax import lax
from jax.experimental import pallas as pl
from jax.experimental.pallas import tpu as pltpu
from jax.sharding import PartitionSpec as P

HEADS = 12
HEAD_DIM = 64
WINDOWS = 2
CORES = 2
TILE_LOCS = 16
GROUP_LOCS = 8
UNIT_ROWS = 256
STEP_PAIRS = 3
ROW_TILE = 256
LANES = 128
QUERY_SCALE = HEAD_DIM ** (-0.5)
VMEM_LIMIT = 28 * 1024 * 1024
WIDE_LIMIT = 52 * 1024 * 1024
LONG = 2**36

F32 = jnp.float32
BF16 = jnp.bfloat16


def dot(left, right):
    return jnp.dot(left, right, preferred_element_type=F32)


def dot_t(left, right):
    return lax.dot_general(left, right, (((1,), (1,)), ((), ())), preferred_element_type=F32)


def norm_rows(values):
    centre = values - jnp.mean(values, axis=-1, keepdims=True)
    spread = jnp.mean(centre * centre, axis=-1, keepdims=True)
    return centre * lax.rsqrt(spread + 1e-05)


def gelu(values):
    inner = values * (0.7978845608028654 + 0.035677408136300125 * (values * values))
    return (0.5 * values) * (1.0 + jnp.tanh(inner))


def call(kernel, out_shape, flops, nbytes, limit=VMEM_LIMIT, **kwargs):
    return pl.pallas_call(
        kernel,
        out_shape=out_shape,
        compiler_params=pltpu.CompilerParams(vmem_limit_bytes=limit),
        cost_estimate=pl.CostEstimate(flops=flops, bytes_accessed=nbytes, transcendentals=0),
        **kwargs,
    )


def exchange(value, axis, step):
    if step == 0:
        return value
    return lax.ppermute(value, axis, [(i, i ^ step) for i in range(lax.axis_size(axis))])


class Plan:
    def __init__(self, tokens):
        self.loc_dev, self.band_dev, self.width = tokens.shape
        self.locs = lax.axis_size("loc")
        self.groups = lax.axis_size("band")
        self.rows_count = self.locs // CORES
        self.share = self.rows_count // self.band_dev
        assert self.share * self.band_dev * CORES == self.locs
        self.block = self.loc_dev // WINDOWS
        self.rows = self.block // self.share
        self.part_rows = self.rows // self.groups
        assert self.part_rows * self.groups * self.share * WINDOWS == self.loc_dev


def location_keys(plan, ids_ref):
    size = plan.loc_dev
    lines = size // LANES
    first = lax.axis_index("loc") * lines
    ids = jnp.concatenate([ids_ref[pl.ds(first + i, 1), :] for i in range(lines)], axis=1)
    ids = ids.astype(F32)
    row = jnp.broadcast_to(ids, (size, size))
    first = lax.broadcasted_iota(jnp.int32, (size, size), 0)
    second = lax.broadcasted_iota(jnp.int32, (size, size), 1)
    column = jnp.sum(jnp.where(first == second, row, 0.0), axis=1, keepdims=True)
    before = jnp.where((column == row) & (first < second), 1.0, 0.0)
    rank = jnp.sum(before, axis=0, keepdims=True)
    return ids * plan.block + rank


SMEM = pl.BlockSpec(memory_space=pltpu.SMEM)
VMEM = pl.BlockSpec(memory_space=pltpu.VMEM)
ANY = pl.BlockSpec(memory_space=pl.ANY)


def pick_rows(plan, window, place_keys, rows, outs):
    row = lax.axis_index("loc") // CORES
    place = lax.broadcasted_iota(jnp.int32, (plan.rows, rows.shape[0]), 0)
    for slot in range(plan.rows_count):
        peer = row ^ slot
        band, part = peer // plan.share, peer % plan.share
        wanted = place + (band * plan.loc_dev + window * plan.block + part * plan.rows)
        pick = jnp.where(wanted.astype(F32) == place_keys, 1.0, 0.0).astype(BF16)
        outs[slot][...] = dot(pick, rows[...]).astype(BF16)


def arrange_first(plan, tokens, ids):
    count = plan.rows_count
    total = plan.loc_dev * plan.band_dev
    assert plan.loc_dev <= 256

    def kernel(ids_ref, x_ref, *rest):
        outs, (rows_ref, keys_ref, place_ref) = rest[:count], rest[count:]
        keys = location_keys(plan, ids_ref)
        keys_ref[...] = keys
        place = lax.broadcasted_iota(jnp.int32, (plan.loc_dev, total), 1)
        location = lax.broadcasted_iota(jnp.int32, (plan.loc_dev, total), 0)
        spread = jnp.where(place // plan.band_dev == location, 1.0, 0.0).astype(BF16)
        wide = dot(jnp.broadcast_to(keys, (16, plan.loc_dev)).astype(BF16), spread)
        band = lax.broadcasted_iota(jnp.int32, (1, total), 1) % plan.band_dev
        place_ref[...] = wide[:1] + (band * plan.loc_dev).astype(F32)
        rows_ref[...] = x_ref[...].reshape(total, plan.width)
        pick_rows(plan, 0, place_ref[...], rows_ref, outs)

    return call(
        kernel,
        [jax.ShapeDtypeStruct((plan.rows, plan.width), BF16)] * count
        + [
            jax.ShapeDtypeStruct((total, plan.width), BF16),
            jax.ShapeDtypeStruct((1, plan.loc_dev), F32),
            jax.ShapeDtypeStruct((1, total), F32),
        ],
        2 * plan.loc_dev * tokens.size,
        4 * tokens.size,
        in_specs=[VMEM] * 2,
        out_specs=[VMEM] * (count + 3),
    )(ids, tokens)


def arrange_next(plan, window, rows, place_keys, after):
    count = plan.rows_count

    def kernel(rows_ref, place_ref, *rest):
        pick_rows(plan, window, place_ref[...], rows_ref, rest[len(after) :])

    return call(
        kernel,
        [jax.ShapeDtypeStruct((plan.rows, plan.width), BF16)] * count,
        2 * plan.loc_dev * rows.size,
        4 * rows.size,
        in_specs=[VMEM] * 2 + [ANY] * len(after),
        out_specs=[VMEM] * count,
    )(rows, place_keys, *after)


def join_slots(plan, slots, after, flops):
    def kernel(*refs):
        for slot in range(len(slots)):
            refs[-1][pl.ds(slot * plan.rows, plan.rows), :] = refs[slot][...]

    return call(
        kernel,
        jax.ShapeDtypeStruct((len(slots) * plan.rows, plan.width), BF16),
        flops,
        4 * len(slots) * plan.rows * plan.width,
        in_specs=[VMEM] * len(slots) + [ANY] * len(after),
        out_specs=VMEM,
    )(*slots, *after)


def embed_row(plan, index_ref, table_ref):
    band = lax.axis_index("loc") // (CORES * plan.share)
    number = index_ref[lax.axis_index("band") * plan.band_dev + band]
    return table_ref[pl.ds(number, 1), :]


def loop(count, step, unroll=1):
    lax.fori_loop(0, count, lambda i, _: (step(i), 0)[1], 0, unroll=unroll)


def aligned(index, size):
    return pl.ds(pl.multiple_of(index * size, size), size)


def norm_into(target, source):
    rows = source.shape[0]
    tile = min(rows, ROW_TILE)
    for first in range(0, rows, tile):
        here = pl.ds(first, tile)
        target[here, :] = norm_rows(source[here, :]).astype(BF16)


def project(plan, tokens, index, table, weights, queries, hide, after=()):
    rows, width = tokens.shape
    tile = min(rows, ROW_TILE)
    names = range(3) if queries else range(1, 3)

    def kernel(index_ref, table_ref, w_ref, x_ref, *rest):
        outs = rest[len(after) :]
        embed = embed_row(plan, index_ref, table_ref)
        for first in range(0, rows, tile):
            here = pl.ds(first, tile)
            normed = norm_rows(x_ref[here, :].astype(F32) + embed).astype(BF16)
            for ref, name in zip(outs, names):
                value = dot(normed, w_ref[:, name * width : (name + 1) * width])
                ref[here, :] = (value * QUERY_SCALE if name == 0 else value).astype(BF16)

    return call(
        kernel,
        [jax.ShapeDtypeStruct((rows, width), BF16)] * len(names),
        hide * 2 * rows * width * len(names) * width,
        hide * 2 * ((1 + len(names)) * rows * width + 3 * width * width),
        in_specs=[SMEM, VMEM, VMEM, VMEM] + [ANY] * len(after),
        out_specs=[VMEM] * len(names),
    )(index, table, weights, tokens, *after)


def head_masks(rows):
    lane = lax.broadcasted_iota(jnp.int32, (rows, LANES), 1)
    return [(lane // HEAD_DIM) == head for head in range(LANES // HEAD_DIM)]


def stack_heads(query):
    return jnp.concatenate(
        [jnp.where(inside, query, jnp.zeros_like(query)) for inside in head_masks(query.shape[0])],
        axis=0,
    )


def join_heads(stacked):
    heads = LANES // HEAD_DIM
    rows = stacked.shape[0] // heads
    joined = stacked[:rows]
    for head, inside in list(enumerate(head_masks(rows)))[1:]:
        joined = jnp.where(inside, stacked[head * rows : (head + 1) * rows], joined)
    return joined


def with_ones(value):
    return jnp.concatenate([value, jnp.ones(value.shape, BF16)], axis=1)


def run_units(units, mask=None):
    def scores_of(unit):
        query, keys, _ = unit
        scores = [dot_t(query, piece) for piece in keys]
        if mask is not None:
            scores = [jnp.where(mask, piece, -1e30) for piece in scores]
        return scores

    results = []
    ahead = scores_of(units[0])
    for number, (_, _, values) in enumerate(units):
        scores = ahead
        if number + 1 < len(units):
            ahead = scores_of(units[number + 1])
        peak = functools.reduce(
            jnp.maximum, [jnp.max(piece, axis=-1, keepdims=True) for piece in scores]
        )
        total = None
        for piece, value in zip(scores, values):
            part = dot(jnp.exp(piece - peak).astype(BF16), value)
            total = part if total is None else total + part
        results.append(
            (join_heads(total[:, :LANES]) / join_heads(total[:, LANES:])).astype(BF16)
        )
    return results


def attend(plan, query, keys, values, tokens, index, table, spatial_out, hide):
    total, width = query.shape
    rows = plan.rows
    pieces = len(keys)
    pairs = width // LANES
    unit = min(total, UNIT_ROWS)

    def kernel(index_ref, table_ref, w_ref, x_ref, q_ref, *rest):
        k_refs, rest = rest[:pieces], rest[pieces:]
        v_refs, (out_ref, result, added) = rest[:pieces], rest[pieces:]

        def step(number):
            units, places = [], []
            for i in range(STEP_PAIRS):
                here = aligned(number * STEP_PAIRS + i, LANES)
                pair_keys = [ref[:, here] for ref in k_refs]
                pair_values = [with_ones(ref[:, here]) for ref in v_refs]
                for first in range(0, total, unit):
                    place = (pl.ds(first, unit), here)
                    units.append((stack_heads(q_ref[place]), pair_keys, pair_values))
                    places.append(place)
            for place, done in zip(places, run_units(units)):
                result[place] = done

        loop(pairs // STEP_PAIRS, step)
        added[...] = dot(result[...], w_ref[...])
        embed = embed_row(plan, index_ref, table_ref)
        row = lax.axis_index("loc") // CORES
        for slot in range(plan.rows_count):
            here = pl.ds(slot * rows, rows)
            mid = (x_ref[here, :].astype(F32) + embed + added[here, :]).astype(BF16)
            for owner in range(plan.groups):
                part = mid[owner * plan.part_rows : (owner + 1) * plan.part_rows]
                out_ref[row ^ slot, owner] = part

    key_rows = sum(piece.shape[0] for piece in keys)
    return call(
        kernel,
        jax.ShapeDtypeStruct((plan.rows_count, plan.groups, plan.part_rows, width), BF16),
        hide * 16 * total * key_rows * width,
        hide * 2 * width * (2 * key_rows + 3 * total + width),
        in_specs=[SMEM] + [VMEM] * (4 + 2 * pieces),
        out_specs=VMEM,
        scratch_shapes=[pltpu.VMEM((total, width), BF16), pltpu.VMEM((total, width), F32)],
    )(index, table, spatial_out, tokens, query, *keys, *values)


def channel(plan, parts, channel_qkv, channel_out, up_weight, down_weight):
    groups, width = plan.groups, plan.width
    bands, _, locations, _ = parts.shape
    tile, small = TILE_LOCS, GROUP_LOCS
    assert locations % tile == 0
    group_rows = groups * bands * small
    rows = groups * bands * locations
    row_tile = min(rows, ROW_TILE)

    def kernel(qkv_hbm, out_hbm, up_hbm, down_hbm, *refs):
        in_ref, *refs = refs
        outs, refs = refs[:groups], refs[groups:]
        mid, normed, packed, attended, qkv_ref, out_ref, up_ref, down_ref, sems = refs
        me = lax.axis_index("band")
        columns = [pl.ds(first, width) for first in range(0, 3 * width, width)]
        copies = []
        for source, target, spots in (
            (qkv_hbm, qkv_ref, [(slice(None), spot) for spot in columns]),
            (out_hbm, out_ref, [(slice(None), slice(None))]),
            (up_hbm, up_ref, [(slice(None), slice(None))]),
            (down_hbm, down_ref, [(slice(None), slice(None))]),
        ):
            for spot in spots:
                copies.append(
                    pltpu.make_async_copy(
                        source.at[spot], target.at[spot], sems.at[len(copies)]
                    )
                )
        for copy in copies:
            copy.start()
        pieces = [
            (owner, band, first)
            for owner in range(groups)
            for band in range(bands)
            for first in range(0, locations, tile)
        ]

        def places(owner, band, first):
            return [
                pl.ds((at // small) * group_rows + (owner * bands + band) * small, small)
                for at in range(first, first + tile, small)
            ]

        for owner, band, first in pieces:
            piece = in_ref[band, me ^ owner, first : first + tile, :].astype(F32)
            for number, place in enumerate(places(owner, band, first)):
                mid[place, :] = piece[number * small : (number + 1) * small]
        norm_into(normed, mid)

        for number, here in enumerate(columns):
            copies[number].wait()
            factor = QUERY_SCALE if number == 0 else 1.0
            packed[:, here] = (dot(normed[...], qkv_ref[:, here]) * factor).astype(BF16)
        pairs = width // LANES
        stacked = group_rows * (LANES // HEAD_DIM)
        one = lax.broadcasted_iota(jnp.int32, (stacked, group_rows), 0)
        other = lax.broadcasted_iota(jnp.int32, (stacked, group_rows), 1)
        mask = (one % small) == (other % small)

        def attention_step(pair):
            units, spots = [], []
            for first in range(0, rows, group_rows):
                mine = pl.ds(first, group_rows)
                query = packed[mine, aligned(pair, LANES)]
                keys = packed[mine, aligned(pair + pairs, LANES)]
                values = packed[mine, aligned(pair + 2 * pairs, LANES)]
                units.append((stack_heads(query), [keys], [with_ones(values)]))
                spots.append((mine, aligned(pair, LANES)))
            for spot, done in zip(spots, run_units(units, mask)):
                attended[spot] = done

        loop(pairs, attention_step, unroll=3)
        copies[3].wait()
        mid[...] += dot(attended[...], out_ref[...])
        norm_into(normed, mid)

        copies[4].wait()
        copies[5].wait()

        def mlp_step(block):
            here = aligned(block, width)
            tiles = [pl.ds(first, row_tile) for first in range(0, rows, row_tile)]
            raised = [dot(normed[mine, :], up_ref[:, here]) for mine in tiles]
            for mine, value in zip(tiles, raised):
                mid[mine, :] += dot(gelu(value).astype(BF16), down_ref[here, :])

        loop(up_weight.shape[1] // width, mlp_step)
        for owner, band, first in pieces:
            piece = jnp.concatenate(
                [mid[place, :] for place in places(owner, band, first)], axis=0
            )
            outs[owner][band, first : first + tile, :] = piece.astype(BF16)

    weights = [channel_qkv, channel_out, up_weight, down_weight]
    size = sum(weight.size for weight in weights)
    return call(
        kernel,
        [jax.ShapeDtypeStruct((bands, locations, width), BF16)] * groups,
        2 * rows * size,
        2 * (2 * rows * width + size),
        limit=WIDE_LIMIT,
        in_specs=[ANY] * 4 + [VMEM],
        out_specs=[VMEM] * groups,
        scratch_shapes=[
            pltpu.VMEM((rows, width), F32),
            pltpu.VMEM((rows, width), BF16),
            pltpu.VMEM((rows, 3 * width), BF16),
            pltpu.VMEM((rows, width), BF16),
        ]
        + [pltpu.VMEM(weight.shape, BF16) for weight in weights]
        + [pltpu.SemaphoreType.DMA((6,))],
    )(*weights, parts)


def restore(plan, keys, returned):
    def kernel(keys_ref, *refs):
        ins, out_ref = refs[:-1], refs[-1]
        group = lax.axis_index("band")
        place = lax.broadcasted_iota(jnp.int32, (plan.loc_dev, plan.loc_dev), 0)
        inner = place % plan.part_rows
        part = (place // plan.part_rows) % plan.share
        owner = (place // (plan.part_rows * plan.share)) % plan.groups ^ group
        window = place // plan.block
        wanted = window * plan.block + part * plan.rows + owner * plan.part_rows + inner
        pick = jnp.where(wanted.astype(F32) == keys_ref[...], 1.0, 0.0).astype(BF16)
        for band in range(plan.band_dev):
            rows = jnp.concatenate([ref[band] for ref in ins], axis=0)
            out_ref[:, band, :] = lax.dot_general(
                pick, rows, (((0,), (0,)), ((), ())), preferred_element_type=F32
            ).astype(BF16)

    arrays = [array for chunk in returned for array in chunk]
    size = plan.loc_dev * plan.band_dev * plan.width
    return call(
        kernel,
        jax.ShapeDtypeStruct((plan.loc_dev, plan.band_dev, plan.width), BF16),
        2 * plan.loc_dev * size,
        4 * size,
    )(keys, *arrays)


def body(
    tokens,
    band_index,
    band_table,
    window_ids,
    spatial_qkv,
    spatial_out,
    channel_qkv,
    channel_out,
    up_weight,
    down_weight,
):
    plan = Plan(tokens)
    ids = window_ids.reshape(-1, LANES)
    *sent, rows, keys, place_keys = arrange_first(plan, tokens, ids)
    arrived = [[exchange(value, "loc", CORES * step) for step, value in enumerate(sent)]]
    following = []
    for window in range(1, WINDOWS):
        following = arrange_next(plan, window, rows, place_keys, arrived[-1][1:2])
        arrived.append(
            [exchange(value, "loc", CORES * step) for step, value in enumerate(following)]
        )
    mids, behind = [], following[:1]
    for window, slots in enumerate(arrived):
        hide = int(window == 0)
        own = join_slots(plan, slots, behind, 0 if hide else LONG)
        if plan.share == 1:
            other = exchange(own, "loc", 1)
            query, *mine = project(plan, own, band_index, band_table, spatial_qkv, True, hide)
            theirs = project(
                plan, other, band_index, band_table, spatial_qkv, False, hide, mine[:1]
            )
            all_keys, all_values = zip(mine, theirs)
        else:
            step = CORES * plan.share
            same = [list(range(at, at + step)) for at in range(0, plan.locs, step)]
            every = lax.all_gather(own, "loc", axis_index_groups=same, tiled=True)
            query, _, _ = project(plan, own, band_index, band_table, spatial_qkv, True, hide)
            all_keys, all_values = zip(
                project(plan, every, band_index, band_table, spatial_qkv, False, hide)
            )
        mid = attend(
            plan, query, all_keys, all_values, own, band_index, band_table, spatial_out, hide
        )
        behind = [mid]
        mids.append(mid)
    same = [
        [g * plan.locs + r * CORES + core for r in range(plan.rows_count) for g in range(plan.groups)]
        for core in range(CORES)
    ]
    returned = []
    for mid in mids:
        parts = lax.all_to_all(
            mid.reshape(-1, plan.part_rows, plan.width),
            ("band", "loc"),
            0,
            0,
            axis_index_groups=same,
            tiled=True,
        )
        parts = parts.reshape(plan.band_dev, plan.share, plan.groups, plan.part_rows, plan.width)
        parts = parts.transpose(0, 2, 1, 3, 4).reshape(plan.band_dev, plan.groups, -1, plan.width)
        done = channel(plan, parts, channel_qkv, channel_out, up_weight, down_weight)
        returned.append([exchange(value, "band", step) for step, value in enumerate(done)])
    return restore(plan, keys, returned)


def solution(mesh):
    placed = (P("loc", "band", None), P(), P(), P(), P(), P(), P(), P(), P(), P())
    return jax.shard_map(
        body, mesh=mesh, in_specs=placed, out_specs=P("loc", "band", None), check_vma=False
    )
```

```python
import functools

import jax
import jax.numpy as jnp
from jax import lax
from jax.experimental import pallas as pl
from jax.experimental.pallas import tpu as pltpu
from jax.sharding import PartitionSpec as P

HEADS = 12
HEAD_DIM = 64
WINDOWS = 2
CORES = 2
TILE_LOCS = 16
GROUP_LOCS = 8
UNIT_ROWS = 256
STEP_PAIRS = 3
ROW_TILE = 256
LANES = 128
QUERY_SCALE = HEAD_DIM ** (-0.5)
VMEM_LIMIT = 28 * 1024 * 1024
WIDE_LIMIT = 52 * 1024 * 1024
LONG = 2**36

F32 = jnp.float32
BF16 = jnp.bfloat16


def dot(left, right):
    return jnp.dot(left, right, preferred_element_type=F32)


def dot_t(left, right):
    return lax.dot_general(left, right, (((1,), (1,)), ((), ())), preferred_element_type=F32)


def norm_rows(values):
    centre = values - jnp.mean(values, axis=-1, keepdims=True)
    spread = jnp.mean(centre * centre, axis=-1, keepdims=True)
    return centre * lax.rsqrt(spread + 1e-05)


def gelu(values):
    inner = values * (0.7978845608028654 + 0.035677408136300125 * (values * values))
    return (0.5 * values) * (1.0 + jnp.tanh(inner))


def call(kernel, out_shape, flops, nbytes, limit=VMEM_LIMIT, **kwargs):
    return pl.pallas_call(
        kernel,
        out_shape=out_shape,
        compiler_params=pltpu.CompilerParams(vmem_limit_bytes=limit),
        cost_estimate=pl.CostEstimate(flops=flops, bytes_accessed=nbytes, transcendentals=0),
        **kwargs,
    )


def exchange(value, axis, step):
    if step == 0:
        return value
    return lax.ppermute(value, axis, [(i, i ^ step) for i in range(lax.axis_size(axis))])


class Plan:
    def __init__(self, tokens):
        self.loc_dev, self.band_dev, self.width = tokens.shape
        self.locs = lax.axis_size("loc")
        self.groups = lax.axis_size("band")
        self.rows_count = self.locs // CORES
        self.share = self.rows_count // self.band_dev
        assert self.share * self.band_dev * CORES == self.locs
        self.block = self.loc_dev // WINDOWS
        self.rows = self.block // self.share
        self.part_rows = self.rows // self.groups
        assert self.part_rows * self.groups * self.share * WINDOWS == self.loc_dev


def location_keys(plan, ids_ref):
    size = plan.loc_dev
    lines = size // LANES
    first = lax.axis_index("loc") * lines
    ids = jnp.concatenate([ids_ref[pl.ds(first + i, 1), :] for i in range(lines)], axis=1)
    ids = ids.astype(F32)
    row = jnp.broadcast_to(ids, (size, size))
    first = lax.broadcasted_iota(jnp.int32, (size, size), 0)
    second = lax.broadcasted_iota(jnp.int32, (size, size), 1)
    column = jnp.sum(jnp.where(first == second, row, 0.0), axis=1, keepdims=True)
    before = jnp.where((column == row) & (first < second), 1.0, 0.0)
    rank = jnp.sum(before, axis=0, keepdims=True)
    return ids * plan.block + rank


SMEM = pl.BlockSpec(memory_space=pltpu.SMEM)
VMEM = pl.BlockSpec(memory_space=pltpu.VMEM)
ANY = pl.BlockSpec(memory_space=pl.ANY)


def pick_rows(plan, window, place_keys, rows, outs):
    row = lax.axis_index("loc") // CORES
    place = lax.broadcasted_iota(jnp.int32, (plan.rows, rows.shape[0]), 0)
    for slot in range(plan.rows_count):
        peer = row ^ slot
        band, part = peer // plan.share, peer % plan.share
        wanted = place + (band * plan.loc_dev + window * plan.block + part * plan.rows)
        pick = jnp.where(wanted.astype(F32) == place_keys, 1.0, 0.0).astype(BF16)
        outs[slot][...] = dot(pick, rows[...]).astype(BF16)


def arrange_first(plan, tokens, ids):
    count = plan.rows_count
    total = plan.loc_dev * plan.band_dev
    assert plan.loc_dev <= 256

    def kernel(ids_ref, x_ref, *rest):
        outs, (rows_ref, keys_ref, place_ref) = rest[:count], rest[count:]
        keys = location_keys(plan, ids_ref)
        keys_ref[...] = keys
        place = lax.broadcasted_iota(jnp.int32, (plan.loc_dev, total), 1)
        location = lax.broadcasted_iota(jnp.int32, (plan.loc_dev, total), 0)
        spread = jnp.where(place // plan.band_dev == location, 1.0, 0.0).astype(BF16)
        wide = dot(jnp.broadcast_to(keys, (16, plan.loc_dev)).astype(BF16), spread)
        band = lax.broadcasted_iota(jnp.int32, (1, total), 1) % plan.band_dev
        place_ref[...] = wide[:1] + (band * plan.loc_dev).astype(F32)
        rows_ref[...] = x_ref[...].reshape(total, plan.width)
        pick_rows(plan, 0, place_ref[...], rows_ref, outs)

    return call(
        kernel,
        [jax.ShapeDtypeStruct((plan.rows, plan.width), BF16)] * count
        + [
            jax.ShapeDtypeStruct((total, plan.width), BF16),
            jax.ShapeDtypeStruct((1, plan.loc_dev), F32),
            jax.ShapeDtypeStruct((1, total), F32),
        ],
        2 * plan.loc_dev * tokens.size,
        4 * tokens.size,
        in_specs=[VMEM] * 2,
        out_specs=[VMEM] * (count + 3),
    )(ids, tokens)


def arrange_next(plan, window, rows, place_keys, after):
    count = plan.rows_count

    def kernel(rows_ref, place_ref, *rest):
        pick_rows(plan, window, place_ref[...], rows_ref, rest[len(after) :])

    return call(
        kernel,
        [jax.ShapeDtypeStruct((plan.rows, plan.width), BF16)] * count,
        2 * plan.loc_dev * rows.size,
        4 * rows.size,
        in_specs=[VMEM] * 2 + [ANY] * len(after),
        out_specs=[VMEM] * count,
    )(rows, place_keys, *after)


def join_slots(plan, slots, after, flops):
    count, rows = len(slots), plan.rows

    def kernel(*refs):
        out_ref, sems = refs[-2:]
        copies = [
            pltpu.make_async_copy(
                refs[slot], out_ref.at[pl.ds(slot * rows, rows), :], sems.at[slot]
            )
            for slot in range(count)
        ]
        for copy in copies:
            copy.start()
        for copy in copies:
            copy.wait()

    return call(
        kernel,
        jax.ShapeDtypeStruct((count * rows, plan.width), BF16),
        flops,
        0,
        in_specs=[ANY] * (count + len(after)),
        out_specs=VMEM,
        scratch_shapes=[pltpu.SemaphoreType.DMA((count,))],
    )(*slots, *after)


def embed_row(plan, index_ref, table_ref):
    band = lax.axis_index("loc") // (CORES * plan.share)
    number = index_ref[lax.axis_index("band") * plan.band_dev + band]
    return table_ref[pl.ds(number, 1), :]


def loop(count, step, unroll=1):
    lax.fori_loop(0, count, lambda i, _: (step(i), 0)[1], 0, unroll=unroll)


def aligned(index, size):
    return pl.ds(pl.multiple_of(index * size, size), size)


def norm_into(target, source):
    rows = source.shape[0]
    tile = min(rows, ROW_TILE)
    for first in range(0, rows, tile):
        here = pl.ds(first, tile)
        target[here, :] = norm_rows(source[here, :]).astype(BF16)


def project(plan, tokens, index, table, weights, queries, hide, after=()):
    width = plan.width
    rows = sum(piece.shape[0] for piece in tokens)
    names = range(3) if queries else range(1, 3)

    def kernel(index_ref, table_ref, w_ref, *rest):
        x_refs, outs = rest[: len(tokens)], rest[len(tokens) + len(after) :]
        embed = embed_row(plan, index_ref, table_ref)
        at = 0
        for x_ref in x_refs:
            count = x_ref.shape[0]
            tile = min(count, ROW_TILE)
            for first in range(0, count, tile):
                normed = norm_rows(x_ref[pl.ds(first, tile), :].astype(F32) + embed).astype(BF16)
                here = pl.ds(at + first, tile)
                for ref, name in zip(outs, names):
                    value = dot(normed, w_ref[:, name * width : (name + 1) * width])
                    ref[here, :] = (value * QUERY_SCALE if name == 0 else value).astype(BF16)
            at += count

    return call(
        kernel,
        [jax.ShapeDtypeStruct((rows, width), BF16)] * len(names),
        hide * 2 * rows * width * len(names) * width,
        hide * 2 * ((1 + len(names)) * rows * width + 3 * width * width),
        in_specs=[SMEM, VMEM, VMEM] + [VMEM] * len(tokens) + [ANY] * len(after),
        out_specs=[VMEM] * len(names),
    )(index, table, weights, *tokens, *after)


def head_masks(rows):
    lane = lax.broadcasted_iota(jnp.int32, (rows, LANES), 1)
    return [(lane // HEAD_DIM) == head for head in range(LANES // HEAD_DIM)]


def stack_heads(query):
    return jnp.concatenate(
        [jnp.where(inside, query, jnp.zeros_like(query)) for inside in head_masks(query.shape[0])],
        axis=0,
    )


def join_heads(stacked):
    heads = LANES // HEAD_DIM
    rows = stacked.shape[0] // heads
    joined = stacked[:rows]
    for head, inside in list(enumerate(head_masks(rows)))[1:]:
        joined = jnp.where(inside, stacked[head * rows : (head + 1) * rows], joined)
    return joined


def with_ones(value):
    return jnp.concatenate([value, jnp.ones(value.shape, BF16)], axis=1)


def run_units(units, mask=None):
    def scores_of(unit):
        query, keys, _ = unit
        scores = [dot_t(query, piece) for piece in keys]
        if mask is not None:
            scores = [jnp.where(mask, piece, -1e30) for piece in scores]
        return scores

    results = []
    ahead = scores_of(units[0])
    for number, (_, _, values) in enumerate(units):
        scores = ahead
        if number + 1 < len(units):
            ahead = scores_of(units[number + 1])
        peak = functools.reduce(
            jnp.maximum, [jnp.max(piece, axis=-1, keepdims=True) for piece in scores]
        )
        total = None
        for piece, value in zip(scores, values):
            part = dot(jnp.exp(piece - peak).astype(BF16), value)
            total = part if total is None else total + part
        results.append(
            (join_heads(total[:, :LANES]) / join_heads(total[:, LANES:])).astype(BF16)
        )
    return results


def attend(plan, query, keys, values, tokens, index, table, spatial_out, hide):
    width, rows = plan.width, plan.rows
    pieces, sources = len(keys), len(query)
    counts = [piece.shape[0] for piece in query]
    total = sum(counts)
    pairs = width // LANES

    def kernel(index_ref, table_ref, w_ref, *rest):
        x_refs, rest = rest[:sources], rest[sources:]
        q_refs, rest = rest[:sources], rest[sources:]
        k_refs, rest = rest[:pieces], rest[pieces:]
        v_refs, (out_ref, result, added) = rest[:pieces], rest[pieces:]

        def step(number):
            units, places = [], []
            for i in range(STEP_PAIRS):
                here = aligned(number * STEP_PAIRS + i, LANES)
                pair_keys = [ref[:, here] for ref in k_refs]
                pair_values = [with_ones(ref[:, here]) for ref in v_refs]
                at = 0
                for ref, count in zip(q_refs, counts):
                    unit = min(count, UNIT_ROWS)
                    for first in range(0, count, unit):
                        query_rows = ref[pl.ds(first, unit), here]
                        units.append((stack_heads(query_rows), pair_keys, pair_values))
                        places.append((pl.ds(at + first, unit), here))
                    at += count
            for place, done in zip(places, run_units(units)):
                result[place] = done

        loop(pairs // STEP_PAIRS, step)
        added[...] = dot(result[...], w_ref[...])
        embed = embed_row(plan, index_ref, table_ref)
        row = lax.axis_index("loc") // CORES
        slot = 0
        for ref, count in zip(x_refs, counts):
            for first in range(0, count, rows):
                start = ref[pl.ds(first, rows), :].astype(F32) + embed
                mid = (start + added[pl.ds(slot * rows, rows), :]).astype(BF16)
                for owner in range(plan.groups):
                    part = mid[owner * plan.part_rows : (owner + 1) * plan.part_rows]
                    out_ref[row ^ slot, owner] = part
                slot += 1

    key_rows = sum(piece.shape[0] for piece in keys)
    return call(
        kernel,
        jax.ShapeDtypeStruct((plan.rows_count, plan.groups, plan.part_rows, width), BF16),
        hide * 16 * total * key_rows * width,
        hide * 2 * width * (2 * key_rows + 3 * total + width),
        in_specs=[SMEM] + [VMEM] * (2 + 2 * sources + 2 * pieces),
        out_specs=VMEM,
        scratch_shapes=[pltpu.VMEM((total, width), BF16), pltpu.VMEM((total, width), F32)],
    )(index, table, spatial_out, *tokens, *query, *keys, *values)


def channel(plan, parts, channel_qkv, channel_out, up_weight, down_weight):
    groups, width = plan.groups, plan.width
    bands, _, locations, _ = parts.shape
    tile, small = TILE_LOCS, GROUP_LOCS
    assert locations % tile == 0
    group_rows = groups * bands * small
    rows = groups * bands * locations
    row_tile = min(rows, ROW_TILE)

    def kernel(qkv_hbm, out_hbm, up_hbm, down_hbm, *refs):
        in_ref, *refs = refs
        outs, refs = refs[:groups], refs[groups:]
        mid, normed, packed, attended, qkv_ref, out_ref, up_ref, down_ref, sems = refs
        me = lax.axis_index("band")
        columns = [pl.ds(first, width) for first in range(0, 3 * width, width)]
        copies = []
        for source, target, spots in (
            (qkv_hbm, qkv_ref, [(slice(None), spot) for spot in columns]),
            (out_hbm, out_ref, [(slice(None), slice(None))]),
            (up_hbm, up_ref, [(slice(None), slice(None))]),
            (down_hbm, down_ref, [(slice(None), slice(None))]),
        ):
            for spot in spots:
                copies.append(
                    pltpu.make_async_copy(
                        source.at[spot], target.at[spot], sems.at[len(copies)]
                    )
                )
        for copy in copies[: len(columns)]:
            copy.start()
        pieces = [
            (owner, band, first)
            for owner in range(groups)
            for band in range(bands)
            for first in range(0, locations, tile)
        ]

        def places(owner, band, first):
            return [
                pl.ds((at // small) * group_rows + (owner * bands + band) * small, small)
                for at in range(first, first + tile, small)
            ]

        for owner, band, first in pieces:
            piece = in_ref[band, me ^ owner, first : first + tile, :].astype(F32)
            for number, place in enumerate(places(owner, band, first)):
                mid[place, :] = piece[number * small : (number + 1) * small]
        norm_into(normed, mid)

        for number, here in enumerate(columns):
            copies[number].wait()
            copies[number + len(columns)].start()
            factor = QUERY_SCALE if number == 0 else 1.0
            packed[:, here] = (dot(normed[...], qkv_ref[:, here]) * factor).astype(BF16)
        pairs = width // LANES
        stacked = group_rows * (LANES // HEAD_DIM)
        one = lax.broadcasted_iota(jnp.int32, (stacked, group_rows), 0)
        other = lax.broadcasted_iota(jnp.int32, (stacked, group_rows), 1)
        mask = (one % small) == (other % small)

        def attention_step(pair):
            units, spots = [], []
            for first in range(0, rows, group_rows):
                mine = pl.ds(first, group_rows)
                query = packed[mine, aligned(pair, LANES)]
                keys = packed[mine, aligned(pair + pairs, LANES)]
                values = packed[mine, aligned(pair + 2 * pairs, LANES)]
                units.append((stack_heads(query), [keys], [with_ones(values)]))
                spots.append((mine, aligned(pair, LANES)))
            for spot, done in zip(spots, run_units(units, mask)):
                attended[spot] = done

        loop(pairs, attention_step, unroll=3)
        copies[3].wait()
        mid[...] += dot(attended[...], out_ref[...])
        norm_into(normed, mid)

        copies[4].wait()
        copies[5].wait()

        def mlp_step(block):
            here = aligned(block, width)
            tiles = [pl.ds(first, row_tile) for first in range(0, rows, row_tile)]
            raised = [dot(normed[mine, :], up_ref[:, here]) for mine in tiles]
            for mine, value in zip(tiles, raised):
                mid[mine, :] += dot(gelu(value).astype(BF16), down_ref[here, :])

        loop(up_weight.shape[1] // width, mlp_step)
        for owner, band, first in pieces:
            piece = jnp.concatenate(
                [mid[place, :] for place in places(owner, band, first)], axis=0
            )
            outs[owner][band, first : first + tile, :] = piece.astype(BF16)

    weights = [channel_qkv, channel_out, up_weight, down_weight]
    size = sum(weight.size for weight in weights)
    return call(
        kernel,
        [jax.ShapeDtypeStruct((bands, locations, width), BF16)] * groups,
        2 * rows * size,
        2 * (2 * rows * width + size),
        limit=WIDE_LIMIT,
        in_specs=[ANY] * 4 + [VMEM],
        out_specs=[VMEM] * groups,
        scratch_shapes=[
            pltpu.VMEM((rows, width), F32),
            pltpu.VMEM((rows, width), BF16),
            pltpu.VMEM((rows, 3 * width), BF16),
            pltpu.VMEM((rows, width), BF16),
        ]
        + [pltpu.VMEM(weight.shape, BF16) for weight in weights]
        + [pltpu.SemaphoreType.DMA((6,))],
    )(*weights, parts)


def restore(plan, keys, returned):
    def kernel(keys_ref, *refs):
        ins, out_ref = refs[:-1], refs[-1]
        group = lax.axis_index("band")
        place = lax.broadcasted_iota(jnp.int32, (plan.loc_dev, plan.loc_dev), 0)
        inner = place % plan.part_rows
        part = (place // plan.part_rows) % plan.share
        owner = (place // (plan.part_rows * plan.share)) % plan.groups ^ group
        window = place // plan.block
        wanted = window * plan.block + part * plan.rows + owner * plan.part_rows + inner
        pick = jnp.where(wanted.astype(F32) == keys_ref[...], 1.0, 0.0).astype(BF16)
        for band in range(plan.band_dev):
            rows = jnp.concatenate([ref[band] for ref in ins], axis=0)
            out_ref[:, band, :] = lax.dot_general(
                pick, rows, (((0,), (0,)), ((), ())), preferred_element_type=F32
            ).astype(BF16)

    arrays = [array for chunk in returned for array in chunk]
    size = plan.loc_dev * plan.band_dev * plan.width
    return call(
        kernel,
        jax.ShapeDtypeStruct((plan.loc_dev, plan.band_dev, plan.width), BF16),
        2 * plan.loc_dev * size,
        4 * size,
    )(keys, *arrays)


def body(
    tokens,
    band_index,
    band_table,
    window_ids,
    spatial_qkv,
    spatial_out,
    channel_qkv,
    channel_out,
    up_weight,
    down_weight,
):
    plan = Plan(tokens)
    ids = window_ids.reshape(-1, LANES)
    *sent, rows, location_key, place_keys = arrange_first(plan, tokens, ids)
    arrived = [[exchange(value, "loc", CORES * step) for step, value in enumerate(sent)]]
    following = []
    for window in range(1, WINDOWS):
        following = arrange_next(plan, window, rows, place_keys, arrived[-1][1:2])
        arrived.append(
            [exchange(value, "loc", CORES * step) for step, value in enumerate(following)]
        )
    mids, behind = [], []
    for window, slots in enumerate(arrived):
        hide = int(window == 0)
        half = len(slots) // 2 if hide and plan.share == 1 else len(slots)
        owns, queries, all_keys, all_values = [], [], [], []
        tables = (band_index, band_table, spatial_qkv)
        for first in range(0, len(slots), half):
            if first > 0:
                behind = [*following[:1], queries[-1]]
            own = join_slots(plan, slots[first : first + half], behind, 0 if hide else LONG)
            query, keys, values = project(plan, [own], *tables, True, hide)
            owns.append(own)
            queries.append(query)
            all_keys.append(keys)
            all_values.append(values)
        if plan.share == 1:
            others = [exchange(own, "loc", 1) for own in owns]
            keys, values = project(plan, others, *tables, False, hide, queries[-1:])
            all_keys.append(keys)
            all_values.append(values)
        else:
            step = CORES * plan.share
            same = [list(range(at, at + step)) for at in range(0, plan.locs, step)]
            every = lax.all_gather(owns[0], "loc", axis_index_groups=same, tiled=True)
            keys, values = project(plan, [every], *tables, False, hide)
            all_keys, all_values = [keys], [values]
        mid = attend(
            plan, queries, all_keys, all_values, owns, band_index, band_table, spatial_out, hide
        )
        behind = [mid]
        mids.append(mid)
    same = [
        [g * plan.locs + r * CORES + core for r in range(plan.rows_count) for g in range(plan.groups)]
        for core in range(CORES)
    ]
    returned = []
    for mid in mids:
        parts = lax.all_to_all(
            mid.reshape(-1, plan.part_rows, plan.width),
            ("band", "loc"),
            0,
            0,
            axis_index_groups=same,
            tiled=True,
        )
        parts = parts.reshape(plan.band_dev, plan.share, plan.groups, plan.part_rows, plan.width)
        parts = parts.transpose(0, 2, 1, 3, 4).reshape(plan.band_dev, plan.groups, -1, plan.width)
        done = channel(plan, parts, channel_qkv, channel_out, up_weight, down_weight)
        returned.append([exchange(value, "band", step) for step, value in enumerate(done)])
    return restore(plan, location_key, returned)


def solution(mesh):
    placed = (P("loc", "band", None), P(), P(), P(), P(), P(), P(), P(), P(), P())
    return jax.shard_map(
        body, mesh=mesh, in_specs=placed, out_specs=P("loc", "band", None), check_vma=False
    )
```

```python
import functools

import jax
import jax.numpy as jnp
from jax import lax
from jax.experimental import pallas as pl
from jax.experimental.pallas import tpu as pltpu
from jax.sharding import PartitionSpec as P

HEADS = 12
HEAD_DIM = 64
WINDOWS = 2
CORES = 2
TILE_LOCS = 16
GROUP_LOCS = 8
UNIT_ROWS = 256
STEP_PAIRS = 3
ROW_TILE = 256
LANES = 128
QUERY_SCALE = HEAD_DIM ** (-0.5)
VMEM_LIMIT = 28 * 1024 * 1024
WIDE_LIMIT = 52 * 1024 * 1024
HEAD_LIMIT = 52 * 1024 * 1024
LONG = 2**36

F32 = jnp.float32
BF16 = jnp.bfloat16


def dot(left, right):
    return jnp.dot(left, right, preferred_element_type=F32)


def dot_t(left, right):
    return lax.dot_general(left, right, (((1,), (1,)), ((), ())), preferred_element_type=F32)


def norm_rows(values):
    centre = values - jnp.mean(values, axis=-1, keepdims=True)
    spread = jnp.mean(centre * centre, axis=-1, keepdims=True)
    return centre * lax.rsqrt(spread + 1e-05)


def gelu(values):
    inner = values * (0.7978845608028654 + 0.035677408136300125 * (values * values))
    return (0.5 * values) * (1.0 + jnp.tanh(inner))


def call(kernel, out_shape, flops, nbytes, limit=VMEM_LIMIT, **kwargs):
    return pl.pallas_call(
        kernel,
        out_shape=out_shape,
        compiler_params=pltpu.CompilerParams(vmem_limit_bytes=limit),
        cost_estimate=pl.CostEstimate(flops=flops, bytes_accessed=nbytes, transcendentals=0),
        **kwargs,
    )


def exchange(value, axis, step):
    if step == 0:
        return value
    return lax.ppermute(value, axis, [(i, i ^ step) for i in range(lax.axis_size(axis))])


class Plan:
    def __init__(self, tokens):
        self.loc_dev, self.band_dev, self.width = tokens.shape
        self.locs = lax.axis_size("loc")
        self.groups = lax.axis_size("band")
        self.rows_count = self.locs // CORES
        self.share = self.rows_count // self.band_dev
        assert self.share * self.band_dev * CORES == self.locs
        self.block = self.loc_dev // WINDOWS
        self.rows = self.block // self.share
        self.part_rows = self.rows // self.groups
        assert self.part_rows * self.groups * self.share * WINDOWS == self.loc_dev


def marker():
    return jax.ShapeDtypeStruct((8, LANES), F32)


def location_keys(plan, ids_ref):
    size = plan.loc_dev
    lines = size // LANES
    first = lax.axis_index("loc") * lines
    ids = jnp.concatenate([ids_ref[pl.ds(first + i, 1), :] for i in range(lines)], axis=1)
    ids = ids.astype(F32)
    row = jnp.broadcast_to(ids, (size, size))
    first = lax.broadcasted_iota(jnp.int32, (size, size), 0)
    second = lax.broadcasted_iota(jnp.int32, (size, size), 1)
    column = jnp.sum(jnp.where(first == second, row, 0.0), axis=1, keepdims=True)
    before = jnp.where((column == row) & (first < second), 1.0, 0.0)
    rank = jnp.sum(before, axis=0, keepdims=True)
    return ids * plan.block + rank


SMEM = pl.BlockSpec(memory_space=pltpu.SMEM)
VMEM = pl.BlockSpec(memory_space=pltpu.VMEM)
ANY = pl.BlockSpec(memory_space=pl.ANY)


def pick_rows(plan, window, place_keys, rows, outs):
    row = lax.axis_index("loc") // CORES
    place = lax.broadcasted_iota(jnp.int32, (plan.rows, rows.shape[0]), 0)
    for slot in range(plan.rows_count):
        peer = row ^ slot
        band, part = peer // plan.share, peer % plan.share
        wanted = place + (band * plan.loc_dev + window * plan.block + part * plan.rows)
        pick = jnp.where(wanted.astype(F32) == place_keys, 1.0, 0.0).astype(BF16)
        outs[slot][...] = dot(pick, rows).astype(BF16)


def arrange(plan, window, tokens, ids, after):
    count = plan.rows_count
    total = plan.loc_dev * plan.band_dev
    assert plan.loc_dev <= 256

    def kernel(ids_hbm, x_hbm, *rest):
        outs, (keys_ref, ids_ref, x_ref, sems) = rest[len(after) : -4], rest[-4:]
        copies = [
            pltpu.make_async_copy(ids_hbm, ids_ref, sems.at[0]),
            pltpu.make_async_copy(x_hbm, x_ref, sems.at[1]),
        ]
        for copy in copies:
            copy.start()
        copies[0].wait()
        keys = location_keys(plan, ids_ref)
        keys_ref[...] = keys
        place = lax.broadcasted_iota(jnp.int32, (plan.loc_dev, total), 1)
        location = lax.broadcasted_iota(jnp.int32, (plan.loc_dev, total), 0)
        spread = jnp.where(place // plan.band_dev == location, 1.0, 0.0).astype(BF16)
        wide = dot(jnp.broadcast_to(keys, (16, plan.loc_dev)).astype(BF16), spread)
        band = lax.broadcasted_iota(jnp.int32, (1, total), 1) % plan.band_dev
        place_keys = wide[:1] + (band * plan.loc_dev).astype(F32)
        copies[1].wait()
        pick_rows(plan, window, place_keys, x_ref[...].reshape(total, plan.width), outs)

    return call(
        kernel,
        [jax.ShapeDtypeStruct((plan.rows, plan.width), BF16)] * count
        + [jax.ShapeDtypeStruct((1, plan.loc_dev), F32)],
        2 * plan.loc_dev * tokens.size,
        4 * tokens.size,
        limit=HEAD_LIMIT,
        in_specs=[ANY] * (2 + len(after)),
        out_specs=[VMEM] * (count + 1),
        scratch_shapes=[
            pltpu.VMEM(ids.shape, jnp.int32),
            pltpu.VMEM(tokens.shape, BF16),
            pltpu.SemaphoreType.DMA((2,)),
        ],
    )(ids, tokens, *after)


def join_slots(plan, slots, after, flops):
    count, rows = len(slots), plan.rows

    def kernel(*refs):
        out_ref, sems = refs[-2:]
        copies = [
            pltpu.make_async_copy(
                refs[slot], out_ref.at[pl.ds(slot * rows, rows), :], sems.at[slot]
            )
            for slot in range(count)
        ]
        for copy in copies:
            copy.start()
        for copy in copies:
            copy.wait()

    return call(
        kernel,
        jax.ShapeDtypeStruct((count * rows, plan.width), BF16),
        flops,
        0,
        in_specs=[ANY] * (count + len(after)),
        out_specs=VMEM,
        scratch_shapes=[pltpu.SemaphoreType.DMA((count,))],
    )(*slots, *after)


def embed_row(plan, index_ref, table_ref):
    band = lax.axis_index("loc") // (CORES * plan.share)
    number = index_ref[lax.axis_index("band") * plan.band_dev + band]
    return table_ref[pl.ds(number, 1), :]


def loop(count, step, unroll=1):
    lax.fori_loop(0, count, lambda i, _: (step(i), 0)[1], 0, unroll=unroll)


def aligned(index, size):
    return pl.ds(pl.multiple_of(index * size, size), size)


def norm_into(target, source):
    rows = source.shape[0]
    tile = min(rows, ROW_TILE)
    for first in range(0, rows, tile):
        here = pl.ds(first, tile)
        target[here, :] = norm_rows(source[here, :]).astype(BF16)


def project(plan, tokens, index, table, weights, queries, hide, after=()):
    width = plan.width
    rows = sum(piece.shape[0] for piece in tokens)
    names = range(3) if queries else range(1, 3)

    def kernel(index_ref, table_ref, w_ref, *rest):
        x_refs, outs = rest[: len(tokens)], rest[len(tokens) + len(after) :]
        embed = embed_row(plan, index_ref, table_ref)
        at = 0
        for x_ref in x_refs:
            count = x_ref.shape[0]
            tile = min(count, ROW_TILE)
            for first in range(0, count, tile):
                normed = norm_rows(x_ref[pl.ds(first, tile), :].astype(F32) + embed).astype(BF16)
                here = pl.ds(at + first, tile)
                for ref, name in zip(outs, names):
                    value = dot(normed, w_ref[:, name * width : (name + 1) * width])
                    ref[here, :] = (value * QUERY_SCALE if name == 0 else value).astype(BF16)
            at += count

    return call(
        kernel,
        [jax.ShapeDtypeStruct((rows, width), BF16)] * len(names),
        hide * 2 * rows * width * len(names) * width,
        hide * 2 * ((1 + len(names)) * rows * width + 3 * width * width),
        in_specs=[SMEM, VMEM, VMEM] + [VMEM] * len(tokens) + [ANY] * len(after),
        out_specs=[VMEM] * len(names),
    )(index, table, weights, *tokens, *after)


def head_masks(rows):
    lane = lax.broadcasted_iota(jnp.int32, (rows, LANES), 1)
    return [(lane // HEAD_DIM) == head for head in range(LANES // HEAD_DIM)]


def stack_heads(query):
    return jnp.concatenate(
        [jnp.where(inside, query, jnp.zeros_like(query)) for inside in head_masks(query.shape[0])],
        axis=0,
    )


def join_heads(stacked):
    heads = LANES // HEAD_DIM
    rows = stacked.shape[0] // heads
    joined = stacked[:rows]
    for head, inside in list(enumerate(head_masks(rows)))[1:]:
        joined = jnp.where(inside, stacked[head * rows : (head + 1) * rows], joined)
    return joined


def with_ones(value):
    return jnp.concatenate([value, jnp.ones(value.shape, BF16)], axis=1)


def run_units(units, mask=None):
    def scores_of(unit):
        query, keys, _ = unit
        scores = [dot_t(query, piece) for piece in keys]
        if mask is not None:
            scores = [jnp.where(mask, piece, -1e30) for piece in scores]
        return scores

    results = []
    ahead = scores_of(units[0])
    for number, (_, _, values) in enumerate(units):
        scores = ahead
        if number + 1 < len(units):
            ahead = scores_of(units[number + 1])
        peak = functools.reduce(
            jnp.maximum, [jnp.max(piece, axis=-1, keepdims=True) for piece in scores]
        )
        total = None
        for piece, value in zip(scores, values):
            part = dot(jnp.exp(piece - peak).astype(BF16), value)
            total = part if total is None else total + part
        results.append(
            (join_heads(total[:, :LANES]) / join_heads(total[:, LANES:])).astype(BF16)
        )
    return results


def attend(plan, query, keys, values, tokens, index, table, spatial_out, hide):
    width, rows = plan.width, plan.rows
    pieces, sources = len(keys), len(query)
    counts = [piece.shape[0] for piece in query]
    total = sum(counts)
    pairs = width // LANES

    def kernel(index_ref, table_ref, w_ref, *rest):
        x_refs, rest = rest[:sources], rest[sources:]
        q_refs, rest = rest[:sources], rest[sources:]
        k_refs, rest = rest[:pieces], rest[pieces:]
        v_refs, (out_ref, marker_ref, result, added) = rest[:pieces], rest[pieces:]
        marker_ref[...] = jnp.zeros_like(marker_ref)

        def step(number):
            units, places = [], []
            for i in range(STEP_PAIRS):
                here = aligned(number * STEP_PAIRS + i, LANES)
                pair_keys = [ref[:, here] for ref in k_refs]
                pair_values = [with_ones(ref[:, here]) for ref in v_refs]
                at = 0
                for ref, count in zip(q_refs, counts):
                    unit = min(count, UNIT_ROWS)
                    for first in range(0, count, unit):
                        query_rows = ref[pl.ds(first, unit), here]
                        units.append((stack_heads(query_rows), pair_keys, pair_values))
                        places.append((pl.ds(at + first, unit), here))
                    at += count
            for place, done in zip(places, run_units(units)):
                result[place] = done

        loop(pairs // STEP_PAIRS, step)
        added[...] = dot(result[...], w_ref[...])
        embed = embed_row(plan, index_ref, table_ref)
        row = lax.axis_index("loc") // CORES
        slot = 0
        for ref, count in zip(x_refs, counts):
            for first in range(0, count, rows):
                start = ref[pl.ds(first, rows), :].astype(F32) + embed
                mid = (start + added[pl.ds(slot * rows, rows), :]).astype(BF16)
                for owner in range(plan.groups):
                    part = mid[owner * plan.part_rows : (owner + 1) * plan.part_rows]
                    out_ref[row ^ slot, owner] = part
                slot += 1

    key_rows = sum(piece.shape[0] for piece in keys)
    return call(
        kernel,
        [
            jax.ShapeDtypeStruct((plan.rows_count, plan.groups, plan.part_rows, width), BF16),
            marker(),
        ],
        hide * 16 * total * key_rows * width,
        hide * 2 * width * (2 * key_rows + 3 * total + width),
        in_specs=[SMEM] + [VMEM] * (2 + 2 * sources + 2 * pieces),
        out_specs=[VMEM] * 2,
        scratch_shapes=[pltpu.VMEM((total, width), BF16), pltpu.VMEM((total, width), F32)],
    )(index, table, spatial_out, *tokens, *query, *keys, *values)


def channel(plan, parts, channel_qkv, channel_out, up_weight, down_weight):
    groups, width = plan.groups, plan.width
    bands, _, locations, _ = parts.shape
    tile, small = TILE_LOCS, GROUP_LOCS
    assert locations % tile == 0
    group_rows = groups * bands * small
    rows = groups * bands * locations
    row_tile = min(rows, ROW_TILE)

    def kernel(qkv_hbm, out_hbm, up_hbm, down_hbm, *refs):
        in_ref, *refs = refs
        outs, refs = refs[:groups], refs[groups:]
        mid, normed, packed, attended, qkv_ref, out_ref, up_ref, down_ref, sems = refs
        me = lax.axis_index("band")
        columns = [pl.ds(first, width) for first in range(0, 3 * width, width)]
        copies = []
        for source, target, spots in (
            (qkv_hbm, qkv_ref, [(slice(None), spot) for spot in columns]),
            (out_hbm, out_ref, [(slice(None), slice(None))]),
            (up_hbm, up_ref, [(slice(None), slice(None))]),
            (down_hbm, down_ref, [(slice(None), slice(None))]),
        ):
            for spot in spots:
                copies.append(
                    pltpu.make_async_copy(
                        source.at[spot], target.at[spot], sems.at[len(copies)]
                    )
                )
        for copy in copies[: len(columns)]:
            copy.start()
        pieces = [
            (owner, band, first)
            for owner in range(groups)
            for band in range(bands)
            for first in range(0, locations, tile)
        ]

        def places(owner, band, first):
            return [
                pl.ds((at // small) * group_rows + (owner * bands + band) * small, small)
                for at in range(first, first + tile, small)
            ]

        for owner, band, first in pieces:
            piece = in_ref[band, me ^ owner, first : first + tile, :].astype(F32)
            for number, place in enumerate(places(owner, band, first)):
                mid[place, :] = piece[number * small : (number + 1) * small]
        norm_into(normed, mid)

        for number, here in enumerate(columns):
            copies[number].wait()
            copies[number + len(columns)].start()
            factor = QUERY_SCALE if number == 0 else 1.0
            packed[:, here] = (dot(normed[...], qkv_ref[:, here]) * factor).astype(BF16)
        pairs = width // LANES
        stacked = group_rows * (LANES // HEAD_DIM)
        one = lax.broadcasted_iota(jnp.int32, (stacked, group_rows), 0)
        other = lax.broadcasted_iota(jnp.int32, (stacked, group_rows), 1)
        mask = (one % small) == (other % small)

        def attention_step(pair):
            units, spots = [], []
            for first in range(0, rows, group_rows):
                mine = pl.ds(first, group_rows)
                query = packed[mine, aligned(pair, LANES)]
                keys = packed[mine, aligned(pair + pairs, LANES)]
                values = packed[mine, aligned(pair + 2 * pairs, LANES)]
                units.append((stack_heads(query), [keys], [with_ones(values)]))
                spots.append((mine, aligned(pair, LANES)))
            for spot, done in zip(spots, run_units(units, mask)):
                attended[spot] = done

        loop(pairs, attention_step, unroll=3)
        copies[3].wait()
        mid[...] += dot(attended[...], out_ref[...])
        norm_into(normed, mid)

        copies[4].wait()
        copies[5].wait()

        def mlp_step(block):
            here = aligned(block, width)
            tiles = [pl.ds(first, row_tile) for first in range(0, rows, row_tile)]
            raised = [dot(normed[mine, :], up_ref[:, here]) for mine in tiles]
            for mine, value in zip(tiles, raised):
                mid[mine, :] += dot(gelu(value).astype(BF16), down_ref[here, :])

        loop(up_weight.shape[1] // width, mlp_step)
        for owner, band, first in pieces:
            piece = jnp.concatenate(
                [mid[place, :] for place in places(owner, band, first)], axis=0
            )
            outs[owner][band, first : first + tile, :] = piece.astype(BF16)

    weights = [channel_qkv, channel_out, up_weight, down_weight]
    size = sum(weight.size for weight in weights)
    return call(
        kernel,
        [jax.ShapeDtypeStruct((bands, locations, width), BF16)] * groups,
        2 * rows * size,
        2 * (2 * rows * width + size),
        limit=WIDE_LIMIT,
        in_specs=[ANY] * 4 + [VMEM],
        out_specs=[VMEM] * groups,
        scratch_shapes=[
            pltpu.VMEM((rows, width), F32),
            pltpu.VMEM((rows, width), BF16),
            pltpu.VMEM((rows, 3 * width), BF16),
            pltpu.VMEM((rows, width), BF16),
        ]
        + [pltpu.VMEM(weight.shape, BF16) for weight in weights]
        + [pltpu.SemaphoreType.DMA((6,))],
    )(*weights, parts)


def restore(plan, keys, returned):
    def kernel(keys_ref, *refs):
        ins, out_ref = refs[:-1], refs[-1]
        group = lax.axis_index("band")
        place = lax.broadcasted_iota(jnp.int32, (plan.loc_dev, plan.loc_dev), 0)
        inner = place % plan.part_rows
        part = (place // plan.part_rows) % plan.share
        owner = (place // (plan.part_rows * plan.share)) % plan.groups ^ group
        window = place // plan.block
        wanted = window * plan.block + part * plan.rows + owner * plan.part_rows + inner
        pick = jnp.where(wanted.astype(F32) == keys_ref[...], 1.0, 0.0).astype(BF16)
        for band in range(plan.band_dev):
            rows = jnp.concatenate([ref[band] for ref in ins], axis=0)
            out_ref[:, band, :] = lax.dot_general(
                pick, rows, (((0,), (0,)), ((), ())), preferred_element_type=F32
            ).astype(BF16)

    arrays = [array for chunk in returned for array in chunk]
    size = plan.loc_dev * plan.band_dev * plan.width
    return call(
        kernel,
        jax.ShapeDtypeStruct((plan.loc_dev, plan.band_dev, plan.width), BF16),
        2 * plan.loc_dev * size,
        4 * size,
    )(keys, *arrays)


def body(
    tokens,
    band_index,
    band_table,
    window_ids,
    spatial_qkv,
    spatial_out,
    channel_qkv,
    channel_out,
    up_weight,
    down_weight,
):
    plan = Plan(tokens)
    ids = window_ids.reshape(-1, LANES)
    arrived, after = [], []
    for window in range(WINDOWS):
        *sent, location_key = arrange(plan, window, tokens, ids, after)
        arrived.append([exchange(value, "loc", CORES * step) for step, value in enumerate(sent)])
        after = arrived[0][1:2]
    mids, behind = [], []
    for window, slots in enumerate(arrived):
        hide = int(window == 0)
        half = len(slots) // 2 if hide and plan.share == 1 else len(slots)
        owns, queries, all_keys, all_values = [], [], [], []
        tables = (band_index, band_table, spatial_qkv)
        for first in range(0, len(slots), half):
            if first > 0:
                behind = [location_key, queries[-1]]
            own = join_slots(plan, slots[first : first + half], behind, 0 if hide else LONG)
            query, keys, values = project(plan, [own], *tables, True, hide)
            owns.append(own)
            queries.append(query)
            all_keys.append(keys)
            all_values.append(values)
        if plan.share == 1:
            others = [exchange(own, "loc", 1) for own in owns]
            keys, values = project(plan, others, *tables, False, hide, queries[-1:])
            all_keys.append(keys)
            all_values.append(values)
        else:
            step = CORES * plan.share
            same = [list(range(at, at + step)) for at in range(0, plan.locs, step)]
            every = lax.all_gather(owns[0], "loc", axis_index_groups=same, tiled=True)
            keys, values = project(plan, [every], *tables, False, hide)
            all_keys, all_values = [keys], [values]
        mid, done = attend(
            plan, queries, all_keys, all_values, owns, band_index, band_table, spatial_out, hide
        )
        behind = [done]
        mids.append(mid)
    same = [
        [g * plan.locs + r * CORES + core for r in range(plan.rows_count) for g in range(plan.groups)]
        for core in range(CORES)
    ]
    returned = []
    for mid in mids:
        parts = lax.all_to_all(
            mid.reshape(-1, plan.part_rows, plan.width),
            ("band", "loc"),
            0,
            0,
            axis_index_groups=same,
            tiled=True,
        )
        parts = parts.reshape(plan.band_dev, plan.share, plan.groups, plan.part_rows, plan.width)
        parts = parts.transpose(0, 2, 1, 3, 4).reshape(plan.band_dev, plan.groups, -1, plan.width)
        done = channel(plan, parts, channel_qkv, channel_out, up_weight, down_weight)
        returned.append([exchange(value, "band", step) for step, value in enumerate(done)])
    return restore(plan, location_key, returned)


def solution(mesh):
    placed = (P("loc", "band", None), P(), P(), P(), P(), P(), P(), P(), P(), P())
    return jax.shard_map(
        body, mesh=mesh, in_specs=placed, out_specs=P("loc", "band", None), check_vma=False
    )
```

```python
import functools

import jax
import jax.numpy as jnp
from jax import lax
from jax.experimental import pallas as pl
from jax.experimental.pallas import tpu as pltpu
from jax.sharding import PartitionSpec as P

HEADS = 12
HEAD_DIM = 64
WINDOWS = 2
CORES = 2
TILE_LOCS = 16
GROUP_LOCS = 8
UNIT_ROWS = 256
STEP_PAIRS = 3
ROW_TILE = 256
LANES = 128
QUERY_SCALE = HEAD_DIM ** (-0.5)
VMEM_LIMIT = 28 * 1024 * 1024
WIDE_LIMIT = 52 * 1024 * 1024
LONG = 2**36

F32 = jnp.float32
BF16 = jnp.bfloat16


def dot(left, right):
    return jnp.dot(left, right, preferred_element_type=F32)


def dot_t(left, right):
    return lax.dot_general(left, right, (((1,), (1,)), ((), ())), preferred_element_type=F32)


def norm_rows(values):
    centre = values - jnp.mean(values, axis=-1, keepdims=True)
    spread = jnp.mean(centre * centre, axis=-1, keepdims=True)
    return centre * lax.rsqrt(spread + 1e-05)


def gelu(values):
    inner = values * (0.7978845608028654 + 0.035677408136300125 * (values * values))
    return (0.5 * values) * (1.0 + jnp.tanh(inner))


def call(kernel, out_shape, flops, nbytes, limit=VMEM_LIMIT, **kwargs):
    return pl.pallas_call(
        kernel,
        out_shape=out_shape,
        compiler_params=pltpu.CompilerParams(vmem_limit_bytes=limit),
        cost_estimate=pl.CostEstimate(flops=flops, bytes_accessed=nbytes, transcendentals=0),
        **kwargs,
    )


def exchange(value, axis, step):
    if step == 0:
        return value
    return lax.ppermute(value, axis, [(i, i ^ step) for i in range(lax.axis_size(axis))])


class Plan:
    def __init__(self, tokens):
        self.loc_dev, self.band_dev, self.width = tokens.shape
        self.locs = lax.axis_size("loc")
        self.groups = lax.axis_size("band")
        self.rows_count = self.locs // CORES
        self.share = self.rows_count // self.band_dev
        assert self.share * self.band_dev * CORES == self.locs
        self.block = self.loc_dev // WINDOWS
        self.rows = self.block // self.share
        self.part_rows = self.rows // self.groups
        assert self.part_rows * self.groups * self.share * WINDOWS == self.loc_dev


def marker():
    return jax.ShapeDtypeStruct((8, LANES), F32)


def location_keys(plan, ids_ref):
    size = plan.loc_dev
    lines = size // LANES
    first = lax.axis_index("loc") * lines
    ids = jnp.concatenate([ids_ref[pl.ds(first + i, 1), :] for i in range(lines)], axis=1)
    ids = ids.astype(F32)
    row = jnp.broadcast_to(ids, (size, size))
    first = lax.broadcasted_iota(jnp.int32, (size, size), 0)
    second = lax.broadcasted_iota(jnp.int32, (size, size), 1)
    column = jnp.sum(jnp.where(first == second, row, 0.0), axis=1, keepdims=True)
    before = jnp.where((column == row) & (first < second), 1.0, 0.0)
    rank = jnp.sum(before, axis=0, keepdims=True)
    return ids * plan.block + rank


SMEM = pl.BlockSpec(memory_space=pltpu.SMEM)
VMEM = pl.BlockSpec(memory_space=pltpu.VMEM)
ANY = pl.BlockSpec(memory_space=pl.ANY)


def pick_rows(plan, window, place_keys, rows, outs):
    row = lax.axis_index("loc") // CORES
    place = lax.broadcasted_iota(jnp.int32, (plan.rows, rows.shape[0]), 0)
    for slot in range(plan.rows_count):
        peer = row ^ slot
        band, part = peer // plan.share, peer % plan.share
        wanted = place + (band * plan.loc_dev + window * plan.block + part * plan.rows)
        pick = jnp.where(wanted.astype(F32) == place_keys, 1.0, 0.0).astype(BF16)
        outs[slot][...] = dot(pick, rows[...]).astype(BF16)


def arrange_first(plan, tokens, ids):
    count = plan.rows_count
    total = plan.loc_dev * plan.band_dev
    assert plan.loc_dev <= 256

    def kernel(ids_ref, x_ref, *rest):
        outs, (rows_ref, keys_ref, place_ref) = rest[:count], rest[count:]
        keys = location_keys(plan, ids_ref)
        keys_ref[...] = keys
        place = lax.broadcasted_iota(jnp.int32, (plan.loc_dev, total), 1)
        location = lax.broadcasted_iota(jnp.int32, (plan.loc_dev, total), 0)
        spread = jnp.where(place // plan.band_dev == location, 1.0, 0.0).astype(BF16)
        wide = dot(jnp.broadcast_to(keys, (16, plan.loc_dev)).astype(BF16), spread)
        band = lax.broadcasted_iota(jnp.int32, (1, total), 1) % plan.band_dev
        place_ref[...] = wide[:1] + (band * plan.loc_dev).astype(F32)
        rows_ref[...] = x_ref[...].reshape(total, plan.width)
        pick_rows(plan, 0, place_ref[...], rows_ref, outs)

    return call(
        kernel,
        [jax.ShapeDtypeStruct((plan.rows, plan.width), BF16)] * count
        + [
            jax.ShapeDtypeStruct((total, plan.width), BF16),
            jax.ShapeDtypeStruct((1, plan.loc_dev), F32),
            jax.ShapeDtypeStruct((1, total), F32),
        ],
        2 * plan.loc_dev * tokens.size,
        4 * tokens.size,
        in_specs=[VMEM] * 2,
        out_specs=[VMEM] * (count + 3),
    )(ids, tokens)


def arrange_next(plan, window, rows, place_keys, after):
    count = plan.rows_count

    def kernel(rows_ref, place_ref, *rest):
        outs = rest[len(after) :]
        outs[-1][...] = jnp.zeros_like(outs[-1])
        pick_rows(plan, window, place_ref[...], rows_ref, outs[:-1])

    return call(
        kernel,
        [jax.ShapeDtypeStruct((plan.rows, plan.width), BF16)] * count + [marker()],
        2 * plan.loc_dev * rows.size,
        4 * rows.size,
        in_specs=[VMEM] * 2 + [ANY] * len(after),
        out_specs=[VMEM] * (count + 1),
    )(rows, place_keys, *after)


def join_slots(plan, slots, after, flops):
    count, rows = len(slots), plan.rows

    def kernel(*refs):
        out_ref, sems = refs[-2:]
        copies = [
            pltpu.make_async_copy(
                refs[slot], out_ref.at[pl.ds(slot * rows, rows), :], sems.at[slot]
            )
            for slot in range(count)
        ]
        for copy in copies:
            copy.start()
        for copy in copies:
            copy.wait()

    return call(
        kernel,
        jax.ShapeDtypeStruct((count * rows, plan.width), BF16),
        flops,
        0,
        in_specs=[ANY] * (count + len(after)),
        out_specs=VMEM,
        scratch_shapes=[pltpu.SemaphoreType.DMA((count,))],
    )(*slots, *after)


def embed_row(plan, index_ref, table_ref):
    band = lax.axis_index("loc") // (CORES * plan.share)
    number = index_ref[lax.axis_index("band") * plan.band_dev + band]
    return table_ref[pl.ds(number, 1), :]


def loop(count, step, unroll=1):
    lax.fori_loop(0, count, lambda i, _: (step(i), 0)[1], 0, unroll=unroll)


def aligned(index, size):
    return pl.ds(pl.multiple_of(index * size, size), size)


def norm_into(target, source):
    rows = source.shape[0]
    tile = rows // pl.cdiv(rows, ROW_TILE)
    for first in range(0, rows, tile):
        here = pl.ds(first, tile)
        target[here, :] = norm_rows(source[here, :]).astype(BF16)


def project(plan, tokens, index, table, weights, queries, hide, after=()):
    width = plan.width
    rows = sum(piece.shape[0] for piece in tokens)
    names = range(3) if queries else range(1, 3)

    def kernel(index_ref, table_ref, w_ref, *rest):
        x_refs, outs = rest[: len(tokens)], rest[len(tokens) + len(after) :]
        embed = embed_row(plan, index_ref, table_ref)
        at = 0
        for x_ref in x_refs:
            count = x_ref.shape[0]
            tile = min(count, ROW_TILE)
            for first in range(0, count, tile):
                normed = norm_rows(x_ref[pl.ds(first, tile), :].astype(F32) + embed).astype(BF16)
                here = pl.ds(at + first, tile)
                for ref, name in zip(outs, names):
                    value = dot(normed, w_ref[:, name * width : (name + 1) * width])
                    ref[here, :] = (value * QUERY_SCALE if name == 0 else value).astype(BF16)
            at += count

    return call(
        kernel,
        [jax.ShapeDtypeStruct((rows, width), BF16)] * len(names),
        hide * 2 * rows * width * len(names) * width,
        hide * 2 * ((1 + len(names)) * rows * width + 3 * width * width),
        in_specs=[SMEM, VMEM, VMEM] + [VMEM] * len(tokens) + [ANY] * len(after),
        out_specs=[VMEM] * len(names),
    )(index, table, weights, *tokens, *after)


def head_masks(rows):
    lane = lax.broadcasted_iota(jnp.int32, (rows, LANES), 1)
    return [(lane // HEAD_DIM) == head for head in range(LANES // HEAD_DIM)]


def stack_heads(query):
    return jnp.concatenate(
        [jnp.where(inside, query, jnp.zeros_like(query)) for inside in head_masks(query.shape[0])],
        axis=0,
    )


def join_heads(stacked):
    heads = LANES // HEAD_DIM
    rows = stacked.shape[0] // heads
    joined = stacked[:rows]
    for head, inside in list(enumerate(head_masks(rows)))[1:]:
        joined = jnp.where(inside, stacked[head * rows : (head + 1) * rows], joined)
    return joined


def with_ones(value):
    return jnp.concatenate([value, jnp.ones(value.shape, BF16)], axis=1)


def run_units(units, mask=None):
    def scores_of(unit):
        query, keys, _ = unit
        scores = [dot_t(query, piece) for piece in keys]
        if mask is not None:
            scores = [jnp.where(mask, piece, -1e30) for piece in scores]
        return scores

    results = []
    ahead = scores_of(units[0])
    for number, (_, _, values) in enumerate(units):
        scores = ahead
        if number + 1 < len(units):
            ahead = scores_of(units[number + 1])
        peak = functools.reduce(
            jnp.maximum, [jnp.max(piece, axis=-1, keepdims=True) for piece in scores]
        )
        total = None
        for piece, value in zip(scores, values):
            part = dot(jnp.exp(piece - peak).astype(BF16), value)
            total = part if total is None else total + part
        results.append(
            (join_heads(total[:, :LANES]) / join_heads(total[:, LANES:])).astype(BF16)
        )
    return results


def attend(plan, query, keys, values, tokens, index, table, spatial_out, hide):
    width, rows = plan.width, plan.rows
    pieces, sources = len(keys), len(query)
    counts = [piece.shape[0] for piece in query]
    total = sum(counts)
    pairs = width // LANES

    def kernel(index_ref, table_ref, w_ref, *rest):
        x_refs, rest = rest[:sources], rest[sources:]
        q_refs, rest = rest[:sources], rest[sources:]
        k_refs, rest = rest[:pieces], rest[pieces:]
        v_refs, (out_ref, marker_ref, result, added) = rest[:pieces], rest[pieces:]
        marker_ref[...] = jnp.zeros_like(marker_ref)

        def step(number):
            units, places = [], []
            for i in range(STEP_PAIRS):
                here = aligned(number * STEP_PAIRS + i, LANES)
                pair_keys = [ref[:, here] for ref in k_refs]
                pair_values = [with_ones(ref[:, here]) for ref in v_refs]
                at = 0
                for ref, count in zip(q_refs, counts):
                    unit = min(count, UNIT_ROWS)
                    for first in range(0, count, unit):
                        query_rows = ref[pl.ds(first, unit), here]
                        units.append((stack_heads(query_rows), pair_keys, pair_values))
                        places.append((pl.ds(at + first, unit), here))
                    at += count
            for place, done in zip(places, run_units(units)):
                result[place] = done

        loop(pairs // STEP_PAIRS, step)
        added[...] = dot(result[...], w_ref[...])
        embed = embed_row(plan, index_ref, table_ref)
        row = lax.axis_index("loc") // CORES
        slot = 0
        for ref, count in zip(x_refs, counts):
            for first in range(0, count, rows):
                start = ref[pl.ds(first, rows), :].astype(F32) + embed
                mid = (start + added[pl.ds(slot * rows, rows), :]).astype(BF16)
                for owner in range(plan.groups):
                    part = mid[owner * plan.part_rows : (owner + 1) * plan.part_rows]
                    out_ref[row ^ slot, owner] = part
                slot += 1

    key_rows = sum(piece.shape[0] for piece in keys)
    return call(
        kernel,
        [
            jax.ShapeDtypeStruct((plan.rows_count, plan.groups, plan.part_rows, width), BF16),
            marker(),
        ],
        hide * 16 * total * key_rows * width,
        hide * 2 * width * (2 * key_rows + 3 * total + width),
        in_specs=[SMEM] + [VMEM] * (2 + 2 * sources + 2 * pieces),
        out_specs=[VMEM] * 2,
        scratch_shapes=[pltpu.VMEM((total, width), BF16), pltpu.VMEM((total, width), F32)],
    )(index, table, spatial_out, *tokens, *query, *keys, *values)


def piece_places(owners, bands, locations):
    stride = len(owners) * bands * GROUP_LOCS
    places = {}
    for position, owner in enumerate(owners):
        for band in range(bands):
            for first in range(0, locations, TILE_LOCS):
                places[owner, band, first] = [
                    pl.ds(at // GROUP_LOCS * stride + (position * bands + band) * GROUP_LOCS, GROUP_LOCS)
                    for at in range(first, first + TILE_LOCS, GROUP_LOCS)
                ]
    return places


def mlp_into(mid, normed, up_ref, down_ref, waits=()):
    rows, width = mid.shape
    row_tile = rows // pl.cdiv(rows, ROW_TILE)
    tiles = [pl.ds(first, row_tile) for first in range(0, rows, row_tile)]
    norm_into(normed, mid)

    def step(here):
        raised = [dot(normed[mine, :], up_ref[:, here]) for mine in tiles]
        for mine, value in zip(tiles, raised):
            mid[mine, :] += dot(gelu(value).astype(BF16), down_ref[here, :])

    blocks = up_ref.shape[1] // width
    if waits:
        for block in range(blocks):
            waits[block]()
            step(pl.ds(block * width, width))
    else:
        loop(blocks, lambda block: step(aligned(block, width)))


def write_pieces(mid, outs, owners, bands, locations):
    for (owner, band, first), places in piece_places(owners, bands, locations).items():
        piece = jnp.concatenate([mid[place, :] for place in places], axis=0)
        outs[owners.index(owner)][band, first : first + TILE_LOCS, :] = piece.astype(BF16)


def finish(plan, rest, owners, bands, up_weight, down_weight):
    rows, width = rest.shape
    locations = rows // (len(owners) * bands)
    blocks = up_weight.shape[1] // width

    def kernel(up_hbm, down_hbm, rest_ref, *refs):
        outs, refs = refs[: len(owners)], refs[len(owners) :]
        mid, normed, up_ref, down_ref, sems = refs
        pairs = []
        for block in range(blocks):
            here = pl.ds(block * width, width)
            pairs.append(
                [
                    pltpu.make_async_copy(
                        up_hbm.at[:, here], up_ref.at[:, here], sems.at[2 * block]
                    ),
                    pltpu.make_async_copy(
                        down_hbm.at[here, :], down_ref.at[here, :], sems.at[2 * block + 1]
                    ),
                ]
            )

        def start(block):
            for copy in pairs[block]:
                copy.start()

        def wait(block):
            for copy in pairs[block]:
                copy.wait()
            if block + 2 < blocks:
                start(block + 2)

        for block in range(min(2, blocks)):
            start(block)
        mid[...] = rest_ref[...]
        waits = [functools.partial(wait, block) for block in range(blocks)]
        mlp_into(mid, normed, up_ref, down_ref, waits)
        write_pieces(mid, outs, owners, bands, locations)

    return call(
        kernel,
        [jax.ShapeDtypeStruct((bands, locations, width), BF16)] * len(owners),
        4 * rows * up_weight.size,
        2 * 2 * up_weight.size,
        limit=WIDE_LIMIT,
        in_specs=[ANY] * 2 + [VMEM],
        out_specs=[VMEM] * len(owners),
        scratch_shapes=[
            pltpu.VMEM((rows, width), F32),
            pltpu.VMEM((rows, width), BF16),
            pltpu.VMEM(up_weight.shape, BF16),
            pltpu.VMEM(down_weight.shape, BF16),
            pltpu.SemaphoreType.DMA((2 * blocks,)),
        ],
    )(up_weight, down_weight, rest)


def channel(plan, parts, now, later, channel_qkv, channel_out, up_weight, down_weight):
    groups, width = plan.groups, plan.width
    bands, _, locations, _ = parts.shape
    small = GROUP_LOCS
    assert locations % TILE_LOCS == 0
    owners = [*now, *later]
    group_rows = groups * bands * small
    rows = groups * bands * locations
    now_rows = rows * len(now) // groups
    count = len(now) + (len(later) > 0)

    def kernel(qkv_hbm, out_hbm, up_hbm, down_hbm, *refs):
        in_ref, *refs = refs
        outs, refs = refs[:count], refs[count:]
        mid, normed, packed, attended, qkv_ref, out_ref, up_ref, down_ref, sems = refs
        me = lax.axis_index("band")
        columns = [pl.ds(first, width) for first in range(0, 3 * width, width)]
        copies = []
        for source, target, spots in (
            (qkv_hbm, qkv_ref, [(slice(None), spot) for spot in columns]),
            (out_hbm, out_ref, [(slice(None), slice(None))]),
            (up_hbm, up_ref, [(slice(None), slice(None))]),
            (down_hbm, down_ref, [(slice(None), slice(None))]),
        ):
            for spot in spots:
                copies.append(
                    pltpu.make_async_copy(
                        source.at[spot], target.at[spot], sems.at[len(copies)]
                    )
                )
        for copy in copies[: len(columns)]:
            copy.start()
        for (owner, band, first), places in piece_places(owners, bands, locations).items():
            piece = in_ref[band, me ^ owner, first : first + TILE_LOCS, :].astype(F32)
            for number, place in enumerate(places):
                mid[place, :] = piece[number * small : (number + 1) * small]
        norm_into(normed, mid)

        for number, here in enumerate(columns):
            copies[number].wait()
            copies[number + len(columns)].start()
            factor = QUERY_SCALE if number == 0 else 1.0
            packed[:, here] = (dot(normed[...], qkv_ref[:, here]) * factor).astype(BF16)
        pairs = width // LANES
        stacked = group_rows * (LANES // HEAD_DIM)
        one = lax.broadcasted_iota(jnp.int32, (stacked, group_rows), 0)
        other = lax.broadcasted_iota(jnp.int32, (stacked, group_rows), 1)
        mask = (one % small) == (other % small)

        def attention_step(pair):
            units, spots = [], []
            for first in range(0, rows, group_rows):
                mine = pl.ds(first, group_rows)
                query = packed[mine, aligned(pair, LANES)]
                keys = packed[mine, aligned(pair + pairs, LANES)]
                values = packed[mine, aligned(pair + 2 * pairs, LANES)]
                units.append((stack_heads(query), [keys], [with_ones(values)]))
                spots.append((mine, aligned(pair, LANES)))
            for spot, done in zip(spots, run_units(units, mask)):
                attended[spot] = done

        loop(pairs, attention_step, unroll=3)
        copies[3].wait()
        mid[...] += dot(attended[...], out_ref[...])
        copies[4].wait()
        copies[5].wait()
        if later:
            head = len(now) * bands * small
            tail = group_rows - head
            for group in range(rows // group_rows):
                at = group * group_rows
                outs[-1][pl.ds(group * tail, tail), :] = mid[pl.ds(at + head, tail), :]
                if group > 0:
                    mid[pl.ds(group * head, head), :] = mid[pl.ds(at, head), :]
        mine = pl.ds(0, now_rows)
        mlp_into(mid.at[mine, :], normed.at[mine, :], up_ref, down_ref)
        write_pieces(mid, outs, now, bands, locations)

    weights = [channel_qkv, channel_out, up_weight, down_weight]
    size = sum(weight.size for weight in weights)
    return call(
        kernel,
        [jax.ShapeDtypeStruct((bands, locations, width), BF16)] * len(now)
        + [jax.ShapeDtypeStruct((rows - now_rows, width), F32)] * (count - len(now)),
        2 * rows * size,
        2 * (2 * rows * width + size),
        limit=WIDE_LIMIT,
        in_specs=[ANY] * 4 + [VMEM],
        out_specs=[VMEM] * count,
        scratch_shapes=[
            pltpu.VMEM((rows, width), F32),
            pltpu.VMEM((rows, width), BF16),
            pltpu.VMEM((rows, 3 * width), BF16),
            pltpu.VMEM((rows, width), BF16),
        ]
        + [pltpu.VMEM(weight.shape, BF16) for weight in weights]
        + [pltpu.SemaphoreType.DMA((6,))],
    )(*weights, parts)


def restore(plan, keys, returned):
    def kernel(keys_ref, *refs):
        ins, out_ref = refs[:-1], refs[-1]
        group = lax.axis_index("band")
        place = lax.broadcasted_iota(jnp.int32, (plan.loc_dev, plan.loc_dev), 0)
        inner = place % plan.part_rows
        part = (place // plan.part_rows) % plan.share
        owner = (place // (plan.part_rows * plan.share)) % plan.groups ^ group
        window = place // plan.block
        wanted = window * plan.block + part * plan.rows + owner * plan.part_rows + inner
        pick = jnp.where(wanted.astype(F32) == keys_ref[...], 1.0, 0.0).astype(BF16)
        for band in range(plan.band_dev):
            rows = jnp.concatenate([ref[band] for ref in ins], axis=0)
            out_ref[:, band, :] = lax.dot_general(
                pick, rows, (((0,), (0,)), ((), ())), preferred_element_type=F32
            ).astype(BF16)

    arrays = [array for chunk in returned for array in chunk]
    size = plan.loc_dev * plan.band_dev * plan.width
    return call(
        kernel,
        jax.ShapeDtypeStruct((plan.loc_dev, plan.band_dev, plan.width), BF16),
        2 * plan.loc_dev * size,
        4 * size,
    )(keys, *arrays)


def body(
    tokens,
    band_index,
    band_table,
    window_ids,
    spatial_qkv,
    spatial_out,
    channel_qkv,
    channel_out,
    up_weight,
    down_weight,
):
    plan = Plan(tokens)
    ids = window_ids.reshape(-1, LANES)
    *sent, rows, location_key, place_keys = arrange_first(plan, tokens, ids)
    arrived = [[exchange(value, "loc", CORES * step) for step, value in enumerate(sent)]]
    arranged = None
    for window in range(1, WINDOWS):
        *sent, arranged = arrange_next(plan, window, rows, place_keys, arrived[0][1:2])
        arrived.append([exchange(value, "loc", CORES * step) for step, value in enumerate(sent)])
    mids, behind = [], []
    for window, slots in enumerate(arrived):
        hide = int(window == 0)
        half = len(slots) // 2 if hide and plan.share == 1 else len(slots)
        owns, queries, all_keys, all_values = [], [], [], []
        tables = (band_index, band_table, spatial_qkv)
        for first in range(0, len(slots), half):
            if first > 0:
                behind = [arranged, queries[-1]]
            own = join_slots(plan, slots[first : first + half], behind, 0 if hide else LONG)
            query, keys, values = project(plan, [own], *tables, True, hide)
            owns.append(own)
            queries.append(query)
            all_keys.append(keys)
            all_values.append(values)
        if plan.share == 1:
            others = [exchange(own, "loc", 1) for own in owns]
            keys, values = project(plan, others, *tables, False, hide, queries[-1:])
            all_keys.append(keys)
            all_values.append(values)
        else:
            step = CORES * plan.share
            same = [list(range(at, at + step)) for at in range(0, plan.locs, step)]
            every = lax.all_gather(owns[0], "loc", axis_index_groups=same, tiled=True)
            keys, values = project(plan, [every], *tables, False, hide)
            all_keys, all_values = [keys], [values]
        mid, done = attend(
            plan, queries, all_keys, all_values, owns, band_index, band_table, spatial_out, hide
        )
        behind = [done]
        mids.append(mid)
    same = [
        [g * plan.locs + r * CORES + core for r in range(plan.rows_count) for g in range(plan.groups)]
        for core in range(CORES)
    ]
    returned = []
    for mid in mids:
        parts = lax.all_to_all(
            mid.reshape(-1, plan.part_rows, plan.width),
            ("band", "loc"),
            0,
            0,
            axis_index_groups=same,
            tiled=True,
        )
        parts = parts.reshape(plan.band_dev, plan.share, plan.groups, plan.part_rows, plan.width)
        parts = parts.transpose(0, 2, 1, 3, 4).reshape(plan.band_dev, plan.groups, -1, plan.width)
        weights = (channel_qkv, channel_out, up_weight, down_weight)
        now, later = list(range(plan.groups)), []
        if mid is mids[-1] and plan.groups > 1:
            now, later = now[1:], now[:1]
        done = channel(plan, parts, now, later, *weights)
        if later:
            *done, rest = done
            done += finish(plan, rest, later, plan.band_dev, up_weight, down_weight)
        done = dict(zip([*now, *later], done))
        returned.append([exchange(done[step], "band", step) for step in range(plan.groups)])
    return restore(plan, location_key, returned)


def solution(mesh):
    placed = (P("loc", "band", None), P(), P(), P(), P(), P(), P(), P(), P(), P())
    return jax.shard_map(
        body, mesh=mesh, in_specs=placed, out_specs=P("loc", "band", None), check_vma=False
    )
```

```python
import functools

import jax
import jax.numpy as jnp
from jax import lax
from jax.experimental import pallas as pl
from jax.experimental.pallas import tpu as pltpu
from jax.sharding import PartitionSpec as P

HEADS = 12
HEAD_DIM = 64
WINDOWS = 2
CORES = 2
TILE_LOCS = 16
GROUP_LOCS = 8
UNIT_ROWS = 256
STEP_PAIRS = 3
ROW_TILE = 256
LANES = 128
QUERY_SCALE = HEAD_DIM ** (-0.5)
VMEM_LIMIT = 28 * 1024 * 1024
WIDE_LIMIT = 52 * 1024 * 1024
LONG = 2**36

F32 = jnp.float32
BF16 = jnp.bfloat16


def dot(left, right):
    return jnp.dot(left, right, preferred_element_type=F32)


def dot_t(left, right):
    return lax.dot_general(left, right, (((1,), (1,)), ((), ())), preferred_element_type=F32)


def norm_rows(values):
    centre = values - jnp.mean(values, axis=-1, keepdims=True)
    spread = jnp.mean(centre * centre, axis=-1, keepdims=True)
    return centre * lax.rsqrt(spread + 1e-05)


def gelu(values):
    inner = values * (0.7978845608028654 + 0.035677408136300125 * (values * values))
    return (0.5 * values) * (1.0 + jnp.tanh(inner))


def call(kernel, out_shape, flops, nbytes, limit=VMEM_LIMIT, **kwargs):
    return pl.pallas_call(
        kernel,
        out_shape=out_shape,
        compiler_params=pltpu.CompilerParams(vmem_limit_bytes=limit),
        cost_estimate=pl.CostEstimate(flops=flops, bytes_accessed=nbytes, transcendentals=0),
        **kwargs,
    )


def exchange(value, axis, step):
    if step == 0:
        return value
    return lax.ppermute(value, axis, [(i, i ^ step) for i in range(lax.axis_size(axis))])


class Plan:
    def __init__(self, tokens):
        self.loc_dev, self.band_dev, self.width = tokens.shape
        self.locs = lax.axis_size("loc")
        self.groups = lax.axis_size("band")
        self.rows_count = self.locs // CORES
        self.share = self.rows_count // self.band_dev
        assert self.share * self.band_dev * CORES == self.locs
        self.block = self.loc_dev // WINDOWS
        self.rows = self.block // self.share
        self.part_rows = self.rows // self.groups
        assert self.part_rows * self.groups * self.share * WINDOWS == self.loc_dev


def marker():
    return jax.ShapeDtypeStruct((8, LANES), F32)


def location_keys(plan, ids_ref):
    size = plan.loc_dev
    lines = size // LANES
    first = lax.axis_index("loc") * lines
    ids = jnp.concatenate([ids_ref[pl.ds(first + i, 1), :] for i in range(lines)], axis=1)
    ids = ids.astype(F32)
    row = jnp.broadcast_to(ids, (size, size))
    first = lax.broadcasted_iota(jnp.int32, (size, size), 0)
    second = lax.broadcasted_iota(jnp.int32, (size, size), 1)
    column = jnp.sum(jnp.where(first == second, row, 0.0), axis=1, keepdims=True)
    before = jnp.where((column == row) & (first < second), 1.0, 0.0)
    rank = jnp.sum(before, axis=0, keepdims=True)
    return ids * plan.block + rank


SMEM = pl.BlockSpec(memory_space=pltpu.SMEM)
VMEM = pl.BlockSpec(memory_space=pltpu.VMEM)
ANY = pl.BlockSpec(memory_space=pl.ANY)


def pick_rows(plan, window, place_keys, rows, outs):
    row = lax.axis_index("loc") // CORES
    place = lax.broadcasted_iota(jnp.int32, (plan.rows, rows.shape[0]), 0)
    for slot in range(plan.rows_count):
        peer = row ^ slot
        band, part = peer // plan.share, peer % plan.share
        wanted = place + (band * plan.loc_dev + window * plan.block + part * plan.rows)
        pick = jnp.where(wanted.astype(F32) == place_keys, 1.0, 0.0).astype(BF16)
        outs[slot][...] = dot(pick, rows[...]).astype(BF16)


def arrange_first(plan, tokens, ids):
    count = plan.rows_count
    total = plan.loc_dev * plan.band_dev
    assert plan.loc_dev <= 256

    def kernel(ids_ref, x_ref, *rest):
        outs, (rows_ref, keys_ref, place_ref) = rest[:count], rest[count:]
        keys = location_keys(plan, ids_ref)
        keys_ref[...] = keys
        place = lax.broadcasted_iota(jnp.int32, (plan.loc_dev, total), 1)
        location = lax.broadcasted_iota(jnp.int32, (plan.loc_dev, total), 0)
        spread = jnp.where(place // plan.band_dev == location, 1.0, 0.0).astype(BF16)
        wide = dot(jnp.broadcast_to(keys, (16, plan.loc_dev)).astype(BF16), spread)
        band = lax.broadcasted_iota(jnp.int32, (1, total), 1) % plan.band_dev
        place_ref[...] = wide[:1] + (band * plan.loc_dev).astype(F32)
        rows_ref[...] = x_ref[...].reshape(total, plan.width)
        pick_rows(plan, 0, place_ref[...], rows_ref, outs)

    return call(
        kernel,
        [jax.ShapeDtypeStruct((plan.rows, plan.width), BF16)] * count
        + [
            jax.ShapeDtypeStruct((total, plan.width), BF16),
            jax.ShapeDtypeStruct((1, plan.loc_dev), F32),
            jax.ShapeDtypeStruct((1, total), F32),
        ],
        2 * plan.loc_dev * tokens.size,
        4 * tokens.size,
        in_specs=[VMEM] * 2,
        out_specs=[VMEM] * (count + 3),
    )(ids, tokens)


def arrange_next(plan, window, rows, place_keys, after):
    count = plan.rows_count

    def kernel(rows_ref, place_ref, *rest):
        outs = rest[len(after) :]
        outs[-1][...] = jnp.zeros_like(outs[-1])
        pick_rows(plan, window, place_ref[...], rows_ref, outs[:-1])

    return call(
        kernel,
        [jax.ShapeDtypeStruct((plan.rows, plan.width), BF16)] * count + [marker()],
        2 * plan.loc_dev * rows.size,
        0,
        in_specs=[VMEM] * 2 + [ANY] * len(after),
        out_specs=[VMEM] * (count + 1),
    )(rows, place_keys, *after)


def join_slots(plan, slots, after, flops):
    count, rows = len(slots), plan.rows

    def kernel(*refs):
        out_ref, sems = refs[-2:]
        copies = [
            pltpu.make_async_copy(
                refs[slot], out_ref.at[pl.ds(slot * rows, rows), :], sems.at[slot]
            )
            for slot in range(count)
        ]
        for copy in copies:
            copy.start()
        for copy in copies:
            copy.wait()

    return call(
        kernel,
        jax.ShapeDtypeStruct((count * rows, plan.width), BF16),
        flops,
        0,
        in_specs=[ANY] * (count + len(after)),
        out_specs=VMEM,
        scratch_shapes=[pltpu.SemaphoreType.DMA((count,))],
    )(*slots, *after)


def embed_row(plan, index_ref, table_ref):
    band = lax.axis_index("loc") // (CORES * plan.share)
    number = index_ref[lax.axis_index("band") * plan.band_dev + band]
    return table_ref[pl.ds(number, 1), :]


def loop(count, step, unroll=1):
    lax.fori_loop(0, count, lambda i, _: (step(i), 0)[1], 0, unroll=unroll)


def aligned(index, size):
    return pl.ds(pl.multiple_of(index * size, size), size)


def norm_into(target, source):
    rows = source.shape[0]
    tile = rows // pl.cdiv(rows, ROW_TILE)
    for first in range(0, rows, tile):
        here = pl.ds(first, tile)
        target[here, :] = norm_rows(source[here, :]).astype(BF16)


def project(plan, tokens, index, table, weights, queries, hide, after=()):
    width = plan.width
    rows = sum(piece.shape[0] for piece in tokens)
    names = range(3) if queries else range(1, 3)

    def kernel(index_ref, table_ref, w_ref, *rest):
        x_refs, outs = rest[: len(tokens)], rest[len(tokens) + len(after) :]
        embed = embed_row(plan, index_ref, table_ref)
        at = 0
        for x_ref in x_refs:
            count = x_ref.shape[0]
            tile = min(count, ROW_TILE)
            for first in range(0, count, tile):
                normed = norm_rows(x_ref[pl.ds(first, tile), :].astype(F32) + embed).astype(BF16)
                here = pl.ds(at + first, tile)
                for ref, name in zip(outs, names):
                    value = dot(normed, w_ref[:, name * width : (name + 1) * width])
                    ref[here, :] = (value * QUERY_SCALE if name == 0 else value).astype(BF16)
            at += count

    return call(
        kernel,
        [jax.ShapeDtypeStruct((rows, width), BF16)] * len(names),
        hide * 2 * rows * width * len(names) * width,
        hide * 2 * ((1 + len(names)) * rows * width + 3 * width * width),
        in_specs=[SMEM, VMEM, VMEM] + [VMEM] * len(tokens) + [ANY] * len(after),
        out_specs=[VMEM] * len(names),
    )(index, table, weights, *tokens, *after)


def head_masks(rows):
    lane = lax.broadcasted_iota(jnp.int32, (rows, LANES), 1)
    return [(lane // HEAD_DIM) == head for head in range(LANES // HEAD_DIM)]


def stack_heads(query):
    return jnp.concatenate(
        [jnp.where(inside, query, jnp.zeros_like(query)) for inside in head_masks(query.shape[0])],
        axis=0,
    )


def join_heads(stacked):
    heads = LANES // HEAD_DIM
    rows = stacked.shape[0] // heads
    joined = stacked[:rows]
    for head, inside in list(enumerate(head_masks(rows)))[1:]:
        joined = jnp.where(inside, stacked[head * rows : (head + 1) * rows], joined)
    return joined


def with_ones(value):
    return jnp.concatenate([value, jnp.ones(value.shape, BF16)], axis=1)


def run_units(units, mask=None):
    def scores_of(unit):
        query, keys, _ = unit
        scores = [dot_t(query, piece) for piece in keys]
        if mask is not None:
            scores = [jnp.where(mask, piece, -1e30) for piece in scores]
        return scores

    results = []
    ahead = scores_of(units[0])
    for number, (_, _, values) in enumerate(units):
        scores = ahead
        if number + 1 < len(units):
            ahead = scores_of(units[number + 1])
        peak = functools.reduce(
            jnp.maximum, [jnp.max(piece, axis=-1, keepdims=True) for piece in scores]
        )
        total = None
        for piece, value in zip(scores, values):
            part = dot(jnp.exp(piece - peak).astype(BF16), value)
            total = part if total is None else total + part
        results.append(
            (join_heads(total[:, :LANES]) / join_heads(total[:, LANES:])).astype(BF16)
        )
    return results


def attend(plan, query, keys, values, tokens, index, table, spatial_out, hide):
    width, rows = plan.width, plan.rows
    pieces, sources = len(keys), len(query)
    counts = [piece.shape[0] for piece in query]
    total = sum(counts)
    pairs = width // LANES

    def kernel(index_ref, table_ref, w_ref, *rest):
        x_refs, rest = rest[:sources], rest[sources:]
        q_refs, rest = rest[:sources], rest[sources:]
        k_refs, rest = rest[:pieces], rest[pieces:]
        v_refs, (out_ref, marker_ref, result, added) = rest[:pieces], rest[pieces:]
        marker_ref[...] = jnp.zeros_like(marker_ref)

        def step(number):
            units, places = [], []
            for i in range(STEP_PAIRS):
                here = aligned(number * STEP_PAIRS + i, LANES)
                pair_keys = [ref[:, here] for ref in k_refs]
                pair_values = [with_ones(ref[:, here]) for ref in v_refs]
                at = 0
                for ref, count in zip(q_refs, counts):
                    unit = min(count, UNIT_ROWS)
                    for first in range(0, count, unit):
                        query_rows = ref[pl.ds(first, unit), here]
                        units.append((stack_heads(query_rows), pair_keys, pair_values))
                        places.append((pl.ds(at + first, unit), here))
                    at += count
            for place, done in zip(places, run_units(units)):
                result[place] = done

        loop(pairs // STEP_PAIRS, step)
        added[...] = dot(result[...], w_ref[...])
        embed = embed_row(plan, index_ref, table_ref)
        row = lax.axis_index("loc") // CORES
        slot = 0
        for ref, count in zip(x_refs, counts):
            for first in range(0, count, rows):
                start = ref[pl.ds(first, rows), :].astype(F32) + embed
                mid = (start + added[pl.ds(slot * rows, rows), :]).astype(BF16)
                for owner in range(plan.groups):
                    part = mid[owner * plan.part_rows : (owner + 1) * plan.part_rows]
                    out_ref[row ^ slot, owner] = part
                slot += 1

    key_rows = sum(piece.shape[0] for piece in keys)
    return call(
        kernel,
        [
            jax.ShapeDtypeStruct((plan.rows_count, plan.groups, plan.part_rows, width), BF16),
            marker(),
        ],
        hide * 16 * total * key_rows * width,
        0,
        in_specs=[SMEM] + [VMEM] * (2 + 2 * sources + 2 * pieces),
        out_specs=[VMEM] * 2,
        scratch_shapes=[pltpu.VMEM((total, width), BF16), pltpu.VMEM((total, width), F32)],
    )(index, table, spatial_out, *tokens, *query, *keys, *values)


def piece_places(owners, bands, locations):
    stride = len(owners) * bands * GROUP_LOCS
    places = {}
    for position, owner in enumerate(owners):
        for band in range(bands):
            for first in range(0, locations, TILE_LOCS):
                places[owner, band, first] = [
                    pl.ds(at // GROUP_LOCS * stride + (position * bands + band) * GROUP_LOCS, GROUP_LOCS)
                    for at in range(first, first + TILE_LOCS, GROUP_LOCS)
                ]
    return places


def mlp_into(mid, normed, up_ref, down_ref, waits=()):
    rows, width = mid.shape
    row_tile = rows // pl.cdiv(rows, ROW_TILE)
    tiles = [pl.ds(first, row_tile) for first in range(0, rows, row_tile)]
    norm_into(normed, mid)

    def step(here):
        raised = [dot(normed[mine, :], up_ref[:, here]) for mine in tiles]
        for mine, value in zip(tiles, raised):
            mid[mine, :] += dot(gelu(value).astype(BF16), down_ref[here, :])

    blocks = up_ref.shape[1] // width
    if waits:
        for block in range(blocks):
            waits[block]()
            step(pl.ds(block * width, width))
    else:
        loop(blocks, lambda block: step(aligned(block, width)))


def write_pieces(mid, outs, owners, bands, locations):
    for (owner, band, first), places in piece_places(owners, bands, locations).items():
        piece = jnp.concatenate([mid[place, :] for place in places], axis=0)
        outs[owners.index(owner)][band, first : first + TILE_LOCS, :] = piece.astype(BF16)


def finish(plan, rest, owners, bands, up_weight, down_weight):
    rows, width = rest.shape
    locations = rows // (len(owners) * bands)
    blocks = up_weight.shape[1] // width

    def kernel(up_hbm, down_hbm, rest_ref, *refs):
        outs, refs = refs[: len(owners)], refs[len(owners) :]
        mid, normed, up_ref, down_ref, sems = refs
        pairs = []
        for block in range(blocks):
            here = pl.ds(block * width, width)
            pairs.append(
                [
                    pltpu.make_async_copy(
                        up_hbm.at[:, here], up_ref.at[:, here], sems.at[2 * block]
                    ),
                    pltpu.make_async_copy(
                        down_hbm.at[here, :], down_ref.at[here, :], sems.at[2 * block + 1]
                    ),
                ]
            )

        def start(block):
            for copy in pairs[block]:
                copy.start()

        def wait(block):
            for copy in pairs[block]:
                copy.wait()
            if block + 2 < blocks:
                start(block + 2)

        for block in range(min(2, blocks)):
            start(block)
        mid[...] = rest_ref[...]
        waits = [functools.partial(wait, block) for block in range(blocks)]
        mlp_into(mid, normed, up_ref, down_ref, waits)
        write_pieces(mid, outs, owners, bands, locations)

    return call(
        kernel,
        [jax.ShapeDtypeStruct((bands, locations, width), BF16)] * len(owners),
        4 * rows * up_weight.size,
        2 * 2 * up_weight.size,
        limit=WIDE_LIMIT,
        in_specs=[ANY] * 2 + [VMEM],
        out_specs=[VMEM] * len(owners),
        scratch_shapes=[
            pltpu.VMEM((rows, width), F32),
            pltpu.VMEM((rows, width), BF16),
            pltpu.VMEM(up_weight.shape, BF16),
            pltpu.VMEM(down_weight.shape, BF16),
            pltpu.SemaphoreType.DMA((2 * blocks,)),
        ],
    )(up_weight, down_weight, rest)


def channel(plan, parts, now, later, fetch, channel_qkv, channel_out, up_weight, down_weight):
    groups, width = plan.groups, plan.width
    bands, _, locations, _ = parts.shape
    small = GROUP_LOCS
    assert locations % TILE_LOCS == 0
    owners = [*now, *later]
    group_rows = groups * bands * small
    rows = groups * bands * locations
    now_rows = rows * len(now) // groups
    count = len(now) + (len(later) > 0)

    def kernel(qkv_hbm, out_hbm, up_hbm, down_hbm, *refs):
        in_ref, *refs = refs
        outs, refs = refs[:count], refs[count:]
        mid, normed, packed, attended, qkv_ref, out_ref, up_ref, down_ref, sems, *held = refs
        if held:
            load = pltpu.make_async_copy(in_ref, held[0], sems.at[6])
            load.start()
            in_ref = held[0]
        me = lax.axis_index("band")
        columns = [pl.ds(first, width) for first in range(0, 3 * width, width)]
        copies = []
        for source, target, spots in (
            (qkv_hbm, qkv_ref, [(slice(None), spot) for spot in columns]),
            (out_hbm, out_ref, [(slice(None), slice(None))]),
            (up_hbm, up_ref, [(slice(None), slice(None))]),
            (down_hbm, down_ref, [(slice(None), slice(None))]),
        ):
            for spot in spots:
                copies.append(
                    pltpu.make_async_copy(
                        source.at[spot], target.at[spot], sems.at[len(copies)]
                    )
                )
        for copy in copies[: len(columns)]:
            copy.start()
        if held:
            load.wait()
        for (owner, band, first), places in piece_places(owners, bands, locations).items():
            piece = in_ref[band, me ^ owner, first : first + TILE_LOCS, :].astype(F32)
            for number, place in enumerate(places):
                mid[place, :] = piece[number * small : (number + 1) * small]
        norm_into(normed, mid)

        for number, here in enumerate(columns):
            copies[number].wait()
            copies[number + len(columns)].start()
            factor = QUERY_SCALE if number == 0 else 1.0
            packed[:, here] = (dot(normed[...], qkv_ref[:, here]) * factor).astype(BF16)
        pairs = width // LANES
        stacked = group_rows * (LANES // HEAD_DIM)
        one = lax.broadcasted_iota(jnp.int32, (stacked, group_rows), 0)
        other = lax.broadcasted_iota(jnp.int32, (stacked, group_rows), 1)
        mask = (one % small) == (other % small)

        def attention_step(pair):
            units, spots = [], []
            for first in range(0, rows, group_rows):
                mine = pl.ds(first, group_rows)
                query = packed[mine, aligned(pair, LANES)]
                keys = packed[mine, aligned(pair + pairs, LANES)]
                values = packed[mine, aligned(pair + 2 * pairs, LANES)]
                units.append((stack_heads(query), [keys], [with_ones(values)]))
                spots.append((mine, aligned(pair, LANES)))
            for spot, done in zip(spots, run_units(units, mask)):
                attended[spot] = done

        loop(pairs, attention_step, unroll=3)
        copies[3].wait()
        mid[...] += dot(attended[...], out_ref[...])
        copies[4].wait()
        copies[5].wait()
        if later:
            head = len(now) * bands * small
            tail = group_rows - head
            for group in range(rows // group_rows):
                at = group * group_rows
                outs[-1][pl.ds(group * tail, tail), :] = mid[pl.ds(at + head, tail), :]
                if group > 0:
                    mid[pl.ds(group * head, head), :] = mid[pl.ds(at, head), :]
        mine = pl.ds(0, now_rows)
        mlp_into(mid.at[mine, :], normed.at[mine, :], up_ref, down_ref)
        write_pieces(mid, outs, now, bands, locations)

    weights = [channel_qkv, channel_out, up_weight, down_weight]
    size = sum(weight.size for weight in weights)
    return call(
        kernel,
        [jax.ShapeDtypeStruct((bands, locations, width), BF16)] * len(now)
        + [jax.ShapeDtypeStruct((rows - now_rows, width), F32)] * (count - len(now)),
        2 * rows * size,
        2 * (2 * rows * width + size),
        limit=WIDE_LIMIT,
        in_specs=[ANY] * 4 + [ANY if fetch else VMEM],
        out_specs=[VMEM] * count,
        scratch_shapes=[
            pltpu.VMEM((rows, width), F32),
            pltpu.VMEM((rows, width), BF16),
            pltpu.VMEM((rows, 3 * width), BF16),
            pltpu.VMEM((rows, width), BF16),
        ]
        + [pltpu.VMEM(weight.shape, BF16) for weight in weights]
        + [pltpu.SemaphoreType.DMA((7,))]
        + [pltpu.VMEM(parts.shape, BF16)] * fetch,
    )(*weights, parts)


def restore(plan, keys, returned):
    def kernel(keys_ref, *refs):
        ins, out_ref = refs[:-1], refs[-1]
        group = lax.axis_index("band")
        place = lax.broadcasted_iota(jnp.int32, (plan.loc_dev, plan.loc_dev), 0)
        inner = place % plan.part_rows
        part = (place // plan.part_rows) % plan.share
        owner = (place // (plan.part_rows * plan.share)) % plan.groups ^ group
        window = place // plan.block
        wanted = window * plan.block + part * plan.rows + owner * plan.part_rows + inner
        pick = jnp.where(wanted.astype(F32) == keys_ref[...], 1.0, 0.0).astype(BF16)
        for band in range(plan.band_dev):
            rows = jnp.concatenate([ref[band] for ref in ins], axis=0)
            out_ref[:, band, :] = lax.dot_general(
                pick, rows, (((0,), (0,)), ((), ())), preferred_element_type=F32
            ).astype(BF16)

    arrays = [array for chunk in returned for array in chunk]
    size = plan.loc_dev * plan.band_dev * plan.width
    return call(
        kernel,
        jax.ShapeDtypeStruct((plan.loc_dev, plan.band_dev, plan.width), BF16),
        2 * plan.loc_dev * size,
        4 * size,
    )(keys, *arrays)


def body(
    tokens,
    band_index,
    band_table,
    window_ids,
    spatial_qkv,
    spatial_out,
    channel_qkv,
    channel_out,
    up_weight,
    down_weight,
):
    plan = Plan(tokens)
    ids = window_ids.reshape(-1, LANES)
    *sent, rows, location_key, place_keys = arrange_first(plan, tokens, ids)
    arrived = [[exchange(value, "loc", CORES * step) for step, value in enumerate(sent)]]
    arranged = None
    for window in range(1, WINDOWS):
        *sent, arranged = arrange_next(plan, window, rows, place_keys, arrived[0][1:2])
        arrived.append([exchange(value, "loc", CORES * step) for step, value in enumerate(sent)])
    mids, behind = [], []
    for window, slots in enumerate(arrived):
        hide = int(window == 0)
        half = len(slots) // 2 if hide and plan.share == 1 else len(slots)
        owns, queries, all_keys, all_values = [], [], [], []
        tables = (band_index, band_table, spatial_qkv)
        for first in range(0, len(slots), half):
            if first > 0:
                behind = [arranged, queries[-1]]
            own = join_slots(plan, slots[first : first + half], behind, 0 if hide else LONG)
            query, keys, values = project(plan, [own], *tables, True, hide)
            owns.append(own)
            queries.append(query)
            all_keys.append(keys)
            all_values.append(values)
        if plan.share == 1:
            others = [exchange(own, "loc", 1) for own in owns]
            keys, values = project(plan, others, *tables, False, hide, queries[-1:])
            all_keys.append(keys)
            all_values.append(values)
        else:
            step = CORES * plan.share
            same = [list(range(at, at + step)) for at in range(0, plan.locs, step)]
            every = lax.all_gather(owns[0], "loc", axis_index_groups=same, tiled=True)
            keys, values = project(plan, [every], *tables, False, hide)
            all_keys, all_values = [keys], [values]
        mid, done = attend(
            plan, queries, all_keys, all_values, owns, band_index, band_table, spatial_out, hide
        )
        behind = [done]
        mids.append(mid)
    same = [
        [g * plan.locs + r * CORES + core for r in range(plan.rows_count) for g in range(plan.groups)]
        for core in range(CORES)
    ]
    returned = []
    for mid in mids:
        parts = lax.all_to_all(
            mid.reshape(-1, plan.part_rows, plan.width),
            ("band", "loc"),
            0,
            0,
            axis_index_groups=same,
            tiled=True,
        )
        parts = parts.reshape(plan.band_dev, plan.share, plan.groups, plan.part_rows, plan.width)
        parts = parts.transpose(0, 2, 1, 3, 4).reshape(plan.band_dev, plan.groups, -1, plan.width)
        weights = (channel_qkv, channel_out, up_weight, down_weight)
        now, later = list(range(plan.groups)), []
        if mid is mids[-1] and plan.groups > 1:
            now, later = now[1:], now[:1]
        done = channel(plan, parts, now, later, mid is not mids[-1], *weights)
        if later:
            *done, rest = done
            done += finish(plan, rest, later, plan.band_dev, up_weight, down_weight)
        done = dict(zip([*now, *later], done))
        returned.append([exchange(done[step], "band", step) for step in range(plan.groups)])
    return restore(plan, location_key, returned)


def solution(mesh):
    placed = (P("loc", "band", None), P(), P(), P(), P(), P(), P(), P(), P(), P())
    return jax.shard_map(
        body, mesh=mesh, in_specs=placed, out_specs=P("loc", "band", None), check_vma=False
    )
```

```python
import functools

import jax
import jax.numpy as jnp
from jax import lax
from jax.experimental import pallas as pl
from jax.experimental.pallas import tpu as pltpu
from jax.sharding import PartitionSpec as P

HEADS = 12
HEAD_DIM = 64
WINDOWS = 2
CORES = 2
TILE_LOCS = 16
GROUP_LOCS = 8
UNIT_ROWS = 256
STEP_PAIRS = 3
ROW_TILE = 256
LANES = 128
QUERY_SCALE = HEAD_DIM ** (-0.5)
VMEM_LIMIT = 28 * 1024 * 1024
WIDE_LIMIT = 52 * 1024 * 1024
LONG = 2**36

F32 = jnp.float32
BF16 = jnp.bfloat16


def dot(left, right):
    return jnp.dot(left, right, preferred_element_type=F32)


def dot_t(left, right):
    return lax.dot_general(left, right, (((1,), (1,)), ((), ())), preferred_element_type=F32)


def norm_rows(values):
    centre = values - jnp.mean(values, axis=-1, keepdims=True)
    spread = jnp.mean(centre * centre, axis=-1, keepdims=True)
    return centre * lax.rsqrt(spread + 1e-05)


def gelu(values):
    inner = values * (0.7978845608028654 + 0.035677408136300125 * (values * values))
    return (0.5 * values) * (1.0 + jnp.tanh(inner))


def call(kernel, out_shape, flops, nbytes, limit=VMEM_LIMIT, **kwargs):
    return pl.pallas_call(
        kernel,
        out_shape=out_shape,
        compiler_params=pltpu.CompilerParams(vmem_limit_bytes=limit),
        cost_estimate=pl.CostEstimate(flops=flops, bytes_accessed=nbytes, transcendentals=0),
        **kwargs,
    )


def exchange(value, axis, step):
    if step == 0:
        return value
    return lax.ppermute(value, axis, [(i, i ^ step) for i in range(lax.axis_size(axis))])


class Plan:
    def __init__(self, tokens):
        self.loc_dev, self.band_dev, self.width = tokens.shape
        self.locs = lax.axis_size("loc")
        self.groups = lax.axis_size("band")
        self.rows_count = self.locs // CORES
        self.share = self.rows_count // self.band_dev
        assert self.share * self.band_dev * CORES == self.locs
        self.block = self.loc_dev // WINDOWS
        self.rows = self.block // self.share
        self.part_rows = self.rows // self.groups
        assert self.part_rows * self.groups * self.share * WINDOWS == self.loc_dev
        self.row_bits = self.rows_count.bit_length() - 1 if self.share == 1 else 0

    def spot(self, row):
        if self.row_bits == 0:
            return row
        bits = range(self.row_bits)
        return sum(((row >> bit) & 1) << (self.row_bits - 1 - bit) for bit in bits)


def marker():
    return jax.ShapeDtypeStruct((8, LANES), F32)


def location_keys(plan, ids_ref):
    size = plan.loc_dev
    lines = size // LANES
    first = lax.axis_index("loc") * lines
    ids = jnp.concatenate([ids_ref[pl.ds(first + i, 1), :] for i in range(lines)], axis=1)
    ids = ids.astype(F32)
    row = jnp.broadcast_to(ids, (size, size))
    first = lax.broadcasted_iota(jnp.int32, (size, size), 0)
    second = lax.broadcasted_iota(jnp.int32, (size, size), 1)
    column = jnp.sum(jnp.where(first == second, row, 0.0), axis=1, keepdims=True)
    before = jnp.where((column == row) & (first < second), 1.0, 0.0)
    rank = jnp.sum(before, axis=0, keepdims=True)
    return ids * plan.block + rank


SMEM = pl.BlockSpec(memory_space=pltpu.SMEM)
VMEM = pl.BlockSpec(memory_space=pltpu.VMEM)
ANY = pl.BlockSpec(memory_space=pl.ANY)


def pick_rows(plan, window, place_keys, rows, outs):
    row = lax.axis_index("loc") // CORES
    place = lax.broadcasted_iota(jnp.int32, (plan.rows, rows.shape[0]), 0)
    for slot in range(plan.rows_count):
        peer = row ^ slot
        band, part = peer // plan.share, peer % plan.share
        wanted = place + (band * plan.loc_dev + window * plan.block + part * plan.rows)
        pick = jnp.where(wanted.astype(F32) == place_keys, 1.0, 0.0).astype(BF16)
        outs[slot][...] = dot(pick, rows[...]).astype(BF16)


def arrange_first(plan, tokens, ids):
    count = plan.rows_count
    total = plan.loc_dev * plan.band_dev
    assert plan.loc_dev <= 256

    def kernel(ids_ref, x_ref, *rest):
        outs, (rows_ref, keys_ref, place_ref) = rest[:count], rest[count:]
        keys = location_keys(plan, ids_ref)
        keys_ref[...] = keys
        place = lax.broadcasted_iota(jnp.int32, (plan.loc_dev, total), 1)
        location = lax.broadcasted_iota(jnp.int32, (plan.loc_dev, total), 0)
        spread = jnp.where(place // plan.band_dev == location, 1.0, 0.0).astype(BF16)
        wide = dot(jnp.broadcast_to(keys, (16, plan.loc_dev)).astype(BF16), spread)
        band = lax.broadcasted_iota(jnp.int32, (1, total), 1) % plan.band_dev
        place_ref[...] = wide[:1] + (band * plan.loc_dev).astype(F32)
        rows_ref[...] = x_ref[...].reshape(total, plan.width)
        pick_rows(plan, 0, place_ref[...], rows_ref, outs)

    return call(
        kernel,
        [jax.ShapeDtypeStruct((plan.rows, plan.width), BF16)] * count
        + [
            jax.ShapeDtypeStruct((total, plan.width), BF16),
            jax.ShapeDtypeStruct((1, plan.loc_dev), F32),
            jax.ShapeDtypeStruct((1, total), F32),
        ],
        2 * plan.loc_dev * tokens.size,
        4 * tokens.size,
        in_specs=[VMEM] * 2,
        out_specs=[VMEM] * (count + 3),
    )(ids, tokens)


def arrange_next(plan, window, rows, place_keys, after):
    count = plan.rows_count

    def kernel(rows_ref, place_ref, *rest):
        outs = rest[len(after) :]
        outs[-1][...] = jnp.zeros_like(outs[-1])
        pick_rows(plan, window, place_ref[...], rows_ref, outs[:-1])

    return call(
        kernel,
        [jax.ShapeDtypeStruct((plan.rows, plan.width), BF16)] * count + [marker()],
        2 * plan.loc_dev * rows.size,
        0,
        in_specs=[VMEM] * 2 + [ANY] * len(after),
        out_specs=[VMEM] * (count + 1),
    )(rows, place_keys, *after)


def join_slots(plan, slots, after, flops):
    count, rows = len(slots), plan.rows

    def kernel(*refs):
        out_ref, sems = refs[-2:]
        copies = [
            pltpu.make_async_copy(
                refs[slot], out_ref.at[pl.ds(slot * rows, rows), :], sems.at[slot]
            )
            for slot in range(count)
        ]
        for copy in copies:
            copy.start()
        for copy in copies:
            copy.wait()

    return call(
        kernel,
        jax.ShapeDtypeStruct((count * rows, plan.width), BF16),
        flops,
        0,
        in_specs=[ANY] * (count + len(after)),
        out_specs=VMEM,
        scratch_shapes=[pltpu.SemaphoreType.DMA((count,))],
    )(*slots, *after)


def embed_row(plan, index_ref, table_ref):
    band = lax.axis_index("loc") // (CORES * plan.share)
    number = index_ref[lax.axis_index("band") * plan.band_dev + band]
    return table_ref[pl.ds(number, 1), :]


def loop(count, step, unroll=1):
    lax.fori_loop(0, count, lambda i, _: (step(i), 0)[1], 0, unroll=unroll)


def aligned(index, size):
    return pl.ds(pl.multiple_of(index * size, size), size)


def norm_into(target, source):
    rows = source.shape[0]
    tile = rows // pl.cdiv(rows, ROW_TILE)
    for first in range(0, rows, tile):
        here = pl.ds(first, tile)
        target[here, :] = norm_rows(source[here, :]).astype(BF16)


def project(plan, tokens, index, table, weights, queries, hide, after=()):
    width = plan.width
    rows = sum(piece.shape[0] for piece in tokens)
    names = range(3) if queries else range(1, 3)

    def kernel(index_ref, table_ref, w_ref, *rest):
        x_refs, outs = rest[: len(tokens)], rest[len(tokens) + len(after) :]
        embed = embed_row(plan, index_ref, table_ref)
        at = 0
        for x_ref in x_refs:
            count = x_ref.shape[0]
            tile = min(count, ROW_TILE)
            for first in range(0, count, tile):
                normed = norm_rows(x_ref[pl.ds(first, tile), :].astype(F32) + embed).astype(BF16)
                here = pl.ds(at + first, tile)
                for ref, name in zip(outs, names):
                    value = dot(normed, w_ref[:, name * width : (name + 1) * width])
                    ref[here, :] = (value * QUERY_SCALE if name == 0 else value).astype(BF16)
            at += count

    return call(
        kernel,
        [jax.ShapeDtypeStruct((rows, width), BF16)] * len(names),
        hide * 2 * rows * width * len(names) * width,
        hide * 2 * ((1 + len(names)) * rows * width + 3 * width * width),
        in_specs=[SMEM, VMEM, VMEM] + [VMEM] * len(tokens) + [ANY] * len(after),
        out_specs=[VMEM] * len(names),
    )(index, table, weights, *tokens, *after)


def head_masks(rows):
    lane = lax.broadcasted_iota(jnp.int32, (rows, LANES), 1)
    return [(lane // HEAD_DIM) == head for head in range(LANES // HEAD_DIM)]


def stack_heads(query):
    return jnp.concatenate(
        [jnp.where(inside, query, jnp.zeros_like(query)) for inside in head_masks(query.shape[0])],
        axis=0,
    )


def join_heads(stacked):
    heads = LANES // HEAD_DIM
    rows = stacked.shape[0] // heads
    joined = stacked[:rows]
    for head, inside in list(enumerate(head_masks(rows)))[1:]:
        joined = jnp.where(inside, stacked[head * rows : (head + 1) * rows], joined)
    return joined


def with_ones(value):
    return jnp.concatenate([value, jnp.ones(value.shape, BF16)], axis=1)


def run_units(units, mask=None):
    def scores_of(unit):
        query, keys, _ = unit
        scores = [dot_t(query, piece) for piece in keys]
        if mask is not None:
            scores = [jnp.where(mask, piece, -1e30) for piece in scores]
        return scores

    results = []
    ahead = scores_of(units[0])
    for number, (_, _, values) in enumerate(units):
        scores = ahead
        if number + 1 < len(units):
            ahead = scores_of(units[number + 1])
        peak = functools.reduce(
            jnp.maximum, [jnp.max(piece, axis=-1, keepdims=True) for piece in scores]
        )
        total = None
        for piece, value in zip(scores, values):
            part = dot(jnp.exp(piece - peak).astype(BF16), value)
            total = part if total is None else total + part
        results.append(
            (join_heads(total[:, :LANES]) / join_heads(total[:, LANES:])).astype(BF16)
        )
    return results


def attend(plan, query, keys, values, tokens, index, table, spatial_out, hide):
    width, rows = plan.width, plan.rows
    pieces, sources = len(keys), len(query)
    counts = [piece.shape[0] for piece in query]
    total = sum(counts)
    pairs = width // LANES

    def kernel(index_ref, table_ref, w_ref, *rest):
        x_refs, rest = rest[:sources], rest[sources:]
        q_refs, rest = rest[:sources], rest[sources:]
        k_refs, rest = rest[:pieces], rest[pieces:]
        v_refs, (out_ref, marker_ref, result, added) = rest[:pieces], rest[pieces:]
        marker_ref[...] = jnp.zeros_like(marker_ref)

        def step(number):
            units, places = [], []
            for i in range(STEP_PAIRS):
                here = aligned(number * STEP_PAIRS + i, LANES)
                pair_keys = [ref[:, here] for ref in k_refs]
                pair_values = [with_ones(ref[:, here]) for ref in v_refs]
                at = 0
                for ref, count in zip(q_refs, counts):
                    unit = min(count, UNIT_ROWS)
                    for first in range(0, count, unit):
                        query_rows = ref[pl.ds(first, unit), here]
                        units.append((stack_heads(query_rows), pair_keys, pair_values))
                        places.append((pl.ds(at + first, unit), here))
                    at += count
            for place, done in zip(places, run_units(units)):
                result[place] = done

        loop(pairs // STEP_PAIRS, step)
        added[...] = dot(result[...], w_ref[...])
        embed = embed_row(plan, index_ref, table_ref)
        row = lax.axis_index("loc") // CORES
        slot = 0
        for ref, count in zip(x_refs, counts):
            for first in range(0, count, rows):
                start = ref[pl.ds(first, rows), :].astype(F32) + embed
                mid = (start + added[pl.ds(slot * rows, rows), :]).astype(BF16)
                for owner in range(plan.groups):
                    part = mid[owner * plan.part_rows : (owner + 1) * plan.part_rows]
                    out_ref[plan.spot(row ^ slot), owner] = part
                slot += 1

    key_rows = sum(piece.shape[0] for piece in keys)
    return call(
        kernel,
        [
            jax.ShapeDtypeStruct((plan.rows_count, plan.groups, plan.part_rows, width), BF16),
            marker(),
        ],
        hide * 16 * total * key_rows * width,
        0,
        in_specs=[SMEM] + [VMEM] * (2 + 2 * sources + 2 * pieces),
        out_specs=[VMEM] * 2,
        scratch_shapes=[pltpu.VMEM((total, width), BF16), pltpu.VMEM((total, width), F32)],
    )(index, table, spatial_out, *tokens, *query, *keys, *values)


def piece_places(owners, bands, locations):
    stride = len(owners) * bands * GROUP_LOCS
    places = {}
    for position, owner in enumerate(owners):
        for band in range(bands):
            for first in range(0, locations, TILE_LOCS):
                places[owner, band, first] = [
                    pl.ds(at // GROUP_LOCS * stride + (position * bands + band) * GROUP_LOCS, GROUP_LOCS)
                    for at in range(first, first + TILE_LOCS, GROUP_LOCS)
                ]
    return places


def mlp_into(mid, normed, up_ref, down_ref, waits=()):
    rows, width = mid.shape
    row_tile = rows // pl.cdiv(rows, ROW_TILE)
    tiles = [pl.ds(first, row_tile) for first in range(0, rows, row_tile)]
    norm_into(normed, mid)

    def step(here):
        raised = [dot(normed[mine, :], up_ref[:, here]) for mine in tiles]
        for mine, value in zip(tiles, raised):
            mid[mine, :] += dot(gelu(value).astype(BF16), down_ref[here, :])

    blocks = up_ref.shape[1] // width
    if waits:
        for block in range(blocks):
            waits[block]()
            step(pl.ds(block * width, width))
    else:
        loop(blocks, lambda block: step(aligned(block, width)))


def write_pieces(mid, outs, owners, bands, locations):
    for (owner, band, first), places in piece_places(owners, bands, locations).items():
        piece = jnp.concatenate([mid[place, :] for place in places], axis=0)
        outs[owners.index(owner)][band, first : first + TILE_LOCS, :] = piece.astype(BF16)


def finish(plan, rest, owners, bands, up_weight, down_weight):
    rows, width = rest.shape
    locations = rows // (len(owners) * bands)
    blocks = up_weight.shape[1] // width

    def kernel(up_hbm, down_hbm, rest_ref, *refs):
        outs, refs = refs[: len(owners)], refs[len(owners) :]
        mid, normed, up_ref, down_ref, sems = refs
        pairs = []
        for block in range(blocks):
            here = pl.ds(block * width, width)
            pairs.append(
                [
                    pltpu.make_async_copy(
                        up_hbm.at[:, here], up_ref.at[:, here], sems.at[2 * block]
                    ),
                    pltpu.make_async_copy(
                        down_hbm.at[here, :], down_ref.at[here, :], sems.at[2 * block + 1]
                    ),
                ]
            )

        def start(block):
            for copy in pairs[block]:
                copy.start()

        def wait(block):
            for copy in pairs[block]:
                copy.wait()
            if block + 2 < blocks:
                start(block + 2)

        for block in range(min(2, blocks)):
            start(block)
        mid[...] = rest_ref[...]
        waits = [functools.partial(wait, block) for block in range(blocks)]
        mlp_into(mid, normed, up_ref, down_ref, waits)
        write_pieces(mid, outs, owners, bands, locations)

    return call(
        kernel,
        [jax.ShapeDtypeStruct((bands, locations, width), BF16)] * len(owners),
        4 * rows * up_weight.size,
        2 * 2 * up_weight.size,
        limit=WIDE_LIMIT,
        in_specs=[ANY] * 2 + [VMEM],
        out_specs=[VMEM] * len(owners),
        scratch_shapes=[
            pltpu.VMEM((rows, width), F32),
            pltpu.VMEM((rows, width), BF16),
            pltpu.VMEM(up_weight.shape, BF16),
            pltpu.VMEM(down_weight.shape, BF16),
            pltpu.SemaphoreType.DMA((2 * blocks,)),
        ],
    )(up_weight, down_weight, rest)


def channel(plan, parts, now, later, fetch, channel_qkv, channel_out, up_weight, down_weight):
    groups, width = plan.groups, plan.width
    bands, _, locations, _ = parts.shape
    small = GROUP_LOCS
    assert locations % TILE_LOCS == 0
    owners = [*now, *later]
    group_rows = groups * bands * small
    rows = groups * bands * locations
    now_rows = rows * len(now) // groups
    count = len(now) + (len(later) > 0)

    def kernel(qkv_hbm, out_hbm, up_hbm, down_hbm, *refs):
        in_ref, *refs = refs
        outs, refs = refs[:count], refs[count:]
        mid, normed, packed, attended, qkv_ref, out_ref, up_ref, down_ref, sems, *held = refs
        if held:
            load = pltpu.make_async_copy(in_ref, held[0], sems.at[6])
            load.start()
            in_ref = held[0]
        me = lax.axis_index("band")
        columns = [pl.ds(first, width) for first in range(0, 3 * width, width)]
        copies = []
        for source, target, spots in (
            (qkv_hbm, qkv_ref, [(slice(None), spot) for spot in columns]),
            (out_hbm, out_ref, [(slice(None), slice(None))]),
            (up_hbm, up_ref, [(slice(None), slice(None))]),
            (down_hbm, down_ref, [(slice(None), slice(None))]),
        ):
            for spot in spots:
                copies.append(
                    pltpu.make_async_copy(
                        source.at[spot], target.at[spot], sems.at[len(copies)]
                    )
                )
        for copy in copies[: len(columns)]:
            copy.start()
        if held:
            load.wait()
        for (owner, band, first), places in piece_places(owners, bands, locations).items():
            piece = in_ref[band, me ^ owner, first : first + TILE_LOCS, :].astype(F32)
            for number, place in enumerate(places):
                mid[place, :] = piece[number * small : (number + 1) * small]
        norm_into(normed, mid)

        for number, here in enumerate(columns):
            copies[number].wait()
            copies[number + len(columns)].start()
            factor = QUERY_SCALE if number == 0 else 1.0
            packed[:, here] = (dot(normed[...], qkv_ref[:, here]) * factor).astype(BF16)
        pairs = width // LANES
        stacked = group_rows * (LANES // HEAD_DIM)
        one = lax.broadcasted_iota(jnp.int32, (stacked, group_rows), 0)
        other = lax.broadcasted_iota(jnp.int32, (stacked, group_rows), 1)
        mask = (one % small) == (other % small)

        def attention_step(pair):
            units, spots = [], []
            for first in range(0, rows, group_rows):
                mine = pl.ds(first, group_rows)
                query = packed[mine, aligned(pair, LANES)]
                keys = packed[mine, aligned(pair + pairs, LANES)]
                values = packed[mine, aligned(pair + 2 * pairs, LANES)]
                units.append((stack_heads(query), [keys], [with_ones(values)]))
                spots.append((mine, aligned(pair, LANES)))
            for spot, done in zip(spots, run_units(units, mask)):
                attended[spot] = done

        loop(pairs, attention_step, unroll=3)
        copies[3].wait()
        mid[...] += dot(attended[...], out_ref[...])
        copies[4].wait()
        copies[5].wait()
        if later:
            head = len(now) * bands * small
            tail = group_rows - head
            for group in range(rows // group_rows):
                at = group * group_rows
                outs[-1][pl.ds(group * tail, tail), :] = mid[pl.ds(at + head, tail), :]
                if group > 0:
                    mid[pl.ds(group * head, head), :] = mid[pl.ds(at, head), :]
        mine = pl.ds(0, now_rows)
        mlp_into(mid.at[mine, :], normed.at[mine, :], up_ref, down_ref)
        write_pieces(mid, outs, now, bands, locations)

    weights = [channel_qkv, channel_out, up_weight, down_weight]
    size = sum(weight.size for weight in weights)
    return call(
        kernel,
        [jax.ShapeDtypeStruct((bands, locations, width), BF16)] * len(now)
        + [jax.ShapeDtypeStruct((rows - now_rows, width), F32)] * (count - len(now)),
        2 * rows * size,
        2 * (2 * rows * width + size),
        limit=WIDE_LIMIT,
        in_specs=[ANY] * 4 + [ANY if fetch else VMEM],
        out_specs=[VMEM] * count,
        scratch_shapes=[
            pltpu.VMEM((rows, width), F32),
            pltpu.VMEM((rows, width), BF16),
            pltpu.VMEM((rows, 3 * width), BF16),
            pltpu.VMEM((rows, width), BF16),
        ]
        + [pltpu.VMEM(weight.shape, BF16) for weight in weights]
        + [pltpu.SemaphoreType.DMA((7,))]
        + [pltpu.VMEM(parts.shape, BF16)] * fetch,
    )(*weights, parts)


def restore(plan, keys, returned):
    def kernel(keys_ref, *refs):
        ins, out_ref = refs[:-1], refs[-1]
        group = lax.axis_index("band")
        place = lax.broadcasted_iota(jnp.int32, (plan.loc_dev, plan.loc_dev), 0)
        inner = place % plan.part_rows
        part = (place // plan.part_rows) % plan.share
        owner = (place // (plan.part_rows * plan.share)) % plan.groups ^ group
        window = place // plan.block
        wanted = window * plan.block + part * plan.rows + owner * plan.part_rows + inner
        pick = jnp.where(wanted.astype(F32) == keys_ref[...], 1.0, 0.0).astype(BF16)
        for band in range(plan.band_dev):
            rows = jnp.concatenate([ref[plan.spot(band)] for ref in ins], axis=0)
            out_ref[:, band, :] = lax.dot_general(
                pick, rows, (((0,), (0,)), ((), ())), preferred_element_type=F32
            ).astype(BF16)

    arrays = [array for chunk in returned for array in chunk]
    size = plan.loc_dev * plan.band_dev * plan.width
    return call(
        kernel,
        jax.ShapeDtypeStruct((plan.loc_dev, plan.band_dev, plan.width), BF16),
        2 * plan.loc_dev * size,
        4 * size,
    )(keys, *arrays)


def body(
    tokens,
    band_index,
    band_table,
    window_ids,
    spatial_qkv,
    spatial_out,
    channel_qkv,
    channel_out,
    up_weight,
    down_weight,
):
    plan = Plan(tokens)
    ids = window_ids.reshape(-1, LANES)
    *sent, rows, location_key, place_keys = arrange_first(plan, tokens, ids)
    arrived = [[exchange(value, "loc", CORES * step) for step, value in enumerate(sent)]]
    arranged = None
    for window in range(1, WINDOWS):
        *sent, arranged = arrange_next(plan, window, rows, place_keys, arrived[0][1:2])
        arrived.append([exchange(value, "loc", CORES * step) for step, value in enumerate(sent)])
    mids, behind = [], []
    for window, slots in enumerate(arrived):
        hide = int(window == 0)
        half = len(slots) // 2 if hide and plan.share == 1 else len(slots)
        owns, queries, all_keys, all_values = [], [], [], []
        tables = (band_index, band_table, spatial_qkv)
        for first in range(0, len(slots), half):
            if first > 0:
                behind = [arranged, queries[-1]]
            own = join_slots(plan, slots[first : first + half], behind, 0 if hide else LONG)
            query, keys, values = project(plan, [own], *tables, True, hide)
            owns.append(own)
            queries.append(query)
            all_keys.append(keys)
            all_values.append(values)
        if plan.share == 1:
            others = [exchange(own, "loc", 1) for own in owns]
            keys, values = project(plan, others, *tables, False, hide, queries[-1:])
            all_keys.append(keys)
            all_values.append(values)
        else:
            step = CORES * plan.share
            same = [list(range(at, at + step)) for at in range(0, plan.locs, step)]
            every = lax.all_gather(owns[0], "loc", axis_index_groups=same, tiled=True)
            keys, values = project(plan, [every], *tables, False, hide)
            all_keys, all_values = [keys], [values]
        mid, done = attend(
            plan, queries, all_keys, all_values, owns, band_index, band_table, spatial_out, hide
        )
        behind = [done]
        mids.append(mid)
    same = [
        [
            g * plan.locs + plan.spot(r) * CORES + core
            for r in range(plan.rows_count)
            for g in range(plan.groups)
        ]
        for core in range(CORES)
    ]
    returned = []
    for mid in mids:
        parts = lax.all_to_all(
            mid.reshape(-1, plan.part_rows, plan.width),
            ("band", "loc"),
            0,
            0,
            axis_index_groups=same,
            tiled=True,
        )
        parts = parts.reshape(plan.band_dev, plan.share, plan.groups, plan.part_rows, plan.width)
        parts = parts.transpose(0, 2, 1, 3, 4).reshape(plan.band_dev, plan.groups, -1, plan.width)
        weights = (channel_qkv, channel_out, up_weight, down_weight)
        now, later = list(range(plan.groups)), []
        if mid is mids[-1] and plan.groups > 1:
            now, later = now[1:], now[:1]
        done = channel(plan, parts, now, later, mid is not mids[-1], *weights)
        if later:
            *done, rest = done
            done += finish(plan, rest, later, plan.band_dev, up_weight, down_weight)
        done = dict(zip([*now, *later], done))
        returned.append([exchange(done[step], "band", step) for step in range(plan.groups)])
    return restore(plan, location_key, returned)


def solution(mesh):
    placed = (P("loc", "band", None), P(), P(), P(), P(), P(), P(), P(), P(), P())
    return jax.shard_map(
        body, mesh=mesh, in_specs=placed, out_specs=P("loc", "band", None), check_vma=False
    )
```

```python
import functools

import jax
import jax.numpy as jnp
from jax import lax
from jax.experimental import pallas as pl
from jax.experimental.pallas import tpu as pltpu
from jax.sharding import PartitionSpec as P

HEADS = 12
HEAD_DIM = 64
WINDOWS = 2
CORES = 2
TILE_LOCS = 16
GROUP_LOCS = 8
UNIT_ROWS = 256
STEP_PAIRS = 3
ROW_TILE = 256
LANES = 128
QUERY_SCALE = HEAD_DIM ** (-0.5)
VMEM_LIMIT = 28 * 1024 * 1024
WIDE_LIMIT = 52 * 1024 * 1024
LONG = 2**36

F32 = jnp.float32
BF16 = jnp.bfloat16


def dot(left, right):
    return jnp.dot(left, right, preferred_element_type=F32)


def dot_t(left, right):
    return lax.dot_general(left, right, (((1,), (1,)), ((), ())), preferred_element_type=F32)


def norm_rows(values):
    centre = values - jnp.mean(values, axis=-1, keepdims=True)
    spread = jnp.mean(centre * centre, axis=-1, keepdims=True)
    return centre * lax.rsqrt(spread + 1e-05)


def gelu(values):
    inner = values * (0.7978845608028654 + 0.035677408136300125 * (values * values))
    return (0.5 * values) * (1.0 + jnp.tanh(inner))


def call(kernel, out_shape, flops, nbytes, limit=VMEM_LIMIT, **kwargs):
    return pl.pallas_call(
        kernel,
        out_shape=out_shape,
        compiler_params=pltpu.CompilerParams(vmem_limit_bytes=limit),
        cost_estimate=pl.CostEstimate(flops=flops, bytes_accessed=nbytes, transcendentals=0),
        **kwargs,
    )


def exchange(value, axis, step):
    if step == 0:
        return value
    return lax.ppermute(value, axis, [(i, i ^ step) for i in range(lax.axis_size(axis))])


class Plan:
    def __init__(self, tokens):
        self.loc_dev, self.band_dev, self.width = tokens.shape
        self.locs = lax.axis_size("loc")
        self.groups = lax.axis_size("band")
        self.rows_count = self.locs // CORES
        self.share = self.rows_count // self.band_dev
        assert self.share * self.band_dev * CORES == self.locs
        self.block = self.loc_dev // WINDOWS
        self.rows = self.block // self.share
        self.part_rows = self.rows // self.groups
        assert self.part_rows * self.groups * self.share * WINDOWS == self.loc_dev
        self.turn = 1 if self.share == 1 else 0

    def row_at(self, spot):
        return (spot + self.turn) % self.rows_count

    def spot(self, row):
        return (row + self.rows_count - self.turn) % self.rows_count


def marker():
    return jax.ShapeDtypeStruct((8, LANES), F32)


def location_keys(plan, ids_ref):
    size = plan.loc_dev
    lines = size // LANES
    first = lax.axis_index("loc") * lines
    ids = jnp.concatenate([ids_ref[pl.ds(first + i, 1), :] for i in range(lines)], axis=1)
    ids = ids.astype(F32)
    row = jnp.broadcast_to(ids, (size, size))
    first = lax.broadcasted_iota(jnp.int32, (size, size), 0)
    second = lax.broadcasted_iota(jnp.int32, (size, size), 1)
    column = jnp.sum(jnp.where(first == second, row, 0.0), axis=1, keepdims=True)
    before = jnp.where((column == row) & (first < second), 1.0, 0.0)
    rank = jnp.sum(before, axis=0, keepdims=True)
    return ids * plan.block + rank


SMEM = pl.BlockSpec(memory_space=pltpu.SMEM)
VMEM = pl.BlockSpec(memory_space=pltpu.VMEM)
ANY = pl.BlockSpec(memory_space=pl.ANY)


def pick_rows(plan, window, place_keys, rows, outs):
    row = lax.axis_index("loc") // CORES
    place = lax.broadcasted_iota(jnp.int32, (plan.rows, rows.shape[0]), 0)
    for slot in range(plan.rows_count):
        peer = row ^ slot
        band, part = peer // plan.share, peer % plan.share
        wanted = place + (band * plan.loc_dev + window * plan.block + part * plan.rows)
        pick = jnp.where(wanted.astype(F32) == place_keys, 1.0, 0.0).astype(BF16)
        outs[slot][...] = dot(pick, rows[...]).astype(BF16)


def arrange_first(plan, tokens, ids):
    count = plan.rows_count
    total = plan.loc_dev * plan.band_dev
    assert plan.loc_dev <= 256

    def kernel(ids_ref, x_ref, *rest):
        outs, (rows_ref, keys_ref, place_ref) = rest[:count], rest[count:]
        keys = location_keys(plan, ids_ref)
        keys_ref[...] = keys
        place = lax.broadcasted_iota(jnp.int32, (plan.loc_dev, total), 1)
        location = lax.broadcasted_iota(jnp.int32, (plan.loc_dev, total), 0)
        spread = jnp.where(place // plan.band_dev == location, 1.0, 0.0).astype(BF16)
        wide = dot(jnp.broadcast_to(keys, (16, plan.loc_dev)).astype(BF16), spread)
        band = lax.broadcasted_iota(jnp.int32, (1, total), 1) % plan.band_dev
        place_ref[...] = wide[:1] + (band * plan.loc_dev).astype(F32)
        rows_ref[...] = x_ref[...].reshape(total, plan.width)
        pick_rows(plan, 0, place_ref[...], rows_ref, outs)

    return call(
        kernel,
        [jax.ShapeDtypeStruct((plan.rows, plan.width), BF16)] * count
        + [
            jax.ShapeDtypeStruct((total, plan.width), BF16),
            jax.ShapeDtypeStruct((1, plan.loc_dev), F32),
            jax.ShapeDtypeStruct((1, total), F32),
        ],
        2 * plan.loc_dev * tokens.size,
        4 * tokens.size,
        in_specs=[VMEM] * 2,
        out_specs=[VMEM] * (count + 3),
    )(ids, tokens)


def arrange_next(plan, window, rows, place_keys, after):
    count = plan.rows_count

    def kernel(rows_ref, place_ref, *rest):
        outs = rest[len(after) :]
        outs[-1][...] = jnp.zeros_like(outs[-1])
        pick_rows(plan, window, place_ref[...], rows_ref, outs[:-1])

    return call(
        kernel,
        [jax.ShapeDtypeStruct((plan.rows, plan.width), BF16)] * count + [marker()],
        2 * plan.loc_dev * rows.size,
        0,
        in_specs=[VMEM] * 2 + [ANY] * len(after),
        out_specs=[VMEM] * (count + 1),
    )(rows, place_keys, *after)


def join_slots(plan, slots, after, flops):
    count, rows = len(slots), plan.rows

    def kernel(*refs):
        out_ref, sems = refs[-2:]
        copies = [
            pltpu.make_async_copy(
                refs[slot], out_ref.at[pl.ds(slot * rows, rows), :], sems.at[slot]
            )
            for slot in range(count)
        ]
        for copy in copies:
            copy.start()
        for copy in copies:
            copy.wait()

    return call(
        kernel,
        jax.ShapeDtypeStruct((count * rows, plan.width), BF16),
        flops,
        0,
        in_specs=[ANY] * (count + len(after)),
        out_specs=VMEM,
        scratch_shapes=[pltpu.SemaphoreType.DMA((count,))],
    )(*slots, *after)


def embed_row(plan, index_ref, table_ref):
    band = lax.axis_index("loc") // (CORES * plan.share)
    number = index_ref[lax.axis_index("band") * plan.band_dev + band]
    return table_ref[pl.ds(number, 1), :]


def loop(count, step, unroll=1):
    lax.fori_loop(0, count, lambda i, _: (step(i), 0)[1], 0, unroll=unroll)


def aligned(index, size):
    return pl.ds(pl.multiple_of(index * size, size), size)


def norm_into(target, source):
    rows = source.shape[0]
    tile = rows // pl.cdiv(rows, ROW_TILE)
    for first in range(0, rows, tile):
        here = pl.ds(first, tile)
        target[here, :] = norm_rows(source[here, :]).astype(BF16)


def project(plan, tokens, index, table, weights, queries, hide, after=()):
    width = plan.width
    rows = sum(piece.shape[0] for piece in tokens)
    names = range(3) if queries else range(1, 3)

    def kernel(index_ref, table_ref, w_ref, *rest):
        x_refs, outs = rest[: len(tokens)], rest[len(tokens) + len(after) :]
        embed = embed_row(plan, index_ref, table_ref)
        at = 0
        for x_ref in x_refs:
            count = x_ref.shape[0]
            tile = min(count, ROW_TILE)
            for first in range(0, count, tile):
                normed = norm_rows(x_ref[pl.ds(first, tile), :].astype(F32) + embed).astype(BF16)
                here = pl.ds(at + first, tile)
                for ref, name in zip(outs, names):
                    value = dot(normed, w_ref[:, name * width : (name + 1) * width])
                    ref[here, :] = (value * QUERY_SCALE if name == 0 else value).astype(BF16)
            at += count

    return call(
        kernel,
        [jax.ShapeDtypeStruct((rows, width), BF16)] * len(names),
        hide * 2 * rows * width * len(names) * width,
        hide * 2 * ((1 + len(names)) * rows * width + 3 * width * width),
        in_specs=[SMEM, VMEM, VMEM] + [VMEM] * len(tokens) + [ANY] * len(after),
        out_specs=[VMEM] * len(names),
    )(index, table, weights, *tokens, *after)


def head_masks(rows):
    lane = lax.broadcasted_iota(jnp.int32, (rows, LANES), 1)
    return [(lane // HEAD_DIM) == head for head in range(LANES // HEAD_DIM)]


def stack_heads(query):
    return jnp.concatenate(
        [jnp.where(inside, query, jnp.zeros_like(query)) for inside in head_masks(query.shape[0])],
        axis=0,
    )


def join_heads(stacked):
    heads = LANES // HEAD_DIM
    rows = stacked.shape[0] // heads
    joined = stacked[:rows]
    for head, inside in list(enumerate(head_masks(rows)))[1:]:
        joined = jnp.where(inside, stacked[head * rows : (head + 1) * rows], joined)
    return joined


def with_ones(value):
    return jnp.concatenate([value, jnp.ones(value.shape, BF16)], axis=1)


def run_units(units, mask=None):
    def scores_of(unit):
        query, keys, _ = unit
        scores = [dot_t(query, piece) for piece in keys]
        if mask is not None:
            scores = [jnp.where(mask, piece, -1e30) for piece in scores]
        return scores

    results = []
    ahead = scores_of(units[0])
    for number, (_, _, values) in enumerate(units):
        scores = ahead
        if number + 1 < len(units):
            ahead = scores_of(units[number + 1])
        peak = functools.reduce(
            jnp.maximum, [jnp.max(piece, axis=-1, keepdims=True) for piece in scores]
        )
        total = None
        for piece, value in zip(scores, values):
            part = dot(jnp.exp(piece - peak).astype(BF16), value)
            total = part if total is None else total + part
        results.append(
            (join_heads(total[:, :LANES]) / join_heads(total[:, LANES:])).astype(BF16)
        )
    return results


def attend(plan, query, keys, values, tokens, index, table, spatial_out, hide):
    width, rows = plan.width, plan.rows
    pieces, sources = len(keys), len(query)
    counts = [piece.shape[0] for piece in query]
    total = sum(counts)
    pairs = width // LANES

    def kernel(index_ref, table_ref, w_ref, *rest):
        x_refs, rest = rest[:sources], rest[sources:]
        q_refs, rest = rest[:sources], rest[sources:]
        k_refs, rest = rest[:pieces], rest[pieces:]
        v_refs, (out_ref, marker_ref, result, added) = rest[:pieces], rest[pieces:]
        marker_ref[...] = jnp.zeros_like(marker_ref)

        def step(number):
            units, places = [], []
            for i in range(STEP_PAIRS):
                here = aligned(number * STEP_PAIRS + i, LANES)
                pair_keys = [ref[:, here] for ref in k_refs]
                pair_values = [with_ones(ref[:, here]) for ref in v_refs]
                at = 0
                for ref, count in zip(q_refs, counts):
                    unit = min(count, UNIT_ROWS)
                    for first in range(0, count, unit):
                        query_rows = ref[pl.ds(first, unit), here]
                        units.append((stack_heads(query_rows), pair_keys, pair_values))
                        places.append((pl.ds(at + first, unit), here))
                    at += count
            for place, done in zip(places, run_units(units)):
                result[place] = done

        loop(pairs // STEP_PAIRS, step)
        added[...] = dot(result[...], w_ref[...])
        embed = embed_row(plan, index_ref, table_ref)
        row = lax.axis_index("loc") // CORES
        slot = 0
        for ref, count in zip(x_refs, counts):
            for first in range(0, count, rows):
                start = ref[pl.ds(first, rows), :].astype(F32) + embed
                mid = (start + added[pl.ds(slot * rows, rows), :]).astype(BF16)
                for owner in range(plan.groups):
                    part = mid[owner * plan.part_rows : (owner + 1) * plan.part_rows]
                    out_ref[plan.spot(row ^ slot), owner] = part
                slot += 1

    key_rows = sum(piece.shape[0] for piece in keys)
    return call(
        kernel,
        [
            jax.ShapeDtypeStruct((plan.rows_count, plan.groups, plan.part_rows, width), BF16),
            marker(),
        ],
        hide * 16 * total * key_rows * width,
        0,
        in_specs=[SMEM] + [VMEM] * (2 + 2 * sources + 2 * pieces),
        out_specs=[VMEM] * 2,
        scratch_shapes=[pltpu.VMEM((total, width), BF16), pltpu.VMEM((total, width), F32)],
    )(index, table, spatial_out, *tokens, *query, *keys, *values)


def piece_places(owners, bands, locations):
    stride = len(owners) * bands * GROUP_LOCS
    places = {}
    for position, owner in enumerate(owners):
        for band in range(bands):
            for first in range(0, locations, TILE_LOCS):
                places[owner, band, first] = [
                    pl.ds(at // GROUP_LOCS * stride + (position * bands + band) * GROUP_LOCS, GROUP_LOCS)
                    for at in range(first, first + TILE_LOCS, GROUP_LOCS)
                ]
    return places


def mlp_into(mid, normed, up_ref, down_ref, waits=()):
    rows, width = mid.shape
    row_tile = rows // pl.cdiv(rows, ROW_TILE)
    tiles = [pl.ds(first, row_tile) for first in range(0, rows, row_tile)]
    norm_into(normed, mid)

    def step(here):
        raised = [dot(normed[mine, :], up_ref[:, here]) for mine in tiles]
        for mine, value in zip(tiles, raised):
            mid[mine, :] += dot(gelu(value).astype(BF16), down_ref[here, :])

    blocks = up_ref.shape[1] // width
    if waits:
        for block in range(blocks):
            waits[block]()
            step(pl.ds(block * width, width))
    else:
        loop(blocks, lambda block: step(aligned(block, width)))


def write_pieces(mid, outs, owners, bands, locations):
    for (owner, band, first), places in piece_places(owners, bands, locations).items():
        piece = jnp.concatenate([mid[place, :] for place in places], axis=0)
        outs[owners.index(owner)][band, first : first + TILE_LOCS, :] = piece.astype(BF16)


def finish(plan, rest, owners, bands, up_weight, down_weight):
    rows, width = rest.shape
    locations = rows // (len(owners) * bands)
    blocks = up_weight.shape[1] // width

    def kernel(up_hbm, down_hbm, rest_ref, *refs):
        outs, refs = refs[: len(owners)], refs[len(owners) :]
        mid, normed, up_ref, down_ref, sems = refs
        pairs = []
        for block in range(blocks):
            here = pl.ds(block * width, width)
            pairs.append(
                [
                    pltpu.make_async_copy(
                        up_hbm.at[:, here], up_ref.at[:, here], sems.at[2 * block]
                    ),
                    pltpu.make_async_copy(
                        down_hbm.at[here, :], down_ref.at[here, :], sems.at[2 * block + 1]
                    ),
                ]
            )

        def start(block):
            for copy in pairs[block]:
                copy.start()

        def wait(block):
            for copy in pairs[block]:
                copy.wait()
            if block + 2 < blocks:
                start(block + 2)

        for block in range(min(2, blocks)):
            start(block)
        mid[...] = rest_ref[...]
        waits = [functools.partial(wait, block) for block in range(blocks)]
        mlp_into(mid, normed, up_ref, down_ref, waits)
        write_pieces(mid, outs, owners, bands, locations)

    return call(
        kernel,
        [jax.ShapeDtypeStruct((bands, locations, width), BF16)] * len(owners),
        4 * rows * up_weight.size,
        2 * 2 * up_weight.size,
        limit=WIDE_LIMIT,
        in_specs=[ANY] * 2 + [VMEM],
        out_specs=[VMEM] * len(owners),
        scratch_shapes=[
            pltpu.VMEM((rows, width), F32),
            pltpu.VMEM((rows, width), BF16),
            pltpu.VMEM(up_weight.shape, BF16),
            pltpu.VMEM(down_weight.shape, BF16),
            pltpu.SemaphoreType.DMA((2 * blocks,)),
        ],
    )(up_weight, down_weight, rest)


def channel(plan, parts, now, later, fetch, channel_qkv, channel_out, up_weight, down_weight):
    groups, width = plan.groups, plan.width
    bands, _, locations, _ = parts.shape
    small = GROUP_LOCS
    assert locations % TILE_LOCS == 0
    owners = [*now, *later]
    group_rows = groups * bands * small
    rows = groups * bands * locations
    now_rows = rows * len(now) // groups
    count = len(now) + (len(later) > 0)

    def kernel(qkv_hbm, out_hbm, up_hbm, down_hbm, *refs):
        in_ref, *refs = refs
        outs, refs = refs[:count], refs[count:]
        mid, normed, packed, attended, qkv_ref, out_ref, up_ref, down_ref, sems, *held = refs
        if held:
            load = pltpu.make_async_copy(in_ref, held[0], sems.at[6])
            load.start()
            in_ref = held[0]
        me = lax.axis_index("band")
        columns = [pl.ds(first, width) for first in range(0, 3 * width, width)]
        copies = []
        for source, target, spots in (
            (qkv_hbm, qkv_ref, [(slice(None), spot) for spot in columns]),
            (out_hbm, out_ref, [(slice(None), slice(None))]),
            (up_hbm, up_ref, [(slice(None), slice(None))]),
            (down_hbm, down_ref, [(slice(None), slice(None))]),
        ):
            for spot in spots:
                copies.append(
                    pltpu.make_async_copy(
                        source.at[spot], target.at[spot], sems.at[len(copies)]
                    )
                )
        for copy in copies[: len(columns)]:
            copy.start()
        if held:
            load.wait()
        for (owner, band, first), places in piece_places(owners, bands, locations).items():
            piece = in_ref[band, me ^ owner, first : first + TILE_LOCS, :].astype(F32)
            for number, place in enumerate(places):
                mid[place, :] = piece[number * small : (number + 1) * small]
        norm_into(normed, mid)

        for number, here in enumerate(columns):
            copies[number].wait()
            copies[number + len(columns)].start()
            factor = QUERY_SCALE if number == 0 else 1.0
            packed[:, here] = (dot(normed[...], qkv_ref[:, here]) * factor).astype(BF16)
        pairs = width // LANES
        stacked = group_rows * (LANES // HEAD_DIM)
        one = lax.broadcasted_iota(jnp.int32, (stacked, group_rows), 0)
        other = lax.broadcasted_iota(jnp.int32, (stacked, group_rows), 1)
        mask = (one % small) == (other % small)

        def attention_step(pair):
            units, spots = [], []
            for first in range(0, rows, group_rows):
                mine = pl.ds(first, group_rows)
                query = packed[mine, aligned(pair, LANES)]
                keys = packed[mine, aligned(pair + pairs, LANES)]
                values = packed[mine, aligned(pair + 2 * pairs, LANES)]
                units.append((stack_heads(query), [keys], [with_ones(values)]))
                spots.append((mine, aligned(pair, LANES)))
            for spot, done in zip(spots, run_units(units, mask)):
                attended[spot] = done

        loop(pairs, attention_step, unroll=3)
        copies[3].wait()
        mid[...] += dot(attended[...], out_ref[...])
        copies[4].wait()
        copies[5].wait()
        if later:
            head = len(now) * bands * small
            tail = group_rows - head
            for group in range(rows // group_rows):
                at = group * group_rows
                outs[-1][pl.ds(group * tail, tail), :] = mid[pl.ds(at + head, tail), :]
                if group > 0:
                    mid[pl.ds(group * head, head), :] = mid[pl.ds(at, head), :]
        mine = pl.ds(0, now_rows)
        mlp_into(mid.at[mine, :], normed.at[mine, :], up_ref, down_ref)
        write_pieces(mid, outs, now, bands, locations)

    weights = [channel_qkv, channel_out, up_weight, down_weight]
    size = sum(weight.size for weight in weights)
    return call(
        kernel,
        [jax.ShapeDtypeStruct((bands, locations, width), BF16)] * len(now)
        + [jax.ShapeDtypeStruct((rows - now_rows, width), F32)] * (count - len(now)),
        2 * rows * size,
        2 * (2 * rows * width + size),
        limit=WIDE_LIMIT,
        in_specs=[ANY] * 4 + [ANY if fetch else VMEM],
        out_specs=[VMEM] * count,
        scratch_shapes=[
            pltpu.VMEM((rows, width), F32),
            pltpu.VMEM((rows, width), BF16),
            pltpu.VMEM((rows, 3 * width), BF16),
            pltpu.VMEM((rows, width), BF16),
        ]
        + [pltpu.VMEM(weight.shape, BF16) for weight in weights]
        + [pltpu.SemaphoreType.DMA((7,))]
        + [pltpu.VMEM(parts.shape, BF16)] * fetch,
    )(*weights, parts)


def restore(plan, keys, returned):
    def kernel(keys_ref, *refs):
        ins, out_ref = refs[:-1], refs[-1]
        group = lax.axis_index("band")
        place = lax.broadcasted_iota(jnp.int32, (plan.loc_dev, plan.loc_dev), 0)
        inner = place % plan.part_rows
        part = (place // plan.part_rows) % plan.share
        owner = (place // (plan.part_rows * plan.share)) % plan.groups ^ group
        window = place // plan.block
        wanted = window * plan.block + part * plan.rows + owner * plan.part_rows + inner
        pick = jnp.where(wanted.astype(F32) == keys_ref[...], 1.0, 0.0).astype(BF16)
        for band in range(plan.band_dev):
            rows = jnp.concatenate([ref[plan.spot(band)] for ref in ins], axis=0)
            out_ref[:, band, :] = lax.dot_general(
                pick, rows, (((0,), (0,)), ((), ())), preferred_element_type=F32
            ).astype(BF16)

    arrays = [array for chunk in returned for array in chunk]
    size = plan.loc_dev * plan.band_dev * plan.width
    return call(
        kernel,
        jax.ShapeDtypeStruct((plan.loc_dev, plan.band_dev, plan.width), BF16),
        2 * plan.loc_dev * size,
        4 * size,
    )(keys, *arrays)


def body(
    tokens,
    band_index,
    band_table,
    window_ids,
    spatial_qkv,
    spatial_out,
    channel_qkv,
    channel_out,
    up_weight,
    down_weight,
):
    plan = Plan(tokens)
    ids = window_ids.reshape(-1, LANES)
    *sent, rows, location_key, place_keys = arrange_first(plan, tokens, ids)
    arrived = [[exchange(value, "loc", CORES * step) for step, value in enumerate(sent)]]
    arranged = None
    for window in range(1, WINDOWS):
        *sent, arranged = arrange_next(plan, window, rows, place_keys, arrived[0][1:2])
        arrived.append([exchange(value, "loc", CORES * step) for step, value in enumerate(sent)])
    mids, behind = [], []
    for window, slots in enumerate(arrived):
        hide = int(window == 0)
        half = len(slots) // 2 if hide and plan.share == 1 else len(slots)
        owns, queries, all_keys, all_values = [], [], [], []
        tables = (band_index, band_table, spatial_qkv)
        for first in range(0, len(slots), half):
            if first > 0:
                behind = [arranged, queries[-1]]
            own = join_slots(plan, slots[first : first + half], behind, 0 if hide else LONG)
            query, keys, values = project(plan, [own], *tables, True, hide)
            owns.append(own)
            queries.append(query)
            all_keys.append(keys)
            all_values.append(values)
        if plan.share == 1:
            others = [exchange(own, "loc", 1) for own in owns]
            keys, values = project(plan, others, *tables, False, hide, queries[-1:])
            all_keys.append(keys)
            all_values.append(values)
        else:
            step = CORES * plan.share
            same = [list(range(at, at + step)) for at in range(0, plan.locs, step)]
            every = lax.all_gather(owns[0], "loc", axis_index_groups=same, tiled=True)
            keys, values = project(plan, [every], *tables, False, hide)
            all_keys, all_values = [keys], [values]
        mid, done = attend(
            plan, queries, all_keys, all_values, owns, band_index, band_table, spatial_out, hide
        )
        behind = [done]
        mids.append(mid)
    same = [
        [
            g * plan.locs + plan.row_at(spot) * CORES + core
            for spot in range(plan.rows_count)
            for g in range(plan.groups)
        ]
        for core in range(CORES)
    ]
    returned = []
    for mid in mids:
        parts = lax.all_to_all(
            mid.reshape(-1, plan.part_rows, plan.width),
            ("band", "loc"),
            0,
            0,
            axis_index_groups=same,
            tiled=True,
        )
        parts = parts.reshape(plan.band_dev, plan.share, plan.groups, plan.part_rows, plan.width)
        parts = parts.transpose(0, 2, 1, 3, 4).reshape(plan.band_dev, plan.groups, -1, plan.width)
        weights = (channel_qkv, channel_out, up_weight, down_weight)
        now, later = list(range(plan.groups)), []
        if mid is mids[-1] and plan.groups > 1:
            now, later = now[1:], now[:1]
        done = channel(plan, parts, now, later, mid is not mids[-1], *weights)
        if later:
            *done, rest = done
            done += finish(plan, rest, later, plan.band_dev, up_weight, down_weight)
        done = dict(zip([*now, *later], done))
        returned.append([exchange(done[step], "band", step) for step in range(plan.groups)])
    return restore(plan, location_key, returned)


def solution(mesh):
    placed = (P("loc", "band", None), P(), P(), P(), P(), P(), P(), P(), P(), P())
    return jax.shard_map(
        body, mesh=mesh, in_specs=placed, out_specs=P("loc", "band", None), check_vma=False
    )
```

```python
import functools

import jax
import jax.numpy as jnp
from jax import lax
from jax.experimental import pallas as pl
from jax.experimental.pallas import tpu as pltpu
from jax.sharding import PartitionSpec as P

HEADS = 12
HEAD_DIM = 64
WINDOWS = 2
CORES = 2
TILE_LOCS = 16
GROUP_LOCS = 8
UNIT_ROWS = 256
STEP_PAIRS = 3
ROW_TILE = 256
LANES = 128
QUERY_SCALE = HEAD_DIM ** (-0.5)
VMEM_LIMIT = 28 * 1024 * 1024
WIDE_LIMIT = 52 * 1024 * 1024
LONG = 2**36

F32 = jnp.float32
BF16 = jnp.bfloat16


def dot(left, right):
    return jnp.dot(left, right, preferred_element_type=F32)


def dot_t(left, right):
    return lax.dot_general(left, right, (((1,), (1,)), ((), ())), preferred_element_type=F32)


def norm_rows(values):
    centre = values - jnp.mean(values, axis=-1, keepdims=True)
    spread = jnp.mean(centre * centre, axis=-1, keepdims=True)
    return centre * lax.rsqrt(spread + 1e-05)


def gelu(values):
    inner = values * (0.7978845608028654 + 0.035677408136300125 * (values * values))
    return (0.5 * values) * (1.0 + jnp.tanh(inner))


def call(kernel, out_shape, flops, nbytes, limit=VMEM_LIMIT, **kwargs):
    return pl.pallas_call(
        kernel,
        out_shape=out_shape,
        compiler_params=pltpu.CompilerParams(vmem_limit_bytes=limit),
        cost_estimate=pl.CostEstimate(flops=flops, bytes_accessed=nbytes, transcendentals=0),
        **kwargs,
    )


def exchange(value, axis, step):
    if step == 0:
        return value
    return lax.ppermute(value, axis, [(i, i ^ step) for i in range(lax.axis_size(axis))])


class Plan:
    def __init__(self, tokens):
        self.loc_dev, self.band_dev, self.width = tokens.shape
        self.locs = lax.axis_size("loc")
        self.groups = lax.axis_size("band")
        self.rows_count = self.locs // CORES
        self.share = self.rows_count // self.band_dev
        assert self.share * self.band_dev * CORES == self.locs
        self.block = self.loc_dev // WINDOWS
        self.rows = self.block // self.share
        self.part_rows = self.rows // self.groups
        assert self.part_rows * self.groups * self.share * WINDOWS == self.loc_dev

    def spot(self, row, group):
        if self.share > 1:
            return row * self.groups + group
        place = (row + self.rows_count - 1) % self.rows_count
        turn = (group + self.rows_count * self.groups - place) % self.groups
        return turn * self.rows_count + place


def marker():
    return jax.ShapeDtypeStruct((8, LANES), F32)


def location_keys(plan, ids_ref):
    size = plan.loc_dev
    lines = size // LANES
    first = lax.axis_index("loc") * lines
    ids = jnp.concatenate([ids_ref[pl.ds(first + i, 1), :] for i in range(lines)], axis=1)
    ids = ids.astype(F32)
    row = jnp.broadcast_to(ids, (size, size))
    first = lax.broadcasted_iota(jnp.int32, (size, size), 0)
    second = lax.broadcasted_iota(jnp.int32, (size, size), 1)
    column = jnp.sum(jnp.where(first == second, row, 0.0), axis=1, keepdims=True)
    before = jnp.where((column == row) & (first < second), 1.0, 0.0)
    rank = jnp.sum(before, axis=0, keepdims=True)
    return ids * plan.block + rank


SMEM = pl.BlockSpec(memory_space=pltpu.SMEM)
VMEM = pl.BlockSpec(memory_space=pltpu.VMEM)
ANY = pl.BlockSpec(memory_space=pl.ANY)


def pick_rows(plan, window, place_keys, rows, outs):
    row = lax.axis_index("loc") // CORES
    place = lax.broadcasted_iota(jnp.int32, (plan.rows, rows.shape[0]), 0)
    for slot in range(plan.rows_count):
        peer = row ^ slot
        band, part = peer // plan.share, peer % plan.share
        wanted = place + (band * plan.loc_dev + window * plan.block + part * plan.rows)
        pick = jnp.where(wanted.astype(F32) == place_keys, 1.0, 0.0).astype(BF16)
        outs[slot][...] = dot(pick, rows[...]).astype(BF16)


def arrange_first(plan, tokens, ids):
    count = plan.rows_count
    total = plan.loc_dev * plan.band_dev
    assert plan.loc_dev <= 256

    def kernel(ids_ref, x_ref, *rest):
        outs, (rows_ref, keys_ref, place_ref) = rest[:count], rest[count:]
        keys = location_keys(plan, ids_ref)
        keys_ref[...] = keys
        place = lax.broadcasted_iota(jnp.int32, (plan.loc_dev, total), 1)
        location = lax.broadcasted_iota(jnp.int32, (plan.loc_dev, total), 0)
        spread = jnp.where(place // plan.band_dev == location, 1.0, 0.0).astype(BF16)
        wide = dot(jnp.broadcast_to(keys, (16, plan.loc_dev)).astype(BF16), spread)
        band = lax.broadcasted_iota(jnp.int32, (1, total), 1) % plan.band_dev
        place_ref[...] = wide[:1] + (band * plan.loc_dev).astype(F32)
        rows_ref[...] = x_ref[...].reshape(total, plan.width)
        pick_rows(plan, 0, place_ref[...], rows_ref, outs)

    return call(
        kernel,
        [jax.ShapeDtypeStruct((plan.rows, plan.width), BF16)] * count
        + [
            jax.ShapeDtypeStruct((total, plan.width), BF16),
            jax.ShapeDtypeStruct((1, plan.loc_dev), F32),
            jax.ShapeDtypeStruct((1, total), F32),
        ],
        2 * plan.loc_dev * tokens.size,
        4 * tokens.size,
        in_specs=[VMEM] * 2,
        out_specs=[VMEM] * (count + 3),
    )(ids, tokens)


def arrange_next(plan, window, rows, place_keys, after):
    count = plan.rows_count

    def kernel(rows_ref, place_ref, *rest):
        outs = rest[len(after) :]
        outs[-1][...] = jnp.zeros_like(outs[-1])
        pick_rows(plan, window, place_ref[...], rows_ref, outs[:-1])

    return call(
        kernel,
        [jax.ShapeDtypeStruct((plan.rows, plan.width), BF16)] * count + [marker()],
        2 * plan.loc_dev * rows.size,
        0,
        in_specs=[VMEM] * 2 + [ANY] * len(after),
        out_specs=[VMEM] * (count + 1),
    )(rows, place_keys, *after)


def join_slots(plan, slots, after, flops):
    count, rows = len(slots), plan.rows

    def kernel(*refs):
        out_ref, sems = refs[-2:]
        copies = [
            pltpu.make_async_copy(
                refs[slot], out_ref.at[pl.ds(slot * rows, rows), :], sems.at[slot]
            )
            for slot in range(count)
        ]
        for copy in copies:
            copy.start()
        for copy in copies:
            copy.wait()

    return call(
        kernel,
        jax.ShapeDtypeStruct((count * rows, plan.width), BF16),
        flops,
        0,
        in_specs=[ANY] * (count + len(after)),
        out_specs=VMEM,
        scratch_shapes=[pltpu.SemaphoreType.DMA((count,))],
    )(*slots, *after)


def embed_row(plan, index_ref, table_ref):
    band = lax.axis_index("loc") // (CORES * plan.share)
    number = index_ref[lax.axis_index("band") * plan.band_dev + band]
    return table_ref[pl.ds(number, 1), :]


def loop(count, step, unroll=1):
    lax.fori_loop(0, count, lambda i, _: (step(i), 0)[1], 0, unroll=unroll)


def aligned(index, size):
    return pl.ds(pl.multiple_of(index * size, size), size)


def norm_into(target, source):
    rows = source.shape[0]
    tile = rows // pl.cdiv(rows, ROW_TILE)
    for first in range(0, rows, tile):
        here = pl.ds(first, tile)
        target[here, :] = norm_rows(source[here, :]).astype(BF16)


def project(plan, tokens, index, table, weights, queries, hide, after=()):
    width = plan.width
    rows = sum(piece.shape[0] for piece in tokens)
    names = range(3) if queries else range(1, 3)

    def kernel(index_ref, table_ref, w_ref, *rest):
        x_refs, outs = rest[: len(tokens)], rest[len(tokens) + len(after) :]
        embed = embed_row(plan, index_ref, table_ref)
        at = 0
        for x_ref in x_refs:
            count = x_ref.shape[0]
            tile = min(count, ROW_TILE)
            for first in range(0, count, tile):
                normed = norm_rows(x_ref[pl.ds(first, tile), :].astype(F32) + embed).astype(BF16)
                here = pl.ds(at + first, tile)
                for ref, name in zip(outs, names):
                    value = dot(normed, w_ref[:, name * width : (name + 1) * width])
                    ref[here, :] = (value * QUERY_SCALE if name == 0 else value).astype(BF16)
            at += count

    return call(
        kernel,
        [jax.ShapeDtypeStruct((rows, width), BF16)] * len(names),
        hide * 2 * rows * width * len(names) * width,
        hide * 2 * ((1 + len(names)) * rows * width + 3 * width * width),
        in_specs=[SMEM, VMEM, VMEM] + [VMEM] * len(tokens) + [ANY] * len(after),
        out_specs=[VMEM] * len(names),
    )(index, table, weights, *tokens, *after)


def head_masks(rows):
    lane = lax.broadcasted_iota(jnp.int32, (rows, LANES), 1)
    return [(lane // HEAD_DIM) == head for head in range(LANES // HEAD_DIM)]


def stack_heads(query):
    return jnp.concatenate(
        [jnp.where(inside, query, jnp.zeros_like(query)) for inside in head_masks(query.shape[0])],
        axis=0,
    )


def join_heads(stacked):
    heads = LANES // HEAD_DIM
    rows = stacked.shape[0] // heads
    joined = stacked[:rows]
    for head, inside in list(enumerate(head_masks(rows)))[1:]:
        joined = jnp.where(inside, stacked[head * rows : (head + 1) * rows], joined)
    return joined


def with_ones(value):
    return jnp.concatenate([value, jnp.ones(value.shape, BF16)], axis=1)


def run_units(units, mask=None):
    def scores_of(unit):
        query, keys, _ = unit
        scores = [dot_t(query, piece) for piece in keys]
        if mask is not None:
            scores = [jnp.where(mask, piece, -1e30) for piece in scores]
        return scores

    results = []
    ahead = scores_of(units[0])
    for number, (_, _, values) in enumerate(units):
        scores = ahead
        if number + 1 < len(units):
            ahead = scores_of(units[number + 1])
        peak = functools.reduce(
            jnp.maximum, [jnp.max(piece, axis=-1, keepdims=True) for piece in scores]
        )
        total = None
        for piece, value in zip(scores, values):
            part = dot(jnp.exp(piece - peak).astype(BF16), value)
            total = part if total is None else total + part
        results.append(
            (join_heads(total[:, :LANES]) / join_heads(total[:, LANES:])).astype(BF16)
        )
    return results


def attend(plan, query, keys, values, tokens, index, table, spatial_out, hide):
    width, rows = plan.width, plan.rows
    pieces, sources = len(keys), len(query)
    counts = [piece.shape[0] for piece in query]
    total = sum(counts)
    pairs = width // LANES

    def kernel(index_ref, table_ref, w_ref, *rest):
        x_refs, rest = rest[:sources], rest[sources:]
        q_refs, rest = rest[:sources], rest[sources:]
        k_refs, rest = rest[:pieces], rest[pieces:]
        v_refs, (out_ref, marker_ref, result, added) = rest[:pieces], rest[pieces:]
        marker_ref[...] = jnp.zeros_like(marker_ref)

        def step(number):
            units, places = [], []
            for i in range(STEP_PAIRS):
                here = aligned(number * STEP_PAIRS + i, LANES)
                pair_keys = [ref[:, here] for ref in k_refs]
                pair_values = [with_ones(ref[:, here]) for ref in v_refs]
                at = 0
                for ref, count in zip(q_refs, counts):
                    unit = min(count, UNIT_ROWS)
                    for first in range(0, count, unit):
                        query_rows = ref[pl.ds(first, unit), here]
                        units.append((stack_heads(query_rows), pair_keys, pair_values))
                        places.append((pl.ds(at + first, unit), here))
                    at += count
            for place, done in zip(places, run_units(units)):
                result[place] = done

        loop(pairs // STEP_PAIRS, step)
        added[...] = dot(result[...], w_ref[...])
        embed = embed_row(plan, index_ref, table_ref)
        row = lax.axis_index("loc") // CORES
        slot = 0
        for ref, count in zip(x_refs, counts):
            for first in range(0, count, rows):
                start = ref[pl.ds(first, rows), :].astype(F32) + embed
                mid = (start + added[pl.ds(slot * rows, rows), :]).astype(BF16)
                for owner in range(plan.groups):
                    part = mid[owner * plan.part_rows : (owner + 1) * plan.part_rows]
                    out_ref[plan.spot(row ^ slot, owner)] = part
                slot += 1

    key_rows = sum(piece.shape[0] for piece in keys)
    return call(
        kernel,
        [
            jax.ShapeDtypeStruct((plan.rows_count * plan.groups, plan.part_rows, width), BF16),
            marker(),
        ],
        hide * 16 * total * key_rows * width,
        0,
        in_specs=[SMEM] + [VMEM] * (2 + 2 * sources + 2 * pieces),
        out_specs=[VMEM] * 2,
        scratch_shapes=[pltpu.VMEM((total, width), BF16), pltpu.VMEM((total, width), F32)],
    )(index, table, spatial_out, *tokens, *query, *keys, *values)


def piece_places(owners, bands, locations):
    stride = len(owners) * bands * GROUP_LOCS
    places = {}
    for position, owner in enumerate(owners):
        for band in range(bands):
            for first in range(0, locations, TILE_LOCS):
                places[owner, band, first] = [
                    pl.ds(at // GROUP_LOCS * stride + (position * bands + band) * GROUP_LOCS, GROUP_LOCS)
                    for at in range(first, first + TILE_LOCS, GROUP_LOCS)
                ]
    return places


def mlp_into(mid, normed, up_ref, down_ref, waits=()):
    rows, width = mid.shape
    row_tile = rows // pl.cdiv(rows, ROW_TILE)
    tiles = [pl.ds(first, row_tile) for first in range(0, rows, row_tile)]
    norm_into(normed, mid)

    def step(here):
        raised = [dot(normed[mine, :], up_ref[:, here]) for mine in tiles]
        for mine, value in zip(tiles, raised):
            mid[mine, :] += dot(gelu(value).astype(BF16), down_ref[here, :])

    blocks = up_ref.shape[1] // width
    if waits:
        for block in range(blocks):
            waits[block]()
            step(pl.ds(block * width, width))
    else:
        loop(blocks, lambda block: step(aligned(block, width)))


def write_pieces(mid, outs, owners, bands, locations):
    for (owner, band, first), places in piece_places(owners, bands, locations).items():
        piece = jnp.concatenate([mid[place, :] for place in places], axis=0)
        outs[owners.index(owner)][band, first : first + TILE_LOCS, :] = piece.astype(BF16)


def finish(plan, rest, owners, bands, up_weight, down_weight):
    rows, width = rest.shape
    locations = rows // (len(owners) * bands)
    blocks = up_weight.shape[1] // width

    def kernel(up_hbm, down_hbm, rest_ref, *refs):
        outs, refs = refs[: len(owners)], refs[len(owners) :]
        mid, normed, up_ref, down_ref, sems = refs
        pairs = []
        for block in range(blocks):
            here = pl.ds(block * width, width)
            pairs.append(
                [
                    pltpu.make_async_copy(
                        up_hbm.at[:, here], up_ref.at[:, here], sems.at[2 * block]
                    ),
                    pltpu.make_async_copy(
                        down_hbm.at[here, :], down_ref.at[here, :], sems.at[2 * block + 1]
                    ),
                ]
            )

        def start(block):
            for copy in pairs[block]:
                copy.start()

        def wait(block):
            for copy in pairs[block]:
                copy.wait()
            if block + 2 < blocks:
                start(block + 2)

        for block in range(min(2, blocks)):
            start(block)
        mid[...] = rest_ref[...]
        waits = [functools.partial(wait, block) for block in range(blocks)]
        mlp_into(mid, normed, up_ref, down_ref, waits)
        write_pieces(mid, outs, owners, bands, locations)

    return call(
        kernel,
        [jax.ShapeDtypeStruct((bands, locations, width), BF16)] * len(owners),
        4 * rows * up_weight.size,
        2 * 2 * up_weight.size,
        limit=WIDE_LIMIT,
        in_specs=[ANY] * 2 + [VMEM],
        out_specs=[VMEM] * len(owners),
        scratch_shapes=[
            pltpu.VMEM((rows, width), F32),
            pltpu.VMEM((rows, width), BF16),
            pltpu.VMEM(up_weight.shape, BF16),
            pltpu.VMEM(down_weight.shape, BF16),
            pltpu.SemaphoreType.DMA((2 * blocks,)),
        ],
    )(up_weight, down_weight, rest)


def channel(plan, parts, now, later, fetch, channel_qkv, channel_out, up_weight, down_weight):
    groups, width = plan.groups, plan.width
    bands, locations = plan.band_dev, parts.shape[1]
    small = GROUP_LOCS
    assert locations % TILE_LOCS == 0
    owners = [*now, *later]
    group_rows = groups * bands * small
    rows = groups * bands * locations
    now_rows = rows * len(now) // groups
    count = len(now) + (len(later) > 0)

    def kernel(qkv_hbm, out_hbm, up_hbm, down_hbm, *refs):
        in_ref, *refs = refs
        outs, refs = refs[:count], refs[count:]
        mid, normed, packed, attended, qkv_ref, out_ref, up_ref, down_ref, sems, *held = refs
        if held:
            load = pltpu.make_async_copy(in_ref, held[0], sems.at[6])
            load.start()
            in_ref = held[0]
        me = lax.axis_index("band")
        columns = [pl.ds(first, width) for first in range(0, 3 * width, width)]
        copies = []
        for source, target, spots in (
            (qkv_hbm, qkv_ref, [(slice(None), spot) for spot in columns]),
            (out_hbm, out_ref, [(slice(None), slice(None))]),
            (up_hbm, up_ref, [(slice(None), slice(None))]),
            (down_hbm, down_ref, [(slice(None), slice(None))]),
        ):
            for spot in spots:
                copies.append(
                    pltpu.make_async_copy(
                        source.at[spot], target.at[spot], sems.at[len(copies)]
                    )
                )
        for copy in copies[: len(columns)]:
            copy.start()
        if held:
            load.wait()
        for (owner, band, first), places in piece_places(owners, bands, locations).items():
            piece = in_ref[plan.spot(band, me ^ owner), first : first + TILE_LOCS, :].astype(F32)
            for number, place in enumerate(places):
                mid[place, :] = piece[number * small : (number + 1) * small]
        norm_into(normed, mid)

        for number, here in enumerate(columns):
            copies[number].wait()
            copies[number + len(columns)].start()
            factor = QUERY_SCALE if number == 0 else 1.0
            packed[:, here] = (dot(normed[...], qkv_ref[:, here]) * factor).astype(BF16)
        pairs = width // LANES
        stacked = group_rows * (LANES // HEAD_DIM)
        one = lax.broadcasted_iota(jnp.int32, (stacked, group_rows), 0)
        other = lax.broadcasted_iota(jnp.int32, (stacked, group_rows), 1)
        mask = (one % small) == (other % small)

        def attention_step(pair):
            units, spots = [], []
            for first in range(0, rows, group_rows):
                mine = pl.ds(first, group_rows)
                query = packed[mine, aligned(pair, LANES)]
                keys = packed[mine, aligned(pair + pairs, LANES)]
                values = packed[mine, aligned(pair + 2 * pairs, LANES)]
                units.append((stack_heads(query), [keys], [with_ones(values)]))
                spots.append((mine, aligned(pair, LANES)))
            for spot, done in zip(spots, run_units(units, mask)):
                attended[spot] = done

        loop(pairs, attention_step, unroll=3)
        copies[3].wait()
        mid[...] += dot(attended[...], out_ref[...])
        copies[4].wait()
        copies[5].wait()
        if later:
            head = len(now) * bands * small
            tail = group_rows - head
            for group in range(rows // group_rows):
                at = group * group_rows
                outs[-1][pl.ds(group * tail, tail), :] = mid[pl.ds(at + head, tail), :]
                if group > 0:
                    mid[pl.ds(group * head, head), :] = mid[pl.ds(at, head), :]
        mine = pl.ds(0, now_rows)
        mlp_into(mid.at[mine, :], normed.at[mine, :], up_ref, down_ref)
        write_pieces(mid, outs, now, bands, locations)

    weights = [channel_qkv, channel_out, up_weight, down_weight]
    size = sum(weight.size for weight in weights)
    return call(
        kernel,
        [jax.ShapeDtypeStruct((bands, locations, width), BF16)] * len(now)
        + [jax.ShapeDtypeStruct((rows - now_rows, width), F32)] * (count - len(now)),
        2 * rows * size,
        2 * (2 * rows * width + size),
        limit=WIDE_LIMIT,
        in_specs=[ANY] * 4 + [ANY if fetch else VMEM],
        out_specs=[VMEM] * count,
        scratch_shapes=[
            pltpu.VMEM((rows, width), F32),
            pltpu.VMEM((rows, width), BF16),
            pltpu.VMEM((rows, 3 * width), BF16),
            pltpu.VMEM((rows, width), BF16),
        ]
        + [pltpu.VMEM(weight.shape, BF16) for weight in weights]
        + [pltpu.SemaphoreType.DMA((7,))]
        + [pltpu.VMEM(parts.shape, BF16)] * fetch,
    )(*weights, parts)


def restore(plan, keys, returned):
    def kernel(keys_ref, *refs):
        ins, out_ref = refs[:-1], refs[-1]
        group = lax.axis_index("band")
        place = lax.broadcasted_iota(jnp.int32, (plan.loc_dev, plan.loc_dev), 0)
        inner = place % plan.part_rows
        part = (place // plan.part_rows) % plan.share
        owner = (place // (plan.part_rows * plan.share)) % plan.groups ^ group
        window = place // plan.block
        wanted = window * plan.block + part * plan.rows + owner * plan.part_rows + inner
        pick = jnp.where(wanted.astype(F32) == keys_ref[...], 1.0, 0.0).astype(BF16)
        for band in range(plan.band_dev):
            rows = jnp.concatenate([ref[band] for ref in ins], axis=0)
            out_ref[:, band, :] = lax.dot_general(
                pick, rows, (((0,), (0,)), ((), ())), preferred_element_type=F32
            ).astype(BF16)

    arrays = [array for chunk in returned for array in chunk]
    size = plan.loc_dev * plan.band_dev * plan.width
    return call(
        kernel,
        jax.ShapeDtypeStruct((plan.loc_dev, plan.band_dev, plan.width), BF16),
        2 * plan.loc_dev * size,
        4 * size,
    )(keys, *arrays)


def body(
    tokens,
    band_index,
    band_table,
    window_ids,
    spatial_qkv,
    spatial_out,
    channel_qkv,
    channel_out,
    up_weight,
    down_weight,
):
    plan = Plan(tokens)
    ids = window_ids.reshape(-1, LANES)
    *sent, rows, location_key, place_keys = arrange_first(plan, tokens, ids)
    arrived = [[exchange(value, "loc", CORES * step) for step, value in enumerate(sent)]]
    arranged = None
    for window in range(1, WINDOWS):
        *sent, arranged = arrange_next(plan, window, rows, place_keys, arrived[0][1:2])
        arrived.append([exchange(value, "loc", CORES * step) for step, value in enumerate(sent)])
    mids, behind = [], []
    for window, slots in enumerate(arrived):
        hide = int(window == 0)
        half = len(slots) // 2 if hide and plan.share == 1 else len(slots)
        owns, queries, all_keys, all_values = [], [], [], []
        tables = (band_index, band_table, spatial_qkv)
        for first in range(0, len(slots), half):
            if first > 0:
                behind = [arranged, queries[-1]]
            own = join_slots(plan, slots[first : first + half], behind, 0 if hide else LONG)
            query, keys, values = project(plan, [own], *tables, True, hide)
            owns.append(own)
            queries.append(query)
            all_keys.append(keys)
            all_values.append(values)
        if plan.share == 1:
            others = [exchange(own, "loc", 1) for own in owns]
            keys, values = project(plan, others, *tables, False, hide, queries[-1:])
            all_keys.append(keys)
            all_values.append(values)
        else:
            step = CORES * plan.share
            same = [list(range(at, at + step)) for at in range(0, plan.locs, step)]
            every = lax.all_gather(owns[0], "loc", axis_index_groups=same, tiled=True)
            keys, values = project(plan, [every], *tables, False, hide)
            all_keys, all_values = [keys], [values]
        mid, done = attend(
            plan, queries, all_keys, all_values, owns, band_index, band_table, spatial_out, hide
        )
        behind = [done]
        mids.append(mid)
    listed = [(r, g) for r in range(plan.rows_count) for g in range(plan.groups)]
    listed.sort(key=lambda device: plan.spot(*device))
    same = [[g * plan.locs + r * CORES + core for r, g in listed] for core in range(CORES)]
    returned = []
    for mid in mids:
        parts = lax.all_to_all(
            mid,
            ("band", "loc"),
            0,
            0,
            axis_index_groups=same,
            tiled=True,
        )
        if plan.share > 1:
            shape = (plan.band_dev, plan.share, plan.groups, plan.part_rows, plan.width)
            parts = parts.reshape(shape).transpose(0, 2, 1, 3, 4)
            parts = parts.reshape(plan.band_dev * plan.groups, -1, plan.width)
        weights = (channel_qkv, channel_out, up_weight, down_weight)
        now, later = list(range(plan.groups)), []
        if mid is mids[-1] and plan.groups > 1:
            now, later = now[1:], now[:1]
        done = channel(plan, parts, now, later, mid is not mids[-1], *weights)
        if later:
            *done, rest = done
            done += finish(plan, rest, later, plan.band_dev, up_weight, down_weight)
        done = dict(zip([*now, *later], done))
        returned.append([exchange(done[step], "band", step) for step in range(plan.groups)])
    return restore(plan, location_key, returned)


def solution(mesh):
    placed = (P("loc", "band", None), P(), P(), P(), P(), P(), P(), P(), P(), P())
    return jax.shard_map(
        body, mesh=mesh, in_specs=placed, out_specs=P("loc", "band", None), check_vma=False
    )
```

```python
import functools

import jax
import jax.numpy as jnp
from jax import lax
from jax.experimental import pallas as pl
from jax.experimental.pallas import tpu as pltpu
from jax.sharding import PartitionSpec as P

HEADS = 12
HEAD_DIM = 64
WINDOWS = 2
CORES = 2
TILE_LOCS = 16
GROUP_LOCS = 8
UNIT_ROWS = 256
STEP_PAIRS = 3
ROW_TILE = 256
LANES = 128
QUERY_SCALE = HEAD_DIM ** (-0.5)
VMEM_LIMIT = 28 * 1024 * 1024
WIDE_LIMIT = 52 * 1024 * 1024
LONG = 2**36

F32 = jnp.float32
BF16 = jnp.bfloat16


def dot(left, right):
    return jnp.dot(left, right, preferred_element_type=F32)


def dot_t(left, right):
    return lax.dot_general(left, right, (((1,), (1,)), ((), ())), preferred_element_type=F32)


def norm_rows(values):
    centre = values - jnp.mean(values, axis=-1, keepdims=True)
    spread = jnp.mean(centre * centre, axis=-1, keepdims=True)
    return centre * lax.rsqrt(spread + 1e-05)


def gelu(values):
    inner = values * (0.7978845608028654 + 0.035677408136300125 * (values * values))
    return (0.5 * values) * (1.0 + jnp.tanh(inner))


def call(kernel, out_shape, flops, nbytes, limit=VMEM_LIMIT, **kwargs):
    return pl.pallas_call(
        kernel,
        out_shape=out_shape,
        compiler_params=pltpu.CompilerParams(vmem_limit_bytes=limit),
        cost_estimate=pl.CostEstimate(flops=flops, bytes_accessed=nbytes, transcendentals=0),
        **kwargs,
    )


def exchange(value, axis, step):
    if step == 0:
        return value
    return lax.ppermute(value, axis, [(i, i ^ step) for i in range(lax.axis_size(axis))])


class Plan:
    def __init__(self, tokens):
        self.loc_dev, self.band_dev, self.width = tokens.shape
        self.locs = lax.axis_size("loc")
        self.groups = lax.axis_size("band")
        self.rows_count = self.locs // CORES
        self.share = self.rows_count // self.band_dev
        assert self.share * self.band_dev * CORES == self.locs
        self.block = self.loc_dev // WINDOWS
        self.rows = self.block // self.share
        self.part_rows = self.rows // self.groups
        assert self.part_rows * self.groups * self.share * WINDOWS == self.loc_dev

    def spot(self, row, group):
        if self.share > 1:
            return row * self.groups + group
        place = (row + self.rows_count - 1) % self.rows_count
        last = self.rows_count + self.groups - 2
        turn = (group + self.rows_count * self.groups + last - place) % self.groups
        return turn * self.rows_count + place


def marker():
    return jax.ShapeDtypeStruct((8, LANES), F32)


def location_keys(plan, ids_ref):
    size = plan.loc_dev
    lines = size // LANES
    first = lax.axis_index("loc") * lines
    ids = jnp.concatenate([ids_ref[pl.ds(first + i, 1), :] for i in range(lines)], axis=1)
    ids = ids.astype(F32)
    row = jnp.broadcast_to(ids, (size, size))
    first = lax.broadcasted_iota(jnp.int32, (size, size), 0)
    second = lax.broadcasted_iota(jnp.int32, (size, size), 1)
    column = jnp.sum(jnp.where(first == second, row, 0.0), axis=1, keepdims=True)
    before = jnp.where((column == row) & (first < second), 1.0, 0.0)
    rank = jnp.sum(before, axis=0, keepdims=True)
    return ids * plan.block + rank


SMEM = pl.BlockSpec(memory_space=pltpu.SMEM)
VMEM = pl.BlockSpec(memory_space=pltpu.VMEM)
ANY = pl.BlockSpec(memory_space=pl.ANY)


def pick_rows(plan, window, place_keys, rows, outs):
    row = lax.axis_index("loc") // CORES
    place = lax.broadcasted_iota(jnp.int32, (plan.rows, rows.shape[0]), 0)
    for slot in range(plan.rows_count):
        peer = row ^ slot
        band, part = peer // plan.share, peer % plan.share
        wanted = place + (band * plan.loc_dev + window * plan.block + part * plan.rows)
        pick = jnp.where(wanted.astype(F32) == place_keys, 1.0, 0.0).astype(BF16)
        outs[slot][...] = dot(pick, rows[...]).astype(BF16)


def arrange_first(plan, tokens, ids):
    count = plan.rows_count
    total = plan.loc_dev * plan.band_dev
    assert plan.loc_dev <= 256

    def kernel(ids_ref, x_ref, *rest):
        outs, (rows_ref, keys_ref, place_ref) = rest[:count], rest[count:]
        keys = location_keys(plan, ids_ref)
        keys_ref[...] = keys
        place = lax.broadcasted_iota(jnp.int32, (plan.loc_dev, total), 1)
        location = lax.broadcasted_iota(jnp.int32, (plan.loc_dev, total), 0)
        spread = jnp.where(place // plan.band_dev == location, 1.0, 0.0).astype(BF16)
        wide = dot(jnp.broadcast_to(keys, (16, plan.loc_dev)).astype(BF16), spread)
        band = lax.broadcasted_iota(jnp.int32, (1, total), 1) % plan.band_dev
        place_ref[...] = wide[:1] + (band * plan.loc_dev).astype(F32)
        rows_ref[...] = x_ref[...].reshape(total, plan.width)
        pick_rows(plan, 0, place_ref[...], rows_ref, outs)

    return call(
        kernel,
        [jax.ShapeDtypeStruct((plan.rows, plan.width), BF16)] * count
        + [
            jax.ShapeDtypeStruct((total, plan.width), BF16),
            jax.ShapeDtypeStruct((1, plan.loc_dev), F32),
            jax.ShapeDtypeStruct((1, total), F32),
        ],
        2 * plan.loc_dev * tokens.size,
        4 * tokens.size,
        in_specs=[VMEM] * 2,
        out_specs=[VMEM] * (count + 3),
    )(ids, tokens)


def arrange_next(plan, window, rows, place_keys, after):
    count = plan.rows_count

    def kernel(rows_ref, place_ref, *rest):
        outs = rest[len(after) :]
        outs[-1][...] = jnp.zeros_like(outs[-1])
        pick_rows(plan, window, place_ref[...], rows_ref, outs[:-1])

    return call(
        kernel,
        [jax.ShapeDtypeStruct((plan.rows, plan.width), BF16)] * count + [marker()],
        2 * plan.loc_dev * rows.size,
        0,
        in_specs=[VMEM] * 2 + [ANY] * len(after),
        out_specs=[VMEM] * (count + 1),
    )(rows, place_keys, *after)


def join_slots(plan, slots, after, flops):
    count, rows = len(slots), plan.rows

    def kernel(*refs):
        out_ref, sems = refs[-2:]
        copies = [
            pltpu.make_async_copy(
                refs[slot], out_ref.at[pl.ds(slot * rows, rows), :], sems.at[slot]
            )
            for slot in range(count)
        ]
        for copy in copies:
            copy.start()
        for copy in copies:
            copy.wait()

    return call(
        kernel,
        jax.ShapeDtypeStruct((count * rows, plan.width), BF16),
        flops,
        0,
        in_specs=[ANY] * (count + len(after)),
        out_specs=VMEM,
        scratch_shapes=[pltpu.SemaphoreType.DMA((count,))],
    )(*slots, *after)


def embed_row(plan, index_ref, table_ref):
    band = lax.axis_index("loc") // (CORES * plan.share)
    number = index_ref[lax.axis_index("band") * plan.band_dev + band]
    return table_ref[pl.ds(number, 1), :]


def loop(count, step, unroll=1):
    lax.fori_loop(0, count, lambda i, _: (step(i), 0)[1], 0, unroll=unroll)


def aligned(index, size):
    return pl.ds(pl.multiple_of(index * size, size), size)


def norm_into(target, source):
    rows = source.shape[0]
    tile = rows // pl.cdiv(rows, ROW_TILE)
    for first in range(0, rows, tile):
        here = pl.ds(first, tile)
        target[here, :] = norm_rows(source[here, :]).astype(BF16)


def project(plan, tokens, index, table, weights, queries, hide, after=()):
    width = plan.width
    rows = sum(piece.shape[0] for piece in tokens)
    names = range(3) if queries else range(1, 3)

    def kernel(index_ref, table_ref, w_ref, *rest):
        x_refs, outs = rest[: len(tokens)], rest[len(tokens) + len(after) :]
        embed = embed_row(plan, index_ref, table_ref)
        at = 0
        for x_ref in x_refs:
            count = x_ref.shape[0]
            tile = min(count, ROW_TILE)
            for first in range(0, count, tile):
                normed = norm_rows(x_ref[pl.ds(first, tile), :].astype(F32) + embed).astype(BF16)
                here = pl.ds(at + first, tile)
                for ref, name in zip(outs, names):
                    value = dot(normed, w_ref[:, name * width : (name + 1) * width])
                    ref[here, :] = (value * QUERY_SCALE if name == 0 else value).astype(BF16)
            at += count

    return call(
        kernel,
        [jax.ShapeDtypeStruct((rows, width), BF16)] * len(names),
        hide * 2 * rows * width * len(names) * width,
        hide * 2 * ((1 + len(names)) * rows * width + 3 * width * width),
        in_specs=[SMEM, VMEM, VMEM] + [VMEM] * len(tokens) + [ANY] * len(after),
        out_specs=[VMEM] * len(names),
    )(index, table, weights, *tokens, *after)


def head_masks(rows):
    lane = lax.broadcasted_iota(jnp.int32, (rows, LANES), 1)
    return [(lane // HEAD_DIM) == head for head in range(LANES // HEAD_DIM)]


def stack_heads(query):
    return jnp.concatenate(
        [jnp.where(inside, query, jnp.zeros_like(query)) for inside in head_masks(query.shape[0])],
        axis=0,
    )


def join_heads(stacked):
    heads = LANES // HEAD_DIM
    rows = stacked.shape[0] // heads
    joined = stacked[:rows]
    for head, inside in list(enumerate(head_masks(rows)))[1:]:
        joined = jnp.where(inside, stacked[head * rows : (head + 1) * rows], joined)
    return joined


def with_ones(value):
    return jnp.concatenate([value, jnp.ones(value.shape, BF16)], axis=1)


def run_units(units, mask=None):
    def scores_of(unit):
        query, keys, _ = unit
        scores = [dot_t(query, piece) for piece in keys]
        if mask is not None:
            scores = [jnp.where(mask, piece, -1e30) for piece in scores]
        return scores

    results = []
    ahead = scores_of(units[0])
    for number, (_, _, values) in enumerate(units):
        scores = ahead
        if number + 1 < len(units):
            ahead = scores_of(units[number + 1])
        peak = functools.reduce(
            jnp.maximum, [jnp.max(piece, axis=-1, keepdims=True) for piece in scores]
        )
        total = None
        for piece, value in zip(scores, values):
            part = dot(jnp.exp(piece - peak).astype(BF16), value)
            total = part if total is None else total + part
        results.append(
            (join_heads(total[:, :LANES]) / join_heads(total[:, LANES:])).astype(BF16)
        )
    return results


def attend(plan, query, keys, values, tokens, index, table, spatial_out, hide):
    width, rows = plan.width, plan.rows
    pieces, sources = len(keys), len(query)
    counts = [piece.shape[0] for piece in query]
    total = sum(counts)
    pairs = width // LANES

    def kernel(index_ref, table_ref, w_ref, *rest):
        x_refs, rest = rest[:sources], rest[sources:]
        q_refs, rest = rest[:sources], rest[sources:]
        k_refs, rest = rest[:pieces], rest[pieces:]
        v_refs, (out_ref, marker_ref, result, added) = rest[:pieces], rest[pieces:]
        marker_ref[...] = jnp.zeros_like(marker_ref)

        def step(number):
            units, places = [], []
            for i in range(STEP_PAIRS):
                here = aligned(number * STEP_PAIRS + i, LANES)
                pair_keys = [ref[:, here] for ref in k_refs]
                pair_values = [with_ones(ref[:, here]) for ref in v_refs]
                at = 0
                for ref, count in zip(q_refs, counts):
                    unit = min(count, UNIT_ROWS)
                    for first in range(0, count, unit):
                        query_rows = ref[pl.ds(first, unit), here]
                        units.append((stack_heads(query_rows), pair_keys, pair_values))
                        places.append((pl.ds(at + first, unit), here))
                    at += count
            for place, done in zip(places, run_units(units)):
                result[place] = done

        loop(pairs // STEP_PAIRS, step)
        added[...] = dot(result[...], w_ref[...])
        embed = embed_row(plan, index_ref, table_ref)
        row = lax.axis_index("loc") // CORES
        slot = 0
        for ref, count in zip(x_refs, counts):
            for first in range(0, count, rows):
                start = ref[pl.ds(first, rows), :].astype(F32) + embed
                mid = (start + added[pl.ds(slot * rows, rows), :]).astype(BF16)
                for owner in range(plan.groups):
                    part = mid[owner * plan.part_rows : (owner + 1) * plan.part_rows]
                    out_ref[plan.spot(row ^ slot, owner)] = part
                slot += 1

    key_rows = sum(piece.shape[0] for piece in keys)
    return call(
        kernel,
        [
            jax.ShapeDtypeStruct((plan.rows_count * plan.groups, plan.part_rows, width), BF16),
            marker(),
        ],
        hide * 16 * total * key_rows * width,
        0,
        in_specs=[SMEM] + [VMEM] * (2 + 2 * sources + 2 * pieces),
        out_specs=[VMEM] * 2,
        scratch_shapes=[pltpu.VMEM((total, width), BF16), pltpu.VMEM((total, width), F32)],
    )(index, table, spatial_out, *tokens, *query, *keys, *values)


def piece_places(owners, bands, locations):
    stride = len(owners) * bands * GROUP_LOCS
    places = {}
    for position, owner in enumerate(owners):
        for band in range(bands):
            for first in range(0, locations, TILE_LOCS):
                places[owner, band, first] = [
                    pl.ds(at // GROUP_LOCS * stride + (position * bands + band) * GROUP_LOCS, GROUP_LOCS)
                    for at in range(first, first + TILE_LOCS, GROUP_LOCS)
                ]
    return places


def mlp_into(mid, normed, up_ref, down_ref, waits=()):
    rows, width = mid.shape
    row_tile = rows // pl.cdiv(rows, ROW_TILE)
    tiles = [pl.ds(first, row_tile) for first in range(0, rows, row_tile)]
    norm_into(normed, mid)

    def step(here):
        raised = [dot(normed[mine, :], up_ref[:, here]) for mine in tiles]
        for mine, value in zip(tiles, raised):
            mid[mine, :] += dot(gelu(value).astype(BF16), down_ref[here, :])

    blocks = up_ref.shape[1] // width
    if waits:
        for block in range(blocks):
            waits[block]()
            step(pl.ds(block * width, width))
    else:
        loop(blocks, lambda block: step(aligned(block, width)))


def write_pieces(mid, outs, owners, bands, locations):
    for (owner, band, first), places in piece_places(owners, bands, locations).items():
        piece = jnp.concatenate([mid[place, :] for place in places], axis=0)
        outs[owners.index(owner)][band, first : first + TILE_LOCS, :] = piece.astype(BF16)


def finish(plan, rest, owners, bands, up_weight, down_weight):
    rows, width = rest.shape
    locations = rows // (len(owners) * bands)
    blocks = up_weight.shape[1] // width

    def kernel(up_hbm, down_hbm, rest_ref, *refs):
        outs, refs = refs[: len(owners)], refs[len(owners) :]
        mid, normed, up_ref, down_ref, sems = refs
        pairs = []
        for block in range(blocks):
            here = pl.ds(block * width, width)
            pairs.append(
                [
                    pltpu.make_async_copy(
                        up_hbm.at[:, here], up_ref.at[:, here], sems.at[2 * block]
                    ),
                    pltpu.make_async_copy(
                        down_hbm.at[here, :], down_ref.at[here, :], sems.at[2 * block + 1]
                    ),
                ]
            )

        def start(block):
            for copy in pairs[block]:
                copy.start()

        def wait(block):
            for copy in pairs[block]:
                copy.wait()
            if block + 2 < blocks:
                start(block + 2)

        for block in range(min(2, blocks)):
            start(block)
        mid[...] = rest_ref[...]
        waits = [functools.partial(wait, block) for block in range(blocks)]
        mlp_into(mid, normed, up_ref, down_ref, waits)
        write_pieces(mid, outs, owners, bands, locations)

    return call(
        kernel,
        [jax.ShapeDtypeStruct((bands, locations, width), BF16)] * len(owners),
        4 * rows * up_weight.size,
        2 * 2 * up_weight.size,
        limit=WIDE_LIMIT,
        in_specs=[ANY] * 2 + [VMEM],
        out_specs=[VMEM] * len(owners),
        scratch_shapes=[
            pltpu.VMEM((rows, width), F32),
            pltpu.VMEM((rows, width), BF16),
            pltpu.VMEM(up_weight.shape, BF16),
            pltpu.VMEM(down_weight.shape, BF16),
            pltpu.SemaphoreType.DMA((2 * blocks,)),
        ],
    )(up_weight, down_weight, rest)


def channel(plan, parts, now, later, fetch, channel_qkv, channel_out, up_weight, down_weight):
    groups, width = plan.groups, plan.width
    bands, locations = plan.band_dev, parts.shape[1]
    small = GROUP_LOCS
    assert locations % TILE_LOCS == 0
    owners = [*now, *later]
    group_rows = groups * bands * small
    rows = groups * bands * locations
    now_rows = rows * len(now) // groups
    count = len(now) + (len(later) > 0)

    def kernel(qkv_hbm, out_hbm, up_hbm, down_hbm, *refs):
        in_ref, *refs = refs
        outs, refs = refs[:count], refs[count:]
        mid, normed, packed, attended, qkv_ref, out_ref, up_ref, down_ref, sems, *held = refs
        if held:
            load = pltpu.make_async_copy(in_ref, held[0], sems.at[6])
            load.start()
            in_ref = held[0]
        me = lax.axis_index("band")
        columns = [pl.ds(first, width) for first in range(0, 3 * width, width)]
        copies = []
        for source, target, spots in (
            (qkv_hbm, qkv_ref, [(slice(None), spot) for spot in columns]),
            (out_hbm, out_ref, [(slice(None), slice(None))]),
            (up_hbm, up_ref, [(slice(None), slice(None))]),
            (down_hbm, down_ref, [(slice(None), slice(None))]),
        ):
            for spot in spots:
                copies.append(
                    pltpu.make_async_copy(
                        source.at[spot], target.at[spot], sems.at[len(copies)]
                    )
                )
        for copy in copies[: len(columns)]:
            copy.start()
        if held:
            load.wait()
        for (owner, band, first), places in piece_places(owners, bands, locations).items():
            piece = in_ref[plan.spot(band, me ^ owner), first : first + TILE_LOCS, :].astype(F32)
            for number, place in enumerate(places):
                mid[place, :] = piece[number * small : (number + 1) * small]
        norm_into(normed, mid)

        for number, here in enumerate(columns):
            copies[number].wait()
            copies[number + len(columns)].start()
            factor = QUERY_SCALE if number == 0 else 1.0
            packed[:, here] = (dot(normed[...], qkv_ref[:, here]) * factor).astype(BF16)
        pairs = width // LANES
        stacked = group_rows * (LANES // HEAD_DIM)
        one = lax.broadcasted_iota(jnp.int32, (stacked, group_rows), 0)
        other = lax.broadcasted_iota(jnp.int32, (stacked, group_rows), 1)
        mask = (one % small) == (other % small)

        def attention_step(pair):
            units, spots = [], []
            for first in range(0, rows, group_rows):
                mine = pl.ds(first, group_rows)
                query = packed[mine, aligned(pair, LANES)]
                keys = packed[mine, aligned(pair + pairs, LANES)]
                values = packed[mine, aligned(pair + 2 * pairs, LANES)]
                units.append((stack_heads(query), [keys], [with_ones(values)]))
                spots.append((mine, aligned(pair, LANES)))
            for spot, done in zip(spots, run_units(units, mask)):
                attended[spot] = done

        loop(pairs, attention_step, unroll=3)
        copies[3].wait()
        mid[...] += dot(attended[...], out_ref[...])
        copies[4].wait()
        copies[5].wait()
        if later:
            head = len(now) * bands * small
            tail = group_rows - head
            for group in range(rows // group_rows):
                at = group * group_rows
                outs[-1][pl.ds(group * tail, tail), :] = mid[pl.ds(at + head, tail), :]
                if group > 0:
                    mid[pl.ds(group * head, head), :] = mid[pl.ds(at, head), :]
        mine = pl.ds(0, now_rows)
        mlp_into(mid.at[mine, :], normed.at[mine, :], up_ref, down_ref)
        write_pieces(mid, outs, now, bands, locations)

    weights = [channel_qkv, channel_out, up_weight, down_weight]
    size = sum(weight.size for weight in weights)
    return call(
        kernel,
        [jax.ShapeDtypeStruct((bands, locations, width), BF16)] * len(now)
        + [jax.ShapeDtypeStruct((rows - now_rows, width), F32)] * (count - len(now)),
        2 * rows * size,
        2 * (2 * rows * width + size),
        limit=WIDE_LIMIT,
        in_specs=[ANY] * 4 + [ANY if fetch else VMEM],
        out_specs=[VMEM] * count,
        scratch_shapes=[
            pltpu.VMEM((rows, width), F32),
            pltpu.VMEM((rows, width), BF16),
            pltpu.VMEM((rows, 3 * width), BF16),
            pltpu.VMEM((rows, width), BF16),
        ]
        + [pltpu.VMEM(weight.shape, BF16) for weight in weights]
        + [pltpu.SemaphoreType.DMA((7,))]
        + [pltpu.VMEM(parts.shape, BF16)] * fetch,
    )(*weights, parts)


def restore(plan, keys, returned):
    def kernel(keys_ref, *refs):
        ins, out_ref = refs[:-1], refs[-1]
        group = lax.axis_index("band")
        place = lax.broadcasted_iota(jnp.int32, (plan.loc_dev, plan.loc_dev), 0)
        inner = place % plan.part_rows
        part = (place // plan.part_rows) % plan.share
        owner = (place // (plan.part_rows * plan.share)) % plan.groups ^ group
        window = place // plan.block
        wanted = window * plan.block + part * plan.rows + owner * plan.part_rows + inner
        pick = jnp.where(wanted.astype(F32) == keys_ref[...], 1.0, 0.0).astype(BF16)
        for band in range(plan.band_dev):
            rows = jnp.concatenate([ref[band] for ref in ins], axis=0)
            out_ref[:, band, :] = lax.dot_general(
                pick, rows, (((0,), (0,)), ((), ())), preferred_element_type=F32
            ).astype(BF16)

    arrays = [array for chunk in returned for array in chunk]
    size = plan.loc_dev * plan.band_dev * plan.width
    return call(
        kernel,
        jax.ShapeDtypeStruct((plan.loc_dev, plan.band_dev, plan.width), BF16),
        2 * plan.loc_dev * size,
        4 * size,
    )(keys, *arrays)


def body(
    tokens,
    band_index,
    band_table,
    window_ids,
    spatial_qkv,
    spatial_out,
    channel_qkv,
    channel_out,
    up_weight,
    down_weight,
):
    plan = Plan(tokens)
    ids = window_ids.reshape(-1, LANES)
    *sent, rows, location_key, place_keys = arrange_first(plan, tokens, ids)
    arrived = [[exchange(value, "loc", CORES * step) for step, value in enumerate(sent)]]
    arranged = None
    for window in range(1, WINDOWS):
        *sent, arranged = arrange_next(plan, window, rows, place_keys, arrived[0][1:2])
        arrived.append([exchange(value, "loc", CORES * step) for step, value in enumerate(sent)])
    mids, behind = [], []
    for window, slots in enumerate(arrived):
        hide = int(window == 0)
        half = len(slots) // 2 if hide and plan.share == 1 else len(slots)
        owns, queries, all_keys, all_values = [], [], [], []
        tables = (band_index, band_table, spatial_qkv)
        for first in range(0, len(slots), half):
            if first > 0:
                behind = [arranged, queries[-1]]
            own = join_slots(plan, slots[first : first + half], behind, 0 if hide else LONG)
            query, keys, values = project(plan, [own], *tables, True, hide)
            owns.append(own)
            queries.append(query)
            all_keys.append(keys)
            all_values.append(values)
        if plan.share == 1:
            others = [exchange(own, "loc", 1) for own in owns]
            keys, values = project(plan, others, *tables, False, hide, queries[-1:])
            all_keys.append(keys)
            all_values.append(values)
        else:
            step = CORES * plan.share
            same = [list(range(at, at + step)) for at in range(0, plan.locs, step)]
            every = lax.all_gather(owns[0], "loc", axis_index_groups=same, tiled=True)
            keys, values = project(plan, [every], *tables, False, hide)
            all_keys, all_values = [keys], [values]
        mid, done = attend(
            plan, queries, all_keys, all_values, owns, band_index, band_table, spatial_out, hide
        )
        behind = [done]
        mids.append(mid)
    listed = [(r, g) for r in range(plan.rows_count) for g in range(plan.groups)]
    listed.sort(key=lambda device: plan.spot(*device))
    same = [[g * plan.locs + r * CORES + core for r, g in listed] for core in range(CORES)]
    returned = []
    for mid in mids:
        parts = lax.all_to_all(
            mid,
            ("band", "loc"),
            0,
            0,
            axis_index_groups=same,
            tiled=True,
        )
        if plan.share > 1:
            shape = (plan.band_dev, plan.share, plan.groups, plan.part_rows, plan.width)
            parts = parts.reshape(shape).transpose(0, 2, 1, 3, 4)
            parts = parts.reshape(plan.band_dev * plan.groups, -1, plan.width)
        weights = (channel_qkv, channel_out, up_weight, down_weight)
        now, later = list(range(plan.groups)), []
        if mid is mids[-1] and plan.groups > 1:
            now, later = now[1:], now[:1]
        done = channel(plan, parts, now, later, mid is not mids[-1], *weights)
        if later:
            *done, rest = done
            done += finish(plan, rest, later, plan.band_dev, up_weight, down_weight)
        done = dict(zip([*now, *later], done))
        returned.append([exchange(done[step], "band", step) for step in range(plan.groups)])
    return restore(plan, location_key, returned)


def solution(mesh):
    placed = (P("loc", "band", None), P(), P(), P(), P(), P(), P(), P(), P(), P())
    return jax.shard_map(
        body, mesh=mesh, in_specs=placed, out_specs=P("loc", "band", None), check_vma=False
    )
```
